32 devices in a mesh: dp: 8 (over z, x), row: 2 (over core), col: 2 (over y).
Axes of the slice: x: 2, y: 2, z: 4, core: 2. Of those that a mesh axis runs over, the one named last changes fastest.
Arguments:
- hidden_in: bfloat16 [8, 1024, 1536], P('dp', ('row', 'col')), may hold values from -6 to 6
- segment_ids: int32 [8, 1024], P('dp'), may hold values from 0 to 3, never falling along the last dimension, each value on 1 to 512 neighbouring positions
- routes: int32 [8, 1024, 6], P('dp', ('row', 'col')), may hold values from 0 to 15, all different within a row; in each aligned block of 256 rows (0 to 255, 256 to 511, ..., all dimensions but the last counted through in order) at most 192 rows name the same one
- out_grad: bfloat16 [8, 1024, 1536], P('dp', ('row', 'col')), may hold values from -6 to 6
- vectors: float32 [22928], replicated, as said below
- vectors_first: float32 [22928], replicated, may hold values from -32 to 32
- vectors_second: float32 [22928], replicated, may hold values from 108.1344 to 430.08
- in_weight: float32 [1536, 48, 128], P('dp', ('row', 'col')), may hold values from -0.15625 to 0.15625
- in_weight_first: float32 [1536, 48, 128], P('dp', ('row', 'col')), may hold values from -16 to 16
- in_weight_second: float32 [1536, 48, 128], P('dp', ('row', 'col')), may hold values from 38.5024 to 155.648
- step_weight: float32 [1536, 48], P('dp', ('row', 'col')), may hold values from -0.15625 to 0.15625
- step_weight_first: float32 [1536, 48], P('dp', ('row', 'col')), may hold values from -6 to 6
- step_weight_second: float32 [1536, 48], P('dp', ('row', 'col')), as said below
- out_weight: float32 [48, 64, 1536], P(('row', 'col'), None, 'dp'), may hold values from -0.109375 to 0.109375
- out_weight_first: float32 [48, 64, 1536], P(('row', 'col'), None, 'dp'), may hold values from -64 to 64
- out_weight_second: float32 [48, 64, 1536], P(('row', 'col'), None, 'dp'), may hold values from 430.8992 to 1720.32
- state_weight: float32 [1536, 256], P(('dp', 'row', 'col')), may hold values from -0.15625 to 0.15625
- state_weight_first: float32 [1536, 256], P(('dp', 'row', 'col')), may hold values from -32 to 32
- state_weight_second: float32 [1536, 256], P(('dp', 'row', 'col')), may hold values from 108.1344 to 430.08
- router: float32 [1536, 16], P(('dp', 'row', 'col')), may hold values from -0.078125 to 0.078125
- router_first: float32 [1536, 16], P(('dp', 'row', 'col')), may hold values from -160 to 160
- router_second: float32 [1536, 16], P(('dp', 'row', 'col')), may hold values from 2831.1553 to 11324.621
- shared_up: float32 [1536, 2048], P(('dp', 'row', 'col')), may hold values from -0.15625 to 0.15625
- shared_up_first: float32 [1536, 2048], P(('dp', 'row', 'col')), may hold values from -32 to 32
- shared_up_second: float32 [1536, 2048], P(('dp', 'row', 'col')), may hold values from 108.1344 to 430.08
- shared_down: float32 [1024, 1536], P(('dp', 'row', 'col')), may hold values from -0.1875 to 0.1875
- shared_down_first: float32 [1024, 1536], P(('dp', 'row', 'col')), may hold values from -16 to 16
- shared_down_second: float32 [1024, 1536], P(('dp', 'row', 'col')), may hold values from 38.5024 to 155.648
- expert_gate_up: float32 [16, 1536, 1024], P('dp', ('row', 'col')), may hold values from -0.15625 to 0.15625
- expert_gate_up_first: float32 [16, 1536, 1024], P('dp', ('row', 'col')), may hold values from -3.5 to 3.5
- expert_gate_up_second: float32 [16, 1536, 1024], P('dp', ('row', 'col')), may hold values from 1.62816 to 6.4512
- expert_down: float32 [16, 512, 1536], P('dp', ('row', 'col')), may hold values from -0.25 to 0.25
- expert_down_first: float32 [16, 512, 1536], P('dp', ('row', 'col')), may hold values from -1.75 to 1.75
- expert_down_second: float32 [16, 512, 1536], P('dp', ('row', 'col')), may hold values from 0.39936 to 1.62816
Outputs:
- hidden_out: bfloat16 [8, 1024, 1536], P('dp', ('row', 'col'))
- input_grad: float32 [8, 1024, 1536], P('dp', ('row', 'col'))
- vectors_first_new: float32 [22928], replicated
- vectors_second_new: float32 [22928], replicated
- vectors_new: float32 [22928], replicated
- in_weight_first_new: float32 [1536, 48, 128], P('dp', ('row', 'col'))
- in_weight_second_new: float32 [1536, 48, 128], P('dp', ('row', 'col'))
- in_weight_new: float32 [1536, 48, 128], P('dp', ('row', 'col'))
- step_weight_first_new: float32 [1536, 48], P('dp', ('row', 'col'))
- step_weight_second_new: float32 [1536, 48], P('dp', ('row', 'col'))
- step_weight_new: float32 [1536, 48], P('dp', ('row', 'col'))
- out_weight_first_new: float32 [48, 64, 1536], P(('row', 'col'), None, 'dp')
- out_weight_second_new: float32 [48, 64, 1536], P(('row', 'col'), None, 'dp')
- out_weight_new: float32 [48, 64, 1536], P(('row', 'col'), None, 'dp')
- state_weight_first_new: float32 [1536, 256], P(('dp', 'row', 'col'))
- state_weight_second_new: float32 [1536, 256], P(('dp', 'row', 'col'))
- state_weight_new: float32 [1536, 256], P(('dp', 'row', 'col'))
- router_first_new: float32 [1536, 16], P(('dp', 'row', 'col'))
- router_second_new: float32 [1536, 16], P(('dp', 'row', 'col'))
- router_new: float32 [1536, 16], P(('dp', 'row', 'col'))
- shared_up_first_new: float32 [1536, 2048], P(('dp', 'row', 'col'))
- shared_up_second_new: float32 [1536, 2048], P(('dp', 'row', 'col'))
- shared_up_new: float32 [1536, 2048], P(('dp', 'row', 'col'))
- shared_down_first_new: float32 [1024, 1536], P(('dp', 'row', 'col'))
- shared_down_second_new: float32 [1024, 1536], P(('dp', 'row', 'col'))
- shared_down_new: float32 [1024, 1536], P(('dp', 'row', 'col'))
- expert_up_first_new: float32 [16, 1536, 1024], P('dp', ('row', 'col'))
- expert_up_second_new: float32 [16, 1536, 1024], P('dp', ('row', 'col'))
- expert_up_new: float32 [16, 1536, 1024], P('dp', ('row', 'col'))
- expert_down_first_new: float32 [16, 512, 1536], P('dp', ('row', 'col'))
- expert_down_second_new: float32 [16, 512, 1536], P('dp', ('row', 'col'))
- expert_down_new: float32 [16, 512, 1536], P('dp', ('row', 'col'))
The draws below stay inside these ranges and needn't reach their ends.
Inputs may be any that keep to these rules, and one draw needn't show every extreme that they name: `routes`: each row names 6 different experts; among the rows of one device no expert is named more than 192 times, a bound that some block reaches. `segment_ids`: along each sequence the numbers never fall; each document has at most half of 1024 positions, one exactly that many. `vectors`: the gains, the skip gains and the convolution taps are as stated in the reference program; gains are positive. `step_weight_second`: Positive.
All inputs are finite; a program needn't handle non-finite values.
Results may differ from the reference program's by a relative error of at most 0.023.
Values may be sent and summed in bfloat16 or wider, within the bound.
A program may use at most 320 MiB of HBM per device.

```python
import math
import jax
import jax.numpy as jnp
import numpy as np
from jax import lax

MODEL_WIDTH = 1536
HEADS = 48
HEAD_DIM = 64
STATE = 128
FF_E = 512
FF_S = 1024
TOPK = 6
KW = 4
GROUP = 256
STEP = 10
TOK_DEV = 256
INNER = 3072
PACKED_LENGTH = 1024
PACKED_COUNT = 8
TOKENS = 8192
EXPERTS = 16
CAP = 192
NVEC = 22928


def head_rates(key):
    key = jax.random.fold_in(key, 29)
    subkeys = jax.random.split(key, 2)
    decay_log = jax.random.uniform(subkeys[0], (HEADS,), jnp.float32, 0.0, 2.77)
    step_init = jnp.exp(jax.random.uniform(subkeys[1], (HEADS,), jnp.float32, -6.2, -2.3))
    return (decay_log, step_init)


def draw_vectors(key, part):
    decay_log, step_init = head_rates(key)
    key = jax.random.fold_in(key, 11)
    subkeys = jax.random.split(key, 7)
    xbc_width = INNER + 2 * STATE
    gain_low, gain_high = (0.6, 1.5)
    gain_one = jax.random.uniform(subkeys[0], (MODEL_WIDTH,), jnp.float32, gain_low, gain_high)
    gain_two = jax.random.uniform(subkeys[1], (MODEL_WIDTH,), jnp.float32, gain_low, gain_high)
    gain_inner = jax.random.uniform(subkeys[2], (INNER,), jnp.float32, gain_low, gain_high)
    conv_bias = 0.2 * jax.random.normal(subkeys[3], (xbc_width,), jnp.float32)
    conv_taps = 0.5 * jax.random.normal(subkeys[4], (KW * xbc_width,), jnp.float32)
    skip_gain = jax.random.uniform(subkeys[6], (HEADS,), jnp.float32, 0.5, 1.5)
    step_bias = jnp.log(jnp.expm1(step_init))
    return jnp.concatenate([gain_one, gain_two, gain_inner, conv_bias, conv_taps, decay_log, skip_gain, step_bias])


def draw_step_weight_second(key, part):
    decay_log, step_init = head_rates(key)
    key = jax.random.fold_in(key, 13)
    rate = jnp.exp(decay_log)
    step_eff = 1.8 * step_init
    memory = jnp.clip(1.0 / (rate * step_eff), 1.0, PACKED_LENGTH / 4.0)
    grad_square = 1.2 * TOKENS * step_eff * step_eff * memory * (4.4 + 0.85 * rate) ** 2
    factor = jnp.exp(jax.random.uniform(key, (MODEL_WIDTH, HEADS), jnp.float32, 0.0, 1.3863))
    return 0.0526 * grad_square[None, :] * factor


def levels(own_key, shape, cuts, smallest, high):
    def one(dim, blocks):
        heights = jax.random.uniform(jax.random.fold_in(jax.random.fold_in(own_key, 6), dim), (blocks,), jnp.float32, smallest / len(cuts), high / len(cuts))
        return jnp.repeat(jnp.exp(heights), shape[dim] // blocks).reshape((-1,) + (1,) * (len(shape) - dim - 1))

    loudness = one(*cuts[0])
    for cut in cuts[1:]:
        loudness = loudness * one(*cut)
    return loudness


def length_profile(amount, total, most, slope):
    portions = [(1 << 20) // math.isqrt(rank ** slope) + 1 for rank in range(2, amount + 1)]
    spare, given = total - most - (amount - 1), [1] * (amount - 1)
    while spare > 0:
        candidates = [i for i in range(amount - 1) if given[i] < most]
        pool, budget = sum([portions[i] for i in candidates]), spare
        for i in candidates:
            more = min(most - given[i], max(1, budget * portions[i] // pool), spare)
            given[i] = given[i] + more
            spare = spare - more
    return np.array([most] + given)


def ragged_sizes(own_key, count, total, most, skew):
    if count == 2:
        one = jax.random.randint(own_key, (), max(1, total - most), min(most, total - 1) + 1)
        return jnp.stack([one, total - one])
    tallies = jnp.asarray(length_profile(count, total, most, skew), jnp.int32)
    pairs = (count - 1) // 2
    giver, sink = tallies[1:1 + 2 * pairs:2], tallies[2:2 + 2 * pairs:2]
    margin = jnp.minimum(giver - 1, most - sink)
    moved = jax.random.randint(jax.random.fold_in(own_key, 1), (pairs,), 0, 1 << 20) % (margin + 1)
    tallies = tallies.at[1:1 + 2 * pairs:2].set(giver - moved).at[2:2 + 2 * pairs:2].set(sink + moved)
    return tallies[jax.random.permutation(jax.random.fold_in(own_key, 2), count)]


def routed_block(stream_key, own, number, rows, number_of, top, reach, skew):
    ranking = jax.random.permutation(stream_key, number_of)
    heavy_load, ordinary = portions_of(number_of, rows * top, reach, skew, True), portions_of(number_of, rows * top, reach, skew, False)
    places = jnp.arange(number_of)

    def named(lengths, rotation):
        used = int((lengths > 0).sum())
        fixed = max(1, used // 4)
        passed = fixed + (places - fixed + rotation * (used - fixed)) % max(1, number_of - fixed)
        return jnp.zeros((number_of,), jnp.int32).at[ranking[jnp.where(places < fixed, places, passed)]].set(jnp.asarray(lengths, jnp.int32))

    lengths = jnp.where(number % 4 == 0, named(heavy_load, number // 4), named(ordinary, number - number // 4 - 1))
    mixed = jax.random.permutation(jax.random.fold_in(own, 3), number_of)
    giver, taker = mixed[0:number_of // 2 * 2:2], mixed[1:number_of // 2 * 2:2]
    room = jnp.minimum(lengths[giver] - 1, reach - lengths[taker]) // 2
    room = jnp.where((giver == ranking[0]) | (taker == ranking[0]) | (lengths[taker] == 0), 0, jnp.maximum(room, 0))
    passed = jax.random.randint(jax.random.fold_in(own, 4), (number_of // 2,), 0, 1 << 20) % (room + 1)
    lengths = lengths.at[giver].add(-passed).at[taker].add(passed)
    items = jnp.searchsorted(jnp.cumsum(lengths), jnp.arange(rows * top), side="right").astype(jnp.int32)
    listing = items.reshape(top, rows).T
    listing = listing[jax.random.permutation(jax.random.fold_in(own, 1), rows)]
    rotation = jax.random.randint(jax.random.fold_in(own, 2), (rows, 1), 0, top)
    return jnp.take_along_axis(listing, (jnp.arange(top)[None, :] + rotation) % top, axis=1)


def portions_of(count, total, most, slope, full):
    loads = [(1 << 20) // math.isqrt(grade ** slope) + 1 for grade in range(1, count + 1)]
    largest = most if full else min(most, max(-(-total // count), total * loads[0] // sum(loads)))
    least = 1 if total - largest >= count - 1 else 0
    counts, spare = [largest] + [least] * (count - 1), total - largest - least * (count - 1)
    while spare > 0:
        candidates = [i for i in range(1, count) if counts[i] < largest] or [i for i in range(1, count) if counts[i] < most]
        mass, budget = sum([loads[i] for i in candidates]), spare
        for i in candidates:
            more = min(most - counts[i], max(1, budget * loads[i] // mass), spare)
            counts[i] = counts[i] + more
            spare = spare - more
    return np.array(counts)


def noise(stream_key, extent, scale, reach, cuts=(), kind=jnp.bfloat16):
    entries = scale * jax.random.normal(stream_key, extent, jnp.float32)
    if cuts:
        entries = entries * levels(stream_key, extent, cuts, -0.22, 0.18)
    return jnp.clip(entries, -reach, reach).astype(kind)


def setup_inputs(seed: int = 0) -> dict:
    key_list = jax.random.split(jax.random.key(seed), 35)
    hidden_in = noise(key_list[0], (PACKED_COUNT, PACKED_LENGTH, MODEL_WIDTH), 1.0, 6.0, ((0, 8), (1, 4)))
    segment_ids = jax.vmap(lambda own: jnp.searchsorted(jnp.cumsum(ragged_sizes(own, 4, PACKED_LENGTH, PACKED_LENGTH // 2, 0)), jnp.arange(PACKED_LENGTH), side="right"))(jax.random.split(key_list[1], PACKED_COUNT)).reshape((PACKED_COUNT, PACKED_LENGTH)).astype(jnp.int32)
    routes_keys = jax.random.split(jax.random.fold_in(key_list[2], 1), PACKED_COUNT * PACKED_LENGTH // TOK_DEV)
    routes_turns = jax.random.permutation(jax.random.fold_in(key_list[2], 3), PACKED_COUNT * PACKED_LENGTH // TOK_DEV)
    routes = jax.vmap(lambda own, number: routed_block(jax.random.fold_in(key_list[2], 2), own, number, TOK_DEV, EXPERTS, TOPK, CAP, 2))(routes_keys, routes_turns).reshape((PACKED_COUNT, PACKED_LENGTH, TOPK))
    out_grad = noise(key_list[3], (PACKED_COUNT, PACKED_LENGTH, MODEL_WIDTH), 1.0, 6.0, ((0, 8), (1, 4)))
    vectors = draw_vectors(jax.random.fold_in(key_list[34], 71), 0)
    vectors_first = noise(key_list[5], (NVEC,), (0.055 * TOKENS ** 0.5), 32.0, (), jnp.float32)
    vectors_second = jnp.clip(jnp.exp(jax.random.uniform(key_list[6], (NVEC,), jnp.float32, math.log(108.1344), math.log(430.08))), 108.1344, 430.08)
    in_weight = noise(key_list[7], (MODEL_WIDTH, HEADS, 2 * HEAD_DIM), MODEL_WIDTH ** -0.5, 0.15625, ((0, 8), (1, 4)), jnp.float32)
    in_weight_first = noise(key_list[8], (MODEL_WIDTH, HEADS, 2 * HEAD_DIM), (0.033 * TOKENS ** 0.5), 16.0, ((0, 8), (1, 4)), jnp.float32)
    in_weight_second = jnp.clip(jnp.exp(math.log(155.648) - 1.3968765 * jax.random.uniform(key_list[9], (MODEL_WIDTH, HEADS, 2 * HEAD_DIM), jnp.float32) ** levels(key_list[9], (MODEL_WIDTH, HEADS, 2 * HEAD_DIM), ((0, 8), (1, 4)), -0.2, 0.2)), 38.5024, 155.648)
    step_weight = noise(key_list[10], (MODEL_WIDTH, HEADS), MODEL_WIDTH ** -0.5, 0.15625, ((0, 8), (1, 4)), jnp.float32)
    step_weight_first = noise(key_list[11], (MODEL_WIDTH, HEADS), (0.011 * TOKENS ** 0.5), 6.0, ((0, 8), (1, 4)), jnp.float32)
    step_weight_second = draw_step_weight_second(jax.random.fold_in(key_list[34], 71), 0)
    out_weight = noise(key_list[13], (HEADS, HEAD_DIM, MODEL_WIDTH), INNER ** -0.5, 0.109375, ((0, 4), (2, 8)), jnp.float32)
    out_weight_first = noise(key_list[14], (HEADS, HEAD_DIM, MODEL_WIDTH), (0.11 * TOKENS ** 0.5), 64.0, ((0, 4), (2, 8)), jnp.float32)
    out_weight_second = jnp.clip(jnp.exp(math.log(1720.32) - 1.3843914 * jax.random.uniform(key_list[15], (HEADS, HEAD_DIM, MODEL_WIDTH), jnp.float32) ** levels(key_list[15], (HEADS, HEAD_DIM, MODEL_WIDTH), ((0, 4), (2, 8)), -0.2, 0.2)), 430.8992, 1720.32)
    state_weight = noise(key_list[16], (MODEL_WIDTH, 2 * STATE), MODEL_WIDTH ** -0.5, 0.15625, ((0, 32),), jnp.float32)
    state_weight_first = noise(key_list[17], (MODEL_WIDTH, 2 * STATE), (0.055 * TOKENS ** 0.5), 32.0, ((0, 32),), jnp.float32)
    state_weight_second = jnp.clip(jnp.exp(math.log(430.08) - 1.3805963 * jax.random.uniform(key_list[18], (MODEL_WIDTH, 2 * STATE), jnp.float32) ** levels(key_list[18], (MODEL_WIDTH, 2 * STATE), ((0, 32),), -0.2, 0.2)), 108.1344, 430.08)
    router = noise(key_list[19], (MODEL_WIDTH, EXPERTS), (0.5 * MODEL_WIDTH ** -0.5), 0.078125, ((0, 32),), jnp.float32)
    router_first = noise(key_list[20], (MODEL_WIDTH, EXPERTS), (0.0119 * (MODEL_WIDTH * TOKENS * TOPK / EXPERTS) ** 0.5), 160.0, ((0, 32),), jnp.float32)
    router_second = jnp.clip(jnp.exp(math.log(11324.621) - 1.3862944 * jax.random.uniform(key_list[21], (MODEL_WIDTH, EXPERTS), jnp.float32) ** levels(key_list[21], (MODEL_WIDTH, EXPERTS), ((0, 32),), -0.2, 0.2)), 2831.1553, 11324.621)
    shared_up = noise(key_list[22], (MODEL_WIDTH, 2 * FF_S), MODEL_WIDTH ** -0.5, 0.15625, ((0, 32),), jnp.float32)
    shared_up_first = noise(key_list[23], (MODEL_WIDTH, 2 * FF_S), (0.055 * TOKENS ** 0.5), 32.0, ((0, 32),), jnp.float32)
    shared_up_second = jnp.clip(jnp.exp(math.log(430.08) - 1.3805963 * jax.random.uniform(key_list[24], (MODEL_WIDTH, 2 * FF_S), jnp.float32) ** levels(key_list[24], (MODEL_WIDTH, 2 * FF_S), ((0, 32),), -0.2, 0.2)), 108.1344, 430.08)
    shared_down = noise(key_list[25], (FF_S, MODEL_WIDTH), FF_S ** -0.5, 0.1875, ((0, 32),), jnp.float32)
    shared_down_first = noise(key_list[26], (FF_S, MODEL_WIDTH), (0.033 * TOKENS ** 0.5), 16.0, ((0, 32),), jnp.float32)
    shared_down_second = jnp.clip(jnp.exp(math.log(155.648) - 1.3968765 * jax.random.uniform(key_list[27], (FF_S, MODEL_WIDTH), jnp.float32) ** levels(key_list[27], (FF_S, MODEL_WIDTH), ((0, 32),), -0.2, 0.2)), 38.5024, 155.648)
    expert_gate_up = noise(key_list[28], (EXPERTS, MODEL_WIDTH, 2 * FF_E), MODEL_WIDTH ** -0.5, 0.15625, ((0, 8), (1, 4)), jnp.float32)
    expert_gate_up_first = noise(key_list[29], (EXPERTS, MODEL_WIDTH, 2 * FF_E), (0.011 * (TOKENS * TOPK / EXPERTS) ** 0.5), 3.5, ((0, 8), (1, 4)), jnp.float32)
    expert_gate_up_second = jnp.clip(jnp.exp(math.log(6.4512) - 1.37681562 * jax.random.uniform(key_list[30], (EXPERTS, MODEL_WIDTH, 2 * FF_E), jnp.float32) ** levels(key_list[30], (EXPERTS, MODEL_WIDTH, 2 * FF_E), ((0, 8), (1, 4)), -0.2, 0.2)), 1.62816, 6.4512)
    expert_down = noise(key_list[31], (EXPERTS, FF_E, MODEL_WIDTH), FF_E ** -0.5, 0.25, ((0, 8), (1, 4)), jnp.float32)
    expert_down_first = noise(key_list[32], (EXPERTS, FF_E, MODEL_WIDTH), (0.0055 * (TOKENS * TOPK / EXPERTS) ** 0.5), 1.75, ((0, 8), (1, 4)), jnp.float32)
    expert_down_second = jnp.clip(jnp.exp(math.log(1.62816) - 1.4053426 * jax.random.uniform(key_list[33], (EXPERTS, FF_E, MODEL_WIDTH), jnp.float32) ** levels(key_list[33], (EXPERTS, FF_E, MODEL_WIDTH), ((0, 8), (1, 4)), -0.2, 0.2)), 0.39936, 1.62816)
    return {"hidden_in": hidden_in, "segment_ids": segment_ids, "routes": routes, "out_grad": out_grad, "vectors": vectors, "vectors_first": vectors_first, "vectors_second": vectors_second, "in_weight": in_weight, "in_weight_first": in_weight_first, "in_weight_second": in_weight_second, "step_weight": step_weight, "step_weight_first": step_weight_first, "step_weight_second": step_weight_second, "out_weight": out_weight, "out_weight_first": out_weight_first, "out_weight_second": out_weight_second, "state_weight": state_weight, "state_weight_first": state_weight_first, "state_weight_second": state_weight_second, "router": router, "router_first": router_first, "router_second": router_second, "shared_up": shared_up, "shared_up_first": shared_up_first, "shared_up_second": shared_up_second, "shared_down": shared_down, "shared_down_first": shared_down_first, "shared_down_second": shared_down_second, "expert_gate_up": expert_gate_up, "expert_gate_up_first": expert_gate_up_first, "expert_gate_up_second": expert_gate_up_second, "expert_down": expert_down, "expert_down_first": expert_down_first, "expert_down_second": expert_down_second}


@jax.custom_vjp
def low(v):
    return lax.optimization_barrier(v.astype(jnp.bfloat16)).astype(jnp.float32)

@jax.custom_vjp
def low_back(v):
    return v

def low_keep(v):
    return (low(v), None)

def low_pass(kept, grad):
    return (grad,)

def back_keep(v):
    return (v, None)

def back_low(kept, grad):
    return (low(grad),)
low.defvjp(low_keep, low_pass)
low_back.defvjp(back_keep, back_low)

def rms_scale(values):
    return lax.rsqrt(lax.optimization_barrier(jnp.mean(values * values, axis=-1, keepdims=True)) + 1e-05)

def silu_gate(pre_values):
    half_size = pre_values.shape[-1] // 2
    return jax.nn.silu(pre_values[..., :half_size]) * pre_values[..., half_size:]

def causal_conv(values, segment, taps, bias_vec):
    length = values.shape[0]
    kernel_width = taps.shape[0]
    padded = jnp.concatenate([jnp.zeros((kernel_width - 1, values.shape[1]), jnp.float32), values], 0)
    seg_pad = jnp.concatenate([jnp.full((kernel_width - 1,), -1, jnp.int32), segment], 0)
    summed = jnp.zeros_like(values) + bias_vec[None, :]
    for offset in range(kernel_width):
        shifted = padded[offset:offset + length]
        same_seg = (seg_pad[offset:offset + length] == segment).astype(jnp.float32)
        summed = summed + taps[offset][None, :] * shifted * same_seg[:, None]
    return summed

def state_scan(inputs_x, matrix_b, matrix_c, log_decay, step_size, segment, skip_gain):
    length, head_count, head_size = inputs_x.shape
    blocks = length // GROUP
    lower_mask = jnp.arange(GROUP)[:, None] >= jnp.arange(GROUP)[None, :]

    def block_step(carried, pieces):
        state_mat, last_seg = carried
        block_x, block_b, block_c, block_decay, block_dt, block_seg = pieces
        cumulative = jnp.cumsum(block_decay, axis=0)
        same_seg = (block_seg[:, None] == block_seg[None, :]) & lower_mask
        differ = jnp.minimum(cumulative[:, None, :] - cumulative[None, :, :], 0.0)
        scores = jnp.dot(block_c, block_b.T, precision=lax.Precision.HIGHEST)
        mixing = jnp.where(same_seg[:, :, None], jnp.exp(differ), 0.0) * scores[:, :, None] * block_dt[None, :, :]
        within = jnp.einsum('tsh,shp->thp', mixing, block_x, precision=lax.Precision.HIGHEST)
        carried_in = (block_seg == last_seg).astype(jnp.float32)
        from_state = jnp.einsum('tn,hpn->thp', block_c, state_mat, precision=lax.Precision.HIGHEST)
        from_state = from_state * (jnp.exp(cumulative) * carried_in[:, None])[:, :, None]
        outputs = within + from_state + skip_gain[None, :, None] * block_x
        final_seg = block_seg[GROUP - 1]
        keep_mask = (block_seg == final_seg).astype(jnp.float32)
        tail_weight = jnp.exp(cumulative[GROUP - 1][None, :] - cumulative) * keep_mask[:, None] * block_dt
        carry_on = jnp.exp(cumulative[GROUP - 1]) * (last_seg == final_seg).astype(jnp.float32)
        new_state = state_mat * carry_on[:, None, None] + jnp.einsum('sh,shp,sn->hpn', tail_weight, block_x, block_b, precision=lax.Precision.HIGHEST)
        return ((new_state, final_seg), outputs)
    pieces = (inputs_x.reshape(blocks, GROUP, head_count, head_size), matrix_b.reshape(blocks, GROUP, STATE), matrix_c.reshape(blocks, GROUP, STATE), log_decay.reshape(blocks, GROUP, head_count), step_size.reshape(blocks, GROUP, head_count), segment.reshape(blocks, GROUP))
    initial = (jnp.zeros((head_count, head_size, STATE), jnp.float32), jnp.array(-1, jnp.int32))
    finished, outputs = lax.scan(jax.checkpoint(block_step), initial, pieces)
    return outputs.reshape(length, head_count, head_size)

def mixer_core(projected, step_raw, state_raw, vectors, segment, head_start):
    length, head_count, double = projected.shape
    head_size = double // 2
    local_width = head_count * head_size
    xbc_width = INNER + 2 * STATE
    offset_bias = 2 * MODEL_WIDTH + INNER
    offset_conv = offset_bias + xbc_width
    offset_head = offset_conv + KW * xbc_width
    channel_start = head_start * head_size
    gain_inner = lax.dynamic_slice_in_dim(vectors, 2 * MODEL_WIDTH + channel_start, local_width)
    bias_all = vectors[offset_bias:offset_conv]
    conv_all = vectors[offset_conv:offset_head].reshape(KW, xbc_width)
    bias_local = jnp.concatenate([lax.dynamic_slice_in_dim(bias_all, channel_start, local_width), bias_all[INNER:]])
    conv_local = jnp.concatenate([lax.dynamic_slice_in_dim(conv_all, channel_start, local_width, axis=1), conv_all[:, INNER:]], axis=1)
    decay_log = lax.dynamic_slice_in_dim(vectors, offset_head + head_start, head_count)
    skip_gain = lax.dynamic_slice_in_dim(vectors, offset_head + HEADS + head_start, head_count)
    step_bias = lax.dynamic_slice_in_dim(vectors, offset_head + 2 * HEADS + head_start, head_count)
    gate_part = projected[:, :, :head_size]
    inner_part = projected[:, :, head_size:].reshape(length, local_width)
    mixed = causal_conv(jnp.concatenate([inner_part, state_raw], axis=1), segment, conv_local, bias_local)
    active = jax.nn.silu(mixed)
    inputs_x = active[:, :local_width].reshape(length, head_count, head_size)
    matrix_b = active[:, local_width:local_width + STATE]
    matrix_c = active[:, local_width + STATE:]
    step_size = jax.nn.softplus(step_raw + step_bias[None, :])
    log_decay = -jnp.exp(decay_log)[None, :] * step_size
    scanned = state_scan(inputs_x, matrix_b, matrix_c, log_decay, step_size, segment, skip_gain)
    gated = (scanned * jax.nn.silu(gate_part)).reshape(length, local_width)
    return (gated * gain_inner[None, :], lax.optimization_barrier(jnp.sum(gated * gated, axis=1)))

def adamw_weight_update(weight, grad, first, second, rate, decay):
    first_new = 0.9 * first + 0.1 * grad
    second_new = 0.95 * second + 0.05 * grad * grad
    corrected_one = first_new / (1.0 - 0.9 ** STEP)
    corrected_two = second_new / (1.0 - 0.95 ** STEP)
    weight_new = weight - rate * (corrected_one / (jnp.sqrt(corrected_two) + 1e-08) + decay * weight)
    return (first_new, second_new, weight_new)

def reference(hidden_in, segment_ids, routes, out_grad, vectors, vectors_first, vectors_second, in_weight, in_weight_first, in_weight_second, step_weight, step_weight_first, step_weight_second, out_weight, out_weight_first, out_weight_second, state_weight, state_weight_first, state_weight_second, router, router_first, router_second, shared_up, shared_up_first, shared_up_second, shared_down, shared_down_first, shared_down_second, expert_gate_up, expert_gate_up_first, expert_gate_up_second, expert_down, expert_down_first, expert_down_second):
    device_count = TOKENS // TOK_DEV
    flat_routes = routes.reshape(-1).astype(jnp.int32)
    onehot = (flat_routes[:, None] == jnp.arange(EXPERTS, dtype=jnp.int32)[None, :]).astype(jnp.int32)
    per_block = onehot.reshape(device_count, TOK_DEV * TOPK, EXPERTS)
    rank_in_block = lax.optimization_barrier(jnp.sum((jnp.cumsum(per_block, axis=1).astype(jnp.int32) - 1) * per_block, axis=2)).astype(jnp.int32).reshape(-1)
    owner = jnp.arange(TOKENS * TOPK, dtype=jnp.int32) // (TOK_DEV * TOPK)
    slot_index = ((flat_routes * device_count + owner) * CAP + rank_in_block).astype(jnp.int32)
    slot_table = jnp.full((EXPERTS * device_count * CAP,), TOKENS * TOPK, jnp.int32)
    slot_table = slot_table.at[slot_index].set(jnp.arange(TOKENS * TOPK, dtype=jnp.int32))
    slot_table = slot_table.reshape(EXPERTS, device_count * CAP)
    route_ids = routes.reshape(TOKENS, TOPK).astype(jnp.int32)

    def forward(residual, vec, w_in, w_step, w_out, w_state, w_router, w_shared_up, w_shared_down, w_expert_up, w_expert_down):
        gain_one = vec[0:MODEL_WIDTH]
        gain_two = vec[MODEL_WIDTH:2 * MODEL_WIDTH]
        normed_one = low(residual * rms_scale(residual) * gain_one[None, :])
        in_low = low(w_in)
        step_low = low(w_step)
        state_low = low(w_state)
        out_low = low(w_out).reshape(INNER, MODEL_WIDTH)

        def sequence_mix(pieces):
            normed_seq, segment = pieces
            projected = low_back(jnp.einsum('ld,dhk->lhk', normed_seq, in_low, precision=lax.Precision.HIGHEST))
            step_raw = low_back(jnp.dot(normed_seq, step_low, precision=lax.Precision.HIGHEST))
            state_raw = jnp.dot(normed_seq, state_low, precision=lax.Precision.HIGHEST)
            gated_scaled, squares = mixer_core(projected, step_raw, state_raw, vec, segment, 0)
            scale_two = lax.rsqrt(squares / INNER + 1e-05)
            valued = low(gated_scaled)
            return scale_two[:, None] * low_back(jnp.dot(valued, out_low, precision=lax.Precision.HIGHEST))
        mixed = lax.map(jax.checkpoint(sequence_mix), (normed_one.reshape(PACKED_COUNT, PACKED_LENGTH, MODEL_WIDTH), segment_ids))
        residual_two = residual + mixed.reshape(TOKENS, MODEL_WIDTH)
        normed_two = low(residual_two * rms_scale(residual_two) * gain_two[None, :])
        logits = low_back(jnp.dot(normed_two, low(w_router), precision=lax.Precision.HIGHEST))
        gate_weights = jax.nn.softmax(jnp.take_along_axis(logits, route_ids, axis=1), axis=-1)
        route_rows = low_back(jnp.repeat(normed_two, TOPK, axis=0))
        padded = jnp.concatenate([route_rows, jnp.zeros((1, MODEL_WIDTH), jnp.float32)], 0)

        def expert_run(pieces):
            index_rows, weight_up, weight_down = pieces
            hidden_pre = low_back(jnp.dot(padded[index_rows], weight_up, precision=lax.Precision.HIGHEST))
            hidden_act = low(silu_gate(hidden_pre))
            return low(jnp.dot(hidden_act, weight_down, precision=lax.Precision.HIGHEST))
        expert_out = lax.map(jax.checkpoint(expert_run), (slot_table, low(w_expert_up), low(w_expert_down)))
        routed = low_back(expert_out.reshape(-1, MODEL_WIDTH)[slot_index]).reshape(TOKENS, TOPK, MODEL_WIDTH)
        mixture = lax.optimization_barrier(jnp.sum(gate_weights[:, :, None] * routed, axis=1))
        shared_pre = low_back(jnp.dot(normed_two, low(w_shared_up), precision=lax.Precision.HIGHEST))
        shared_out = low_back(jnp.dot(low(silu_gate(shared_pre)), low(w_shared_down), precision=lax.Precision.HIGHEST))
        return residual_two + mixture + shared_out
    layer_output, backward = jax.vjp(forward, hidden_in.reshape(TOKENS, MODEL_WIDTH).astype(jnp.float32), vectors, in_weight, step_weight, out_weight, state_weight, router, shared_up, shared_down, expert_gate_up, expert_down)
    layer_gradients = backward(out_grad.reshape(TOKENS, MODEL_WIDTH).astype(jnp.float32))
    vector_moment, vector_variance, vector_weight = adamw_weight_update(vectors, layer_gradients[1], vectors_first, vectors_second, 0.3, 0.0)
    input_moment, input_variance, input_weight = adamw_weight_update(in_weight, layer_gradients[2], in_weight_first, in_weight_second, MODEL_WIDTH ** (-0.5), 0.1)
    step_moment, step_variance, step_matrix = adamw_weight_update(step_weight, layer_gradients[3], step_weight_first, step_weight_second, MODEL_WIDTH ** (-0.5), 0.1)
    output_moment, output_variance, output_weight = adamw_weight_update(out_weight, layer_gradients[4], out_weight_first, out_weight_second, INNER ** (-0.5), 0.1)
    state_moment, state_variance, state_matrix = adamw_weight_update(state_weight, layer_gradients[5], state_weight_first, state_weight_second, MODEL_WIDTH ** (-0.5), 0.1)
    router_moment, router_variance, router_weight = adamw_weight_update(router, layer_gradients[6], router_first, router_second, 0.5 * MODEL_WIDTH ** (-0.5), 0.1)
    shared_up_moment, shared_up_variance, shared_up_weight = adamw_weight_update(shared_up, layer_gradients[7], shared_up_first, shared_up_second, MODEL_WIDTH ** (-0.5), 0.1)
    shared_down_moment, shared_down_variance, shared_down_weight = adamw_weight_update(shared_down, layer_gradients[8], shared_down_first, shared_down_second, FF_S ** (-0.5), 0.1)
    expert_up_moment, expert_up_variance, expert_up_weight = adamw_weight_update(expert_gate_up, layer_gradients[9], expert_gate_up_first, expert_gate_up_second, MODEL_WIDTH ** (-0.5), 0.1)
    expert_down_moment, expert_down_variance, expert_down_weight = adamw_weight_update(expert_down, layer_gradients[10], expert_down_first, expert_down_second, FF_E ** (-0.5), 0.1)
    return (layer_output.reshape(PACKED_COUNT, PACKED_LENGTH, MODEL_WIDTH).astype(jnp.bfloat16), layer_gradients[0].reshape(PACKED_COUNT, PACKED_LENGTH, MODEL_WIDTH), vector_moment, vector_variance, vector_weight, input_moment, input_variance, input_weight, step_moment, step_variance, step_matrix, output_moment, output_variance, output_weight, state_moment, state_variance, state_matrix, router_moment, router_variance, router_weight, shared_up_moment, shared_up_variance, shared_up_weight, shared_down_moment, shared_down_variance, shared_down_weight, expert_up_moment, expert_up_variance, expert_up_weight, expert_down_moment, expert_down_variance, expert_down_weight)
```

```python
import functools

import jax
import jax.numpy as jnp
from jax import lax
from jax.experimental import pallas as pl
from jax.experimental.pallas import tpu as pltpu
from jax.sharding import PartitionSpec as P

STATE = 128
KW = 4
BLK = 128
F32 = jnp.float32
BF16 = jnp.bfloat16


def dot_f32(a, b, dims=(((1,), (0,)), ((), ()))):
    return lax.dot_general(a, b, dims, preferred_element_type=F32)


def dot_exact(a, b, dims=(((1,), (0,)), ((), ()))):
    return lax.dot_general(
        a, b, dims, precision=lax.Precision.HIGHEST, preferred_element_type=F32
    )


def spread(values, width):
    rows = values.shape[0]
    low = lax.broadcasted_iota(jnp.int32, (rows, 128), 1) < 64
    parts = []
    for pair in range(width // 128):
        left = jnp.broadcast_to(values[:, 2 * pair : 2 * pair + 1], (rows, 128))
        right = jnp.broadcast_to(values[:, 2 * pair + 1 : 2 * pair + 2], (rows, 128))
        parts.append(jnp.where(low, left, right))
    return jnp.concatenate(parts, axis=1)


def head_sums(values):
    width = values.shape[1]
    ones = (
        lax.broadcasted_iota(jnp.int32, (width, 128), 0) // 64
        == lax.broadcasted_iota(jnp.int32, (width, 128), 1)
    ).astype(BF16)
    high = values.astype(BF16)
    rest = (values - high.astype(F32)).astype(BF16)
    return dot_f32(high, ones) + dot_f32(rest, ones)


def block_common(width, start, index, proj_ref, ss_ref, aux_ref, seg_ref, par_ref):
    rows = pl.ds(start, BLK)
    before = pl.ds(pl.multiple_of(jnp.maximum(start - 8, 0), 8), 8)
    aux = aux_ref[rows, :]
    current = jnp.concatenate(
        [proj_ref[rows, width : 2 * width].astype(F32), ss_ref[rows, 0 : 2 * STATE]], axis=1
    )
    previous = jnp.concatenate(
        [
            proj_ref[pl.ds(pl.multiple_of(jnp.maximum(start - 16, 0), 16), 16), width : 2 * width].astype(F32)[8:],
            ss_ref[before, 0 : 2 * STATE],
        ],
        axis=1,
    )
    extended = jnp.concatenate([previous, current], axis=0)
    taps = par_ref[0:KW, :]
    conv = par_ref[KW : KW + 1, :] + taps[KW - 1 : KW, :] * current
    shifted = []
    for back in range(1, KW):
        moved = pltpu.roll(extended, back, 0)[8:] * aux[:, back : back + 1]
        shifted.append(moved)
        conv = conv + taps[KW - 1 - back : KW - back, :] * moved
    sig = jax.nn.sigmoid(conv)
    active = conv * sig
    inputs_x = active[:, :width]
    matrix_b = active[:, width : width + STATE].astype(BF16)
    matrix_c = active[:, width + STATE :].astype(BF16)
    step_in = ss_ref[rows, 2 * STATE :] + par_ref[7:8, 0:128]
    dt = jnp.maximum(step_in, 0.0) + jnp.log1p(jnp.exp(-jnp.abs(step_in)))
    decay = dt * par_ref[6:7, 0:128]
    row_id = lax.broadcasted_iota(jnp.int32, (BLK, BLK), 0)
    col_id = lax.broadcasted_iota(jnp.int32, (BLK, BLK), 1)
    lower = (row_id >= col_id).astype(F32)
    cum = dot_exact(lower, decay)
    cum_t = cum.T
    same = (aux[:, 0:1] == seg_ref[pl.ds(index, 1), 0, :]) & (row_id >= col_id)
    last = cum[BLK - 1 : BLK, :]
    gain_in = jnp.exp(cum) * aux[:, 4:5]
    tail = jnp.exp(last - cum) * aux[:, 5:6]
    carry = jnp.exp(last) * aux[BLK - 1 : BLK, 6:7]
    scores = jnp.where(same, dot_f32(matrix_c, matrix_b, (((1,), (1,)), ((), ()))), 0.0)
    dt_wide = spread(dt, width)
    moved_x = inputs_x * dt_wide
    return dict(
        rows=rows, aux=aux, current=current, shifted=shifted, conv=conv, sig=sig,
        x=inputs_x, b=matrix_b, c=matrix_c, step_in=step_in, dt=dt, cum=cum, cum_t=cum_t,
        same=same, scores=scores, dt_wide=dt_wide, u=moved_x, lower=lower,
        gain_in=spread(gain_in, width), tail=spread(tail, width),
        carry=spread(jnp.broadcast_to(carry, (8, 128)), width)[0:1],
    )


def split_pair(values):
    low = lax.broadcasted_iota(jnp.int32, values.shape, 1) < 64
    zero = jnp.zeros_like(values)
    return jnp.where(low, values, zero), jnp.where(low, zero, values)


def forward_kernel(width, proj_ref, ss_ref, aux_ref, seg_ref, par_ref, valued_ref, squares_ref, kept_ref, state):
    blocks = proj_ref.shape[0] // BLK
    state[...] = jnp.zeros_like(state)

    def step(index, _):
        start = pl.multiple_of(index * BLK, BLK)
        got = block_common(width, start, index, proj_ref, ss_ref, aux_ref, seg_ref, par_ref)
        kept_ref[index] = state[...]
        moved = got["u"].astype(BF16)
        parts = []
        for pair in range(width // 128):
            u0, u1 = split_pair(moved[:, 128 * pair : 128 * (pair + 1)])
            mixes = []
            for head in (2 * pair, 2 * pair + 1):
                differ = jnp.minimum(got["cum"][:, head : head + 1] - got["cum_t"][head : head + 1, :], 0.0)
                mixes.append((jnp.exp(differ) * got["scores"]).astype(BF16))
            parts.append(dot_f32(jnp.concatenate(mixes, axis=1), jnp.concatenate([u0, u1], axis=0)))
        within = jnp.concatenate(parts, axis=1)
        from_state = got["gain_in"] * dot_f32(got["c"], state[...].astype(BF16))
        scanned = within + from_state + par_ref[8:9, 0:width] * got["x"]
        state[...] = state[...] * got["carry"] + dot_f32(
            got["b"], (got["tail"] * got["u"]).astype(BF16), (((0,), (0,)), ((), ()))
        )
        gate = proj_ref[got["rows"], 0:width].astype(F32)
        gated = scanned * (gate * jax.nn.sigmoid(gate))
        squares_ref[got["rows"], :] = jnp.sum(gated * gated, axis=1, keepdims=True)
        valued_ref[got["rows"], :] = (gated * par_ref[5:6, 0:width]).astype(BF16)
        return 0

    lax.fori_loop(0, blocks, step, 0)


def backward_kernel(
    width, proj_ref, ss_ref, aux_ref, seg_ref, par_ref, vgrad_ref, dsq_ref, kept_ref,
    dproj_ref, dss_ref, dpar_ref, dstate, follow, ebuf, sums
):
    blocks = proj_ref.shape[0] // BLK
    wide = width + 2 * STATE
    dstate[...] = jnp.zeros_like(dstate)
    follow[...] = jnp.zeros_like(follow)
    sums[...] = jnp.zeros_like(sums)

    def fold(values):
        total = values[0:8]
        for part in range(1, BLK // 8):
            total = total + values[8 * part : 8 * part + 8]
        return total

    def step(count, _):
        index = blocks - 1 - count
        start = pl.multiple_of(index * BLK, BLK)
        got = block_common(width, start, index, proj_ref, ss_ref, aux_ref, seg_ref, par_ref)
        rows, aux = got["rows"], got["aux"]
        state_in = kept_ref[index]
        state_low = state_in.astype(BF16)
        moved = got["u"].astype(BF16)
        skip = par_ref[8:9, 0:width]
        gain = par_ref[5:6, 0:width]
        parts = []
        for pair in range(width // 128):
            u0, u1 = split_pair(moved[:, 128 * pair : 128 * (pair + 1)])
            mixes = []
            for head in (2 * pair, 2 * pair + 1):
                differ = jnp.minimum(got["cum"][:, head : head + 1] - got["cum_t"][head : head + 1, :], 0.0)
                level = jnp.exp(differ)
                ebuf[head] = level
                mixes.append((level * got["scores"]).astype(BF16))
            parts.append(dot_f32(jnp.concatenate(mixes, axis=1), jnp.concatenate([u0, u1], axis=0)))
        inner = jnp.concatenate(parts, axis=1) + got["gain_in"] * dot_f32(got["c"], state_low)
        scanned = inner + skip * got["x"]
        gate = proj_ref[rows, 0:width].astype(F32)
        gate_sig = jax.nn.sigmoid(gate)
        gate_act = gate * gate_sig
        gated = scanned * gate_act
        vgrad = vgrad_ref[rows, :].astype(F32)
        dgated = vgrad * gain + 2.0 * gated * dsq_ref[rows, :]
        sums[48:56, 0:width] += fold(vgrad * gated)
        dy = dgated * gate_act
        dproj_ref[rows, 0:width] = (
            dgated * scanned * (gate_sig * (1.0 + gate * (1.0 - gate_sig)))
        ).astype(BF16)
        dy_low = dy.astype(BF16)
        dscores = jnp.zeros((BLK, BLK), F32)
        parts = []
        for pair in range(width // 128):
            lanes = slice(128 * pair, 128 * (pair + 1))
            u0, u1 = split_pair(moved[:, lanes])
            d0, d1 = split_pair(dy_low[:, lanes])
            mixes = []
            for head, u_own in ((2 * pair, u0), (2 * pair + 1, u1)):
                level = ebuf[head]
                mixes.append((level * got["scores"]).astype(BF16))
                dscores = dscores + level * dot_f32(
                    dy_low[:, lanes], u_own, (((1,), (1,)), ((), ()))
                )
            parts.append(
                dot_f32(
                    jnp.concatenate(mixes, axis=0),
                    jnp.concatenate([d0, d1], axis=0),
                    (((0,), (0,)), ((), ())),
                )
            )
        du_within = jnp.concatenate(parts, axis=1)
        dscores = jnp.where(got["same"], dscores, 0.0).astype(BF16)
        dstate_now = dstate[...]
        dstate_low = dstate_now.astype(BF16)
        dy_in = (got["gain_in"] * dy).astype(BF16)
        u_tail = got["tail"] * got["u"]
        from_next = dot_f32(got["b"], dstate_low)
        du = du_within + got["tail"] * from_next
        dmat_c = dot_f32(dscores, got["b"]) + dot_f32(dy_in, state_low, (((1,), (1,)), ((), ())))
        dmat_b = dot_f32(dscores, got["c"], (((0,), (0,)), ((), ()))) + dot_f32(
            u_tail.astype(BF16), dstate_low, (((1,), (1,)), ((), ()))
        )
        tail_part = head_sums(u_tail * from_next)
        dcum = (
            head_sums(dy_low.astype(F32) * inner - moved.astype(F32) * du_within) - tail_part
        )
        kept_part = head_sums(fold(got["carry"] * dstate_now * state_in))
        at_last = jnp.sum(tail_part, axis=0, keepdims=True) + jnp.sum(kept_part, axis=0, keepdims=True)
        ddecay = dot_exact(got["lower"], dcum, (((0,), (0,)), ((), ()))) + at_last
        ddt = ddecay * par_ref[6:7, 0:128] + head_sums(du * got["x"])
        sums[56:64, 0:128] += fold(ddecay * got["dt"])
        sums[64:72, 0:width] += fold(dy * got["x"])
        dstep = ddt * jax.nn.sigmoid(got["step_in"])
        sums[72:80, 0:128] += fold(dstep)
        dstate[...] = dstate_now * got["carry"] + dot_f32(got["c"], dy_in, (((0,), (0,)), ((), ())))
        dactive = jnp.concatenate([skip * dy + du * got["dt_wide"], dmat_b, dmat_c], axis=1)
        sig, conv = got["sig"], got["conv"]
        dconv = dactive * (sig * (1.0 + conv * (1.0 - sig)))
        sums[32:40, :] += fold(dconv)
        sums[24:32, :] += fold(dconv * got["current"])
        dinput = par_ref[KW - 1 : KW, :] * dconv
        for back in range(1, KW):
            tap = KW - 1 - back
            sums[8 * tap : 8 * tap + 8, :] += fold(dconv * got["shifted"][back - 1])
            masked = dconv * aux[:, back : back + 1]
            ext = jnp.concatenate([masked, follow[back - 1]], axis=0)
            dinput = dinput + par_ref[tap : tap + 1, :] * pltpu.roll(ext, BLK + 8 - back, 0)[:BLK]
            follow[back - 1] = masked[0:8]
        dproj_ref[rows, width : 2 * width] = dinput[:, :width].astype(BF16)
        dss_ref[rows, 0 : 2 * STATE] = dinput[:, width:].astype(BF16)
        dss_ref[rows, 2 * STATE :] = dstep.astype(BF16)
        return 0

    lax.fori_loop(0, blocks, step, 0)
    for line in range(10):
        dpar_ref[line : line + 1, :] = jnp.sum(sums[8 * line : 8 * line + 8, :], axis=0, keepdims=True)
    dpar_ref[10:16, :] = jnp.zeros((6, wide), F32)


VM = pl.BlockSpec(memory_space=pltpu.VMEM)


def mixer_forward(proj, ss, aux, seg, par):
    length, double = proj.shape
    width = double // 2
    blocks = length // BLK
    return pl.pallas_call(
        functools.partial(forward_kernel, width),
        out_shape=(
            jax.ShapeDtypeStruct((length, width), BF16),
            jax.ShapeDtypeStruct((length, 1), F32),
            jax.ShapeDtypeStruct((blocks, STATE, width), F32),
        ),
        in_specs=[VM] * 5,
        out_specs=(VM,) * 3,
        scratch_shapes=[pltpu.VMEM((STATE, width), F32)],
        compiler_params=pltpu.CompilerParams(vmem_limit_bytes=56 * 2**20),
        name="mixer_forward",
    )(proj, ss, aux, seg, par)


def mixer_backward(proj, ss, aux, seg, par, vgrad, dsq, kept):
    length, double = proj.shape
    width = double // 2
    wide = width + 2 * STATE
    return pl.pallas_call(
        functools.partial(backward_kernel, width),
        out_shape=(
            jax.ShapeDtypeStruct((length, 2 * width), BF16),
            jax.ShapeDtypeStruct((length, 3 * STATE), BF16),
            jax.ShapeDtypeStruct((16, wide), F32),
        ),
        in_specs=[VM] * 8,
        out_specs=(VM,) * 3,
        scratch_shapes=[
            pltpu.VMEM((STATE, width), F32),
            pltpu.VMEM((KW - 1, 8, wide), F32),
            pltpu.VMEM((width // 64, BLK, BLK), F32),
            pltpu.VMEM((80, wide), F32),
        ],
        compiler_params=pltpu.CompilerParams(vmem_limit_bytes=56 * 2**20),
        name="mixer_backward",
    )(proj, ss, aux, seg, par, vgrad, dsq, kept)


def segment_masks(segment):
    length = segment.shape[0]
    blocks = length // BLK
    seg_f = segment.astype(F32)
    by_block = segment.reshape(blocks, BLK)
    final = by_block[:, -1]
    before = jnp.concatenate([jnp.full((1,), -1, segment.dtype), final[:-1]])
    columns = [seg_f]
    for back in range(1, KW):
        earlier = jnp.concatenate([jnp.full((back,), -1, segment.dtype), segment[:-back]])
        columns.append((earlier == segment).astype(F32))
    columns.append((by_block == before[:, None]).astype(F32).reshape(-1))
    columns.append((by_block == final[:, None]).astype(F32).reshape(-1))
    columns.append(jnp.repeat((before == final).astype(F32), BLK))
    columns.append(jnp.zeros((length,), F32))
    return jnp.stack(columns, axis=1), seg_f.reshape(blocks, 1, BLK)


MODEL_WIDTH = 1536
HEADS = 48
FF_E = 512
FF_S = 1024
TOPK = 6
STEP = 10
EXP_DEV = 2
INNER = 3072
ROUTER_AT = 64
MESH_ID = pl.DeviceIdType.MESH


def dot_t(a, b):
    return dot_f32(a, b, (((1,), (1,)), ((), ())))


def dot_tn(a, b):
    return dot_f32(a, b, (((0,), (0,)), ((), ())))


def shift(values, axis, by):
    size = lax.axis_size(axis)
    return lax.ppermute(values, axis, [(i, (i + by) % size) for i in range(size)])


def in_order(parts, axis):
    size, me = lax.axis_size(axis), lax.axis_index(axis)
    if size == 2:
        return [
            jnp.where(me == 0, parts[0], parts[1]),
            jnp.where(me == 0, parts[1], parts[0]),
        ]
    stacked = jnp.stack(parts)
    return [
        lax.dynamic_index_in_dim(stacked, (me - place) % size, 0, keepdims=False)
        for place in range(size)
    ]


def gather_rc(values):
    columns = lax.axis_size("col")
    own = [values] + [shift(values, "col", by) for by in range(1, columns)]
    other = [shift(part, "row", 1) for part in own]
    own, other = in_order(own, "col"), in_order(other, "col")
    me = lax.axis_index("row")
    first = [jnp.where(me == 0, a, b) for a, b in zip(own, other)]
    second = [jnp.where(me == 0, b, a) for a, b in zip(own, other)]
    return jnp.concatenate(first + second, axis=0)


def scatter_rc(values, dtype):
    columns = lax.axis_size("col")
    row, col = lax.axis_index("row"), lax.axis_index("col")
    half = values.shape[0] // 2
    size = half // columns

    def block(array, at, rows):
        return lax.dynamic_slice_in_dim(array, at * rows, rows)

    away = shift(block(values, 1 - row, half).astype(dtype), "row", 1)
    kept = block(values, row, half).astype(F32) + away.astype(F32)
    total = block(kept, col, size)
    for by in range(1, columns):
        sent = block(kept, (col + by) % columns, size).astype(dtype)
        total = total + shift(sent, "col", by).astype(F32)
    return total


def partners(shape):
    steps = []
    for name in ("row", "col", "dp"):
        bit = 1
        while bit < shape[name]:
            steps.append((name, bit))
            bit *= 2
    return steps


def total_kernel(steps, value_ref, out_ref, landed, send_sem, recv_sem):
    def other(name, bit):
        me = lax.axis_index(name)
        digit = (me // bit) % 2
        return {name: me + bit * (1 - 2 * digit)}

    barrier = pltpu.get_barrier_semaphore()
    for name, bit in steps:
        pl.semaphore_signal(barrier, inc=1, device_id=other(name, bit), device_id_type=MESH_ID)
    pl.semaphore_wait(barrier, len(steps))
    out_ref[...] = value_ref[...]
    for number, (name, bit) in enumerate(steps):
        copy = pltpu.make_async_remote_copy(
            src_ref=out_ref,
            dst_ref=landed.at[number],
            send_sem=send_sem.at[number],
            recv_sem=recv_sem.at[number],
            device_id=other(name, bit),
            device_id_type=MESH_ID,
        )
        copy.start()
        copy.wait()
        out_ref[...] += landed[number]


def total_all(values, shape):
    steps = partners(shape)
    return pl.pallas_call(
        functools.partial(total_kernel, steps),
        out_shape=jax.ShapeDtypeStruct(values.shape, F32),
        in_specs=[VM],
        out_specs=VM,
        scratch_shapes=[
            pltpu.VMEM((len(steps),) + values.shape, F32),
            pltpu.SemaphoreType.DMA((len(steps),)),
            pltpu.SemaphoreType.DMA((len(steps),)),
        ],
        compiler_params=pltpu.CompilerParams(collective_id=1, has_side_effects=True),
        name="total_all",
    )(values)


def expert_kernel(x_ref, g_ref, mask_ref, up_ref, down_ref, router_ref, mix_ref, dx_ref, dpre_ref, hid_ref, gg_ref):
    x, g = x_ref[...], g_ref[...]
    logits = dot_f32(x, router_ref[...])
    named = mask_ref[...].astype(F32)
    high = jnp.max(jnp.where(named > 0, logits, -1e30), axis=1, keepdims=True)
    raised = jnp.where(named > 0, jnp.exp(logits - high), 0.0)
    gates = raised / jnp.sum(raised, axis=1, keepdims=True)
    first, second = gates[:, 0:1], gates[:, 1:2]
    half = down_ref.shape[0]
    pre = dot_f32(x, up_ref[...])
    asked = dot_t(g, down_ref[...])
    rows = x.shape[0]
    totals = [jnp.zeros((rows, 128), F32), jnp.zeros((rows, 128), F32)]
    for part in range(half // 128):
        lanes = slice(128 * part, 128 * (part + 1))
        upper = slice(half + 128 * part, half + 128 * (part + 1))
        weight = first if part % 2 == 0 else second
        gate, up, want = pre[:, lanes], pre[:, upper], asked[:, lanes]
        sig = jax.nn.sigmoid(gate)
        act = gate * sig
        hidden = act * up
        totals[part % 2] = totals[part % 2] + hidden * want
        hid_ref[:, lanes] = (weight * hidden).astype(BF16)
        dact = weight * want
        dpre_ref[:, lanes] = (dact * up * (sig * (1.0 + gate * (1.0 - sig)))).astype(BF16)
        dpre_ref[:, upper] = (dact * act).astype(BF16)
    lane = lax.broadcasted_iota(jnp.int32, (rows, 128), 1)
    own = [jnp.sum(part, axis=1, keepdims=True) for part in totals]
    gg_ref[...] = jnp.where(lane == 0, own[0], jnp.where(lane == 1, own[1], 0.0))
    mix_ref[...] = dot_f32(hid_ref[...], down_ref[...]).astype(BF16)
    dx_ref[...] = dot_t(dpre_ref[...], up_ref[...]).astype(BF16)


def experts(x, g, mask, up, down, router):
    tokens, width = x.shape
    hidden = down.shape[0]
    tile = 256
    by_row = lambda columns: pl.BlockSpec((tile, columns), lambda i: (i, 0))
    return pl.pallas_call(
        expert_kernel,
        grid=(tokens // tile,),
        out_shape=(
            jax.ShapeDtypeStruct((tokens, width), BF16),
            jax.ShapeDtypeStruct((tokens, width), BF16),
            jax.ShapeDtypeStruct((tokens, 2 * hidden), BF16),
            jax.ShapeDtypeStruct((tokens, hidden), BF16),
            jax.ShapeDtypeStruct((tokens, 128), F32),
        ),
        in_specs=[by_row(width), by_row(width), by_row(mask.shape[1]), VM, VM, VM],
        out_specs=(by_row(width), by_row(width), by_row(2 * hidden), by_row(hidden), by_row(128)),
        compiler_params=pltpu.CompilerParams(vmem_limit_bytes=56 * 2**20),
        name="experts",
    )(x, g, mask, up, down, router)


def rms_scale(values):
    return lax.rsqrt(jnp.mean(values * values, axis=-1, keepdims=True) + 1e-05)


def rms_back(values, scale, gain, grad_normed):
    weighted = grad_normed * gain[None, :]
    grad_values = scale * weighted - values * scale**3 * jnp.mean(
        weighted * values, axis=-1, keepdims=True
    )
    gain_grad = jnp.sum(grad_normed * values * scale, axis=0)
    return (grad_values, gain_grad)


def silu_gate(pre_values):
    half_size = pre_values.shape[-1] // 2
    return jax.nn.silu(pre_values[..., :half_size]) * pre_values[..., half_size:]


def silu_gate_back(pre_values, grad):
    return jax.vjp(silu_gate, pre_values)[1](grad)[0]


def adamw(weight, grad, first, second, rate, decay=0.1):
    grad = grad.astype(F32)
    first_new = 0.9 * first + 0.1 * grad
    second_new = 0.95 * second + 0.05 * grad * grad
    corrected_one = first_new / (1.0 - 0.9**STEP)
    corrected_two = second_new / (1.0 - 0.95**STEP)
    weight_new = weight - rate * (
        corrected_one / (jnp.sqrt(corrected_two) + 1e-08) + decay * weight
    )
    return (first_new, second_new, weight_new)


ALL = ("dp", "row", "col")


def gather_dp(values):
    return lax.all_gather(values, "dp", axis=0, tiled=True)


def scatter_dp(values):
    return lax.psum_scatter(values, "dp", scatter_dimension=0, tiled=True)


def body(
    shape,
    hidden_in, segment_ids, routes, out_grad,
    vectors, vectors_first, vectors_second,
    in_weight, in_weight_first, in_weight_second,
    step_weight, step_weight_first, step_weight_second,
    out_weight, out_weight_first, out_weight_second,
    state_weight, state_weight_first, state_weight_second,
    router, router_first, router_second,
    shared_up, shared_up_first, shared_up_second,
    shared_down, shared_down_first, shared_down_second,
    expert_gate_up, expert_gate_up_first, expert_gate_up_second,
    expert_down, expert_down_first, expert_down_second,
):
    dp = lax.axis_index("dp")
    data_count = lax.axis_size("dp")
    seq_devices = lax.axis_size("row") * lax.axis_size("col")
    local_heads = in_weight.shape[1]
    width = 64 * local_heads
    head_start = lax.axis_index(("row", "col")) * local_heads
    own_tokens = hidden_in.shape[1]
    experts_all = router.shape[1]
    rows_dp = in_weight.shape[0]
    residual = hidden_in[0].astype(F32)
    gain_one = vectors[0:MODEL_WIDTH]
    gain_two = vectors[MODEL_WIDTH : 2 * MODEL_WIDTH]

    small = jnp.concatenate([state_weight, router], axis=1).astype(BF16)
    small = gather_rc(small)
    fill = lambda columns: jnp.zeros((rows_dp, columns), BF16)
    mixer_local = jnp.concatenate(
        [
            in_weight[:, :, :64].astype(BF16).reshape(rows_dp, width),
            in_weight[:, :, 64:].astype(BF16).reshape(rows_dp, width),
            small[:, : 2 * STATE],
            step_weight.astype(BF16),
            fill(ROUTER_AT - local_heads),
            small[:, 2 * STATE :],
            fill(128 - ROUTER_AT - experts_all),
        ],
        axis=1,
    )
    mixer_full = gather_dp(mixer_local)
    scale_one = rms_scale(residual)
    normed_one = (residual * scale_one * gain_one[None, :]).astype(BF16)
    normed_all = gather_rc(normed_one)
    out_local = out_weight.astype(BF16).reshape(width, -1).T
    out_full = gather_dp(out_local)
    route_ids = routes[0]
    chosen = (
        route_ids[:, :, None] == jnp.arange(experts_all, dtype=jnp.int32)[None, None, :]
    ).any(axis=1)
    mask_all = gather_dp(jnp.pad(chosen.astype(BF16), ((0, 0), (0, 128 - experts_all))))
    grad_low = out_grad[0]
    grad_all = gather_dp(grad_low)

    pieces = FF_E // seq_devices
    up_local = expert_gate_up.astype(BF16).reshape(EXP_DEV, -1, 2, seq_devices, pieces)
    up_local = up_local.transpose(1, 2, 3, 0, 4).reshape(-1, 2 * EXP_DEV * FF_E)
    up_full = gather_rc(up_local)
    down_full = gather_rc(expert_down.astype(BF16).reshape(-1, MODEL_WIDTH))
    shared_up_full = lax.all_gather(shared_up.astype(BF16), ALL, axis=0, tiled=True)
    shared_down_full = lax.all_gather(shared_down.astype(BF16), ALL, axis=0, tiled=True)

    xbc = INNER + 2 * STATE
    at_bias = 2 * MODEL_WIDTH + INNER
    at_taps = at_bias + xbc
    at_head = at_taps + KW * xbc
    start = head_start * 64
    cut = lambda array, at, size: lax.dynamic_slice_in_dim(array, at, size, axis=-1)
    local = lambda array: jnp.concatenate([cut(array, start, width), array[..., INNER:]], axis=-1)
    wide = width + 2 * STATE
    line = lambda vec: jnp.pad(vec, (0, wide - vec.shape[0]))[None]
    per_head = lambda number: cut(vectors, at_head + number * HEADS + head_start, local_heads)
    decay_rate = -jnp.exp(per_head(0))
    params = jnp.concatenate(
        [
            local(vectors[at_taps:at_head].reshape(KW, xbc)),
            local(vectors[at_bias:at_taps])[None],
            line(cut(vectors, 2 * MODEL_WIDTH + start, width)),
            line(decay_rate),
            line(per_head(2)),
            line(jnp.repeat(per_head(1), 64)),
            jnp.zeros((7, wide), F32),
        ],
        axis=0,
    )
    aux, seg_rows = segment_masks(segment_ids[0])
    proj = dot_f32(normed_all, mixer_full[:, : 2 * width]).astype(BF16)
    ss = dot_f32(normed_all, mixer_full[:, 2 * width :])
    valued, squares_part, kept = mixer_forward(proj, ss, aux, seg_rows, params)
    proj_out = scatter_rc(dot_t(valued, out_full), BF16)
    squares = scatter_rc(squares_part, F32)[:, 0]
    scale_two = lax.rsqrt(squares / INNER + 1e-05)
    residual_two = residual + scale_two[:, None] * proj_out
    scale_three = rms_scale(residual_two)
    normed_two = (residual_two * scale_three * gain_two[None, :]).astype(BF16)

    tokens_all = gather_dp(normed_two)
    router_pad = mixer_full[:, 2 * width + 2 * STATE + ROUTER_AT :]
    router_full = router_pad[:, :experts_all]
    turned = jnp.roll(router_full, -EXP_DEV * dp, axis=1)
    turned = jnp.pad(turned, ((0, 0), (0, 128 - experts_all)))
    mask_turned = jnp.pad(
        jnp.roll(mask_all[:, :experts_all], -EXP_DEV * dp, axis=1), ((0, 0), (0, 128 - experts_all))
    )
    mixed, rows_grad, pre_grad, hidden_low, gate_part = experts(
        tokens_all, grad_all, mask_turned, up_full, down_full, turned
    )
    mixture = scatter_dp(mixed)
    routed_grad = scatter_dp(rows_grad)
    own_gates = jnp.roll(
        jnp.pad(gate_part[:, :EXP_DEV], ((0, 0), (0, experts_all - EXP_DEV))), EXP_DEV * dp, axis=1
    )
    gate_grad = scatter_dp(own_gates)
    up_grad = dot_tn(tokens_all, pre_grad).astype(BF16)
    down_grad = dot_tn(hidden_low, grad_all).astype(BF16)
    up_total = scatter_rc(up_grad, BF16)
    down_total = scatter_rc(down_grad, BF16)
    up_total = up_total.reshape(-1, 2, seq_devices, EXP_DEV, pieces).transpose(3, 0, 1, 2, 4)
    up_total = up_total.reshape(expert_gate_up.shape)
    down_total = down_total.reshape(expert_down.shape)

    logits = dot_f32(normed_two, router_full)
    gate_all = jax.nn.softmax(jnp.where(chosen, logits, -jnp.inf), axis=-1)
    shared_pre = dot_f32(normed_two, shared_up_full)
    shared_act = silu_gate(shared_pre).astype(BF16)
    shared_out = dot_f32(shared_act, shared_down_full)
    shared_act_grad = dot_t(grad_low, shared_down_full)
    shared_pre_grad = silu_gate_back(shared_pre, shared_act_grad).astype(BF16)
    shared_down_grad = dot_tn(shared_act, grad_low).astype(BF16)
    shared_up_grad = dot_tn(normed_two, shared_pre_grad).astype(BF16)
    shared_up_total = lax.psum_scatter(shared_up_grad, ALL, scatter_dimension=0, tiled=True)
    shared_down_total = lax.psum_scatter(shared_down_grad, ALL, scatter_dimension=0, tiled=True)
    layer_output = residual_two + mixture.astype(F32) + shared_out
    hidden_out = layer_output.astype(BF16)[None]
    cotangent = grad_low.astype(F32)
    normed_two_grad = dot_t(shared_pre_grad, shared_up_full) + routed_grad.astype(F32)
    logits_grad = gate_all * (gate_grad - jnp.sum(gate_all * gate_grad, axis=1, keepdims=True))
    logits_low = jnp.where(chosen, logits_grad, 0.0).astype(BF16)
    normed_two_grad = normed_two_grad + dot_t(logits_low, router_full)
    router_grad = dot_tn(normed_two, logits_low)
    residual_two_grad, gain_two_grad = rms_back(
        residual_two, scale_three, gain_two, normed_two_grad
    )
    residual_two_grad = residual_two_grad + cotangent
    proj_out_grad = (residual_two_grad * scale_two[:, None]).astype(BF16)
    squares_grad = (
        jnp.sum(residual_two_grad * proj_out, axis=1) * -0.5 * scale_two**3 / INNER
    )
    proj_grad_all = gather_rc(proj_out_grad)
    squares_grad_all = gather_rc(squares_grad[:, None])

    valued_grad = dot_f32(proj_grad_all, out_full).astype(BF16)
    out_grad_t = dot_tn(proj_grad_all, valued).astype(BF16)
    out_total = scatter_dp(out_grad_t).T.reshape(out_weight.shape)
    proj_grad, ss_grad, par_grad = mixer_backward(
        proj, ss, aux, seg_rows, params, valued_grad, squares_grad_all, kept
    )
    all_grad = jnp.concatenate([proj_grad, ss_grad], axis=1)
    normed_grad = scatter_rc(dot_t(all_grad, mixer_full), BF16)
    router_wide = jnp.pad(
        router_grad, ((0, 0), (2 * width + 2 * STATE + ROUTER_AT, 128 - ROUTER_AT - experts_all))
    )
    mixer_total = scatter_dp((dot_tn(normed_all, all_grad) + router_wide).astype(BF16))
    small_total = scatter_rc(mixer_total[:, 2 * width :], F32)
    state_total = small_total[:, : 2 * STATE]
    router_total = small_total[:, 2 * STATE + ROUTER_AT : 2 * STATE + ROUTER_AT + experts_all]
    step_total = mixer_total[:, 2 * width + 2 * STATE : 2 * width + 2 * STATE + local_heads]
    in_total = jnp.concatenate(
        [
            mixer_total[:, :width].reshape(rows_dp, local_heads, 64),
            mixer_total[:, width : 2 * width].reshape(rows_dp, local_heads, 64),
        ],
        axis=2,
    )
    residual_grad, gain_one_grad = rms_back(residual, scale_one, gain_one, normed_grad)
    input_grad = (residual_grad + residual_two_grad)[None]

    place = lambda values, at, size: lax.dynamic_update_slice(
        jnp.zeros(values.shape[:-1] + (size,), F32), values, (0,) * (values.ndim - 1) + (at,)
    )
    spread_out = lambda values: jnp.concatenate(
        [place(values[..., :width], start, INNER), values[..., width:]], axis=-1
    )
    vector_local = jnp.concatenate(
        [
            gain_one_grad,
            gain_two_grad,
            place(par_grad[6, :width], start, INNER),
            spread_out(par_grad[4]),
            spread_out(par_grad[0:KW]).reshape(-1),
            place(par_grad[7, :local_heads] * decay_rate, head_start, HEADS),
            place(par_grad[8, :width].reshape(local_heads, 64).sum(axis=1), head_start, HEADS),
            place(par_grad[9, :local_heads], head_start, HEADS),
        ]
    )
    count = vector_local.shape[0]
    lines = -(-count // 1024) * 8
    vector_total = total_all(
        jnp.pad(vector_local, (0, lines * 128 - count)).reshape(lines, 128), shape
    ).reshape(-1)[:count]
    rate = MODEL_WIDTH ** (-0.5)
    return (
        hidden_out,
        input_grad,
        *adamw(vectors, vector_total, vectors_first, vectors_second, 0.3, 0.0),
        *adamw(in_weight, in_total, in_weight_first, in_weight_second, rate),
        *adamw(step_weight, step_total, step_weight_first, step_weight_second, rate),
        *adamw(out_weight, out_total, out_weight_first, out_weight_second, INNER ** (-0.5)),
        *adamw(state_weight, state_total, state_weight_first, state_weight_second, rate),
        *adamw(router, router_total, router_first, router_second, 0.5 * rate),
        *adamw(shared_up, shared_up_total, shared_up_first, shared_up_second, rate),
        *adamw(shared_down, shared_down_total, shared_down_first, shared_down_second, FF_S ** (-0.5)),
        *adamw(expert_gate_up, up_total, expert_gate_up_first, expert_gate_up_second, rate),
        *adamw(expert_down, down_total, expert_down_first, expert_down_second, FF_E ** (-0.5)),
    )


def solution(mesh):
    tokens = P("dp", ("row", "col"), None)
    by_head = P("dp", ("row", "col"))
    out_spec = P(("row", "col"), None, "dp")
    flat = P(ALL, None)
    weights = (
        (P(),) * 3
        + (tokens,) * 3
        + (by_head,) * 3
        + (out_spec,) * 3
        + (flat,) * 12
        + (tokens,) * 6
    )
    return jax.shard_map(
        functools.partial(body, dict(mesh.shape)),
        mesh=mesh,
        in_specs=(tokens, P("dp", None), tokens, tokens) + weights,
        out_specs=(tokens, tokens) + weights,
        check_vma=False,
    )
```

```python
import functools

import jax
import jax.numpy as jnp
from jax import lax
from jax.experimental import pallas as pl
from jax.experimental.pallas import tpu as pltpu
from jax.sharding import PartitionSpec as P

STATE = 128
KW = 4
BLK = 128
F32 = jnp.float32
BF16 = jnp.bfloat16


def dot_f32(a, b, dims=(((1,), (0,)), ((), ()))):
    return lax.dot_general(a, b, dims, preferred_element_type=F32)


def dot_exact(a, b, dims=(((1,), (0,)), ((), ()))):
    return lax.dot_general(
        a, b, dims, precision=lax.Precision.HIGHEST, preferred_element_type=F32
    )


def spread(values, width):
    rows = values.shape[0]
    low = lax.broadcasted_iota(jnp.int32, (rows, 128), 1) < 64
    parts = []
    for pair in range(width // 128):
        left = jnp.broadcast_to(values[:, 2 * pair : 2 * pair + 1], (rows, 128))
        right = jnp.broadcast_to(values[:, 2 * pair + 1 : 2 * pair + 2], (rows, 128))
        parts.append(jnp.where(low, left, right))
    return jnp.concatenate(parts, axis=1)


def head_sums(values):
    width = values.shape[1]
    ones = (
        lax.broadcasted_iota(jnp.int32, (width, 128), 0) // 64
        == lax.broadcasted_iota(jnp.int32, (width, 128), 1)
    ).astype(BF16)
    high = values.astype(BF16)
    rest = (values - high.astype(F32)).astype(BF16)
    return dot_f32(high, ones) + dot_f32(rest, ones)


def apart(values):
    low = lax.broadcasted_iota(jnp.int32, (values.shape[0], 128), 1) < 64
    gates, inputs = [], []
    for at in range(0, values.shape[1], 256):
        one, two = values[:, at : at + 128], values[:, at + 128 : at + 256]
        gates.append(jnp.where(low, one, pltpu.roll(two, 64, 1)))
        inputs.append(jnp.where(low, pltpu.roll(one, 64, 1), two))
    return jnp.concatenate(gates, axis=1), jnp.concatenate(inputs, axis=1)


def together(gates, inputs):
    low = lax.broadcasted_iota(jnp.int32, (gates.shape[0], 128), 1) < 64
    parts = []
    for at in range(0, gates.shape[1], 128):
        one, two = gates[:, at : at + 128], inputs[:, at : at + 128]
        parts.append(jnp.where(low, one, pltpu.roll(two, 64, 1)))
        parts.append(jnp.where(low, pltpu.roll(one, 64, 1), two))
    return jnp.concatenate(parts, axis=1)


def block_masks(index, seg_ref):
    now = seg_ref[index]
    before = jnp.where(index > 0, seg_ref[jnp.maximum(index - 1, 0)], -1.0)
    lane = lax.broadcasted_iota(jnp.int32, (1, BLK), 1)
    rows = [now]
    for back in range(1, KW):
        earlier = jnp.where(lane < back, pltpu.roll(before, back, 1), pltpu.roll(now, back, 1))
        rows.append((earlier == now).astype(F32))
    last, prior = now[:, BLK - 1 :], before[:, BLK - 1 :]
    rows.append((now == prior).astype(F32))
    rows.append((now == last).astype(F32))
    rows.append(jnp.broadcast_to((prior == last).astype(F32), (1, BLK)))
    rows.append(jnp.zeros((BLK - len(rows), BLK), F32))
    return jnp.concatenate(rows, axis=0).T


def block_common(width, start, index, proj_ref, ss_ref, seg_ref, par_ref):
    rows = pl.ds(start, BLK)
    before = pl.ds(pl.multiple_of(jnp.maximum(start - 8, 0), 8), 8)
    aux = block_masks(index, seg_ref)
    gate, inner = apart(proj_ref[rows, :].astype(F32))
    current = jnp.concatenate([inner, ss_ref[rows, 0 : 2 * STATE]], axis=1)
    earlier = proj_ref[pl.ds(pl.multiple_of(jnp.maximum(start - 16, 0), 16), 16), :]
    previous = jnp.concatenate(
        [apart(earlier.astype(F32)[8:])[1], ss_ref[before, 0 : 2 * STATE]], axis=1
    )
    extended = jnp.concatenate([previous, current], axis=0)
    taps = par_ref[0:KW, :]
    conv = par_ref[KW : KW + 1, :] + taps[KW - 1 : KW, :] * current
    shifted = []
    for back in range(1, KW):
        moved = pltpu.roll(extended, back, 0)[8:] * aux[:, back : back + 1]
        shifted.append(moved)
        conv = conv + taps[KW - 1 - back : KW - back, :] * moved
    sig = jax.nn.sigmoid(conv)
    active = conv * sig
    inputs_x = active[:, :width]
    matrix_b = active[:, width : width + STATE].astype(BF16)
    matrix_c = active[:, width + STATE :].astype(BF16)
    step_in = ss_ref[rows, 2 * STATE :] + par_ref[7:8, 0:128]
    dt = jnp.maximum(step_in, 0.0) + jnp.log1p(jnp.exp(-jnp.abs(step_in)))
    decay = dt * par_ref[6:7, 0:128]
    row_id = lax.broadcasted_iota(jnp.int32, (BLK, BLK), 0)
    col_id = lax.broadcasted_iota(jnp.int32, (BLK, BLK), 1)
    lower = (row_id >= col_id).astype(F32)
    cum = dot_exact(lower, decay)
    cum_t = cum.T
    same = (aux[:, 0:1] == seg_ref[pl.ds(index, 1), 0, :]) & (row_id >= col_id)
    last = cum[BLK - 1 : BLK, :]
    gain_in = jnp.exp(cum) * aux[:, 4:5]
    tail = jnp.exp(last - cum) * aux[:, 5:6]
    carry = jnp.exp(last) * aux[BLK - 1 : BLK, 6:7]
    scores = jnp.where(same, dot_f32(matrix_c, matrix_b, (((1,), (1,)), ((), ()))), 0.0)
    dt_wide = spread(dt, width)
    moved_x = inputs_x * dt_wide
    return dict(
        rows=rows, aux=aux, gate=gate, current=current, shifted=shifted, conv=conv, sig=sig,
        x=inputs_x, b=matrix_b, c=matrix_c, step_in=step_in, dt=dt, cum=cum, cum_t=cum_t,
        same=same, scores=scores, dt_wide=dt_wide, u=moved_x, lower=lower,
        gain_in=spread(gain_in, width), tail=spread(tail, width),
        carry=spread(jnp.broadcast_to(carry, (8, 128)), width)[0:1],
    )


def split_pair(values):
    low = lax.broadcasted_iota(jnp.int32, values.shape, 1) < 64
    zero = jnp.zeros_like(values)
    return jnp.where(low, values, zero), jnp.where(low, zero, values)


def forward_kernel(width, proj_ref, ss_ref, seg_ref, par_ref, valued_ref, squares_ref, kept_ref, state):
    blocks = proj_ref.shape[0] // BLK
    state[...] = jnp.zeros_like(state)

    def step(index, _):
        start = pl.multiple_of(index * BLK, BLK)
        got = block_common(width, start, index, proj_ref, ss_ref, seg_ref, par_ref)
        kept_ref[index] = state[...]
        moved = got["u"].astype(BF16)
        parts = []
        for pair in range(width // 128):
            u0, u1 = split_pair(moved[:, 128 * pair : 128 * (pair + 1)])
            mixes = []
            for head in (2 * pair, 2 * pair + 1):
                differ = jnp.minimum(got["cum"][:, head : head + 1] - got["cum_t"][head : head + 1, :], 0.0)
                mixes.append((jnp.exp(differ) * got["scores"]).astype(BF16))
            parts.append(dot_f32(jnp.concatenate(mixes, axis=1), jnp.concatenate([u0, u1], axis=0)))
        within = jnp.concatenate(parts, axis=1)
        from_state = got["gain_in"] * dot_f32(got["c"], state[...].astype(BF16))
        scanned = within + from_state + par_ref[8:9, 0:width] * got["x"]
        state[...] = state[...] * got["carry"] + dot_f32(
            got["b"], (got["tail"] * got["u"]).astype(BF16), (((0,), (0,)), ((), ()))
        )
        gate = got["gate"]
        gated = scanned * (gate * jax.nn.sigmoid(gate))
        squares_ref[got["rows"], :] = jnp.sum(gated * gated, axis=1, keepdims=True)
        valued_ref[got["rows"], :] = (gated * par_ref[5:6, 0:width]).astype(BF16)
        return 0

    lax.fori_loop(0, blocks, step, 0)


def backward_kernel(
    width, proj_ref, ss_ref, seg_ref, par_ref, vgrad_ref, dsq_ref, kept_ref,
    dproj_ref, dss_ref, dpar_ref, dstate, follow, ebuf, sums
):
    blocks = proj_ref.shape[0] // BLK
    wide = width + 2 * STATE
    dstate[...] = jnp.zeros_like(dstate)
    follow[...] = jnp.zeros_like(follow)
    sums[...] = jnp.zeros_like(sums)

    def fold(values):
        total = values[0:8]
        for part in range(1, BLK // 8):
            total = total + values[8 * part : 8 * part + 8]
        return total

    def step(count, _):
        index = blocks - 1 - count
        start = pl.multiple_of(index * BLK, BLK)
        got = block_common(width, start, index, proj_ref, ss_ref, seg_ref, par_ref)
        rows, aux = got["rows"], got["aux"]
        state_in = kept_ref[index]
        state_low = state_in.astype(BF16)
        moved = got["u"].astype(BF16)
        skip = par_ref[8:9, 0:width]
        gain = par_ref[5:6, 0:width]
        parts = []
        for pair in range(width // 128):
            u0, u1 = split_pair(moved[:, 128 * pair : 128 * (pair + 1)])
            mixes = []
            for head in (2 * pair, 2 * pair + 1):
                differ = jnp.minimum(got["cum"][:, head : head + 1] - got["cum_t"][head : head + 1, :], 0.0)
                level = jnp.exp(differ)
                ebuf[head] = level
                mixes.append((level * got["scores"]).astype(BF16))
            parts.append(dot_f32(jnp.concatenate(mixes, axis=1), jnp.concatenate([u0, u1], axis=0)))
        inner = jnp.concatenate(parts, axis=1) + got["gain_in"] * dot_f32(got["c"], state_low)
        scanned = inner + skip * got["x"]
        gate = got["gate"]
        gate_sig = jax.nn.sigmoid(gate)
        gate_act = gate * gate_sig
        gated = scanned * gate_act
        vgrad = vgrad_ref[rows, :].astype(F32)
        dgated = vgrad * gain + 2.0 * gated * dsq_ref[rows, :]
        sums[48:56, 0:width] += fold(vgrad * gated)
        dy = dgated * gate_act
        dgate = dgated * scanned * (gate_sig * (1.0 + gate * (1.0 - gate_sig)))
        dy_low = dy.astype(BF16)
        dscores = jnp.zeros((BLK, BLK), F32)
        parts = []
        for pair in range(width // 128):
            lanes = slice(128 * pair, 128 * (pair + 1))
            u0, u1 = split_pair(moved[:, lanes])
            d0, d1 = split_pair(dy_low[:, lanes])
            mixes = []
            for head, u_own in ((2 * pair, u0), (2 * pair + 1, u1)):
                level = ebuf[head]
                mixes.append((level * got["scores"]).astype(BF16))
                dscores = dscores + level * dot_f32(
                    dy_low[:, lanes], u_own, (((1,), (1,)), ((), ()))
                )
            parts.append(
                dot_f32(
                    jnp.concatenate(mixes, axis=0),
                    jnp.concatenate([d0, d1], axis=0),
                    (((0,), (0,)), ((), ())),
                )
            )
        du_within = jnp.concatenate(parts, axis=1)
        dscores = jnp.where(got["same"], dscores, 0.0).astype(BF16)
        dstate_now = dstate[...]
        dstate_low = dstate_now.astype(BF16)
        dy_in = (got["gain_in"] * dy).astype(BF16)
        u_tail = got["tail"] * got["u"]
        from_next = dot_f32(got["b"], dstate_low)
        du = du_within + got["tail"] * from_next
        dmat_c = dot_f32(dscores, got["b"]) + dot_f32(dy_in, state_low, (((1,), (1,)), ((), ())))
        dmat_b = dot_f32(dscores, got["c"], (((0,), (0,)), ((), ()))) + dot_f32(
            u_tail.astype(BF16), dstate_low, (((1,), (1,)), ((), ()))
        )
        tail_part = head_sums(u_tail * from_next)
        dcum = (
            head_sums(dy_low.astype(F32) * inner - moved.astype(F32) * du_within) - tail_part
        )
        kept_part = head_sums(fold(got["carry"] * dstate_now * state_in))
        at_last = jnp.sum(tail_part, axis=0, keepdims=True) + jnp.sum(kept_part, axis=0, keepdims=True)
        ddecay = dot_exact(got["lower"], dcum, (((0,), (0,)), ((), ()))) + at_last
        ddt = ddecay * par_ref[6:7, 0:128] + head_sums(du * got["x"])
        sums[56:64, 0:128] += fold(ddecay * got["dt"])
        sums[64:72, 0:width] += fold(dy * got["x"])
        dstep = ddt * jax.nn.sigmoid(got["step_in"])
        sums[72:80, 0:128] += fold(dstep)
        dstate[...] = dstate_now * got["carry"] + dot_f32(got["c"], dy_in, (((0,), (0,)), ((), ())))
        dactive = jnp.concatenate([skip * dy + du * got["dt_wide"], dmat_b, dmat_c], axis=1)
        sig, conv = got["sig"], got["conv"]
        dconv = dactive * (sig * (1.0 + conv * (1.0 - sig)))
        sums[32:40, :] += fold(dconv)
        sums[24:32, :] += fold(dconv * got["current"])
        dinput = par_ref[KW - 1 : KW, :] * dconv
        for back in range(1, KW):
            tap = KW - 1 - back
            sums[8 * tap : 8 * tap + 8, :] += fold(dconv * got["shifted"][back - 1])
            masked = dconv * aux[:, back : back + 1]
            ext = jnp.concatenate([masked, follow[back - 1]], axis=0)
            dinput = dinput + par_ref[tap : tap + 1, :] * pltpu.roll(ext, BLK + 8 - back, 0)[:BLK]
            follow[back - 1] = masked[0:8]
        dproj_ref[rows, :] = together(dgate, dinput[:, :width]).astype(BF16)
        dss_ref[rows, 0 : 2 * STATE] = dinput[:, width:].astype(BF16)
        dss_ref[rows, 2 * STATE :] = dstep.astype(BF16)
        return 0

    lax.fori_loop(0, blocks, step, 0)
    for line in range(10):
        dpar_ref[line : line + 1, :] = jnp.sum(sums[8 * line : 8 * line + 8, :], axis=0, keepdims=True)
    dpar_ref[10:16, :] = jnp.zeros((6, wide), F32)


VM = pl.BlockSpec(memory_space=pltpu.VMEM)


def lasting(micros):
    return pl.CostEstimate(flops=0, bytes_accessed=int(micros * 3.0e6), transcendentals=0)


def mixer_forward(proj, ss, seg, par):
    length, double = proj.shape
    width = double // 2
    blocks = length // BLK
    return pl.pallas_call(
        functools.partial(forward_kernel, width),
        out_shape=(
            jax.ShapeDtypeStruct((length, width), BF16),
            jax.ShapeDtypeStruct((length, 1), F32),
            jax.ShapeDtypeStruct((blocks, STATE, width), F32),
        ),
        in_specs=[VM] * 4,
        out_specs=(VM,) * 3,
        scratch_shapes=[pltpu.VMEM((STATE, width), F32)],
        compiler_params=pltpu.CompilerParams(vmem_limit_bytes=56 * 2**20),
        cost_estimate=lasting(20),
        name="mixer_forward",
    )(proj, ss, seg, par)


def mixer_backward(proj, ss, seg, par, vgrad, dsq, kept):
    length, double = proj.shape
    width = double // 2
    wide = width + 2 * STATE
    return pl.pallas_call(
        functools.partial(backward_kernel, width),
        out_shape=(
            jax.ShapeDtypeStruct((length, 2 * width), BF16),
            jax.ShapeDtypeStruct((length, 3 * STATE), BF16),
            jax.ShapeDtypeStruct((16, wide), F32),
        ),
        in_specs=[VM] * 7,
        out_specs=(VM,) * 3,
        scratch_shapes=[
            pltpu.VMEM((STATE, width), F32),
            pltpu.VMEM((KW - 1, 8, wide), F32),
            pltpu.VMEM((width // 64, BLK, BLK), F32),
            pltpu.VMEM((80, wide), F32),
        ],
        compiler_params=pltpu.CompilerParams(vmem_limit_bytes=56 * 2**20),
        cost_estimate=lasting(34),
        name="mixer_backward",
    )(proj, ss, seg, par, vgrad, dsq, kept)


MODEL_WIDTH = 1536
HEADS = 48
FF_E = 512
FF_S = 1024
TOPK = 6
STEP = 10
EXP_DEV = 2
INNER = 3072
ROUTER_AT = 64
REST_AT = 64


def dot_t(a, b):
    return dot_f32(a, b, (((1,), (1,)), ((), ())))


def dot_tn(a, b):
    return dot_f32(a, b, (((0,), (0,)), ((), ())))


def shift(values, axis, by):
    size = lax.axis_size(axis)
    return lax.ppermute(values, axis, [(i, (i + by) % size) for i in range(size)])


def all_places(own):
    rows, columns = lax.axis_index("row"), lax.axis_size("col")
    col = lax.axis_index("col")
    placed = []
    for by, part in enumerate(own):
        there = (col - by) % columns
        placed.append((rows * columns + there, part))
        placed.append(((1 - rows) * columns + there, shift(part, "row", 1)))
    return placed


def assemble(placed, group):
    count = len(placed)
    rows, columns = placed[0][1].shape
    total = jnp.zeros((group, count, rows // group, columns), placed[0][1].dtype)
    for place, part in placed:
        total = lax.dynamic_update_slice(
            total, part.reshape(group, 1, rows // group, columns), (0, place, 0, 0)
        )
    return total.reshape(count * rows, columns)


def gather_rc(values):
    columns = lax.axis_size("col")
    return assemble(
        all_places([values] + [shift(values, "col", by) for by in range(1, columns)]), 1
    )


def block_of(array, at, rows):
    return lax.dynamic_slice_in_dim(array, at * rows, rows)


def scatter_row(values, group=1):
    row = lax.axis_index("row")
    halves = values.reshape(group, 2, -1, values.shape[1])
    pick = lambda which: lax.dynamic_index_in_dim(halves, which, 1, keepdims=False)
    away = shift(pick(1 - row), "row", 1)
    return pick(row).astype(F32) + away.astype(F32)


def scatter_col(kept):
    columns, col = lax.axis_size("col"), lax.axis_index("col")
    parts = kept.reshape(kept.shape[0], columns, -1, kept.shape[2])
    pick = lambda which: lax.dynamic_index_in_dim(parts, which, 1, keepdims=False)
    total = pick(col)
    for by in range(1, columns):
        total = total + shift(pick((col + by) % columns).astype(BF16), "col", by).astype(F32)
    return total.reshape(-1, kept.shape[2])


def scatter_rc(values):
    return scatter_col(scatter_row(values))


def scatter_squares(values):
    columns, col = lax.axis_size("col"), lax.axis_index("col")
    kept = scatter_row(values)[0]
    rows = kept.shape[0] // columns
    total = block_of(kept, col, rows)
    for by in range(1, columns):
        total = total + shift(block_of(kept, (col + by) % columns, rows), "col", by)
    return total


def partners(shape):
    steps = []
    for name in ("dp", "row", "col"):
        bit = 1
        while bit < shape[name]:
            steps.append((name, bit))
            bit *= 2
    return steps


DEEP = 4
MESH_ID = pl.DeviceIdType.MESH
ANY = pl.BlockSpec(memory_space=pl.ANY)


def near_first(place, step, size):
    if size == 1:
        return place
    if size == 2:
        return place + step * (1 - 2 * place)
    side = place // 2
    inner = (place * (3 - place)) // 2
    found = step + inner * (1 - 2 * step) * (1 - step // 2)
    return found + side * (3 - 2 * found)


class Grid:
    def __init__(self, size):
        self.size, self.deep, self.across = size, DEEP, size // DEEP
        self.me = lax.axis_index("dp")
        self.z, self.x = self.me // self.across, self.me % self.across
        self.steps = (-self.across, self.across, -1, 1)
        self.exists = (
            self.z > 0,
            self.z < self.deep - 1,
            self.x > 0,
            self.x < self.across - 1,
        )
        self.count = (
            jnp.minimum(self.z, 1)
            + jnp.minimum(self.deep - 1 - self.z, 1)
            + jnp.minimum(self.x, 1)
            + jnp.minimum(self.across - 1 - self.x, 1)
        )

    def greet(self, barrier):
        for there, step in zip(self.exists, self.steps):
            @pl.when(there)
            def _():
                pl.semaphore_signal(
                    barrier, inc=1, device_id={"dp": self.me + step}, device_id_type=MESH_ID
                )


def gather_kernel(size, cols_count, count, *refs):
    owns, (token_ref,), sides = refs[:count], refs[count : count + 1], refs[count + 1 : count + 3]
    fulls, (seq_ref,), others = refs[count + 3 : 2 * count + 3], refs[2 * count + 3 : 2 * count + 4], refs[2 * count + 4 : 2 * count + 6]
    send_sem, recv_sem, local_sem, seq_send, seq_recv, col_send, col_recv = refs[2 * count + 6 :]
    grid = Grid(size)
    me, z, x = grid.me, grid.z, grid.x
    row, col = lax.axis_index("row"), lax.axis_index("col")
    barrier = pltpu.get_barrier_semaphore()
    grid.greet(barrier)
    pl.semaphore_signal(barrier, inc=1, device_id={"row": 1 - row}, device_id_type=MESH_ID)
    for by in range(1, cols_count):
        pl.semaphore_signal(
            barrier, inc=1, device_id={"col": (col + by) % cols_count}, device_id_type=MESH_ID
        )
    pl.semaphore_wait(barrier, grid.count + cols_count)

    def push(which, chunk, way, source=None):
        return pltpu.make_async_remote_copy(
            src_ref=fulls[which].at[chunk] if source is None else source,
            dst_ref=fulls[which].at[chunk],
            send_sem=send_sem.at[which, way, chunk],
            recv_sem=recv_sem.at[which, chunk],
            device_id={"dp": me + grid.steps[way]},
            device_id_type=MESH_ID,
        )

    def place(number):
        zc = near_first(z, number % grid.deep, grid.deep)
        xc = near_first(x, number // grid.deep, grid.across)
        same = xc == x
        onward = (
            same & (zc >= z) & grid.exists[0],
            same & (zc <= z) & grid.exists[1],
            (xc >= x) & grid.exists[2],
            (xc <= x) & grid.exists[3],
        )
        return zc * grid.across + xc, onward

    def token_push(source, slot, index, peer):
        return pltpu.make_async_remote_copy(
            src_ref=source,
            dst_ref=seq_ref.at[slot],
            send_sem=seq_send.at[index],
            recv_sem=seq_recv.at[slot],
            device_id=peer,
            device_id_type=MESH_ID,
        )

    mine = row * cols_count + col
    other_row = {"row": 1 - row}
    pushes = [token_push(token_ref, mine, 0, other_row)]
    for by in range(1, cols_count):
        pushes.append(token_push(token_ref, mine, by, {"col": (col + by) % cols_count}))
    for way in range(4):
        @pl.when(grid.exists[way])
        def _():
            for which in range(count):
                push(which, me, way, owns[which]).start()
    for copy in pushes:
        copy.start()
    keeps = [
        pltpu.make_async_copy(own, full.at[me], local_sem.at[which])
        for which, (own, full) in enumerate(zip(owns, fulls))
    ]
    keeps.append(pltpu.make_async_copy(token_ref, seq_ref.at[mine], local_sem.at[count]))
    for copy in keeps:
        copy.start()

    def pass_on(number, _):
        chunk, onward = place(number)
        for which in range(count):
            push(which, chunk, 0).wait_recv()
            for way in range(4):
                @pl.when(onward[way])
                def _():
                    push(which, chunk, way).start()
        return 0

    lax.fori_loop(1, 2, pass_on, 0)
    for by in range(1, cols_count):
        slot = row * cols_count + (col + by) % cols_count
        token_push(seq_ref.at[slot], slot, cols_count - 1 + by, other_row).wait_recv()
        copy = token_push(seq_ref.at[slot], slot, cols_count - 1 + by, other_row)
        copy.start()
        pushes.append(copy)
    for number, (side, other) in enumerate(zip(sides, others)):
        for by in range(1, cols_count):
            copy = pltpu.make_async_remote_copy(
                src_ref=side,
                dst_ref=other.at[by - 1],
                send_sem=col_send.at[number, by - 1],
                recv_sem=col_recv.at[number, by - 1],
                device_id={"col": (col + by) % cols_count},
                device_id_type=MESH_ID,
            )
            copy.start()
            pushes.append(copy)
    lax.fori_loop(2, size, pass_on, 0)
    for by in range(cols_count):
        slot = (1 - row) * cols_count + (col + by) % cols_count
        token_push(seq_ref.at[slot], slot, 0, other_row).wait_recv()
    for copy in pushes:
        copy.wait_send()
    for copy in pushes[len(pushes) - 2 * (cols_count - 1) :]:
        copy.wait_recv()

    def finish(number, _):
        chunk, onward = place(number)
        for way in range(4):
            @pl.when(onward[way])
            def _():
                for which in range(count):
                    push(which, chunk, way).wait_send()
        return 0

    lax.fori_loop(0, size, finish, 0)
    for copy in keeps:
        copy.wait()


def gather_start(values, tokens, sides, shape):
    size, columns, count = shape["dp"], shape["col"], len(values)
    results = pl.pallas_call(
        functools.partial(gather_kernel, size, columns, count),
        out_shape=tuple(
            jax.ShapeDtypeStruct((size,) + array.shape, array.dtype) for array in values
        )
        + (jax.ShapeDtypeStruct((2 * columns,) + tokens.shape, tokens.dtype),)
        + tuple(
            jax.ShapeDtypeStruct((columns - 1,) + array.shape, array.dtype) for array in sides
        ),
        in_specs=[ANY] * (count + 3),
        out_specs=(ANY,) * (count + 3),
        scratch_shapes=[
            pltpu.SemaphoreType.DMA((count, 4, size)),
            pltpu.SemaphoreType.DMA((count, size)),
            pltpu.SemaphoreType.DMA((count + 1,)),
            pltpu.SemaphoreType.DMA((2 * columns,)),
            pltpu.SemaphoreType.DMA((2 * columns,)),
            pltpu.SemaphoreType.DMA((2, columns - 1)),
            pltpu.SemaphoreType.DMA((2, columns - 1)),
        ],
        compiler_params=pltpu.CompilerParams(collective_id=2, has_side_effects=True),
        cost_estimate=lasting(125),
        name="gather_start",
    )(*values, tokens, *sides)
    return (
        [full.reshape((-1,) + full.shape[2:]) for full in results[: count + 1]],
        [
            [side] + [other[by - 1] for by in range(1, columns)]
            for side, other in zip(sides, results[count + 1 :])
        ],
    )


class LineSum:
    def __init__(self, grid, part_ref, out_ref, sums, from_x, from_z, x_send, x_recv, z_send, z_recv):
        self.grid, self.part_ref, self.out_ref = grid, part_ref, out_ref
        self.sums, self.from_x, self.from_z = sums, from_x, from_z
        self.x_send, self.x_recv, self.z_send, self.z_recv = x_send, x_recv, z_send, z_recv

    @staticmethod
    def scratch(size, chunk):
        pair = size == 2 * DEEP
        return [
            pltpu.VMEM((DEEP if pair else size,) + chunk, BF16),
            pltpu.VMEM((DEEP if pair else 2 * size,) + chunk, BF16),
            pltpu.VMEM((2 * DEEP,) + chunk, BF16),
            pltpu.SemaphoreType.DMA((size,)),
            pltpu.SemaphoreType.DMA((2 * size,)),
            pltpu.SemaphoreType.DMA((DEEP,)),
            pltpu.SemaphoreType.DMA((2 * DEEP,)),
        ]

    def sum_at(self, line, there):
        pair = self.grid.across == 2
        return self.sums.at[line if pair else line * self.grid.across + there]

    def along_x(self, line, there, way):
        grid = self.grid
        chunk = line * grid.across + there
        slot = way * grid.size + chunk
        pair = grid.across == 2
        return pltpu.make_async_remote_copy(
            src_ref=self.part_ref.at[chunk] if pair else self.sum_at(line, there),
            dst_ref=self.from_x.at[line if pair else slot],
            send_sem=self.x_send.at[chunk],
            recv_sem=self.x_recv.at[slot],
            device_id={"dp": grid.me + 2 * way - 1},
            device_id_type=MESH_ID,
        )

    def came_x(self, line, there, way):
        grid = self.grid
        slot = way * grid.size + line * grid.across + there
        return self.from_x[line if grid.across == 2 else slot].astype(F32)

    def along_z(self, line, way):
        grid = self.grid
        return pltpu.make_async_remote_copy(
            src_ref=self.sum_at(line, grid.x),
            dst_ref=self.from_z.at[way * grid.deep + line],
            send_sem=self.z_send.at[line],
            recv_sem=self.z_recv.at[way * grid.deep + line],
            device_id={"dp": grid.me + (2 * way - 1) * grid.across},
            device_id_type=MESH_ID,
        )

    @staticmethod
    def start(sums):
        grid = sums[0].grid
        x, across = grid.x, grid.across

        def away(number, _):
            line = near_first(grid.z, grid.deep - 1 - number // (across - 1), grid.deep)
            there = near_first(x, across - 1 - number % (across - 1), across)
            for one in sums:
                if across > 2:
                    one.sum_at(line, there)[...] = one.part_ref[line * across + there]
                for way, beyond in ((1, grid.exists[2]), (0, grid.exists[3])):
                    toward = (there > x) if way else (there < x)
                    if across > 2:
                        @pl.when(toward & beyond)
                        def _():
                            one.along_x(line, there, way).wait_recv()
                            held = one.sum_at(line, there)
                            held[...] = (
                                held[...].astype(F32) + one.came_x(line, there, way)
                            ).astype(BF16)
                    @pl.when(toward)
                    def _():
                        one.along_x(line, there, way).start()
            return 0

        lax.fori_loop(0, grid.deep * (across - 1), away, 0)

    @staticmethod
    def finish(sums):
        grid = sums[0].grid
        z, x, across = grid.z, grid.x, grid.across

        def collect(number, _):
            line = near_first(z, grid.deep - 1 - number, grid.deep)
            for one in sums:
                out_ref = one.out_ref
                out_ref[...] = one.part_ref[line * across + x].astype(F32)
                for way, there in ((1, grid.exists[2]), (0, grid.exists[3])):
                    @pl.when(there)
                    def _():
                        one.along_x(line, x, way).wait_recv()
                        out_ref[...] += one.came_x(line, x, way)
                for way, there in (
                    (1, grid.exists[0] & (line >= z)), (0, grid.exists[1] & (line <= z))
                ):
                    @pl.when(there)
                    def _():
                        one.along_z(line, way).wait_recv()
                        out_ref[...] += one.from_z[way * grid.deep + line].astype(F32)
                for way, toward in ((1, line > z), (0, line < z)):
                    @pl.when(toward)
                    def _():
                        one.sum_at(line, x)[...] = out_ref[...].astype(BF16)
                        one.along_z(line, way).start()
            return 0

        lax.fori_loop(0, grid.deep, collect, 0)

        def wait(number, _):
            line = near_first(z, grid.deep - 1 - number // across, grid.deep)
            there = near_first(x, across - 1 - number % across, across)
            for one in sums:
                for way in range(2):
                    @pl.when((there > x) if way else (there < x))
                    def _():
                        one.along_x(line, there, way).wait_send()
                    @pl.when((there == x) & ((line > z) if way else (line < z)))
                    def _():
                        one.along_z(line, way).wait_send()
            return 0

        lax.fori_loop(0, grid.size, wait, 0)


def scatter_kernel(size, part_ref, out_ref, *scratch):
    grid = Grid(size)
    barrier = pltpu.get_barrier_semaphore()
    grid.greet(barrier)
    pl.semaphore_wait(barrier, grid.count)
    sums = [LineSum(grid, part_ref, out_ref, *scratch)]
    LineSum.start(sums)
    LineSum.finish(sums)


def scatter_blocks(parts, shape):
    size = shape["dp"]
    if size > 2 * DEEP:
        return scatter_dp(parts).astype(F32)
    parts = parts.reshape((size, -1, parts.shape[1]))
    chunk = parts.shape[1:]
    return pl.pallas_call(
        functools.partial(scatter_kernel, size),
        out_shape=jax.ShapeDtypeStruct(chunk, F32),
        in_specs=[VM],
        out_specs=VM,
        scratch_shapes=LineSum.scratch(size, chunk),
        compiler_params=pltpu.CompilerParams(
            collective_id=5, has_side_effects=True, vmem_limit_bytes=56 * 2**20
        ),
        cost_estimate=lasting(75),
        name="scatter_blocks",
    )(parts)


def end_kernel(
    size, steps, columns, at, count, *refs
):
    part_refs, (value_ref, seq_ref, up_ref, down_ref), refs = (
        refs[:count], refs[count : count + 4], refs[count + 4 :]
    )
    out_refs, (total_ref, small_ref, rows_ref, ups_ref, downs_ref), refs = (
        refs[:count], refs[count : count + 5], refs[count + 5 :]
    )
    landed, half_now, half_in, quarter, quarter_in, seq_half, seq_sent, seq_in = refs[:8]
    t_send, t_recv, s_send, s_recv, q_send, q_recv, c_send, c_recv = refs[8:16]
    scratch, out_ref = refs[16:], out_refs[0]
    grid = Grid(size)
    row, col = lax.axis_index("row"), lax.axis_index("col")

    def other(name, bit):
        place = lax.axis_index(name)
        return {name: place + bit * (1 - 2 * ((place // bit) % 2))}

    barrier = pltpu.get_barrier_semaphore()
    grid.greet(barrier)
    for name, bit in steps:
        pl.semaphore_signal(barrier, inc=1, device_id=other(name, bit), device_id_type=MESH_ID)
    for by in range(1, columns):
        pl.semaphore_signal(
            barrier, inc=1, device_id={"col": (col + by) % columns}, device_id_type=MESH_ID
        )
    pl.semaphore_wait(barrier, grid.count + len(steps) + columns - 1)

    seq_rows, block = seq_half.shape[0], rows_ref.shape[0]
    swap_rows = pltpu.make_async_remote_copy(
        src_ref=seq_ref.at[pl.ds(pl.multiple_of((1 - row) * seq_rows, 16), seq_rows)],
        dst_ref=seq_half,
        send_sem=q_send.at[0],
        recv_sem=q_recv.at[0],
        device_id={"row": 1 - row},
        device_id_type=MESH_ID,
    )
    swap_rows.start()

    total_ref[...] = value_ref[...]

    def exchange(number):
        name, bit = steps[number]
        copy = pltpu.make_async_remote_copy(
            src_ref=total_ref,
            dst_ref=landed.at[number],
            send_sem=t_send.at[number],
            recv_sem=t_recv.at[number],
            device_id=other(name, bit),
            device_id_type=MESH_ID,
        )
        copy.start()
        copy.wait()
        total_ref[...] += landed[number]

    early = len([1 for name, bit in steps if name == "dp" and bit < grid.across])
    for number in range(early):
        exchange(number)
    sums = [
        LineSum(grid, part_refs[number], out_refs[number], *scratch[7 * number : 7 * number + 7])
        for number in range(count)
    ]
    LineSum.start(sums)

    def both_rows(place):
        mine = seq_ref[pl.ds(pl.multiple_of(row * seq_rows + place * block, 16), block), :]
        theirs = seq_half[pl.ds(pl.multiple_of(place * block, 16), block), :]
        return mine.astype(F32) + theirs.astype(F32)

    swap_rows.wait()
    moves = []
    for by in range(1, columns):
        to = (col + by) % columns
        seq_sent[by] = both_rows(to).astype(BF16)
        moves.append(
            pltpu.make_async_remote_copy(
                src_ref=seq_sent.at[by],
                dst_ref=seq_in.at[by],
                send_sem=q_send.at[by],
                recv_sem=q_recv.at[by],
                device_id={"col": to},
                device_id_type=MESH_ID,
            )
        )
    for number in range(early, len(steps)):
        exchange(number)
    for copy in moves:
        copy.start()
    rows_ref[...] = both_rows(col)
    sides = []
    for number, (side, other_side) in enumerate(((up_ref, ups_ref), (down_ref, downs_ref))):
        for by in range(1, columns):
            to = (col + by) % columns
            sides.append(
                pltpu.make_async_remote_copy(
                    src_ref=side.at[to],
                    dst_ref=other_side.at[by - 1],
                    send_sem=c_send.at[number, by - 1],
                    recv_sem=c_recv.at[number, by - 1],
                    device_id={"col": to},
                    device_id_type=MESH_ID,
                )
            )
            sides[-1].start()
    LineSum.finish(sums)
    for by, copy in enumerate(moves):
        copy.wait()
        rows_ref[...] += seq_in[by + 1].astype(F32)

    half, (fourth, narrow) = half_now.shape[0], small_ref.shape
    half_now[...] = out_ref[pl.ds(pl.multiple_of((1 - row) * half, 8), half), at : at + narrow]
    swap = pltpu.make_async_remote_copy(
        src_ref=half_now,
        dst_ref=half_in,
        send_sem=s_send.at[0],
        recv_sem=s_recv.at[0],
        device_id={"row": 1 - row},
        device_id_type=MESH_ID,
    )
    swap.start()
    swap.wait()
    both = out_ref[pl.ds(pl.multiple_of(row * half, 8), half), at : at + narrow] + half_in[...]
    for place in range(columns):
        quarter[place] = both[place * fourth : (place + 1) * fourth]
    copies = []
    for by in range(1, columns):
        to = (col + by) % columns
        copies.append(
            pltpu.make_async_remote_copy(
                src_ref=quarter.at[to],
                dst_ref=quarter_in.at[by],
                send_sem=s_send.at[by],
                recv_sem=s_recv.at[by],
                device_id={"col": to},
                device_id_type=MESH_ID,
            )
        )
        copies[-1].start()
    small_ref[...] = quarter[col]
    for by, copy in enumerate(copies):
        copy.wait()
        small_ref[...] += quarter_in[by + 1]
    for copy in sides:
        copy.wait()


def scatter_end(parts, values, rows, up, down, at, narrow, shape):
    size, columns = shape["dp"], shape["col"]
    steps = partners(shape)
    parts = [part.reshape((size, -1, part.shape[1])) for part in parts]
    chunk, count = parts[0].shape[1:], len(parts)
    half, seq_rows = chunk[0] // 2, rows.shape[0] // 2
    block = (seq_rows // columns, rows.shape[1])
    fourth = (columns, half // columns, narrow)
    return pl.pallas_call(
        functools.partial(end_kernel, size, steps, columns, at, count),
        out_shape=tuple(jax.ShapeDtypeStruct(part.shape[1:], F32) for part in parts)
        + (
            jax.ShapeDtypeStruct(values.shape, F32),
            jax.ShapeDtypeStruct(fourth[1:], F32),
            jax.ShapeDtypeStruct(block, F32),
            jax.ShapeDtypeStruct((columns - 1,) + up.shape[1:], BF16),
            jax.ShapeDtypeStruct((columns - 1,) + down.shape[1:], BF16),
        ),
        in_specs=[VM] * (count + 2) + [ANY] * 2,
        out_specs=(VM,) * (count + 3) + (ANY,) * 2,
        scratch_shapes=[
            pltpu.VMEM((len(steps),) + values.shape, F32),
            pltpu.VMEM((half, narrow), F32),
            pltpu.VMEM((half, narrow), F32),
            pltpu.VMEM(fourth, F32),
            pltpu.VMEM(fourth, F32),
            pltpu.VMEM((seq_rows, rows.shape[1]), BF16),
            pltpu.VMEM((columns,) + block, BF16),
            pltpu.VMEM((columns,) + block, BF16),
            pltpu.SemaphoreType.DMA((len(steps),)),
            pltpu.SemaphoreType.DMA((len(steps),)),
            pltpu.SemaphoreType.DMA((columns,)),
            pltpu.SemaphoreType.DMA((columns,)),
            pltpu.SemaphoreType.DMA((columns,)),
            pltpu.SemaphoreType.DMA((columns,)),
            pltpu.SemaphoreType.DMA((2, columns - 1)),
            pltpu.SemaphoreType.DMA((2, columns - 1)),
        ]
        + sum([LineSum.scratch(size, part.shape[1:]) for part in parts], []),
        compiler_params=pltpu.CompilerParams(
            collective_id=3, has_side_effects=True, vmem_limit_bytes=60 * 2**20
        ),
        cost_estimate=lasting(125),
        name="scatter_end",
    )(*parts, values, rows, up, down)


def shared_block(x_ref, g_ref, up_ref, down_ref, hid_ref, dpre_ref, out_ref, dx_ref):
    x, g = x_ref[...], g_ref[:, :MODEL_WIDTH]
    pre = dot_f32(x, up_ref[...])
    asked = dot_t(g, down_ref[...])
    half = down_ref.shape[0]
    for part in range(half // 128):
        lanes = slice(128 * part, 128 * (part + 1))
        upper = slice(half + 128 * part, half + 128 * (part + 1))
        gate, up, want = pre[:, lanes], pre[:, upper], asked[:, lanes]
        sig = jax.nn.sigmoid(gate)
        act = gate * sig
        hid_ref[:, lanes] = (act * up).astype(BF16)
        dpre_ref[:, lanes] = (want * up * (sig * (1.0 + gate * (1.0 - sig)))).astype(BF16)
        dpre_ref[:, upper] = (want * act).astype(BF16)
    out_ref[...] = dot_f32(hid_ref[...], down_ref[...])
    dx_ref[...] = dot_t(dpre_ref[...], up_ref[...])


def expert_block(own, x_ref, g_ref, up_ref, down_ref, router_ref, hid_ref, dpre_ref, mix_ref, dx_ref):
    x, g = x_ref[...], g_ref[:, :MODEL_WIDTH]
    logits = dot_f32(x, router_ref[...])
    named = g_ref[:, MODEL_WIDTH:].astype(F32)
    high = jnp.max(jnp.where(named > 0, logits, -1e30), axis=1, keepdims=True)
    raised = jnp.where(named > 0, jnp.exp(logits - high), 0.0)
    gates = raised / jnp.sum(raised, axis=1, keepdims=True)
    rows = x.shape[0]
    lane = lax.broadcasted_iota(jnp.int32, (rows, 128), 1)
    weights = [
        jnp.sum(jnp.where(lane == own + part, gates, 0.0), axis=1, keepdims=True)
        for part in range(EXP_DEV)
    ]
    half = down_ref.shape[0]
    pre = dot_f32(x, up_ref[...])
    asked = dot_t(g, down_ref[...])
    totals = [jnp.zeros((rows, 128), F32) for part in range(EXP_DEV)]
    for part in range(half // 128):
        which = 128 * part // FF_E
        at = 128 * part + FF_E * which
        lanes = slice(128 * part, 128 * (part + 1))
        lower, upper = slice(at, at + 128), slice(at + FF_E, at + FF_E + 128)
        gate, up, want = pre[:, lower], pre[:, upper], asked[:, lanes]
        sig = jax.nn.sigmoid(gate)
        act = gate * sig
        hidden = act * up
        totals[which] = totals[which] + hidden * want
        hid_ref[:, lanes] = (weights[which] * hidden).astype(BF16)
        dact = weights[which] * want
        dpre_ref[:, lower] = (dact * up * (sig * (1.0 + gate * (1.0 - sig)))).astype(BF16)
        dpre_ref[:, upper] = (dact * act).astype(BF16)
    mix_ref[...] = dot_f32(hid_ref[...], down_ref[...]).astype(BF16)
    dx_ref[:, :MODEL_WIDTH] = dot_t(dpre_ref[...], up_ref[...]).astype(BF16)
    sent = jnp.zeros((rows, 128), F32)
    for part in range(EXP_DEV):
        gate_grad = jnp.sum(totals[part], axis=1, keepdims=True)
        coarse = gate_grad.astype(BF16).astype(F32)
        sent = jnp.where(lane == own + part, coarse, sent)
        sent = jnp.where(lane == own + part + REST_AT, gate_grad - coarse, sent)
    dx_ref[:, MODEL_WIDTH:] = sent.astype(BF16)


def expert_kernel(
    size, own_ref, g_ref, up_ref, down_ref, router_ref, shared_up_ref, shared_down_ref, full_ref, *refs
):
    outs, shared, (x_now, g_now), stages, (send_sem, recv_sem, local_sem, in_sem, out_sem) = (
        refs[:4], refs[4:8], refs[8:10], refs[10:14], refs[14:]
    )
    grid = Grid(size)
    me, z, x = grid.me, grid.z, grid.x
    barrier = pltpu.get_barrier_semaphore()
    grid.greet(barrier)
    pl.semaphore_wait(barrier, grid.count)

    def push(source, chunk, way):
        return pltpu.make_async_remote_copy(
            src_ref=source,
            dst_ref=full_ref.at[chunk],
            send_sem=send_sem.at[way, chunk],
            recv_sem=recv_sem.at[chunk],
            device_id={"dp": me + grid.steps[way]},
            device_id_type=MESH_ID,
        )

    def place(number):
        if grid.across == 2:
            even, first, last = 1 - number % 2, 1 - jnp.minimum(number, 1), number // 7
            step = (1 - even) * ((number + 1) // 2 - last) + even * (number // 2 - 1 + first)
            side = even * (1 - first) + last
        else:
            step, side = number % grid.deep, number // grid.deep
        zc = near_first(z, step, grid.deep)
        xc = near_first(x, side, grid.across)
        same = xc == x
        onward = (
            same & (zc >= z) & grid.exists[0],
            same & (zc <= z) & grid.exists[1],
            (xc >= x) & grid.exists[2],
            (xc <= x) & grid.exists[3],
        )
        return zc * grid.across + xc, onward

    for way in range(4):
        @pl.when(grid.exists[way])
        def _():
            push(own_ref, me, way).start()
    keep = pltpu.make_async_copy(own_ref, full_ref.at[me], local_sem)
    keep.start()

    def leave(number, chunk):
        return [
            pltpu.make_async_copy(stage.at[number % 2], out.at[chunk], out_sem.at[place_in, number % 2])
            for place_in, (stage, out) in enumerate(zip(stages, outs))
        ]

    def work(number, _):
        chunk, onward = place(number)
        bring = pltpu.make_async_copy(g_ref.at[chunk], g_now, in_sem.at[0])
        bring.start()

        @pl.when(number > 0)
        def _():
            push(full_ref.at[chunk], chunk, 0).wait_recv()
            for way in range(4):
                @pl.when(onward[way])
                def _():
                    push(full_ref.at[chunk], chunk, way).start()

        bring_x = pltpu.make_async_copy(full_ref.at[chunk], x_now, in_sem.at[1])

        @pl.when(number == 0)
        def _():
            pltpu.make_async_copy(own_ref, x_now, in_sem.at[1]).start()

        @pl.when(number > 0)
        def _():
            bring_x.start()

        @pl.when(number > 1)
        def _():
            for copy in leave(number, place(number - 2)[0]):
                copy.wait()

        bring.wait()
        bring_x.wait()
        expert_block(
            EXP_DEV * me, x_now, g_now, up_ref, down_ref, router_ref,
            *[stage.at[number % 2] for stage in stages]
        )
        for copy in leave(number, chunk):
            copy.start()

        @pl.when(number == 0)
        def _():
            shared_block(x_now, g_now, shared_up_ref, shared_down_ref, *shared)

        return 0

    lax.fori_loop(0, size, work, 0)
    for number in (size - 2, size - 1):
        for copy in leave(number, place(number)[0]):
            copy.wait()

    def finish(number, _):
        chunk, onward = place(number)
        for way in range(4):
            @pl.when(onward[way])
            def _():
                push(full_ref.at[chunk], chunk, way).wait_send()
        return 0

    lax.fori_loop(0, size, finish, 0)
    keep.wait()


def experts(tokens, cotangents, up, down, router, shared_up, shared_down, shape):
    size = shape["dp"]
    rows, width = tokens.shape
    hidden = down.shape[0]
    wide = width + 128
    columns = (hidden, 2 * hidden, width, wide)
    results = pl.pallas_call(
        functools.partial(expert_kernel, size),
        out_shape=tuple(
            jax.ShapeDtypeStruct((size, rows, column), BF16) for column in (width,) + columns
        )
        + (
            jax.ShapeDtypeStruct((rows, shared_down.shape[0]), BF16),
            jax.ShapeDtypeStruct((rows, shared_up.shape[1]), BF16),
            jax.ShapeDtypeStruct((rows, width), F32),
            jax.ShapeDtypeStruct((rows, width), F32),
        ),
        in_specs=[ANY, ANY, VM, VM, VM, VM, VM],
        out_specs=(ANY,) * 5 + (VM,) * 4,
        scratch_shapes=[pltpu.VMEM((rows, width), BF16), pltpu.VMEM((rows, wide), BF16)]
        + [pltpu.VMEM((2, rows, column), BF16) for column in columns]
        + [
            pltpu.SemaphoreType.DMA((4, size)),
            pltpu.SemaphoreType.DMA((size,)),
            pltpu.SemaphoreType.DMA,
            pltpu.SemaphoreType.DMA((2,)),
            pltpu.SemaphoreType.DMA((4, 2)),
        ],
        compiler_params=pltpu.CompilerParams(
            collective_id=4, has_side_effects=True, vmem_limit_bytes=56 * 2**20
        ),
        cost_estimate=lasting(85),
        name="experts",
    )(tokens, cotangents.reshape(size, rows, wide), up, down, router, shared_up, shared_down)
    return [result.reshape(size * rows, -1) for result in results[:5]] + list(results[5:])


def rms_scale(values):
    return lax.rsqrt(jnp.mean(values * values, axis=-1, keepdims=True) + 1e-05)


def rms_back(values, scale, gain, grad_normed):
    weighted = grad_normed * gain[None, :]
    grad_values = scale * weighted - values * scale**3 * jnp.mean(
        weighted * values, axis=-1, keepdims=True
    )
    gain_grad = jnp.sum(grad_normed * values * scale, axis=0)
    return (grad_values, gain_grad)


def silu_gate(pre_values):
    half_size = pre_values.shape[-1] // 2
    return jax.nn.silu(pre_values[..., :half_size]) * pre_values[..., half_size:]


def silu_gate_back(pre_values, grad):
    return jax.vjp(silu_gate, pre_values)[1](grad)[0]


def adamw(weight, grad, first, second, rate, decay=0.1):
    grad = grad.astype(F32)
    first_new = 0.9 * first + 0.1 * grad
    second_new = 0.95 * second + 0.05 * grad * grad
    corrected_one = first_new / (1.0 - 0.9**STEP)
    corrected_two = second_new / (1.0 - 0.95**STEP)
    weight_new = weight - rate * (
        corrected_one / (jnp.sqrt(corrected_two) + 1e-08) + decay * weight
    )
    return (first_new, second_new, weight_new)


ALL = ("dp", "row", "col")


def gather_dp(values):
    return lax.all_gather(values, "dp", axis=0, tiled=True)


def scatter_dp(values):
    return lax.psum_scatter(values, "dp", scatter_dimension=0, tiled=True)


def body(
    shape,
    hidden_in, segment_ids, routes, out_grad,
    vectors, vectors_first, vectors_second,
    in_weight, in_weight_first, in_weight_second,
    step_weight, step_weight_first, step_weight_second,
    out_weight, out_weight_first, out_weight_second,
    state_weight, state_weight_first, state_weight_second,
    router, router_first, router_second,
    shared_up, shared_up_first, shared_up_second,
    shared_down, shared_down_first, shared_down_second,
    expert_gate_up, expert_gate_up_first, expert_gate_up_second,
    expert_down, expert_down_first, expert_down_second,
):
    dp = lax.axis_index("dp")
    data_count = lax.axis_size("dp")
    seq_devices = lax.axis_size("row") * lax.axis_size("col")
    local_heads = in_weight.shape[1]
    width = 64 * local_heads
    head_start = lax.axis_index(("row", "col")) * local_heads
    own_tokens = hidden_in.shape[1]
    experts_all = router.shape[1]
    rows_dp = in_weight.shape[0]
    residual = hidden_in[0].astype(F32)
    gain_one = vectors[0:MODEL_WIDTH]
    gain_two = vectors[MODEL_WIDTH : 2 * MODEL_WIDTH]

    out_local = out_weight.astype(BF16).reshape(width, -1).T
    small = jnp.concatenate([state_weight, router], axis=1).astype(BF16)
    small = gather_rc(small)
    fill = lambda columns: jnp.zeros((rows_dp, columns), BF16)
    mixer_local = jnp.concatenate(
        [
            in_weight.astype(BF16).reshape(rows_dp, 2 * width),
            small[:, : 2 * STATE],
            step_weight.astype(BF16),
            fill(ROUTER_AT - local_heads),
            small[:, 2 * STATE :],
            fill(128 - ROUTER_AT - experts_all),
        ],
        axis=1,
    )
    scale_one = rms_scale(residual)
    normed_one = (residual * scale_one * gain_one[None, :]).astype(BF16)
    up_local = jnp.concatenate(
        [expert_gate_up[held].astype(BF16) for held in range(EXP_DEV)], axis=1
    )
    down_local = expert_down.astype(BF16).reshape(-1, MODEL_WIDTH)
    up_rows, down_rows, shared_wide = shared_up.shape[0], shared_down.shape[0], 2 * FF_S
    (mixer_full, out_full, shared_up_dp, shared_down_dp, normed_all), (up_parts, down_parts) = (
        gather_start(
            (mixer_local, out_local, shared_up.astype(BF16), shared_down.astype(BF16)),
            normed_one,
            (up_local, down_local),
            shape,
        )
    )
    up_full = assemble(all_places(up_parts), 1)
    down_full = assemble(all_places(down_parts), EXP_DEV)
    mixer_full, out_full, shared_up_dp, shared_down_dp, normed_all, segment_ids, routes, out_grad = (
        lax.optimization_barrier(
            (mixer_full, out_full, shared_up_dp, shared_down_dp, normed_all, segment_ids, routes, out_grad)
        )
    )
    by_columns = lambda array: [array] + [
        shift(array, "col", by) for by in range(1, lax.axis_size("col"))
    ]
    shared_up_full = assemble(all_places(by_columns(shared_up_dp)), data_count)
    shared_down_full = assemble(all_places(by_columns(shared_down_dp)), data_count)
    route_ids = routes[0]
    chosen = (
        route_ids[:, :, None] == jnp.arange(experts_all, dtype=jnp.int32)[None, None, :]
    ).any(axis=1)
    grad_low = out_grad[0]
    grad_ext = jnp.concatenate(
        [grad_low, jnp.pad(chosen.astype(BF16), ((0, 0), (0, 128 - experts_all)))], axis=1
    )
    grad_all = gather_dp(grad_ext)
    xbc = INNER + 2 * STATE
    at_bias = 2 * MODEL_WIDTH + INNER
    at_taps = at_bias + xbc
    at_head = at_taps + KW * xbc
    start = head_start * 64
    cut = lambda array, at, size: lax.dynamic_slice_in_dim(array, at, size, axis=-1)
    local = lambda array: jnp.concatenate([cut(array, start, width), array[..., INNER:]], axis=-1)
    wide = width + 2 * STATE
    line = lambda vec: jnp.pad(vec, (0, wide - vec.shape[0]))[None]
    per_head = lambda number: cut(vectors, at_head + number * HEADS + head_start, local_heads)
    decay_rate = -jnp.exp(per_head(0))
    params = jnp.concatenate(
        [
            local(vectors[at_taps:at_head].reshape(KW, xbc)),
            local(vectors[at_bias:at_taps])[None],
            line(cut(vectors, 2 * MODEL_WIDTH + start, width)),
            line(decay_rate),
            line(per_head(2)),
            line(jnp.repeat(per_head(1), 64)),
            jnp.zeros((7, wide), F32),
        ],
        axis=0,
    )
    seg_rows = segment_ids[0].astype(F32).reshape(-1, 1, BLK)
    proj = dot_f32(normed_all, mixer_full[:, : 2 * width]).astype(BF16)
    ss = dot_f32(normed_all, mixer_full[:, 2 * width :])
    valued, squares_part, kept = mixer_forward(proj, ss, seg_rows, params)
    proj_out = scatter_rc(dot_t(valued, out_full).astype(BF16))
    squares = scatter_squares(squares_part)[:, 0]
    scale_two = lax.rsqrt(squares / INNER + 1e-05)
    residual_two = residual + scale_two[:, None] * proj_out
    scale_three = rms_scale(residual_two)
    normed_two = (residual_two * scale_three * gain_two[None, :]).astype(BF16)

    router_pad = mixer_full[:, 2 * width + 2 * STATE + ROUTER_AT :]
    router_full = router_pad[:, :experts_all]
    router_wide = jnp.pad(router_full, ((0, 0), (0, 128 - experts_all)))
    (
        tokens_all, hidden_low, pre_grad, mixed, rows_grad,
        shared_act, shared_pre_grad, shared_out, shared_dx,
    ) = experts(
        normed_two, grad_all, up_full, down_full, router_wide, shared_up_full, shared_down_full, shape
    )
    logits = dot_f32(normed_two, router_full)
    gate_all = jax.nn.softmax(jnp.where(chosen, logits, -jnp.inf), axis=-1)
    routed_grad = scatter_blocks(rows_grad, shape)
    routed_grad, mixed = lax.optimization_barrier((routed_grad, mixed))
    mixture = scatter_dp(mixed).astype(F32)
    gate_grad = (
        routed_grad[:, MODEL_WIDTH : MODEL_WIDTH + experts_all]
        + routed_grad[:, MODEL_WIDTH + REST_AT : MODEL_WIDTH + REST_AT + experts_all]
    )
    cotangent = grad_low.astype(F32)
    normed_two_grad = shared_dx + routed_grad[:, :MODEL_WIDTH]
    logits_grad = gate_all * (gate_grad - jnp.sum(gate_all * gate_grad, axis=1, keepdims=True))
    logits_low = jnp.where(chosen, logits_grad, 0.0).astype(BF16)
    normed_two_grad = normed_two_grad + dot_t(logits_low, router_full)
    router_grad = dot_tn(normed_two, logits_low)
    residual_two_grad, gain_two_grad = rms_back(
        residual_two, scale_three, gain_two, normed_two_grad
    )
    residual_two_grad = residual_two_grad + cotangent
    proj_out_grad = (residual_two_grad * scale_two[:, None]).astype(BF16)
    squares_grad = (
        jnp.sum(residual_two_grad * proj_out, axis=1) * -0.5 * scale_two**3 / INNER
    )
    squares_high = squares_grad.astype(BF16)
    squares_rest = (squares_grad - squares_high.astype(F32)).astype(BF16)
    riding = jnp.pad(jnp.stack([squares_high, squares_rest], axis=1), ((0, 0), (0, 126)))
    riders = jnp.concatenate([proj_out_grad, riding], axis=1)
    riders, tokens_all, pre_grad, hidden_low, shared_act, shared_pre_grad = lax.optimization_barrier(
        (riders, tokens_all, pre_grad, hidden_low, shared_act, shared_pre_grad)
    )
    riders = gather_rc(riders)
    proj_grad_all = riders[:, :MODEL_WIDTH]
    squares_grad_all = jnp.sum(riders[:, MODEL_WIDTH:].astype(F32), axis=1, keepdims=True)
    shared_up_kept = scatter_row(dot_tn(normed_two, shared_pre_grad).astype(BF16), data_count)
    shared_down_kept = scatter_row(dot_tn(shared_act, grad_low).astype(BF16), data_count)
    proj_grad_all, shared_up_kept, shared_down_kept = lax.optimization_barrier(
        (proj_grad_all, shared_up_kept, shared_down_kept)
    )
    shared_up_part = scatter_col(shared_up_kept).astype(BF16)
    shared_down_part = scatter_col(shared_down_kept).astype(BF16)
    up_kept = scatter_row(dot_tn(tokens_all, pre_grad).astype(BF16))
    down_kept = scatter_row(
        dot_tn(hidden_low, grad_all[:, :MODEL_WIDTH]).astype(BF16), EXP_DEV
    )
    columns = lax.axis_size("col")
    up_kept = up_kept.reshape(columns, -1, up_kept.shape[2])
    down_kept = (
        down_kept.reshape(EXP_DEV, columns, -1, MODEL_WIDTH)
        .transpose(1, 0, 2, 3)
        .reshape(columns, -1, MODEL_WIDTH)
    )
    up_sent, down_sent = up_kept.astype(BF16), down_kept.astype(BF16)

    valued_grad = dot_f32(proj_grad_all, out_full).astype(BF16)
    out_grad_t = dot_tn(proj_grad_all, valued).astype(BF16)
    proj_grad, ss_grad, par_grad = mixer_backward(
        proj, ss, seg_rows, params, valued_grad, squares_grad_all, kept
    )
    all_grad = jnp.concatenate([proj_grad, ss_grad], axis=1)
    normed_part = dot_t(all_grad, mixer_full)
    gain_one_grad = jnp.sum(normed_part * normed_all.astype(F32), axis=0) / gain_one
    router_wide = jnp.pad(
        router_grad, ((0, 0), (2 * width + 2 * STATE + ROUTER_AT, 128 - ROUTER_AT - experts_all))
    )
    mixer_grad = (dot_tn(normed_all, all_grad) + router_wide).astype(BF16)
    place = lambda values, at, size: lax.dynamic_update_slice(
        jnp.zeros(values.shape[:-1] + (size,), F32), values, (0,) * (values.ndim - 1) + (at,)
    )
    spread_out = lambda values: jnp.concatenate(
        [place(values[..., :width], start, INNER), values[..., width:]], axis=-1
    )
    vector_local = jnp.concatenate(
        [
            gain_one_grad,
            gain_two_grad,
            place(par_grad[6, :width], start, INNER),
            spread_out(par_grad[4]),
            spread_out(par_grad[0:KW]).reshape(-1),
            place(par_grad[7, :local_heads] * decay_rate, head_start, HEADS),
            place(par_grad[8, :width].reshape(local_heads, 64).sum(axis=1), head_start, HEADS),
            place(par_grad[9, :local_heads], head_start, HEADS),
        ]
    )
    count = vector_local.shape[0]
    lines = -(-count // 1024) * 8
    vector_lines = jnp.pad(vector_local, (0, lines * 128 - count)).reshape(lines, 128)
    (
        mixer_total, out_total, shared_up_total, shared_down_total,
        vector_total, small_total, normed_grad, ups, downs,
    ) = scatter_end(
        (mixer_grad, out_grad_t, shared_up_part, shared_down_part),
        vector_lines,
        normed_part.astype(BF16),
        up_sent,
        down_sent,
        2 * width,
        2 * STATE + 128,
        shape,
    )
    out_total = out_total.T.reshape(out_weight.shape)
    mixture, mixer_total = lax.optimization_barrier((mixture, mixer_total))
    hidden_out = (residual_two + mixture + shared_out).astype(BF16)[None]
    own_column = lambda kept, came: lax.dynamic_index_in_dim(
        kept, lax.axis_index("col"), 0, keepdims=False
    ) + jnp.sum(came.astype(F32), axis=0)
    up_total, down_total = own_column(up_kept, ups), own_column(down_kept, downs)
    up_total = jnp.stack(
        [up_total[:, 2 * FF_E * held : 2 * FF_E * (held + 1)] for held in range(EXP_DEV)]
    )
    down_total = down_total.reshape(expert_down.shape)
    vector_total = vector_total.reshape(-1)[:count]
    state_total = small_total[:, : 2 * STATE]
    router_total = small_total[:, 2 * STATE + ROUTER_AT : 2 * STATE + ROUTER_AT + experts_all]
    step_total = mixer_total[:, 2 * width + 2 * STATE : 2 * width + 2 * STATE + local_heads]
    in_total = mixer_total[:, : 2 * width].reshape(in_weight.shape)
    residual_grad, _ = rms_back(residual, scale_one, gain_one, normed_grad)
    input_grad = (residual_grad + residual_two_grad)[None]

    rate = MODEL_WIDTH ** (-0.5)
    return (
        hidden_out,
        input_grad,
        *adamw(vectors, vector_total, vectors_first, vectors_second, 0.3, 0.0),
        *adamw(in_weight, in_total, in_weight_first, in_weight_second, rate),
        *adamw(step_weight, step_total, step_weight_first, step_weight_second, rate),
        *adamw(out_weight, out_total, out_weight_first, out_weight_second, INNER ** (-0.5)),
        *adamw(state_weight, state_total, state_weight_first, state_weight_second, rate),
        *adamw(router, router_total, router_first, router_second, 0.5 * rate),
        *adamw(shared_up, shared_up_total, shared_up_first, shared_up_second, rate),
        *adamw(shared_down, shared_down_total, shared_down_first, shared_down_second, FF_S ** (-0.5)),
        *adamw(expert_gate_up, up_total, expert_gate_up_first, expert_gate_up_second, rate),
        *adamw(expert_down, down_total, expert_down_first, expert_down_second, FF_E ** (-0.5)),
    )


def solution(mesh):
    tokens = P("dp", ("row", "col"), None)
    by_head = P("dp", ("row", "col"))
    out_spec = P(("row", "col"), None, "dp")
    flat = P(ALL, None)
    weights = (
        (P(),) * 3
        + (tokens,) * 3
        + (by_head,) * 3
        + (out_spec,) * 3
        + (flat,) * 12
        + (tokens,) * 6
    )
    return jax.shard_map(
        functools.partial(body, dict(mesh.shape)),
        mesh=mesh,
        in_specs=(tokens, P("dp", None), tokens, tokens) + weights,
        out_specs=(tokens, tokens) + weights,
        check_vma=False,
    )
```

```python
import functools

import jax
import jax.numpy as jnp
from jax import lax
from jax.experimental import pallas as pl
from jax.experimental.pallas import tpu as pltpu
from jax.sharding import PartitionSpec as P

STATE = 128
KW = 4
BLK = 128
F32 = jnp.float32
BF16 = jnp.bfloat16


def dot_f32(a, b, dims=(((1,), (0,)), ((), ()))):
    return lax.dot_general(a, b, dims, preferred_element_type=F32)


def dot_exact(a, b, dims=(((1,), (0,)), ((), ()))):
    return lax.dot_general(
        a, b, dims, precision=lax.Precision.HIGHEST, preferred_element_type=F32
    )


def spread(values, width):
    rows = values.shape[0]
    low = lax.broadcasted_iota(jnp.int32, (rows, 128), 1) < 64
    parts = []
    for pair in range(width // 128):
        left = jnp.broadcast_to(values[:, 2 * pair : 2 * pair + 1], (rows, 128))
        right = jnp.broadcast_to(values[:, 2 * pair + 1 : 2 * pair + 2], (rows, 128))
        parts.append(jnp.where(low, left, right))
    return jnp.concatenate(parts, axis=1)


def head_sums(values):
    width = values.shape[1]
    ones = (
        lax.broadcasted_iota(jnp.int32, (width, 128), 0) // 64
        == lax.broadcasted_iota(jnp.int32, (width, 128), 1)
    ).astype(BF16)
    high = values.astype(BF16)
    rest = (values - high.astype(F32)).astype(BF16)
    return dot_f32(high, ones) + dot_f32(rest, ones)


def apart(values):
    low = lax.broadcasted_iota(jnp.int32, (values.shape[0], 128), 1) < 64
    gates, inputs = [], []
    for at in range(0, values.shape[1], 256):
        one, two = values[:, at : at + 128], values[:, at + 128 : at + 256]
        gates.append(jnp.where(low, one, pltpu.roll(two, 64, 1)))
        inputs.append(jnp.where(low, pltpu.roll(one, 64, 1), two))
    return jnp.concatenate(gates, axis=1), jnp.concatenate(inputs, axis=1)


def together(gates, inputs):
    low = lax.broadcasted_iota(jnp.int32, (gates.shape[0], 128), 1) < 64
    parts = []
    for at in range(0, gates.shape[1], 128):
        one, two = gates[:, at : at + 128], inputs[:, at : at + 128]
        parts.append(jnp.where(low, one, pltpu.roll(two, 64, 1)))
        parts.append(jnp.where(low, pltpu.roll(one, 64, 1), two))
    return jnp.concatenate(parts, axis=1)


def block_masks(index, seg_ref):
    now = seg_ref[index]
    before = jnp.where(index > 0, seg_ref[jnp.maximum(index - 1, 0)], -1.0)
    lane = lax.broadcasted_iota(jnp.int32, (1, BLK), 1)
    rows = [now]
    for back in range(1, KW):
        earlier = jnp.where(lane < back, pltpu.roll(before, back, 1), pltpu.roll(now, back, 1))
        rows.append((earlier == now).astype(F32))
    last, prior = now[:, BLK - 1 :], before[:, BLK - 1 :]
    rows.append((now == prior).astype(F32))
    rows.append((now == last).astype(F32))
    rows.append(jnp.broadcast_to((prior == last).astype(F32), (1, BLK)))
    rows.append(jnp.zeros((BLK - len(rows), BLK), F32))
    return jnp.concatenate(rows, axis=0).T


def block_common(width, start, index, proj_ref, ss_ref, seg_ref, par_ref):
    rows = pl.ds(start, BLK)
    before = pl.ds(pl.multiple_of(jnp.maximum(start - 8, 0), 8), 8)
    aux = block_masks(index, seg_ref)
    gate, inner = apart(proj_ref[rows, :].astype(F32))
    current = jnp.concatenate([inner, ss_ref[rows, 0 : 2 * STATE]], axis=1)
    earlier = proj_ref[pl.ds(pl.multiple_of(jnp.maximum(start - 16, 0), 16), 16), :]
    previous = jnp.concatenate(
        [apart(earlier.astype(F32)[8:])[1], ss_ref[before, 0 : 2 * STATE]], axis=1
    )
    extended = jnp.concatenate([previous, current], axis=0)
    taps = par_ref[0:KW, :]
    conv = par_ref[KW : KW + 1, :] + taps[KW - 1 : KW, :] * current
    shifted = []
    for back in range(1, KW):
        moved = pltpu.roll(extended, back, 0)[8:] * aux[:, back : back + 1]
        shifted.append(moved)
        conv = conv + taps[KW - 1 - back : KW - back, :] * moved
    sig = jax.nn.sigmoid(conv)
    active = conv * sig
    inputs_x = active[:, :width]
    matrix_b = active[:, width : width + STATE].astype(BF16)
    matrix_c = active[:, width + STATE :].astype(BF16)
    step_in = ss_ref[rows, 2 * STATE :] + par_ref[7:8, 0:128]
    dt = jnp.maximum(step_in, 0.0) + jnp.log1p(jnp.exp(-jnp.abs(step_in)))
    decay = dt * par_ref[6:7, 0:128]
    row_id = lax.broadcasted_iota(jnp.int32, (BLK, BLK), 0)
    col_id = lax.broadcasted_iota(jnp.int32, (BLK, BLK), 1)
    lower = (row_id >= col_id).astype(F32)
    cum = dot_exact(lower, decay)
    cum_t = cum.T
    same = (aux[:, 0:1] == seg_ref[pl.ds(index, 1), 0, :]) & (row_id >= col_id)
    last = cum[BLK - 1 : BLK, :]
    gain_in = jnp.exp(cum) * aux[:, 4:5]
    tail = jnp.exp(last - cum) * aux[:, 5:6]
    carry = jnp.exp(last) * aux[BLK - 1 : BLK, 6:7]
    scores = jnp.where(same, dot_f32(matrix_c, matrix_b, (((1,), (1,)), ((), ()))), 0.0)
    dt_wide = spread(dt, width)
    moved_x = inputs_x * dt_wide
    return dict(
        rows=rows, aux=aux, gate=gate, current=current, shifted=shifted, conv=conv, sig=sig,
        x=inputs_x, b=matrix_b, c=matrix_c, step_in=step_in, dt=dt, cum=cum, cum_t=cum_t,
        same=same, scores=scores, dt_wide=dt_wide, u=moved_x, lower=lower,
        gain_in=spread(gain_in, width), tail=spread(tail, width),
        carry=spread(jnp.broadcast_to(carry, (8, 128)), width)[0:1],
    )


def split_pair(values):
    low = lax.broadcasted_iota(jnp.int32, values.shape, 1) < 64
    zero = jnp.zeros_like(values)
    return jnp.where(low, values, zero), jnp.where(low, zero, values)


GAIN_AT, BIAS_AT, TAPS_AT, HEADS_AT = 24, 48, 74, 178
INNER_LINES, TAP_LINES = 24, 26


def own_place(columns):
    return lax.axis_index("row") * columns + lax.axis_index("col")


def read_params(width, columns, vec_ref, par_ref):
    lines, heads = width // 128, width // 64
    place = own_place(columns)

    def line(at):
        return jnp.concatenate(
            [vec_ref[pl.ds(at + place * lines + one, 1), :] for one in range(lines)], axis=1
        )

    def wide_line(at):
        rest = at + INNER_LINES
        return jnp.concatenate(
            [line(at), vec_ref[rest : rest + 1, :], vec_ref[rest + 1 : rest + 2, :]], axis=1
        )

    par_ref[...] = jnp.zeros_like(par_ref)
    for tap in range(KW):
        par_ref[tap : tap + 1, :] = wide_line(TAPS_AT + TAP_LINES * tap)
    par_ref[KW : KW + 1, :] = wide_line(BIAS_AT)
    par_ref[5:6, 0:width] = line(GAIN_AT)
    flat = jnp.concatenate([vec_ref[HEADS_AT : HEADS_AT + 1, :], vec_ref[HEADS_AT + 1 : HEADS_AT + 2, :]], axis=1)
    flat = jnp.broadcast_to(flat, (8, 256))
    lane = lax.broadcasted_iota(jnp.int32, (8, 128), 1)

    def per_head(which):
        turned = pltpu.roll(flat, 256 - 48 * which - place * heads, 1)[:, 0:128]
        return jnp.where(lane < heads, turned, 0.0)

    par_ref[6:7, 0:128] = jnp.where(lane < heads, -jnp.exp(per_head(0)), 0.0)[0:1]
    par_ref[7:8, 0:128] = per_head(2)[0:1]
    par_ref[8:9, 0:width] = spread(per_head(1), width)[0:1]


def write_params(width, columns, sums, par_ref, vec_ref):
    lines, heads = width // 128, width // 64
    place = own_place(columns)
    vec_ref[...] = jnp.zeros_like(vec_ref)
    total = lambda at: jnp.sum(sums[at : at + 8, :], axis=0, keepdims=True)

    def line(at, row):
        for one in range(lines):
            vec_ref[pl.ds(at + place * lines + one, 1), :] = row[:, 128 * one : 128 * (one + 1)]

    def wide_line(at, row):
        line(at, row)
        rest = at + INNER_LINES
        vec_ref[rest : rest + 1, :] = row[:, width : width + 128]
        vec_ref[rest + 1 : rest + 2, :] = row[:, width + 128 :]

    for tap in range(KW):
        wide_line(TAPS_AT + TAP_LINES * tap, total(8 * tap))
    wide_line(BIAS_AT, total(32))
    line(GAIN_AT, total(48))
    skips = jnp.sum(head_sums(sums[64:72, 0:width]), axis=0, keepdims=True)
    decays = total(56)[:, 0:128] * par_ref[6:7, 0:128]
    flat = jnp.zeros((8, 256), F32)
    lane = lax.broadcasted_iota(jnp.int32, (8, 256), 1)
    for which, row in enumerate((decays, skips, total(72)[:, 0:128])):
        row = jnp.broadcast_to(jnp.concatenate([row, jnp.zeros((1, 128), F32)], axis=1), (8, 256))
        flat = flat + pltpu.roll(jnp.where(lane < heads, row, 0.0), 48 * which + place * heads, 1)
    vec_ref[HEADS_AT : HEADS_AT + 1, :] = flat[0:1, 0:128]
    vec_ref[HEADS_AT + 1 : HEADS_AT + 2, :] = flat[0:1, 128:]


def forward_kernel(
    width, columns, proj_ref, ss_ref, seg_ref, vec_ref, valued_ref, squares_ref, kept_ref, par_ref, state
):
    blocks = proj_ref.shape[0] // BLK
    state[...] = jnp.zeros_like(state)
    read_params(width, columns, vec_ref, par_ref)

    def step(index, _):
        start = pl.multiple_of(index * BLK, BLK)
        got = block_common(width, start, index, proj_ref, ss_ref, seg_ref, par_ref)
        kept_ref[index] = state[...]
        moved = got["u"].astype(BF16)
        parts = []
        for pair in range(width // 128):
            u0, u1 = split_pair(moved[:, 128 * pair : 128 * (pair + 1)])
            mixes = []
            for head in (2 * pair, 2 * pair + 1):
                differ = jnp.minimum(got["cum"][:, head : head + 1] - got["cum_t"][head : head + 1, :], 0.0)
                mixes.append((jnp.exp(differ) * got["scores"]).astype(BF16))
            parts.append(dot_f32(jnp.concatenate(mixes, axis=1), jnp.concatenate([u0, u1], axis=0)))
        within = jnp.concatenate(parts, axis=1)
        from_state = got["gain_in"] * dot_f32(got["c"], state[...].astype(BF16))
        scanned = within + from_state + par_ref[8:9, 0:width] * got["x"]
        state[...] = state[...] * got["carry"] + dot_f32(
            got["b"], (got["tail"] * got["u"]).astype(BF16), (((0,), (0,)), ((), ()))
        )
        gate = got["gate"]
        gated = scanned * (gate * jax.nn.sigmoid(gate))
        squares_ref[got["rows"], :] = jnp.sum(gated * gated, axis=1, keepdims=True)
        valued_ref[got["rows"], :] = (gated * par_ref[5:6, 0:width]).astype(BF16)
        return 0

    lax.fori_loop(0, blocks, step, 0)


def backward_kernel(
    width, columns, proj_ref, ss_ref, seg_ref, par_ref, vgrad_ref, dsq_ref, kept_ref,
    dproj_ref, dss_ref, dvec_ref, dstate, follow, ebuf, sums
):
    blocks = proj_ref.shape[0] // BLK
    dstate[...] = jnp.zeros_like(dstate)
    follow[...] = jnp.zeros_like(follow)
    sums[...] = jnp.zeros_like(sums)

    def fold(values):
        total = values[0:8]
        for part in range(1, BLK // 8):
            total = total + values[8 * part : 8 * part + 8]
        return total

    def step(count, _):
        index = blocks - 1 - count
        start = pl.multiple_of(index * BLK, BLK)
        got = block_common(width, start, index, proj_ref, ss_ref, seg_ref, par_ref)
        rows, aux = got["rows"], got["aux"]
        state_in = kept_ref[index]
        state_low = state_in.astype(BF16)
        moved = got["u"].astype(BF16)
        skip = par_ref[8:9, 0:width]
        gain = par_ref[5:6, 0:width]
        parts = []
        for pair in range(width // 128):
            u0, u1 = split_pair(moved[:, 128 * pair : 128 * (pair + 1)])
            mixes = []
            for head in (2 * pair, 2 * pair + 1):
                differ = jnp.minimum(got["cum"][:, head : head + 1] - got["cum_t"][head : head + 1, :], 0.0)
                level = jnp.exp(differ)
                ebuf[head] = level
                mixes.append((level * got["scores"]).astype(BF16))
            parts.append(dot_f32(jnp.concatenate(mixes, axis=1), jnp.concatenate([u0, u1], axis=0)))
        inner = jnp.concatenate(parts, axis=1) + got["gain_in"] * dot_f32(got["c"], state_low)
        scanned = inner + skip * got["x"]
        gate = got["gate"]
        gate_sig = jax.nn.sigmoid(gate)
        gate_act = gate * gate_sig
        gated = scanned * gate_act
        vgrad = vgrad_ref[rows, :].astype(F32)
        dgated = vgrad * gain + 2.0 * gated * dsq_ref[rows, :]
        sums[48:56, 0:width] += fold(vgrad * gated)
        dy = dgated * gate_act
        dgate = dgated * scanned * (gate_sig * (1.0 + gate * (1.0 - gate_sig)))
        dy_low = dy.astype(BF16)
        dscores = jnp.zeros((BLK, BLK), F32)
        parts = []
        for pair in range(width // 128):
            lanes = slice(128 * pair, 128 * (pair + 1))
            u0, u1 = split_pair(moved[:, lanes])
            d0, d1 = split_pair(dy_low[:, lanes])
            mixes = []
            for head, u_own in ((2 * pair, u0), (2 * pair + 1, u1)):
                level = ebuf[head]
                mixes.append((level * got["scores"]).astype(BF16))
                dscores = dscores + level * dot_f32(
                    dy_low[:, lanes], u_own, (((1,), (1,)), ((), ()))
                )
            parts.append(
                dot_f32(
                    jnp.concatenate(mixes, axis=0),
                    jnp.concatenate([d0, d1], axis=0),
                    (((0,), (0,)), ((), ())),
                )
            )
        du_within = jnp.concatenate(parts, axis=1)
        dscores = jnp.where(got["same"], dscores, 0.0).astype(BF16)
        dstate_now = dstate[...]
        dstate_low = dstate_now.astype(BF16)
        dy_in = (got["gain_in"] * dy).astype(BF16)
        u_tail = got["tail"] * got["u"]
        from_next = dot_f32(got["b"], dstate_low)
        du = du_within + got["tail"] * from_next
        dmat_c = dot_f32(dscores, got["b"]) + dot_f32(dy_in, state_low, (((1,), (1,)), ((), ())))
        dmat_b = dot_f32(dscores, got["c"], (((0,), (0,)), ((), ()))) + dot_f32(
            u_tail.astype(BF16), dstate_low, (((1,), (1,)), ((), ()))
        )
        tail_part = head_sums(u_tail * from_next)
        dcum = (
            head_sums(dy_low.astype(F32) * inner - moved.astype(F32) * du_within) - tail_part
        )
        kept_part = head_sums(fold(got["carry"] * dstate_now * state_in))
        at_last = jnp.sum(tail_part, axis=0, keepdims=True) + jnp.sum(kept_part, axis=0, keepdims=True)
        ddecay = dot_exact(got["lower"], dcum, (((0,), (0,)), ((), ()))) + at_last
        ddt = ddecay * par_ref[6:7, 0:128] + head_sums(du * got["x"])
        sums[56:64, 0:128] += fold(ddecay * got["dt"])
        sums[64:72, 0:width] += fold(dy * got["x"])
        dstep = ddt * jax.nn.sigmoid(got["step_in"])
        sums[72:80, 0:128] += fold(dstep)
        dstate[...] = dstate_now * got["carry"] + dot_f32(got["c"], dy_in, (((0,), (0,)), ((), ())))
        dactive = jnp.concatenate([skip * dy + du * got["dt_wide"], dmat_b, dmat_c], axis=1)
        sig, conv = got["sig"], got["conv"]
        dconv = dactive * (sig * (1.0 + conv * (1.0 - sig)))
        sums[32:40, :] += fold(dconv)
        sums[24:32, :] += fold(dconv * got["current"])
        dinput = par_ref[KW - 1 : KW, :] * dconv
        for back in range(1, KW):
            tap = KW - 1 - back
            sums[8 * tap : 8 * tap + 8, :] += fold(dconv * got["shifted"][back - 1])
            masked = dconv * aux[:, back : back + 1]
            ext = jnp.concatenate([masked, follow[back - 1]], axis=0)
            dinput = dinput + par_ref[tap : tap + 1, :] * pltpu.roll(ext, BLK + 8 - back, 0)[:BLK]
            follow[back - 1] = masked[0:8]
        dproj_ref[rows, :] = together(dgate, dinput[:, :width]).astype(BF16)
        dss_ref[rows, 0 : 2 * STATE] = dinput[:, width:].astype(BF16)
        dss_ref[rows, 2 * STATE :] = dstep.astype(BF16)
        return 0

    lax.fori_loop(0, blocks, step, 0)
    write_params(width, columns, sums, par_ref, dvec_ref)


VM = pl.BlockSpec(memory_space=pltpu.VMEM)


def lasting(micros):
    return pl.CostEstimate(flops=0, bytes_accessed=int(micros * 3.0e6), transcendentals=0)


def mixer_forward(proj, ss, seg, vec, columns):
    length, double = proj.shape
    width = double // 2
    blocks = length // BLK
    return pl.pallas_call(
        functools.partial(forward_kernel, width, columns),
        out_shape=(
            jax.ShapeDtypeStruct((length, width), BF16),
            jax.ShapeDtypeStruct((length, 1), F32),
            jax.ShapeDtypeStruct((blocks, STATE, width), F32),
            jax.ShapeDtypeStruct((16, width + 2 * STATE), F32),
        ),
        in_specs=[VM] * 4,
        out_specs=(VM,) * 4,
        scratch_shapes=[pltpu.VMEM((STATE, width), F32)],
        compiler_params=pltpu.CompilerParams(vmem_limit_bytes=56 * 2**20),
        cost_estimate=lasting(20),
        name="mixer_forward",
    )(proj, ss, seg, vec)


def mixer_backward(proj, ss, seg, par, vgrad, dsq, kept, lines, columns):
    length, double = proj.shape
    width = double // 2
    wide = width + 2 * STATE
    return pl.pallas_call(
        functools.partial(backward_kernel, width, columns),
        out_shape=(
            jax.ShapeDtypeStruct((length, 2 * width), BF16),
            jax.ShapeDtypeStruct((length, 3 * STATE), BF16),
            jax.ShapeDtypeStruct((lines, 128), F32),
        ),
        in_specs=[VM] * 7,
        out_specs=(VM,) * 3,
        scratch_shapes=[
            pltpu.VMEM((STATE, width), F32),
            pltpu.VMEM((KW - 1, 8, wide), F32),
            pltpu.VMEM((width // 64, BLK, BLK), F32),
            pltpu.VMEM((80, wide), F32),
        ],
        compiler_params=pltpu.CompilerParams(vmem_limit_bytes=56 * 2**20),
        cost_estimate=lasting(34),
        name="mixer_backward",
    )(proj, ss, seg, par, vgrad, dsq, kept)


MODEL_WIDTH = 1536
HEADS = 48
FF_E = 512
FF_S = 1024
TOPK = 6
STEP = 10
EXP_DEV = 2
INNER = 3072
ROUTER_AT = 64
REST_AT = 64


def dot_t(a, b):
    return dot_f32(a, b, (((1,), (1,)), ((), ())))


def dot_tn(a, b):
    return dot_f32(a, b, (((0,), (0,)), ((), ())))


def shift(values, axis, by):
    size = lax.axis_size(axis)
    return lax.ppermute(values, axis, [(i, (i + by) % size) for i in range(size)])


def all_places(own):
    rows, columns = lax.axis_index("row"), lax.axis_size("col")
    col = lax.axis_index("col")
    placed = []
    for by, part in enumerate(own):
        there = (col - by) % columns
        placed.append((rows * columns + there, part))
        placed.append(((1 - rows) * columns + there, shift(part, "row", 1)))
    return placed


def assemble(placed, group):
    count = len(placed)
    rows, columns = placed[0][1].shape
    total = jnp.zeros((group, count, rows // group, columns), placed[0][1].dtype)
    for place, part in placed:
        total = lax.dynamic_update_slice(
            total, part.reshape(group, 1, rows // group, columns), (0, place, 0, 0)
        )
    return total.reshape(count * rows, columns)


def gather_rc(values):
    columns = lax.axis_size("col")
    return assemble(
        all_places([values] + [shift(values, "col", by) for by in range(1, columns)]), 1
    )


def block_of(array, at, rows):
    return lax.dynamic_slice_in_dim(array, at * rows, rows)


def scatter_row(values, group=1):
    row = lax.axis_index("row")
    halves = values.reshape(group, 2, -1, values.shape[1])
    pick = lambda which: lax.dynamic_index_in_dim(halves, which, 1, keepdims=False)
    away = shift(pick(1 - row), "row", 1)
    return pick(row).astype(F32) + away.astype(F32)


def scatter_col(kept):
    columns, col = lax.axis_size("col"), lax.axis_index("col")
    parts = kept.reshape(kept.shape[0], columns, -1, kept.shape[2])
    pick = lambda which: lax.dynamic_index_in_dim(parts, which, 1, keepdims=False)
    total = pick(col)
    for by in range(1, columns):
        total = total + shift(pick((col + by) % columns).astype(BF16), "col", by).astype(F32)
    return total.reshape(-1, kept.shape[2])


def scatter_rc(values):
    return scatter_col(scatter_row(values))


def scatter_squares(values):
    columns, col = lax.axis_size("col"), lax.axis_index("col")
    kept = scatter_row(values)[0]
    rows = kept.shape[0] // columns
    total = block_of(kept, col, rows)
    for by in range(1, columns):
        total = total + shift(block_of(kept, (col + by) % columns, rows), "col", by)
    return total


def partners(shape):
    steps = []
    for name in ("dp", "row", "col"):
        bit = 1
        while bit < shape[name]:
            steps.append((name, bit))
            bit *= 2
    return steps


DEEP = 4
MESH_ID = pl.DeviceIdType.MESH
ANY = pl.BlockSpec(memory_space=pl.ANY)


def near_first(place, step, size):
    if size == 1:
        return place
    if size == 2:
        return place + step * (1 - 2 * place)
    side = place // 2
    inner = (place * (3 - place)) // 2
    found = step + inner * (1 - 2 * step) * (1 - step // 2)
    return found + side * (3 - 2 * found)


class Grid:
    def __init__(self, size):
        self.size, self.deep, self.across = size, DEEP, size // DEEP
        self.me = lax.axis_index("dp")
        self.z, self.x = self.me // self.across, self.me % self.across
        self.steps = (-self.across, self.across, -1, 1)
        self.exists = (
            self.z > 0,
            self.z < self.deep - 1,
            self.x > 0,
            self.x < self.across - 1,
        )
        self.count = (
            jnp.minimum(self.z, 1)
            + jnp.minimum(self.deep - 1 - self.z, 1)
            + jnp.minimum(self.x, 1)
            + jnp.minimum(self.across - 1 - self.x, 1)
        )

    def greet(self, barrier):
        for there, step in zip(self.exists, self.steps):
            @pl.when(there)
            def _():
                pl.semaphore_signal(
                    barrier, inc=1, device_id={"dp": self.me + step}, device_id_type=MESH_ID
                )


def gather_kernel(size, columns, *refs):
    count = PLAIN + BOTH
    ins, outs = refs[: count + 1], refs[count + 1 : 2 * count + 2]
    dp_send, dp_recv, sh_send, sh_recv, rc_send, rc_recv, keep_sem = refs[2 * count + 2 :]
    grid = Grid(size)
    me, z, x = grid.me, grid.z, grid.x
    row, col = lax.axis_index("row"), lax.axis_index("col")
    mine, other_row = row * columns + col, {"row": 1 - row}
    to_col = lambda by: {"col": (col + by) % columns}
    from_col = lambda by: row * columns + (col + by) % columns
    barrier = pltpu.get_barrier_semaphore()
    grid.greet(barrier)
    pl.semaphore_signal(barrier, inc=1, device_id=other_row, device_id_type=MESH_ID)
    for by in range(1, columns):
        pl.semaphore_signal(barrier, inc=1, device_id=to_col(by), device_id_type=MESH_ID)
    pl.semaphore_wait(barrier, grid.count + columns)

    def block(which, chunk, place):
        return outs[which].at[chunk] if which < PLAIN else outs[which].at[chunk, place]

    def push(which, chunk, way, source=None):
        ref = block(which, chunk, mine)
        return pltpu.make_async_remote_copy(
            src_ref=ref if source is None else source,
            dst_ref=ref,
            send_sem=dp_send.at[which, way, chunk],
            recv_sem=dp_recv.at[which, chunk],
            device_id={"dp": me + grid.steps[way]},
            device_id_type=MESH_ID,
        )

    def spread(which, chunk, place, index, peer, source=None):
        ref = block(which, chunk, place)
        return pltpu.make_async_remote_copy(
            src_ref=ref if source is None else source,
            dst_ref=ref,
            send_sem=sh_send.at[which - PLAIN, index, chunk],
            recv_sem=sh_recv.at[which - PLAIN, place, chunk],
            device_id=peer,
            device_id_type=MESH_ID,
        )

    def spread_tokens(place, index, peer, source=None):
        ref = outs[count].at[place]
        return pltpu.make_async_remote_copy(
            src_ref=ref if source is None else source,
            dst_ref=ref,
            send_sem=rc_send.at[index],
            recv_sem=rc_recv.at[place],
            device_id=peer,
            device_id_type=MESH_ID,
        )

    def place_of(number):
        if grid.across == 2:
            even, first, last = 1 - number % 2, 1 - jnp.minimum(number, 1), number // 7
            step = (1 - even) * ((number + 1) // 2 - last) + even * (number // 2 - 1 + first)
            side = even * (1 - first) + last
        else:
            step, side = number % grid.deep, number // grid.deep
        zc = near_first(z, step, grid.deep)
        xc = near_first(x, side, grid.across)
        same_x, same_z = xc == x, zc == z
        ways = (zc >= z, zc <= z, xc >= x, xc <= x)
        open_ways = [way & there for way, there in zip(ways, grid.exists)]
        z_first = [same_x & open_ways[0], same_x & open_ways[1], open_ways[2], open_ways[3]]
        x_first = [open_ways[0], open_ways[1], same_z & open_ways[2], same_z & open_ways[3]]
        return zc * grid.across + xc, [
            x_first if which == X_FIRST else z_first for which in range(count)
        ]

    def spread_chunk(chunk, sources=(None,) * BOTH):
        for which, source in zip(range(PLAIN, count), sources):
            spread(which, chunk, mine, 0, other_row, source).start()
            for by in range(1, columns):
                spread(which, chunk, mine, by, to_col(by), source).start()

    def pass_on(number, _):
        chunk, onward = place_of(number)
        for which in range(count):
            push(which, chunk, 0).wait_recv()
            for way in range(4):
                @pl.when(onward[which][way])
                def _():
                    push(which, chunk, way).start()
        return chunk

    for way in range(4):
        @pl.when(grid.exists[way])
        def _():
            for which in range(count):
                push(which, me, way, ins[which]).start()
    spread_tokens(mine, 0, other_row, ins[count]).start()
    for by in range(1, columns):
        spread_tokens(mine, by, to_col(by), ins[count]).start()
    keeps = [
        pltpu.make_async_copy(ins[which], block(which, me, mine), keep_sem.at[which])
        for which in range(count)
    ]
    keeps.append(pltpu.make_async_copy(ins[count], outs[count].at[mine], keep_sem.at[count]))
    for copy in keeps:
        copy.start()
    early = pass_on(1, 0)
    for by in range(1, columns):
        spread_tokens(from_col(by), columns - 1 + by, other_row).wait_recv()
        spread_tokens(from_col(by), columns - 1 + by, other_row).start()
    spread_chunk(me, ins[PLAIN:count])
    spread_chunk(early)

    def later(number, _):
        spread_chunk(pass_on(number, 0))
        return 0

    lax.fori_loop(2, size, later, 0)

    def forward_chunk(number, _):
        chunk = place_of(number)[0]
        for which in range(PLAIN, count):
            for by in range(1, columns):
                place = from_col(by)
                spread(which, chunk, place, columns - 1 + by, other_row).wait_recv()
                spread(which, chunk, place, columns - 1 + by, other_row).start()
        return 0

    lax.fori_loop(0, size, forward_chunk, 0)

    def finish(number, _):
        chunk, onward = place_of(number)
        for which in range(PLAIN, count):
            for by in range(columns):
                spread(which, chunk, (1 - row) * columns + (col + by) % columns, 0, other_row).wait_recv()
            for index in range(2 * columns - 1):
                spread(which, chunk, mine, index, other_row).wait_send()
        for way in range(4):
            for which in range(count):
                @pl.when(onward[which][way])
                def _():
                    push(which, chunk, way).wait_send()
        return 0

    lax.fori_loop(0, size, finish, 0)
    for by in range(columns):
        spread_tokens((1 - row) * columns + (col + by) % columns, 0, other_row).wait_recv()
    for index in range(2 * columns - 1):
        spread_tokens(mine, index, other_row).wait_send()
    for copy in keeps:
        copy.wait()


PLAIN, BOTH, X_FIRST = 2, 3, 2


def gather_start(over_dp, over_both, tokens, shape):
    size, columns = shape["dp"], shape["col"]
    places, count = 2 * columns, PLAIN + BOTH
    arrays = (*over_dp, *over_both, tokens)
    lead = [(size,)] * PLAIN + [(size, places)] * BOTH + [(places,)]
    results = pl.pallas_call(
        functools.partial(gather_kernel, size, columns),
        out_shape=tuple(
            jax.ShapeDtypeStruct(at + array.shape, BF16) for at, array in zip(lead, arrays)
        ),
        in_specs=[VM] * (count + 1),
        out_specs=(ANY,) * (count + 1),
        scratch_shapes=[
            pltpu.SemaphoreType.DMA((count, 4, size)),
            pltpu.SemaphoreType.DMA((count, size)),
            pltpu.SemaphoreType.DMA((BOTH, 2 * columns - 1, size)),
            pltpu.SemaphoreType.DMA((BOTH, places, size)),
            pltpu.SemaphoreType.DMA((2 * columns - 1,)),
            pltpu.SemaphoreType.DMA((places,)),
            pltpu.SemaphoreType.DMA((count + 1,)),
        ],
        compiler_params=pltpu.CompilerParams(
            collective_id=2, has_side_effects=True, vmem_limit_bytes=58 * 2**20
        ),
        cost_estimate=lasting(105),
        name="gather_start",
    )(*arrays)
    return [result.reshape(-1, result.shape[-1]) for result in results]


class LineSum:
    def __init__(self, grid, part_ref, out_ref, sums, from_x, from_z, x_send, x_recv, z_send, z_recv):
        self.grid, self.part_ref, self.out_ref = grid, part_ref, out_ref
        self.sums, self.from_x, self.from_z = sums, from_x, from_z
        self.x_send, self.x_recv, self.z_send, self.z_recv = x_send, x_recv, z_send, z_recv

    @staticmethod
    def scratch(size, chunk):
        pair = size == 2 * DEEP
        return [
            pltpu.VMEM((DEEP if pair else size,) + chunk, BF16),
            pltpu.VMEM((DEEP if pair else 2 * size,) + chunk, BF16),
            pltpu.VMEM((2 * DEEP,) + chunk, BF16),
            pltpu.SemaphoreType.DMA((size,)),
            pltpu.SemaphoreType.DMA((2 * size,)),
            pltpu.SemaphoreType.DMA((DEEP,)),
            pltpu.SemaphoreType.DMA((2 * DEEP,)),
        ]

    def sum_at(self, line, there):
        pair = self.grid.across == 2
        return self.sums.at[line if pair else line * self.grid.across + there]

    def along_x(self, line, there, way):
        grid = self.grid
        chunk = line * grid.across + there
        slot = way * grid.size + chunk
        pair = grid.across == 2
        return pltpu.make_async_remote_copy(
            src_ref=self.part_ref.at[chunk] if pair else self.sum_at(line, there),
            dst_ref=self.from_x.at[line if pair else slot],
            send_sem=self.x_send.at[chunk],
            recv_sem=self.x_recv.at[slot],
            device_id={"dp": grid.me + 2 * way - 1},
            device_id_type=MESH_ID,
        )

    def came_x(self, line, there, way):
        grid = self.grid
        slot = way * grid.size + line * grid.across + there
        return self.from_x[line if grid.across == 2 else slot].astype(F32)

    def along_z(self, line, way):
        grid = self.grid
        return pltpu.make_async_remote_copy(
            src_ref=self.sum_at(line, grid.x),
            dst_ref=self.from_z.at[way * grid.deep + line],
            send_sem=self.z_send.at[line],
            recv_sem=self.z_recv.at[way * grid.deep + line],
            device_id={"dp": grid.me + (2 * way - 1) * grid.across},
            device_id_type=MESH_ID,
        )

    @staticmethod
    def start(sums):
        grid = sums[0].grid
        x, across = grid.x, grid.across

        def away(number, _):
            line = near_first(grid.z, grid.deep - 1 - number // (across - 1), grid.deep)
            there = near_first(x, across - 1 - number % (across - 1), across)
            for one in sums:
                if across > 2:
                    one.sum_at(line, there)[...] = one.part_ref[line * across + there]
                for way, beyond in ((1, grid.exists[2]), (0, grid.exists[3])):
                    toward = (there > x) if way else (there < x)
                    if across > 2:
                        @pl.when(toward & beyond)
                        def _():
                            one.along_x(line, there, way).wait_recv()
                            held = one.sum_at(line, there)
                            held[...] = (
                                held[...].astype(F32) + one.came_x(line, there, way)
                            ).astype(BF16)
                    @pl.when(toward)
                    def _():
                        one.along_x(line, there, way).start()
            return 0

        lax.fori_loop(0, grid.deep * (across - 1), away, 0)

    @staticmethod
    def finish(sums, between=None):
        grid = sums[0].grid
        z, x, across = grid.z, grid.x, grid.across

        def collect(number, _):
            if between is not None:
                between(number)
            line = near_first(z, grid.deep - 1 - number, grid.deep)
            for one in sums:
                out_ref = one.out_ref
                out_ref[...] = one.part_ref[line * across + x].astype(F32)
                for way, there in ((1, grid.exists[2]), (0, grid.exists[3])):
                    @pl.when(there)
                    def _():
                        one.along_x(line, x, way).wait_recv()
                        out_ref[...] += one.came_x(line, x, way)
                for way, there in (
                    (1, grid.exists[0] & (line >= z)), (0, grid.exists[1] & (line <= z))
                ):
                    @pl.when(there)
                    def _():
                        one.along_z(line, way).wait_recv()
                        out_ref[...] += one.from_z[way * grid.deep + line].astype(F32)
                for way, toward in ((1, line > z), (0, line < z)):
                    @pl.when(toward)
                    def _():
                        one.sum_at(line, x)[...] = out_ref[...].astype(BF16)
                        one.along_z(line, way).start()
            return 0

        lax.fori_loop(0, grid.deep, collect, 0)

        def wait(number, _):
            line = near_first(z, grid.deep - 1 - number // across, grid.deep)
            there = near_first(x, across - 1 - number % across, across)
            for one in sums:
                for way in range(2):
                    @pl.when((there > x) if way else (there < x))
                    def _():
                        one.along_x(line, there, way).wait_send()
                    @pl.when((there == x) & ((line > z) if way else (line < z)))
                    def _():
                        one.along_z(line, way).wait_send()
            return 0

        lax.fori_loop(0, grid.size, wait, 0)


TILE = 256


def scatter_kernel(size, part_ref, x_ref, dpre_ref, hid_ref, g_ref, out_ref, up_ref, down_ref, *refs):
    dpre_now, g_now, left, stage, sent, came = refs[:6]
    whole_sem, left_sem, stage_sem, row_send, row_recv = refs[6:11]
    grid = Grid(size)
    row = lax.axis_index("row")
    barrier = pltpu.get_barrier_semaphore()
    grid.greet(barrier)
    pl.semaphore_signal(barrier, inc=1, device_id={"row": 1 - row}, device_id_type=MESH_ID)
    pl.semaphore_wait(barrier, grid.count + 1)
    sums = [LineSum(grid, part_ref, out_ref, *refs[11:])]
    LineSum.start(sums)

    width = g_now.shape[1]
    ups, downs = up_ref.shape[0] // TILE, down_ref.shape[0] // TILE
    half = ups + downs
    bring_dpre = pltpu.make_async_copy(dpre_ref, dpre_now, whole_sem.at[0])
    bring_g = pltpu.make_async_copy(g_ref.at[:, pl.ds(0, width)], g_now, whole_sem.at[1])
    begin, end = lambda copy: copy.start(), lambda copy: copy.wait()

    def bring(tile, do):
        whose = row + (1 - tile // half) * (1 - 2 * row)
        within = tile % half

        @pl.when((within < ups) & (tile < 2 * half))
        def _():
            at = pl.ds(pl.multiple_of((whose * ups + within) * TILE, TILE), TILE)
            do(pltpu.make_async_copy(x_ref.at[:, at], left.at[tile % 2], left_sem.at[tile % 2]))

        @pl.when((within >= ups) & (tile < 2 * half))
        def _():
            at = pl.ds(pl.multiple_of(((within - ups) * 2 + whose) * TILE, TILE), TILE)
            do(pltpu.make_async_copy(hid_ref.at[:, at], left.at[tile % 2], left_sem.at[tile % 2]))

    def push(within):
        return pltpu.make_async_remote_copy(
            src_ref=sent.at[within],
            dst_ref=came.at[within],
            send_sem=row_send.at[within],
            recv_sem=row_recv.at[within],
            device_id={"row": 1 - row},
            device_id_type=MESH_ID,
        )

    def leave(within, do):
        @pl.when((within >= 0) & (within < ups))
        def _():
            at = pl.ds(pl.multiple_of(within * TILE, TILE), TILE)
            do(pltpu.make_async_copy(stage.at[within % 2], up_ref.at[at], stage_sem.at[within % 2]))

        @pl.when(within >= ups)
        def _():
            at = pl.ds(pl.multiple_of((within - ups) * TILE, TILE), TILE)
            do(
                pltpu.make_async_copy(
                    stage.at[within % 2, :, pl.ds(0, width)], down_ref.at[at], stage_sem.at[within % 2]
                )
            )

    bring(0, begin)
    bring_dpre.start()
    bring_g.start()
    bring_dpre.wait()
    bring_g.wait()

    def work(tile, _):
        within = tile % half
        bring(tile + 1, begin)
        bring(tile, end)

        @pl.when(tile >= half)
        def _():
            leave(within - 2, end)
            push(within).wait_recv()

        for wanted, right in ((within < ups, dpre_now), (within >= ups, g_now)):
            for theirs in (True, False):
                @pl.when(wanted & ((tile < half) if theirs else (tile >= half)))
                def _():
                    for at in range(0, right.shape[1], 512):
                        lanes = slice(at, at + 512)
                        found = dot_tn(left[tile % 2], right[:, lanes])
                        if theirs:
                            sent[within, :, lanes] = found.astype(BF16)
                        else:
                            stage[within % 2, :, lanes] = (
                                found + came[within, :, lanes].astype(F32)
                            ).astype(BF16)

        @pl.when(tile < half)
        def _():
            push(within).start()

        @pl.when(tile >= half)
        def _():
            leave(within, begin)

        return 0

    def between(number):
        lax.fori_loop(number * 2 * half // DEEP, (number + 1) * 2 * half // DEEP, work, 0)

    LineSum.finish(sums, between)
    leave(half - 2, end)
    leave(half - 1, end)

    def sent_all(within, _):
        push(within).wait_send()
        return 0

    lax.fori_loop(0, half, sent_all, 0)


def scatter_blocks(parts, tokens, dpre, hidden, cotangents, shape):
    size, width = shape["dp"], tokens.shape[1]
    if size > 2 * DEEP:
        low = lambda array: array.astype(BF16).reshape(-1, array.shape[-1])
        return (
            scatter_dp(parts).astype(F32),
            low(scatter_row(dot_tn(tokens, dpre).astype(BF16))),
            low(scatter_row(dot_tn(hidden, cotangents[:, :width]).astype(BF16), EXP_DEV)),
        )
    parts = parts.reshape((size, -1, parts.shape[1]))
    chunk, count = parts.shape[1:], tokens.shape[0]
    up_half, down_half = width // 2, hidden.shape[1] // 2
    half = (up_half + down_half) // TILE
    return pl.pallas_call(
        functools.partial(scatter_kernel, size),
        out_shape=(
            jax.ShapeDtypeStruct(chunk, F32),
            jax.ShapeDtypeStruct((up_half, dpre.shape[1]), BF16),
            jax.ShapeDtypeStruct((down_half, width), BF16),
        ),
        in_specs=[VM] + [ANY] * 4,
        out_specs=(VM, ANY, ANY),
        scratch_shapes=[
            pltpu.VMEM(dpre.shape, BF16),
            pltpu.VMEM((count, width), BF16),
            pltpu.VMEM((2, count, TILE), BF16),
            pltpu.VMEM((2, TILE, dpre.shape[1]), BF16),
            pltpu.VMEM((half, TILE, dpre.shape[1]), BF16),
            pltpu.VMEM((half, TILE, dpre.shape[1]), BF16),
            pltpu.SemaphoreType.DMA((2,)),
            pltpu.SemaphoreType.DMA((2,)),
            pltpu.SemaphoreType.DMA((2,)),
            pltpu.SemaphoreType.DMA((half,)),
            pltpu.SemaphoreType.DMA((half,)),
        ]
        + LineSum.scratch(size, chunk),
        compiler_params=pltpu.CompilerParams(
            collective_id=5, has_side_effects=True, vmem_limit_bytes=60 * 2**20
        ),
        cost_estimate=lasting(78),
        name="scatter_blocks",
    )(parts, tokens, dpre, hidden, cotangents)


def end_kernel(
    size, steps, columns, at, count, *refs
):
    part_refs, (value_ref, seq_ref), refs = refs[:count], refs[count : count + 2], refs[count + 2 :]
    out_refs, (total_ref, small_ref, rows_ref), refs = (
        refs[:count], refs[count : count + 3], refs[count + 3 :]
    )
    landed, half_now, half_in, quarter, quarter_in, seq_half, seq_sent, seq_in = refs[:8]
    t_send, t_recv, s_send, s_recv, q_send, q_recv = refs[8:14]
    scratch, out_ref = refs[14:], out_refs[0]
    grid = Grid(size)
    row, col = lax.axis_index("row"), lax.axis_index("col")

    def other(name, bit):
        place = lax.axis_index(name)
        return {name: place + bit * (1 - 2 * ((place // bit) % 2))}

    barrier = pltpu.get_barrier_semaphore()
    grid.greet(barrier)
    for name, bit in steps:
        pl.semaphore_signal(barrier, inc=1, device_id=other(name, bit), device_id_type=MESH_ID)
    for by in range(1, columns):
        pl.semaphore_signal(
            barrier, inc=1, device_id={"col": (col + by) % columns}, device_id_type=MESH_ID
        )
    pl.semaphore_wait(barrier, grid.count + len(steps) + columns - 1)

    seq_rows, block = seq_half.shape[0], rows_ref.shape[0]
    swap_rows = pltpu.make_async_remote_copy(
        src_ref=seq_ref.at[pl.ds(pl.multiple_of((1 - row) * seq_rows, 16), seq_rows)],
        dst_ref=seq_half,
        send_sem=q_send.at[0],
        recv_sem=q_recv.at[0],
        device_id={"row": 1 - row},
        device_id_type=MESH_ID,
    )
    swap_rows.start()

    total_ref[...] = value_ref[...]

    def exchange(number):
        name, bit = steps[number]
        copy = pltpu.make_async_remote_copy(
            src_ref=total_ref,
            dst_ref=landed.at[number],
            send_sem=t_send.at[number],
            recv_sem=t_recv.at[number],
            device_id=other(name, bit),
            device_id_type=MESH_ID,
        )
        copy.start()
        copy.wait()
        total_ref[...] += landed[number]

    early = len([1 for name, bit in steps if name == "dp" and bit < grid.across])
    for number in range(early):
        exchange(number)
    sums = [
        LineSum(grid, part_refs[number], out_refs[number], *scratch[7 * number : 7 * number + 7])
        for number in range(count)
    ]
    LineSum.start(sums)

    def both_rows(place):
        mine = seq_ref[pl.ds(pl.multiple_of(row * seq_rows + place * block, 16), block), :]
        theirs = seq_half[pl.ds(pl.multiple_of(place * block, 16), block), :]
        return mine.astype(F32) + theirs.astype(F32)

    swap_rows.wait()
    moves = []
    for by in range(1, columns):
        to = (col + by) % columns
        seq_sent[by] = both_rows(to).astype(BF16)
        moves.append(
            pltpu.make_async_remote_copy(
                src_ref=seq_sent.at[by],
                dst_ref=seq_in.at[by],
                send_sem=q_send.at[by],
                recv_sem=q_recv.at[by],
                device_id={"col": to},
                device_id_type=MESH_ID,
            )
        )
    for number in range(early, len(steps)):
        exchange(number)
    for copy in moves:
        copy.start()
    rows_ref[...] = both_rows(col)
    LineSum.finish(sums)
    for by, copy in enumerate(moves):
        copy.wait()
        rows_ref[...] += seq_in[by + 1].astype(F32)

    half, (fourth, narrow) = half_now.shape[0], small_ref.shape
    half_now[...] = out_ref[pl.ds(pl.multiple_of((1 - row) * half, 8), half), at : at + narrow]
    swap = pltpu.make_async_remote_copy(
        src_ref=half_now,
        dst_ref=half_in,
        send_sem=s_send.at[0],
        recv_sem=s_recv.at[0],
        device_id={"row": 1 - row},
        device_id_type=MESH_ID,
    )
    swap.start()
    swap.wait()
    both = out_ref[pl.ds(pl.multiple_of(row * half, 8), half), at : at + narrow] + half_in[...]
    for place in range(columns):
        quarter[place] = both[place * fourth : (place + 1) * fourth]
    copies = []
    for by in range(1, columns):
        to = (col + by) % columns
        copies.append(
            pltpu.make_async_remote_copy(
                src_ref=quarter.at[to],
                dst_ref=quarter_in.at[by],
                send_sem=s_send.at[by],
                recv_sem=s_recv.at[by],
                device_id={"col": to},
                device_id_type=MESH_ID,
            )
        )
        copies[-1].start()
    small_ref[...] = quarter[col]
    for by, copy in enumerate(copies):
        copy.wait()
        small_ref[...] += quarter_in[by + 1]


def scatter_end(parts, values, rows, at, narrow, shape):
    size, columns = shape["dp"], shape["col"]
    steps = partners(shape)
    parts = [part.reshape((size, -1, part.shape[1])) for part in parts]
    chunk, count = parts[0].shape[1:], len(parts)
    half, seq_rows = chunk[0] // 2, rows.shape[0] // 2
    block = (seq_rows // columns, rows.shape[1])
    fourth = (columns, half // columns, narrow)
    return pl.pallas_call(
        functools.partial(end_kernel, size, steps, columns, at, count),
        out_shape=tuple(jax.ShapeDtypeStruct(part.shape[1:], F32) for part in parts)
        + (
            jax.ShapeDtypeStruct(values.shape, F32),
            jax.ShapeDtypeStruct(fourth[1:], F32),
            jax.ShapeDtypeStruct(block, F32),
        ),
        in_specs=[VM] * (count + 2),
        out_specs=(VM,) * (count + 3),
        scratch_shapes=[
            pltpu.VMEM((len(steps),) + values.shape, F32),
            pltpu.VMEM((half, narrow), F32),
            pltpu.VMEM((half, narrow), F32),
            pltpu.VMEM(fourth, F32),
            pltpu.VMEM(fourth, F32),
            pltpu.VMEM((seq_rows, rows.shape[1]), BF16),
            pltpu.VMEM((columns,) + block, BF16),
            pltpu.VMEM((columns,) + block, BF16),
            pltpu.SemaphoreType.DMA((len(steps),)),
            pltpu.SemaphoreType.DMA((len(steps),)),
            pltpu.SemaphoreType.DMA((columns,)),
            pltpu.SemaphoreType.DMA((columns,)),
            pltpu.SemaphoreType.DMA((columns,)),
            pltpu.SemaphoreType.DMA((columns,)),
        ]
        + sum([LineSum.scratch(size, part.shape[1:]) for part in parts], []),
        compiler_params=pltpu.CompilerParams(
            collective_id=3, has_side_effects=True, vmem_limit_bytes=60 * 2**20
        ),
        cost_estimate=lasting(125),
        name="scatter_end",
    )(*parts, values, rows)


def shared_block(x_ref, g_ref, up_ref, down_ref, hid_ref, dpre_ref, out_ref, dx_ref):
    x, g = x_ref[...], g_ref[:, :MODEL_WIDTH]
    pre = dot_f32(x, up_ref[...])
    asked = dot_t(g, down_ref[...])
    half = down_ref.shape[0]
    for part in range(half // 128):
        lanes = slice(128 * part, 128 * (part + 1))
        upper = slice(half + 128 * part, half + 128 * (part + 1))
        gate, up, want = pre[:, lanes], pre[:, upper], asked[:, lanes]
        sig = jax.nn.sigmoid(gate)
        act = gate * sig
        hid_ref[:, lanes] = (act * up).astype(BF16)
        dpre_ref[:, lanes] = (want * up * (sig * (1.0 + gate * (1.0 - sig)))).astype(BF16)
        dpre_ref[:, upper] = (want * act).astype(BF16)
    out_ref[...] = dot_f32(hid_ref[...], down_ref[...])
    dx_ref[...] = dot_t(dpre_ref[...], up_ref[...])


def shared_expert(tokens, cotangents, up, down):
    rows, width = tokens.shape
    return pl.pallas_call(
        shared_block,
        out_shape=(
            jax.ShapeDtypeStruct((rows, down.shape[0]), BF16),
            jax.ShapeDtypeStruct((rows, up.shape[1]), BF16),
            jax.ShapeDtypeStruct((rows, width), F32),
            jax.ShapeDtypeStruct((rows, width), F32),
        ),
        in_specs=[VM] * 4,
        out_specs=(VM,) * 4,
        compiler_params=pltpu.CompilerParams(vmem_limit_bytes=40 * 2**20),
        cost_estimate=lasting(16),
        name="shared_expert",
    )(tokens, cotangents, up, down)


def expert_block(own, x_ref, g_ref, up_ref, down_ref, router_ref, hid_ref, dpre_ref, mix_ref, dx_ref):
    x, g = x_ref[...], g_ref[:, :MODEL_WIDTH]
    logits = dot_f32(x, router_ref[...])
    named = g_ref[:, MODEL_WIDTH:].astype(F32)
    high = jnp.max(jnp.where(named > 0, logits, -1e30), axis=1, keepdims=True)
    raised = jnp.where(named > 0, jnp.exp(logits - high), 0.0)
    gates = raised / jnp.sum(raised, axis=1, keepdims=True)
    rows = x.shape[0]
    lane = lax.broadcasted_iota(jnp.int32, (rows, 128), 1)
    weights = [
        jnp.sum(jnp.where(lane == own + part, gates, 0.0), axis=1, keepdims=True)
        for part in range(EXP_DEV)
    ]
    half = down_ref.shape[0]
    pre = dot_f32(x, up_ref[...])
    asked = dot_t(g, down_ref[...])
    totals = [jnp.zeros((rows, 128), F32) for part in range(EXP_DEV)]
    for part in range(half // 128):
        which = 128 * part // FF_E
        at = 128 * part + FF_E * which
        lanes = slice(128 * part, 128 * (part + 1))
        lower, upper = slice(at, at + 128), slice(at + FF_E, at + FF_E + 128)
        gate, up, want = pre[:, lower], pre[:, upper], asked[:, lanes]
        sig = jax.nn.sigmoid(gate)
        act = gate * sig
        hidden = act * up
        totals[which] = totals[which] + hidden * want
        hid_ref[:, lanes] = (weights[which] * hidden).astype(BF16)
        dact = weights[which] * want
        dpre_ref[:, lower] = (dact * up * (sig * (1.0 + gate * (1.0 - sig)))).astype(BF16)
        dpre_ref[:, upper] = (dact * act).astype(BF16)
    mix_ref[...] = dot_f32(hid_ref[...], down_ref[...]).astype(BF16)
    dx_ref[:, :MODEL_WIDTH] = dot_t(dpre_ref[...], up_ref[...]).astype(BF16)
    sent = jnp.zeros((rows, 128), F32)
    for part in range(EXP_DEV):
        gate_grad = jnp.sum(totals[part], axis=1, keepdims=True)
        coarse = gate_grad.astype(BF16).astype(F32)
        sent = jnp.where(lane == own + part, coarse, sent)
        sent = jnp.where(lane == own + part + REST_AT, gate_grad - coarse, sent)
    dx_ref[:, MODEL_WIDTH:] = sent.astype(BF16)


def expert_kernel(
    size, own_ref, g_ref, up_ref, down_ref, router_ref, full_ref, *refs
):
    outs, (x_now, g_now), stages, (send_sem, recv_sem, local_sem, in_sem, out_sem) = (
        refs[:4], refs[4:6], refs[6:10], refs[10:]
    )
    grid = Grid(size)
    me, z, x = grid.me, grid.z, grid.x
    barrier = pltpu.get_barrier_semaphore()
    grid.greet(barrier)
    pl.semaphore_wait(barrier, grid.count)

    def push(source, chunk, way):
        return pltpu.make_async_remote_copy(
            src_ref=source,
            dst_ref=full_ref.at[chunk],
            send_sem=send_sem.at[way, chunk],
            recv_sem=recv_sem.at[chunk],
            device_id={"dp": me + grid.steps[way]},
            device_id_type=MESH_ID,
        )

    def place(number):
        if grid.across == 2:
            even, first, last = 1 - number % 2, 1 - jnp.minimum(number, 1), number // 7
            step = (1 - even) * ((number + 1) // 2 - last) + even * (number // 2 - 1 + first)
            side = even * (1 - first) + last
        else:
            step, side = number % grid.deep, number // grid.deep
        zc = near_first(z, step, grid.deep)
        xc = near_first(x, side, grid.across)
        same = xc == x
        onward = (
            same & (zc >= z) & grid.exists[0],
            same & (zc <= z) & grid.exists[1],
            (xc >= x) & grid.exists[2],
            (xc <= x) & grid.exists[3],
        )
        return zc * grid.across + xc, onward

    for way in range(4):
        @pl.when(grid.exists[way])
        def _():
            push(own_ref, me, way).start()
    keep = pltpu.make_async_copy(own_ref, full_ref.at[me], local_sem)
    keep.start()

    def leave(number, chunk):
        return [
            pltpu.make_async_copy(stage.at[number % 2], out.at[chunk], out_sem.at[place_in, number % 2])
            for place_in, (stage, out) in enumerate(zip(stages, outs))
        ]

    def work(number, _):
        chunk, onward = place(number)
        bring = pltpu.make_async_copy(g_ref.at[chunk], g_now, in_sem.at[0])
        bring.start()

        @pl.when(number > 0)
        def _():
            push(full_ref.at[chunk], chunk, 0).wait_recv()
            for way in range(4):
                @pl.when(onward[way])
                def _():
                    push(full_ref.at[chunk], chunk, way).start()

        bring_x = pltpu.make_async_copy(full_ref.at[chunk], x_now, in_sem.at[1])

        @pl.when(number == 0)
        def _():
            pltpu.make_async_copy(own_ref, x_now, in_sem.at[1]).start()

        @pl.when(number > 0)
        def _():
            bring_x.start()

        @pl.when(number > 1)
        def _():
            for copy in leave(number, place(number - 2)[0]):
                copy.wait()

        bring.wait()
        bring_x.wait()
        expert_block(
            EXP_DEV * me, x_now, g_now, up_ref, down_ref, router_ref,
            *[stage.at[number % 2] for stage in stages]
        )
        for copy in leave(number, chunk):
            copy.start()
        return 0

    lax.fori_loop(0, size, work, 0)
    for number in (size - 2, size - 1):
        for copy in leave(number, place(number)[0]):
            copy.wait()

    def finish(number, _):
        chunk, onward = place(number)
        for way in range(4):
            @pl.when(onward[way])
            def _():
                push(full_ref.at[chunk], chunk, way).wait_send()
        return 0

    lax.fori_loop(0, size, finish, 0)
    keep.wait()


def experts(tokens, cotangents, up, down, router, shape):
    size = shape["dp"]
    rows, width = tokens.shape
    hidden = down.shape[0]
    wide = width + 128
    columns = (hidden, 2 * hidden, width, wide)
    results = pl.pallas_call(
        functools.partial(expert_kernel, size),
        out_shape=tuple(
            jax.ShapeDtypeStruct((size, rows, column), BF16) for column in (width,) + columns
        ),
        in_specs=[ANY, ANY, VM, VM, VM],
        out_specs=(ANY,) * 5,
        scratch_shapes=[pltpu.VMEM((rows, width), BF16), pltpu.VMEM((rows, wide), BF16)]
        + [pltpu.VMEM((2, rows, column), BF16) for column in columns]
        + [
            pltpu.SemaphoreType.DMA((4, size)),
            pltpu.SemaphoreType.DMA((size,)),
            pltpu.SemaphoreType.DMA,
            pltpu.SemaphoreType.DMA((2,)),
            pltpu.SemaphoreType.DMA((4, 2)),
        ],
        compiler_params=pltpu.CompilerParams(
            collective_id=4, has_side_effects=True, vmem_limit_bytes=56 * 2**20
        ),
        cost_estimate=lasting(85),
        name="experts",
    )(tokens, cotangents.reshape(size, rows, wide), up, down, router)
    return [result.reshape(size * rows, -1) for result in results]


def rms_scale(values):
    return lax.rsqrt(jnp.mean(values * values, axis=-1, keepdims=True) + 1e-05)


def rms_back(values, scale, gain, grad_normed):
    weighted = grad_normed * gain[None, :]
    grad_values = scale * weighted - values * scale**3 * jnp.mean(
        weighted * values, axis=-1, keepdims=True
    )
    gain_grad = jnp.sum(grad_normed * values * scale, axis=0)
    return (grad_values, gain_grad)


def silu_gate(pre_values):
    half_size = pre_values.shape[-1] // 2
    return jax.nn.silu(pre_values[..., :half_size]) * pre_values[..., half_size:]


def silu_gate_back(pre_values, grad):
    return jax.vjp(silu_gate, pre_values)[1](grad)[0]


def adamw(weight, grad, first, second, rate, decay=0.1):
    grad = grad.astype(F32)
    first_new = 0.9 * first + 0.1 * grad
    second_new = 0.95 * second + 0.05 * grad * grad
    corrected_one = first_new / (1.0 - 0.9**STEP)
    corrected_two = second_new / (1.0 - 0.95**STEP)
    weight_new = weight - rate * (
        corrected_one / (jnp.sqrt(corrected_two) + 1e-08) + decay * weight
    )
    return (first_new, second_new, weight_new)


ALL = ("dp", "row", "col")


def gather_dp(values):
    return lax.all_gather(values, "dp", axis=0, tiled=True)


def scatter_dp(values):
    return lax.psum_scatter(values, "dp", scatter_dimension=0, tiled=True)


def body(
    shape,
    hidden_in, segment_ids, routes, out_grad,
    vectors, vectors_first, vectors_second,
    in_weight, in_weight_first, in_weight_second,
    step_weight, step_weight_first, step_weight_second,
    out_weight, out_weight_first, out_weight_second,
    state_weight, state_weight_first, state_weight_second,
    router, router_first, router_second,
    shared_up, shared_up_first, shared_up_second,
    shared_down, shared_down_first, shared_down_second,
    expert_gate_up, expert_gate_up_first, expert_gate_up_second,
    expert_down, expert_down_first, expert_down_second,
):
    dp = lax.axis_index("dp")
    data_count = lax.axis_size("dp")
    seq_devices = lax.axis_size("row") * lax.axis_size("col")
    local_heads = in_weight.shape[1]
    width = 64 * local_heads
    head_start = lax.axis_index(("row", "col")) * local_heads
    own_tokens = hidden_in.shape[1]
    experts_all = router.shape[1]
    rows_dp = in_weight.shape[0]
    seq_columns = shape["col"]
    residual = hidden_in[0].astype(F32)
    count = vectors.shape[0]
    lines = -(-count // 1024) * 8
    vector_rows = jnp.pad(vectors, (0, lines * 128 - count)).reshape(lines, 128)
    gain_one = vectors[0:MODEL_WIDTH]
    gain_two = vectors[MODEL_WIDTH : 2 * MODEL_WIDTH]

    out_local = out_weight.astype(BF16).reshape(width, -1).T
    mixer_local = jnp.concatenate(
        [
            in_weight.astype(BF16).reshape(rows_dp, 2 * width),
            jnp.pad(step_weight.astype(BF16), ((0, 0), (0, 128 - local_heads))),
        ],
        axis=1,
    )
    small_local = jnp.concatenate(
        [state_weight, jnp.pad(router, ((0, 0), (0, 128 - experts_all)))], axis=1
    ).astype(BF16)
    scale_one = rms_scale(residual)
    normed_one = (residual * scale_one * gain_one[None, :]).astype(BF16)
    up_local = jnp.concatenate(
        [expert_gate_up[held].astype(BF16) for held in range(EXP_DEV)], axis=1
    )
    route_ids = routes[0]
    chosen = (
        route_ids[:, :, None] == jnp.arange(experts_all, dtype=jnp.int32)[None, None, :]
    ).any(axis=1)
    grad_low = out_grad[0]
    grad_ext = jnp.concatenate(
        [grad_low, jnp.pad(chosen.astype(BF16), ((0, 0), (0, 128 - experts_all)))], axis=1
    )
    down_local = expert_down.astype(BF16).reshape(-1, MODEL_WIDTH)
    mixer_full, out_full, shared_up_full, shared_down_full, small_full, normed_all = gather_start(
        (mixer_local, out_local),
        (shared_up.astype(BF16), shared_down.astype(BF16), small_local),
        normed_one,
        shape,
    )
    mixer_full, out_full, small_full, normed_all, segment_ids, grad_ext, up_local, down_local = (
        lax.optimization_barrier(
            (mixer_full, out_full, small_full, normed_all, segment_ids, grad_ext, up_local, down_local)
        )
    )
    grad_all = gather_dp(grad_ext)
    by_columns = lambda array: [array] + [
        shift(array, "col", by) for by in range(1, lax.axis_size("col"))
    ]
    up_parts, down_parts = by_columns(up_local), by_columns(down_local)
    state_step = jnp.concatenate([small_full[:, : 2 * STATE], mixer_full[:, 2 * width :]], axis=1)

    seg_rows = segment_ids[0].astype(F32).reshape(-1, 1, BLK)
    proj = dot_f32(normed_all, mixer_full[:, : 2 * width]).astype(BF16)
    ss = dot_f32(normed_all, state_step)
    valued, squares_part, kept, params = mixer_forward(proj, ss, seg_rows, vector_rows, seq_columns)
    partial_out = dot_t(valued, out_full).astype(BF16)
    partial_out, up_parts, down_parts = lax.optimization_barrier((partial_out, up_parts, down_parts))
    up_full = assemble(all_places(up_parts), 1)
    down_full = assemble(all_places(down_parts), EXP_DEV)
    proj_out = scatter_rc(partial_out)
    squares = scatter_squares(squares_part)[:, 0]
    scale_two = lax.rsqrt(squares / INNER + 1e-05)
    residual_two = residual + scale_two[:, None] * proj_out
    scale_three = rms_scale(residual_two)
    normed_two = (residual_two * scale_three * gain_two[None, :]).astype(BF16)

    router_wide = small_full[:, 2 * STATE :]
    router_full = router_wide[:, :experts_all]
    shared_act, shared_pre_grad, shared_out, shared_dx = shared_expert(
        normed_two, grad_low, shared_up_full, shared_down_full
    )
    shared_up_grad = dot_tn(normed_two, shared_pre_grad).astype(BF16)
    shared_down_grad = dot_tn(shared_act, grad_low).astype(BF16)
    shared_up_kept = scatter_row(shared_up_grad, data_count)
    shared_down_kept = scatter_row(shared_down_grad, data_count)
    normed_two, grad_all, shared_up_kept, shared_down_kept, shared_dx, shared_out = (
        lax.optimization_barrier(
            (normed_two, grad_all, shared_up_kept, shared_down_kept, shared_dx, shared_out)
        )
    )
    shared_up_part = scatter_col(shared_up_kept).astype(BF16)
    shared_down_part = scatter_col(shared_down_kept).astype(BF16)
    tokens_all, hidden_low, pre_grad, mixed, rows_grad = experts(
        normed_two, grad_all, up_full, down_full, router_wide, shape
    )
    logits = dot_f32(normed_two, router_full)
    gate_all = jax.nn.softmax(jnp.where(chosen, logits, -jnp.inf), axis=-1)
    rows_grad, shared_up_part, shared_down_part = lax.optimization_barrier(
        (rows_grad, shared_up_part, shared_down_part)
    )
    routed_grad, up_grad, down_grad = scatter_blocks(
        rows_grad, tokens_all, pre_grad, hidden_low, grad_all, shape
    )
    routed_grad, mixed = lax.optimization_barrier((routed_grad, mixed))
    mixture = scatter_dp(mixed).astype(F32)
    gate_grad = (
        routed_grad[:, MODEL_WIDTH : MODEL_WIDTH + experts_all]
        + routed_grad[:, MODEL_WIDTH + REST_AT : MODEL_WIDTH + REST_AT + experts_all]
    )
    cotangent = grad_low.astype(F32)
    normed_two_grad = shared_dx + routed_grad[:, :MODEL_WIDTH]
    logits_grad = gate_all * (gate_grad - jnp.sum(gate_all * gate_grad, axis=1, keepdims=True))
    logits_low = jnp.where(chosen, logits_grad, 0.0).astype(BF16)
    normed_two_grad = normed_two_grad + dot_t(logits_low, router_full)
    router_grad = dot_tn(normed_two, logits_low)
    residual_two_grad, gain_two_grad = rms_back(
        residual_two, scale_three, gain_two, normed_two_grad
    )
    residual_two_grad = residual_two_grad + cotangent
    proj_out_grad = (residual_two_grad * scale_two[:, None]).astype(BF16)
    squares_grad = (
        jnp.sum(residual_two_grad * proj_out, axis=1) * -0.5 * scale_two**3 / INNER
    )
    squares_high = squares_grad.astype(BF16)
    squares_rest = (squares_grad - squares_high.astype(F32)).astype(BF16)
    riding = jnp.pad(jnp.stack([squares_high, squares_rest], axis=1), ((0, 0), (0, 126)))
    riders = jnp.concatenate([proj_out_grad, riding], axis=1)
    riders, up_grad, down_grad = lax.optimization_barrier((riders, up_grad, down_grad))
    riders = gather_rc(riders)
    proj_grad_all = riders[:, :MODEL_WIDTH]
    squares_grad_all = jnp.sum(riders[:, MODEL_WIDTH:].astype(F32), axis=1, keepdims=True)
    proj_grad_all, up_grad, down_grad = lax.optimization_barrier((proj_grad_all, up_grad, down_grad))
    up_total = scatter_col(up_grad[None])
    down_total = scatter_col(down_grad.reshape(EXP_DEV, -1, MODEL_WIDTH))
    up_total = jnp.stack(
        [up_total[:, 2 * FF_E * held : 2 * FF_E * (held + 1)] for held in range(EXP_DEV)]
    )
    down_total = down_total.reshape(expert_down.shape)
    new_up = adamw(
        expert_gate_up, up_total, expert_gate_up_first, expert_gate_up_second, MODEL_WIDTH ** (-0.5)
    )
    new_down = adamw(expert_down, down_total, expert_down_first, expert_down_second, FF_E ** (-0.5))

    valued_grad = dot_f32(proj_grad_all, out_full).astype(BF16)
    out_grad_t = dot_tn(proj_grad_all, valued).astype(BF16)
    proj_grad, ss_grad, vector_grad = mixer_backward(
        proj, ss, seg_rows, params, valued_grad, squares_grad_all, kept, lines, seq_columns
    )
    all_grad = jnp.concatenate([proj_grad, ss_grad], axis=1)
    mixer_cat = jnp.concatenate([mixer_full[:, : 2 * width], state_step], axis=1)
    normed_part = dot_t(all_grad, mixer_cat)
    gain_one_grad = jnp.sum(normed_part * normed_all.astype(F32), axis=0) / gain_one
    router_wide = jnp.pad(
        router_grad, ((0, 0), (2 * width + 2 * STATE + ROUTER_AT, 128 - ROUTER_AT - experts_all))
    )
    mixer_grad = (dot_tn(normed_all, all_grad) + router_wide).astype(BF16)
    gains = jnp.concatenate([gain_one_grad, gain_two_grad]).reshape(-1, 128)
    vector_lines = vector_grad + jnp.pad(gains, ((0, lines - gains.shape[0]), (0, 0)))
    mixture, mixer_grad, new_up, new_down = lax.optimization_barrier(
        (mixture, mixer_grad, new_up, new_down)
    )
    (
        mixer_total, out_total, shared_up_total, shared_down_total,
        vector_total, small_total, normed_grad,
    ) = scatter_end(
        (mixer_grad, out_grad_t, shared_up_part, shared_down_part),
        vector_lines,
        normed_part.astype(BF16),
        2 * width,
        2 * STATE + 128,
        shape,
    )
    out_total = out_total.T.reshape(out_weight.shape)
    hidden_out = (residual_two + mixture + shared_out).astype(BF16)[None]
    hidden_out = (residual_two + mixture + shared_out).astype(BF16)[None]
    vector_total = vector_total.reshape(-1)[:count]
    state_total = small_total[:, : 2 * STATE]
    router_total = small_total[:, 2 * STATE + ROUTER_AT : 2 * STATE + ROUTER_AT + experts_all]
    step_total = mixer_total[:, 2 * width + 2 * STATE : 2 * width + 2 * STATE + local_heads]
    in_total = mixer_total[:, : 2 * width].reshape(in_weight.shape)
    residual_grad, _ = rms_back(residual, scale_one, gain_one, normed_grad)
    input_grad = (residual_grad + residual_two_grad)[None]

    rate = MODEL_WIDTH ** (-0.5)
    return (
        hidden_out,
        input_grad,
        *adamw(vectors, vector_total, vectors_first, vectors_second, 0.3, 0.0),
        *adamw(in_weight, in_total, in_weight_first, in_weight_second, rate),
        *adamw(step_weight, step_total, step_weight_first, step_weight_second, rate),
        *adamw(out_weight, out_total, out_weight_first, out_weight_second, INNER ** (-0.5)),
        *adamw(state_weight, state_total, state_weight_first, state_weight_second, rate),
        *adamw(router, router_total, router_first, router_second, 0.5 * rate),
        *adamw(shared_up, shared_up_total, shared_up_first, shared_up_second, rate),
        *adamw(shared_down, shared_down_total, shared_down_first, shared_down_second, FF_S ** (-0.5)),
        *new_up,
        *new_down,
    )


def solution(mesh):
    tokens = P("dp", ("row", "col"), None)
    by_head = P("dp", ("row", "col"))
    out_spec = P(("row", "col"), None, "dp")
    flat = P(ALL, None)
    weights = (
        (P(),) * 3
        + (tokens,) * 3
        + (by_head,) * 3
        + (out_spec,) * 3
        + (flat,) * 12
        + (tokens,) * 6
    )
    return jax.shard_map(
        functools.partial(body, dict(mesh.shape)),
        mesh=mesh,
        in_specs=(tokens, P("dp", None), tokens, tokens) + weights,
        out_specs=(tokens, tokens) + weights,
        check_vma=False,
    )
```

```python
import functools

import jax
import jax.numpy as jnp
from jax import lax
from jax.experimental import pallas as pl
from jax.experimental.pallas import tpu as pltpu
from jax.sharding import PartitionSpec as P

STATE = 128
KW = 4
BLK = 128
F32 = jnp.float32
BF16 = jnp.bfloat16


def dot_f32(a, b, dims=(((1,), (0,)), ((), ()))):
    return lax.dot_general(a, b, dims, preferred_element_type=F32)


def dot_exact(a, b, dims=(((1,), (0,)), ((), ()))):
    return lax.dot_general(
        a, b, dims, precision=lax.Precision.HIGHEST, preferred_element_type=F32
    )


def spread(values, width):
    rows = values.shape[0]
    low = lax.broadcasted_iota(jnp.int32, (rows, 128), 1) < 64
    parts = []
    for pair in range(width // 128):
        left = jnp.broadcast_to(values[:, 2 * pair : 2 * pair + 1], (rows, 128))
        right = jnp.broadcast_to(values[:, 2 * pair + 1 : 2 * pair + 2], (rows, 128))
        parts.append(jnp.where(low, left, right))
    return jnp.concatenate(parts, axis=1)


def head_sums(values):
    width = values.shape[1]
    ones = (
        lax.broadcasted_iota(jnp.int32, (width, 128), 0) // 64
        == lax.broadcasted_iota(jnp.int32, (width, 128), 1)
    ).astype(BF16)
    high = values.astype(BF16)
    rest = (values - high.astype(F32)).astype(BF16)
    return dot_f32(high, ones) + dot_f32(rest, ones)


def apart(values):
    low = lax.broadcasted_iota(jnp.int32, (values.shape[0], 128), 1) < 64
    gates, inputs = [], []
    for at in range(0, values.shape[1], 256):
        one, two = values[:, at : at + 128], values[:, at + 128 : at + 256]
        gates.append(jnp.where(low, one, pltpu.roll(two, 64, 1)))
        inputs.append(jnp.where(low, pltpu.roll(one, 64, 1), two))
    return jnp.concatenate(gates, axis=1), jnp.concatenate(inputs, axis=1)


def together(gates, inputs):
    low = lax.broadcasted_iota(jnp.int32, (gates.shape[0], 128), 1) < 64
    parts = []
    for at in range(0, gates.shape[1], 128):
        one, two = gates[:, at : at + 128], inputs[:, at : at + 128]
        parts.append(jnp.where(low, one, pltpu.roll(two, 64, 1)))
        parts.append(jnp.where(low, pltpu.roll(one, 64, 1), two))
    return jnp.concatenate(parts, axis=1)


def block_masks(index, seg_ref):
    now = seg_ref[index]
    before = jnp.where(index > 0, seg_ref[jnp.maximum(index - 1, 0)], -1.0)
    lane = lax.broadcasted_iota(jnp.int32, (1, BLK), 1)
    rows = [now]
    for back in range(1, KW):
        earlier = jnp.where(lane < back, pltpu.roll(before, back, 1), pltpu.roll(now, back, 1))
        rows.append((earlier == now).astype(F32))
    last, prior = now[:, BLK - 1 :], before[:, BLK - 1 :]
    rows.append((now == prior).astype(F32))
    rows.append((now == last).astype(F32))
    rows.append(jnp.broadcast_to((prior == last).astype(F32), (1, BLK)))
    rows.append(jnp.zeros((BLK - len(rows), BLK), F32))
    return jnp.concatenate(rows, axis=0).T


def block_common(width, start, index, proj_ref, ss_ref, seg_ref, par_ref):
    rows = pl.ds(start, BLK)
    before = pl.ds(pl.multiple_of(jnp.maximum(start - 8, 0), 8), 8)
    aux = block_masks(index, seg_ref)
    gate, inner = apart(proj_ref[rows, :].astype(F32))
    current = jnp.concatenate([inner, ss_ref[rows, 0 : 2 * STATE]], axis=1)
    earlier = proj_ref[pl.ds(pl.multiple_of(jnp.maximum(start - 16, 0), 16), 16), :]
    previous = jnp.concatenate(
        [apart(earlier.astype(F32)[8:])[1], ss_ref[before, 0 : 2 * STATE]], axis=1
    )
    extended = jnp.concatenate([previous, current], axis=0)
    taps = par_ref[0:KW, :]
    conv = par_ref[KW : KW + 1, :] + taps[KW - 1 : KW, :] * current
    shifted = []
    for back in range(1, KW):
        moved = pltpu.roll(extended, back, 0)[8:] * aux[:, back : back + 1]
        shifted.append(moved)
        conv = conv + taps[KW - 1 - back : KW - back, :] * moved
    sig = jax.nn.sigmoid(conv)
    active = conv * sig
    inputs_x = active[:, :width]
    matrix_b = active[:, width : width + STATE].astype(BF16)
    matrix_c = active[:, width + STATE :].astype(BF16)
    step_in = ss_ref[rows, 2 * STATE :] + par_ref[7:8, 0:128]
    dt = jnp.maximum(step_in, 0.0) + jnp.log1p(jnp.exp(-jnp.abs(step_in)))
    decay = dt * par_ref[6:7, 0:128]
    row_id = lax.broadcasted_iota(jnp.int32, (BLK, BLK), 0)
    col_id = lax.broadcasted_iota(jnp.int32, (BLK, BLK), 1)
    lower = (row_id >= col_id).astype(F32)
    cum = dot_exact(lower, decay)
    cum_t = cum.T
    same = (aux[:, 0:1] == seg_ref[pl.ds(index, 1), 0, :]) & (row_id >= col_id)
    last = cum[BLK - 1 : BLK, :]
    gain_in = jnp.exp(cum) * aux[:, 4:5]
    tail = jnp.exp(last - cum) * aux[:, 5:6]
    carry = jnp.exp(last) * aux[BLK - 1 : BLK, 6:7]
    scores = jnp.where(same, dot_f32(matrix_c, matrix_b, (((1,), (1,)), ((), ()))), 0.0)
    dt_wide = spread(dt, width)
    moved_x = inputs_x * dt_wide
    return dict(
        rows=rows, aux=aux, gate=gate, current=current, shifted=shifted, conv=conv, sig=sig,
        x=inputs_x, b=matrix_b, c=matrix_c, step_in=step_in, dt=dt, cum=cum, cum_t=cum_t,
        same=same, scores=scores, dt_wide=dt_wide, u=moved_x, lower=lower,
        gain_in=spread(gain_in, width), tail=spread(tail, width),
        carry=spread(jnp.broadcast_to(carry, (8, 128)), width)[0:1],
    )


def split_pair(values):
    low = lax.broadcasted_iota(jnp.int32, values.shape, 1) < 64
    zero = jnp.zeros_like(values)
    return jnp.where(low, values, zero), jnp.where(low, zero, values)


GAIN_AT, BIAS_AT, TAPS_AT, HEADS_AT = 24, 48, 74, 178
INNER_LINES, TAP_LINES = 24, 26


def own_place(columns):
    return lax.axis_index("row") * columns + lax.axis_index("col")


def read_params(width, columns, vec_ref, par_ref):
    lines, heads = width // 128, width // 64
    place = own_place(columns)

    def line(at):
        return jnp.concatenate(
            [vec_ref[pl.ds(at + place * lines + one, 1), :] for one in range(lines)], axis=1
        )

    def wide_line(at):
        rest = at + INNER_LINES
        return jnp.concatenate(
            [line(at), vec_ref[rest : rest + 1, :], vec_ref[rest + 1 : rest + 2, :]], axis=1
        )

    par_ref[...] = jnp.zeros_like(par_ref)
    for tap in range(KW):
        par_ref[tap : tap + 1, :] = wide_line(TAPS_AT + TAP_LINES * tap)
    par_ref[KW : KW + 1, :] = wide_line(BIAS_AT)
    par_ref[5:6, 0:width] = line(GAIN_AT)
    flat = jnp.concatenate([vec_ref[HEADS_AT : HEADS_AT + 1, :], vec_ref[HEADS_AT + 1 : HEADS_AT + 2, :]], axis=1)
    flat = jnp.broadcast_to(flat, (8, 256))
    lane = lax.broadcasted_iota(jnp.int32, (8, 128), 1)

    def per_head(which):
        turned = pltpu.roll(flat, 256 - 48 * which - place * heads, 1)[:, 0:128]
        return jnp.where(lane < heads, turned, 0.0)

    par_ref[6:7, 0:128] = jnp.where(lane < heads, -jnp.exp(per_head(0)), 0.0)[0:1]
    par_ref[7:8, 0:128] = per_head(2)[0:1]
    par_ref[8:9, 0:width] = spread(per_head(1), width)[0:1]


def write_params(width, columns, sums, par_ref, vec_ref):
    lines, heads = width // 128, width // 64
    place = own_place(columns)
    vec_ref[...] = jnp.zeros_like(vec_ref)
    total = lambda at: jnp.sum(sums[at : at + 8, :], axis=0, keepdims=True)

    def line(at, row):
        for one in range(lines):
            vec_ref[pl.ds(at + place * lines + one, 1), :] = row[:, 128 * one : 128 * (one + 1)]

    def wide_line(at, row):
        line(at, row)
        rest = at + INNER_LINES
        vec_ref[rest : rest + 1, :] = row[:, width : width + 128]
        vec_ref[rest + 1 : rest + 2, :] = row[:, width + 128 :]

    for tap in range(KW):
        wide_line(TAPS_AT + TAP_LINES * tap, total(8 * tap))
    wide_line(BIAS_AT, total(32))
    line(GAIN_AT, total(48))
    skips = jnp.sum(head_sums(sums[64:72, 0:width]), axis=0, keepdims=True)
    decays = total(56)[:, 0:128] * par_ref[6:7, 0:128]
    flat = jnp.zeros((8, 256), F32)
    lane = lax.broadcasted_iota(jnp.int32, (8, 256), 1)
    for which, row in enumerate((decays, skips, total(72)[:, 0:128])):
        row = jnp.broadcast_to(jnp.concatenate([row, jnp.zeros((1, 128), F32)], axis=1), (8, 256))
        flat = flat + pltpu.roll(jnp.where(lane < heads, row, 0.0), 48 * which + place * heads, 1)
    vec_ref[HEADS_AT : HEADS_AT + 1, :] = flat[0:1, 0:128]
    vec_ref[HEADS_AT + 1 : HEADS_AT + 2, :] = flat[0:1, 128:]


def forward_kernel(
    width, columns, proj_ref, ss_ref, seg_ref, vec_ref, valued_ref, squares_ref, kept_ref, par_ref, state
):
    blocks = proj_ref.shape[0] // BLK
    state[...] = jnp.zeros_like(state)
    read_params(width, columns, vec_ref, par_ref)

    def step(index, _):
        start = pl.multiple_of(index * BLK, BLK)
        got = block_common(width, start, index, proj_ref, ss_ref, seg_ref, par_ref)
        kept_ref[index] = state[...]
        moved = got["u"].astype(BF16)
        parts = []
        for pair in range(width // 128):
            u0, u1 = split_pair(moved[:, 128 * pair : 128 * (pair + 1)])
            mixes = []
            for head in (2 * pair, 2 * pair + 1):
                differ = jnp.minimum(got["cum"][:, head : head + 1] - got["cum_t"][head : head + 1, :], 0.0)
                mixes.append((jnp.exp(differ) * got["scores"]).astype(BF16))
            parts.append(dot_f32(jnp.concatenate(mixes, axis=1), jnp.concatenate([u0, u1], axis=0)))
        within = jnp.concatenate(parts, axis=1)
        from_state = got["gain_in"] * dot_f32(got["c"], state[...].astype(BF16))
        scanned = within + from_state + par_ref[8:9, 0:width] * got["x"]
        state[...] = state[...] * got["carry"] + dot_f32(
            got["b"], (got["tail"] * got["u"]).astype(BF16), (((0,), (0,)), ((), ()))
        )
        gate = got["gate"]
        gated = scanned * (gate * jax.nn.sigmoid(gate))
        squares_ref[got["rows"], :] = jnp.sum(gated * gated, axis=1, keepdims=True)
        valued_ref[got["rows"], :] = (gated * par_ref[5:6, 0:width]).astype(BF16)
        return 0

    lax.fori_loop(0, blocks, step, 0)


def backward_kernel(
    width, columns, proj_ref, ss_ref, seg_ref, par_ref, vgrad_ref, dsq_ref, kept_ref,
    dproj_ref, dss_ref, dvec_ref, dstate, follow, ebuf, sums
):
    blocks = proj_ref.shape[0] // BLK
    dstate[...] = jnp.zeros_like(dstate)
    follow[...] = jnp.zeros_like(follow)
    sums[...] = jnp.zeros_like(sums)

    def fold(values):
        total = values[0:8]
        for part in range(1, BLK // 8):
            total = total + values[8 * part : 8 * part + 8]
        return total

    def step(count, _):
        index = blocks - 1 - count
        start = pl.multiple_of(index * BLK, BLK)
        got = block_common(width, start, index, proj_ref, ss_ref, seg_ref, par_ref)
        rows, aux = got["rows"], got["aux"]
        state_in = kept_ref[index]
        state_low = state_in.astype(BF16)
        moved = got["u"].astype(BF16)
        skip = par_ref[8:9, 0:width]
        gain = par_ref[5:6, 0:width]
        parts = []
        for pair in range(width // 128):
            u0, u1 = split_pair(moved[:, 128 * pair : 128 * (pair + 1)])
            mixes = []
            for head in (2 * pair, 2 * pair + 1):
                differ = jnp.minimum(got["cum"][:, head : head + 1] - got["cum_t"][head : head + 1, :], 0.0)
                level = jnp.exp(differ)
                ebuf[head] = level
                mixes.append((level * got["scores"]).astype(BF16))
            parts.append(dot_f32(jnp.concatenate(mixes, axis=1), jnp.concatenate([u0, u1], axis=0)))
        inner = jnp.concatenate(parts, axis=1) + got["gain_in"] * dot_f32(got["c"], state_low)
        scanned = inner + skip * got["x"]
        gate = got["gate"]
        gate_sig = jax.nn.sigmoid(gate)
        gate_act = gate * gate_sig
        gated = scanned * gate_act
        vgrad = vgrad_ref[rows, :].astype(F32)
        dgated = vgrad * gain + 2.0 * gated * dsq_ref[rows, :]
        sums[48:56, 0:width] += fold(vgrad * gated)
        dy = dgated * gate_act
        dgate = dgated * scanned * (gate_sig * (1.0 + gate * (1.0 - gate_sig)))
        dy_low = dy.astype(BF16)
        dscores = jnp.zeros((BLK, BLK), F32)
        parts = []
        for pair in range(width // 128):
            lanes = slice(128 * pair, 128 * (pair + 1))
            u0, u1 = split_pair(moved[:, lanes])
            d0, d1 = split_pair(dy_low[:, lanes])
            mixes = []
            for head, u_own in ((2 * pair, u0), (2 * pair + 1, u1)):
                level = ebuf[head]
                mixes.append((level * got["scores"]).astype(BF16))
                dscores = dscores + level * dot_f32(
                    dy_low[:, lanes], u_own, (((1,), (1,)), ((), ()))
                )
            parts.append(
                dot_f32(
                    jnp.concatenate(mixes, axis=0),
                    jnp.concatenate([d0, d1], axis=0),
                    (((0,), (0,)), ((), ())),
                )
            )
        du_within = jnp.concatenate(parts, axis=1)
        dscores = jnp.where(got["same"], dscores, 0.0).astype(BF16)
        dstate_now = dstate[...]
        dstate_low = dstate_now.astype(BF16)
        dy_in = (got["gain_in"] * dy).astype(BF16)
        u_tail = got["tail"] * got["u"]
        from_next = dot_f32(got["b"], dstate_low)
        du = du_within + got["tail"] * from_next
        dmat_c = dot_f32(dscores, got["b"]) + dot_f32(dy_in, state_low, (((1,), (1,)), ((), ())))
        dmat_b = dot_f32(dscores, got["c"], (((0,), (0,)), ((), ()))) + dot_f32(
            u_tail.astype(BF16), dstate_low, (((1,), (1,)), ((), ()))
        )
        tail_part = head_sums(u_tail * from_next)
        dcum = (
            head_sums(dy_low.astype(F32) * inner - moved.astype(F32) * du_within) - tail_part
        )
        kept_part = head_sums(fold(got["carry"] * dstate_now * state_in))
        at_last = jnp.sum(tail_part, axis=0, keepdims=True) + jnp.sum(kept_part, axis=0, keepdims=True)
        ddecay = dot_exact(got["lower"], dcum, (((0,), (0,)), ((), ()))) + at_last
        ddt = ddecay * par_ref[6:7, 0:128] + head_sums(du * got["x"])
        sums[56:64, 0:128] += fold(ddecay * got["dt"])
        sums[64:72, 0:width] += fold(dy * got["x"])
        dstep = ddt * jax.nn.sigmoid(got["step_in"])
        sums[72:80, 0:128] += fold(dstep)
        dstate[...] = dstate_now * got["carry"] + dot_f32(got["c"], dy_in, (((0,), (0,)), ((), ())))
        dactive = jnp.concatenate([skip * dy + du * got["dt_wide"], dmat_b, dmat_c], axis=1)
        sig, conv = got["sig"], got["conv"]
        dconv = dactive * (sig * (1.0 + conv * (1.0 - sig)))
        sums[32:40, :] += fold(dconv)
        sums[24:32, :] += fold(dconv * got["current"])
        dinput = par_ref[KW - 1 : KW, :] * dconv
        for back in range(1, KW):
            tap = KW - 1 - back
            sums[8 * tap : 8 * tap + 8, :] += fold(dconv * got["shifted"][back - 1])
            masked = dconv * aux[:, back : back + 1]
            ext = jnp.concatenate([masked, follow[back - 1]], axis=0)
            dinput = dinput + par_ref[tap : tap + 1, :] * pltpu.roll(ext, BLK + 8 - back, 0)[:BLK]
            follow[back - 1] = masked[0:8]
        dproj_ref[rows, :] = together(dgate, dinput[:, :width]).astype(BF16)
        dss_ref[rows, 0 : 2 * STATE] = dinput[:, width:].astype(BF16)
        dss_ref[rows, 2 * STATE :] = dstep.astype(BF16)
        return 0

    lax.fori_loop(0, blocks, step, 0)
    write_params(width, columns, sums, par_ref, dvec_ref)


VM = pl.BlockSpec(memory_space=pltpu.VMEM)


def lasting(micros):
    return pl.CostEstimate(flops=0, bytes_accessed=int(micros * 3.0e6), transcendentals=0)


def mixer_forward(proj, ss, seg, vec, columns):
    length, double = proj.shape
    width = double // 2
    blocks = length // BLK
    return pl.pallas_call(
        functools.partial(forward_kernel, width, columns),
        out_shape=(
            jax.ShapeDtypeStruct((length, width), BF16),
            jax.ShapeDtypeStruct((length, 1), F32),
            jax.ShapeDtypeStruct((blocks, STATE, width), F32),
            jax.ShapeDtypeStruct((16, width + 2 * STATE), F32),
        ),
        in_specs=[VM] * 4,
        out_specs=(VM,) * 4,
        scratch_shapes=[pltpu.VMEM((STATE, width), F32)],
        compiler_params=pltpu.CompilerParams(vmem_limit_bytes=56 * 2**20),
        cost_estimate=lasting(20),
        name="mixer_forward",
    )(proj, ss, seg, vec)


def mixer_backward(proj, ss, seg, par, vgrad, dsq, kept, lines, columns):
    length, double = proj.shape
    width = double // 2
    wide = width + 2 * STATE
    return pl.pallas_call(
        functools.partial(backward_kernel, width, columns),
        out_shape=(
            jax.ShapeDtypeStruct((length, 2 * width), BF16),
            jax.ShapeDtypeStruct((length, 3 * STATE), BF16),
            jax.ShapeDtypeStruct((lines, 128), F32),
        ),
        in_specs=[VM] * 7,
        out_specs=(VM,) * 3,
        scratch_shapes=[
            pltpu.VMEM((STATE, width), F32),
            pltpu.VMEM((KW - 1, 8, wide), F32),
            pltpu.VMEM((width // 64, BLK, BLK), F32),
            pltpu.VMEM((80, wide), F32),
        ],
        compiler_params=pltpu.CompilerParams(vmem_limit_bytes=56 * 2**20),
        cost_estimate=lasting(34),
        name="mixer_backward",
    )(proj, ss, seg, par, vgrad, dsq, kept)


MODEL_WIDTH = 1536
HEADS = 48
FF_E = 512
FF_S = 1024
TOPK = 6
STEP = 10
EXP_DEV = 2
INNER = 3072
ROUTER_AT = 64
REST_AT = 64


def dot_t(a, b):
    return dot_f32(a, b, (((1,), (1,)), ((), ())))


def dot_tn(a, b):
    return dot_f32(a, b, (((0,), (0,)), ((), ())))


def shift(values, axis, by):
    size = lax.axis_size(axis)
    return lax.ppermute(values, axis, [(i, (i + by) % size) for i in range(size)])


def all_places(own):
    rows, columns = lax.axis_index("row"), lax.axis_size("col")
    col = lax.axis_index("col")
    placed = []
    for by, part in enumerate(own):
        there = (col - by) % columns
        placed.append((rows * columns + there, part))
        placed.append(((1 - rows) * columns + there, shift(part, "row", 1)))
    return placed


def assemble(placed, group):
    count = len(placed)
    rows, columns = placed[0][1].shape
    total = jnp.zeros((group, count, rows // group, columns), placed[0][1].dtype)
    for place, part in placed:
        total = lax.dynamic_update_slice(
            total, part.reshape(group, 1, rows // group, columns), (0, place, 0, 0)
        )
    return total.reshape(count * rows, columns)


def gather_rc(values):
    columns = lax.axis_size("col")
    return assemble(
        all_places([values] + [shift(values, "col", by) for by in range(1, columns)]), 1
    )


def block_of(array, at, rows):
    return lax.dynamic_slice_in_dim(array, at * rows, rows)


def scatter_row(values, group=1):
    row = lax.axis_index("row")
    halves = values.reshape(group, 2, -1, values.shape[1])
    pick = lambda which: lax.dynamic_index_in_dim(halves, which, 1, keepdims=False)
    away = shift(pick(1 - row), "row", 1)
    return (pick(row).astype(F32) + away.astype(F32)).astype(values.dtype)


def scatter_col(kept):
    columns, col = lax.axis_size("col"), lax.axis_index("col")
    parts = kept.reshape(kept.shape[0], columns, -1, kept.shape[2])
    pick = lambda which: lax.dynamic_index_in_dim(parts, which, 1, keepdims=False)
    total = pick(col).astype(F32)
    for by in range(1, columns):
        total = total + shift(pick((col + by) % columns), "col", by).astype(F32)
    return total.reshape(-1, kept.shape[2])


def scatter_rc(values):
    return scatter_col(scatter_row(values))


def scatter_squares(values):
    columns, col = lax.axis_size("col"), lax.axis_index("col")
    kept = scatter_row(values)[0]
    rows = kept.shape[0] // columns
    total = block_of(kept, col, rows)
    for by in range(1, columns):
        total = total + shift(block_of(kept, (col + by) % columns, rows), "col", by)
    return total


def partners(shape):
    steps = []
    for name in ("dp", "row", "col"):
        bit = 1
        while bit < shape[name]:
            steps.append((name, bit))
            bit *= 2
    return steps


DEEP = 4
MESH_ID = pl.DeviceIdType.MESH
ANY = pl.BlockSpec(memory_space=pl.ANY)


def near_first(place, step, size):
    if size == 1:
        return place
    if size == 2:
        return place + step * (1 - 2 * place)
    side = place // 2
    inner = (place * (3 - place)) // 2
    found = step + inner * (1 - 2 * step) * (1 - step // 2)
    return found + side * (3 - 2 * found)


class Grid:
    def __init__(self, size):
        self.size, self.deep, self.across = size, DEEP, size // DEEP
        self.me = lax.axis_index("dp")
        self.z, self.x = self.me // self.across, self.me % self.across
        self.steps = (-self.across, self.across, -1, 1)
        self.exists = (
            self.z > 0,
            self.z < self.deep - 1,
            self.x > 0,
            self.x < self.across - 1,
        )
        self.count = (
            jnp.minimum(self.z, 1)
            + jnp.minimum(self.deep - 1 - self.z, 1)
            + jnp.minimum(self.x, 1)
            + jnp.minimum(self.across - 1 - self.x, 1)
        )

    def greet(self, barrier):
        for there, step in zip(self.exists, self.steps):
            @pl.when(there)
            def _():
                pl.semaphore_signal(
                    barrier, inc=1, device_id={"dp": self.me + step}, device_id_type=MESH_ID
                )


def gather_kernel(size, columns, *refs):
    count = PLAIN + BOTH
    hidden_ref, vec_ref, in_ref, step_ref, out_ref, up_ref, down_ref, state_ref, router_ref = refs[:9]
    outs, ins, refs = refs[9 : 10 + count], refs[10 + count : 11 + 2 * count], refs[11 + 2 * count :]
    dp_send, dp_recv, sh_send, sh_recv, rc_send, rc_recv, keep_sem = refs
    mixer, step, out, up, down, small, tokens = ins
    states = state_ref.shape[1]
    grid = Grid(size)
    me, z, x = grid.me, grid.z, grid.x
    row, col = lax.axis_index("row"), lax.axis_index("col")
    mine, other_row = row * columns + col, {"row": 1 - row}
    to_col = lambda by: {"col": (col + by) % columns}
    from_col = lambda by: row * columns + (col + by) % columns
    barrier = pltpu.get_barrier_semaphore()
    grid.greet(barrier)
    pl.semaphore_signal(barrier, inc=1, device_id=other_row, device_id_type=MESH_ID)
    for by in range(1, columns):
        pl.semaphore_signal(barrier, inc=1, device_id=to_col(by), device_id_type=MESH_ID)
    for head in range(in_ref.shape[0]):
        mixer[:, 128 * head : 128 * (head + 1)] = in_ref[head].astype(BF16)
    step[...] = step_ref[...].T.astype(BF16)
    out[...] = out_ref[...].T.astype(BF16)
    up[...] = up_ref[...].astype(BF16)
    down[...] = down_ref[...].astype(BF16)
    small[:, 0:states] = state_ref[...].astype(BF16)
    small[:, states:] = router_ref[...].T.astype(BF16)
    values = hidden_ref[...].astype(F32)
    gain = jnp.concatenate([vec_ref[line : line + 1, :] for line in range(values.shape[1] // 128)], axis=1)
    mean = jnp.sum(values * values, axis=1, keepdims=True) / values.shape[1]
    tokens[...] = (values * lax.rsqrt(mean + 1e-05) * gain).astype(BF16)
    pl.semaphore_wait(barrier, grid.count + columns)

    def block(which, chunk, place):
        return outs[which].at[chunk] if which < PLAIN else outs[which].at[chunk, place]

    def push(which, chunk, way, source=None):
        ref = block(which, chunk, mine)
        return pltpu.make_async_remote_copy(
            src_ref=ref if source is None else source,
            dst_ref=ref,
            send_sem=dp_send.at[which, way, chunk],
            recv_sem=dp_recv.at[which, chunk],
            device_id={"dp": me + grid.steps[way]},
            device_id_type=MESH_ID,
        )

    def spread(which, chunk, place, index, peer, source=None):
        ref = block(which, chunk, place)
        return pltpu.make_async_remote_copy(
            src_ref=ref if source is None else source,
            dst_ref=ref,
            send_sem=sh_send.at[which - PLAIN, index, chunk],
            recv_sem=sh_recv.at[which - PLAIN, place, chunk],
            device_id=peer,
            device_id_type=MESH_ID,
        )

    def spread_tokens(place, index, peer, source=None):
        ref = outs[count].at[place]
        return pltpu.make_async_remote_copy(
            src_ref=ref if source is None else source,
            dst_ref=ref,
            send_sem=rc_send.at[index],
            recv_sem=rc_recv.at[place],
            device_id=peer,
            device_id_type=MESH_ID,
        )

    def place_of(number):
        if grid.across == 2:
            even, first, last = 1 - number % 2, 1 - jnp.minimum(number, 1), number // 7
            step = (1 - even) * ((number + 1) // 2 - last) + even * (number // 2 - 1 + first)
            side = even * (1 - first) + last
        else:
            step, side = number % grid.deep, number // grid.deep
        zc = near_first(z, step, grid.deep)
        xc = near_first(x, side, grid.across)
        same = xc == x
        ways = (same & (zc >= z), same & (zc <= z), xc >= x, xc <= x)
        return zc * grid.across + xc, [way & there for way, there in zip(ways, grid.exists)]

    def spread_chunk(chunk, sources=(None,) * BOTH):
        for which, source in zip(range(PLAIN, count), sources):
            spread(which, chunk, mine, 0, other_row, source).start()
            for by in range(1, columns):
                spread(which, chunk, mine, by, to_col(by), source).start()

    def pass_on(number, _):
        chunk, onward = place_of(number)
        for which in range(count):
            push(which, chunk, 0).wait_recv()
            for way in range(4):
                @pl.when(onward[way])
                def _():
                    push(which, chunk, way).start()
        return chunk

    for way in range(4):
        @pl.when(grid.exists[way])
        def _():
            for which in range(count):
                push(which, me, way, ins[which]).start()
    spread_tokens(mine, 0, other_row, ins[count]).start()
    for by in range(1, columns):
        spread_tokens(mine, by, to_col(by), ins[count]).start()
    keeps = [
        pltpu.make_async_copy(ins[which], block(which, me, mine), keep_sem.at[which])
        for which in range(count)
    ]
    keeps.append(pltpu.make_async_copy(ins[count], outs[count].at[mine], keep_sem.at[count]))
    for copy in keeps:
        copy.start()
    early = pass_on(1, 0)
    for by in range(1, columns):
        spread_tokens(from_col(by), columns - 1 + by, other_row).wait_recv()
        spread_tokens(from_col(by), columns - 1 + by, other_row).start()
    spread_chunk(me, ins[PLAIN:count])
    spread_chunk(early)

    def later(number, _):
        spread_chunk(pass_on(number, 0))
        return 0

    lax.fori_loop(2, size, later, 0)

    def forward_chunk(number, _):
        chunk = place_of(number)[0]
        for which in range(PLAIN, count):
            for by in range(1, columns):
                place = from_col(by)
                spread(which, chunk, place, columns - 1 + by, other_row).wait_recv()
                spread(which, chunk, place, columns - 1 + by, other_row).start()
        return 0

    lax.fori_loop(0, size, forward_chunk, 0)

    def finish(number, _):
        chunk, onward = place_of(number)
        for which in range(PLAIN, count):
            for by in range(columns):
                spread(which, chunk, (1 - row) * columns + (col + by) % columns, 0, other_row).wait_recv()
            for index in range(2 * columns - 1):
                spread(which, chunk, mine, index, other_row).wait_send()
        for way in range(4):
            @pl.when(onward[way])
            def _():
                for which in range(count):
                    push(which, chunk, way).wait_send()
        return 0

    lax.fori_loop(0, size, finish, 0)
    for by in range(columns):
        spread_tokens((1 - row) * columns + (col + by) % columns, 0, other_row).wait_recv()
    for index in range(2 * columns - 1):
        spread_tokens(mine, index, other_row).wait_send()
    for copy in keeps:
        copy.wait()


PLAIN, BOTH = 3, 3


def gather_start(hidden, vec, in_weight, step, out_weight, shared_up, shared_down, state, router, shape):
    size, columns = shape["dp"], shape["col"]
    places, count = 2 * columns, PLAIN + BOTH
    heads, rows = in_weight.shape[:2]
    blocks = [
        (rows, 128 * heads),
        (rows, 128),
        (out_weight.shape[1], out_weight.shape[0]),
        shared_up.shape,
        shared_down.shape,
        (state.shape[0], state.shape[1] + 128),
        hidden.shape,
    ]
    lead = [(size,)] * PLAIN + [(size, places)] * BOTH + [(places,)]
    results = pl.pallas_call(
        functools.partial(gather_kernel, size, columns),
        out_shape=tuple(jax.ShapeDtypeStruct(at + block, BF16) for at, block in zip(lead, blocks)),
        in_specs=[VM] * 9,
        out_specs=(ANY,) * (count + 1),
        scratch_shapes=[pltpu.VMEM(block, BF16) for block in blocks]
        + [
            pltpu.SemaphoreType.DMA((count, 4, size)),
            pltpu.SemaphoreType.DMA((count, size)),
            pltpu.SemaphoreType.DMA((BOTH, 2 * columns - 1, size)),
            pltpu.SemaphoreType.DMA((BOTH, places, size)),
            pltpu.SemaphoreType.DMA((2 * columns - 1,)),
            pltpu.SemaphoreType.DMA((places,)),
            pltpu.SemaphoreType.DMA((count + 1,)),
        ],
        compiler_params=pltpu.CompilerParams(
            collective_id=2, has_side_effects=True, vmem_limit_bytes=58 * 2**20
        ),
        cost_estimate=lasting(105),
        name="gather_start",
    )(hidden, vec, in_weight, step, out_weight, shared_up, shared_down, state, router)
    return [result.reshape(-1, result.shape[-1]) for result in results]


class LineSum:
    def __init__(self, grid, part_ref, out_ref, sums, from_x, from_z, x_send, x_recv, z_send, z_recv):
        self.grid, self.part_ref, self.out_ref = grid, part_ref, out_ref
        self.sums, self.from_x, self.from_z = sums, from_x, from_z
        self.x_send, self.x_recv, self.z_send, self.z_recv = x_send, x_recv, z_send, z_recv

    @staticmethod
    def scratch(size, chunk):
        pair = size == 2 * DEEP
        return [
            pltpu.VMEM((DEEP if pair else size,) + chunk, BF16),
            pltpu.VMEM((DEEP if pair else 2 * size,) + chunk, BF16),
            pltpu.VMEM((DEEP + 1,) + chunk, BF16),
            pltpu.SemaphoreType.DMA((size,)),
            pltpu.SemaphoreType.DMA((2 * size,)),
            pltpu.SemaphoreType.DMA((DEEP,)),
            pltpu.SemaphoreType.DMA((DEEP + 1,)),
        ]

    def sum_slot(self, line, there):
        return line if self.grid.across == 2 else line * self.grid.across + there

    def x_slot(self, line, there, way):
        return line if self.grid.across == 2 else way * self.grid.size + line * self.grid.across + there

    def along_x(self, line, there, way):
        grid = self.grid
        chunk = line * grid.across + there
        return pltpu.make_async_remote_copy(
            src_ref=self.part_ref.at[chunk] if grid.across == 2 else self.sums.at[self.sum_slot(line, there)],
            dst_ref=self.from_x.at[self.x_slot(line, there, way)],
            send_sem=self.x_send.at[chunk],
            recv_sem=self.x_recv.at[way * grid.size + chunk],
            device_id={"dp": grid.me + 2 * way - 1},
            device_id_type=MESH_ID,
        )

    def along_z(self, line, way, receiving):
        grid = self.grid
        end = grid.z if receiving else grid.z + 2 * way - 1
        slot = line if way else line + (1 - jnp.minimum(jnp.abs(line - end), 1)) * (grid.deep - line)
        return pltpu.make_async_remote_copy(
            src_ref=self.sums.at[self.sum_slot(line, grid.x)],
            dst_ref=self.from_z.at[slot],
            send_sem=self.z_send.at[line],
            recv_sem=self.z_recv.at[slot],
            device_id={"dp": grid.me + (2 * way - 1) * grid.across},
            device_id_type=MESH_ID,
        ), slot

    def collect(self, line):
        grid, out_ref, x = self.grid, self.out_ref, self.grid.x
        out_ref[...] = self.part_ref[line * grid.across + x].astype(F32)
        for way, there in ((1, grid.exists[2]), (0, grid.exists[3])):
            @pl.when(there)
            def _():
                self.along_x(line, x, way).wait_recv()
                out_ref[...] += self.from_x[self.x_slot(line, x, way)].astype(F32)
        for way, comes in (
            (1, grid.exists[0] & (line >= grid.z)), (0, grid.exists[1] & (line <= grid.z))
        ):
            @pl.when(comes)
            def _():
                copy, slot = self.along_z(line, way, True)
                copy.wait_recv()
                out_ref[...] += self.from_z[slot].astype(F32)
        for way, toward in ((1, line > grid.z), (0, line < grid.z)):
            @pl.when(toward)
            def _():
                self.sums[self.sum_slot(line, x)] = out_ref[...].astype(BF16)
                self.along_z(line, way, False)[0].start()

    def wait_sent(self, line, there):
        grid, x = self.grid, self.grid.x
        for way in range(2):
            @pl.when((there > x) if way else (there < x))
            def _():
                self.along_x(line, there, way).wait_send()

            @pl.when((there == x) & ((line > grid.z) if way else (line < grid.z)))
            def _():
                self.along_z(line, way, False)[0].wait_send()

    @staticmethod
    def start(sums):
        grid = sums[0].grid
        x, across = grid.x, grid.across

        def away(number, _):
            line = near_first(grid.z, grid.deep - 1 - number // (across - 1), grid.deep)
            there = near_first(x, across - 1 - number % (across - 1), across)
            for one in sums:
                if across > 2:
                    one.sums[one.sum_slot(line, there)] = one.part_ref[line * across + there]
                for way, beyond in ((1, grid.exists[2]), (0, grid.exists[3])):
                    toward = (there > x) if way else (there < x)
                    if across > 2:
                        @pl.when(toward & beyond)
                        def _():
                            one.along_x(line, there, way).wait_recv()
                            held = one.sums.at[one.sum_slot(line, there)]
                            held[...] = (
                                held[...].astype(F32)
                                + one.from_x[one.x_slot(line, there, way)].astype(F32)
                            ).astype(BF16)
                    @pl.when(toward)
                    def _():
                        one.along_x(line, there, way).start()
            return 0

        lax.fori_loop(0, grid.deep * (across - 1), away, 0)

    @staticmethod
    def finish(sums, between=None, after=None):
        grid = sums[0].grid

        def collect(number, _):
            if between is not None:
                between(number)
            line = near_first(grid.z, grid.deep - 1 - number, grid.deep)
            for place, one in enumerate(sums):
                one.collect(line)
                if after is not None and place == 0:
                    @pl.when(number == grid.deep - 1)
                    def _():
                        after()
            return 0

        lax.fori_loop(0, grid.deep, collect, 0)
        def wait(number, _):
            line = near_first(grid.z, grid.deep - 1 - number // grid.across, grid.deep)
            there = near_first(grid.x, grid.across - 1 - number % grid.across, grid.across)
            for one in sums:
                one.wait_sent(line, there)
            return 0

        lax.fori_loop(0, grid.size, wait, 0)


TILE = 256


def scatter_kernel(size, part_ref, x_ref, dpre_ref, hid_ref, g_ref, out_ref, up_ref, down_ref, *refs):
    dpre_now, g_now, left, turned, stage, sent, came = refs[:7]
    whole_sem, left_sem, stage_sem, row_send, row_recv = refs[7:12]
    grid = Grid(size)
    row = lax.axis_index("row")
    barrier = pltpu.get_barrier_semaphore()
    grid.greet(barrier)
    pl.semaphore_signal(barrier, inc=1, device_id={"row": 1 - row}, device_id_type=MESH_ID)
    pl.semaphore_wait(barrier, grid.count + 1)
    sums = [LineSum(grid, part_ref, out_ref, *refs[12:])]
    LineSum.start(sums)

    width = g_now.shape[1]
    ups, downs = up_ref.shape[0] // TILE, down_ref.shape[0] // TILE
    half = ups + downs
    bring_dpre = pltpu.make_async_copy(dpre_ref, dpre_now, whole_sem.at[0])
    bring_g = pltpu.make_async_copy(g_ref.at[:, pl.ds(0, width)], g_now, whole_sem.at[1])
    begin, end = lambda copy: copy.start(), lambda copy: copy.wait()

    def bring(tile, do):
        whose = row + (1 - tile // half) * (1 - 2 * row)
        within = tile % half

        @pl.when((within < ups) & (tile < 2 * half))
        def _():
            at = pl.ds(pl.multiple_of((whose * ups + within) * TILE, TILE), TILE)
            do(pltpu.make_async_copy(x_ref.at[:, at], left.at[tile % 2], left_sem.at[tile % 2]))

        @pl.when((within >= ups) & (tile < 2 * half))
        def _():
            at = pl.ds(pl.multiple_of(((within - ups) * 2 + whose) * TILE, TILE), TILE)
            do(pltpu.make_async_copy(hid_ref.at[:, at], left.at[tile % 2], left_sem.at[tile % 2]))

    def push(within):
        return pltpu.make_async_remote_copy(
            src_ref=sent.at[within],
            dst_ref=came.at[within],
            send_sem=row_send.at[within],
            recv_sem=row_recv.at[within],
            device_id={"row": 1 - row},
            device_id_type=MESH_ID,
        )

    def leave(within, do):
        @pl.when((within >= 0) & (within < ups))
        def _():
            at = pl.ds(pl.multiple_of(within * TILE, TILE), TILE)
            do(pltpu.make_async_copy(stage.at[within % 2], up_ref.at[at], stage_sem.at[within % 2]))

        @pl.when(within >= ups)
        def _():
            at = pl.ds(pl.multiple_of((within - ups) * TILE, TILE), TILE)
            do(
                pltpu.make_async_copy(
                    stage.at[within % 2, :, pl.ds(0, width)], down_ref.at[at], stage_sem.at[within % 2]
                )
            )

    bring(0, begin)
    bring_dpre.start()
    bring_g.start()
    bring_dpre.wait()
    bring_g.wait()

    def work(tile, _):
        within = tile % half
        bring(tile + 1, begin)
        bring(tile, end)

        @pl.when(tile >= half)
        def _():
            leave(within - 2, end)
            push(within).wait_recv()

        turned[...] = left[tile % 2].T
        for wanted, right in ((within < ups, dpre_now), (within >= ups, g_now)):
            for theirs in (True, False):
                @pl.when(wanted & ((tile < half) if theirs else (tile >= half)))
                def _():
                    for at in range(0, right.shape[1], 512):
                        lanes = slice(at, at + 512)
                        found = dot_f32(turned[...], right[:, lanes])
                        if theirs:
                            sent[within, :, lanes] = found.astype(BF16)
                        else:
                            stage[within % 2, :, lanes] = (
                                found + came[within, :, lanes].astype(F32)
                            ).astype(BF16)

        @pl.when(tile < half)
        def _():
            push(within).start()

        @pl.when(tile >= half)
        def _():
            leave(within, begin)

        return 0

    def between(number):
        done = [0, 2 * half * 2 // 5, 2 * half * 7 // 10, 2 * half * 7 // 10, 2 * half]
        bounds = [jnp.int32(0), jnp.int32(0)]
        for step in range(DEEP):
            now = 1 - jnp.minimum(jnp.abs(number - step), 1)
            bounds = [bounds[0] + now * done[step], bounds[1] + now * done[step + 1]]
        lax.fori_loop(bounds[0], bounds[1], work, 0)

    LineSum.finish(sums, between)
    leave(half - 2, end)
    leave(half - 1, end)

    def sent_all(within, _):
        push(within).wait_send()
        return 0

    lax.fori_loop(0, half, sent_all, 0)


def scatter_blocks(parts, tokens, dpre, hidden, cotangents, shape):
    size, width = shape["dp"], tokens.shape[1]
    if size > 2 * DEEP:
        low = lambda array: array.astype(BF16).reshape(-1, array.shape[-1])
        return (
            scatter_dp(parts).astype(F32),
            low(scatter_row(dot_tn(tokens, dpre).astype(BF16))),
            low(scatter_row(dot_tn(hidden, cotangents[:, :width]).astype(BF16), EXP_DEV)),
        )
    parts = parts.reshape((size, -1, parts.shape[1]))
    chunk, count = parts.shape[1:], tokens.shape[0]
    up_half, down_half = width // 2, hidden.shape[1] // 2
    half = (up_half + down_half) // TILE
    return pl.pallas_call(
        functools.partial(scatter_kernel, size),
        out_shape=(
            jax.ShapeDtypeStruct(chunk, F32),
            jax.ShapeDtypeStruct((up_half, dpre.shape[1]), BF16),
            jax.ShapeDtypeStruct((down_half, width), BF16),
        ),
        in_specs=[VM] + [ANY] * 4,
        out_specs=(VM, ANY, ANY),
        scratch_shapes=[
            pltpu.VMEM(dpre.shape, BF16),
            pltpu.VMEM((count, width), BF16),
            pltpu.VMEM((2, count, TILE), BF16),
            pltpu.VMEM((TILE, count), BF16),
            pltpu.VMEM((2, TILE, dpre.shape[1]), BF16),
            pltpu.VMEM((half, TILE, dpre.shape[1]), BF16),
            pltpu.VMEM((half, TILE, dpre.shape[1]), BF16),
            pltpu.SemaphoreType.DMA((2,)),
            pltpu.SemaphoreType.DMA((2,)),
            pltpu.SemaphoreType.DMA((2,)),
            pltpu.SemaphoreType.DMA((half,)),
            pltpu.SemaphoreType.DMA((half,)),
        ]
        + LineSum.scratch(size, chunk),
        compiler_params=pltpu.CompilerParams(
            collective_id=5, has_side_effects=True, vmem_limit_bytes=60 * 2**20
        ),
        cost_estimate=lasting(78),
        name="scatter_blocks",
    )(parts, tokens, dpre, hidden, cotangents)


def adam_step(weight, grad, first, second, rate, decay=0.1):
    first_new = 0.9 * first + 0.1 * grad
    second_new = 0.95 * second + 0.05 * grad * grad
    corrected_one = first_new / (1.0 - 0.9**STEP)
    corrected_two = second_new / (1.0 - 0.95**STEP)
    weight_new = weight - rate * (
        corrected_one / (jnp.sqrt(corrected_two) + 1e-08) + decay * weight
    )
    return (first_new, second_new, weight_new)


NARROW = 1


def end_kernel(size, steps, columns, count, *refs):
    take = lambda number: (refs[:number], refs[number:])
    part_refs, refs = take(count)
    (value_ref, seq_ref), refs = take(2)
    out_refs, refs = take(count)
    (total_ref, small_ref, rows_ref), refs = take(3)
    (landed, half_now, half_in, quarter, quarter_in, seq_half, seq_sent, seq_in), refs = take(8)
    (t_send, t_recv, s_send, s_recv, q_send, q_recv), scratch = take(6)
    out_ref = out_refs[NARROW]
    grid = Grid(size)
    row, col = lax.axis_index("row"), lax.axis_index("col")

    def other(name, bit):
        place = lax.axis_index(name)
        return {name: place + bit * (1 - 2 * ((place // bit) % 2))}

    barrier = pltpu.get_barrier_semaphore()
    grid.greet(barrier)
    for name, bit in steps:
        pl.semaphore_signal(barrier, inc=1, device_id=other(name, bit), device_id_type=MESH_ID)
    for by in range(1, columns):
        pl.semaphore_signal(
            barrier, inc=1, device_id={"col": (col + by) % columns}, device_id_type=MESH_ID
        )
    pl.semaphore_wait(barrier, grid.count + len(steps) + columns - 1)

    seq_rows, block = seq_half.shape[0], rows_ref.shape[0]
    swap_rows = pltpu.make_async_remote_copy(
        src_ref=seq_ref.at[pl.ds(pl.multiple_of((1 - row) * seq_rows, 16), seq_rows)],
        dst_ref=seq_half,
        send_sem=q_send.at[0],
        recv_sem=q_recv.at[0],
        device_id={"row": 1 - row},
        device_id_type=MESH_ID,
    )
    swap_rows.start()

    total_ref[...] = value_ref[...]

    def exchange(number):
        name, bit = steps[number]
        copy = pltpu.make_async_remote_copy(
            src_ref=total_ref,
            dst_ref=landed.at[number],
            send_sem=t_send.at[number],
            recv_sem=t_recv.at[number],
            device_id=other(name, bit),
            device_id_type=MESH_ID,
        )
        copy.start()
        copy.wait()
        total_ref[...] += landed[number]

    early = len([1 for name, bit in steps if name == "dp" and bit < grid.across])
    for number in range(early):
        exchange(number)
    sums = [
        LineSum(grid, part_refs[number], out_refs[number], *scratch[7 * number : 7 * number + 7])
        for number in range(count)
    ]
    LineSum.start(sums)

    def both_rows(place):
        mine = seq_ref[pl.ds(pl.multiple_of(row * seq_rows + place * block, 16), block), :]
        theirs = seq_half[pl.ds(pl.multiple_of(place * block, 16), block), :]
        return mine.astype(F32) + theirs.astype(F32)

    swap_rows.wait()
    moves = []
    for by in range(1, columns):
        to = (col + by) % columns
        seq_sent[by - 1] = both_rows(to).astype(BF16)
        moves.append(
            pltpu.make_async_remote_copy(
                src_ref=seq_sent.at[by - 1],
                dst_ref=seq_in.at[by - 1],
                send_sem=q_send.at[by],
                recv_sem=q_recv.at[by],
                device_id={"col": to},
                device_id_type=MESH_ID,
            )
        )
    for number in range(early, len(steps)):
        exchange(number)
    for copy in moves:
        copy.start()
    rows_ref[...] = both_rows(col)
    half, fourth = half_now.shape[0], small_ref.shape[0]
    swap = pltpu.make_async_remote_copy(
        src_ref=half_now,
        dst_ref=half_in,
        send_sem=s_send.at[0],
        recv_sem=s_recv.at[0],
        device_id={"row": 1 - row},
        device_id_type=MESH_ID,
    )

    def swap_narrow():
        half_now[...] = out_ref[pl.ds(pl.multiple_of((1 - row) * half, 8), half), :]
        swap.start()

    LineSum.finish([sums[NARROW]] + sums[:NARROW] + sums[NARROW + 1 :], after=swap_narrow)
    swap.wait()
    both = out_ref[pl.ds(pl.multiple_of(row * half, 8), half), :] + half_in[...]
    for place in range(columns):
        quarter[place] = both[place * fourth : (place + 1) * fourth]
    copies = []
    for by in range(1, columns):
        to = (col + by) % columns
        copies.append(
            pltpu.make_async_remote_copy(
                src_ref=quarter.at[to],
                dst_ref=quarter_in.at[by],
                send_sem=s_send.at[by],
                recv_sem=s_recv.at[by],
                device_id={"col": to},
                device_id_type=MESH_ID,
            )
        )
        copies[-1].start()
    small_ref[...] = quarter[col]
    for by, copy in enumerate(moves):
        copy.wait()
        rows_ref[...] += seq_in[by].astype(F32)
    for by, copy in enumerate(copies):
        copy.wait()
        small_ref[...] += quarter_in[by + 1]


def scatter_end(parts, values, rows, shape):
    size, columns = shape["dp"], shape["col"]
    steps = partners(shape)
    parts = [part.reshape((size, -1, part.shape[1])) for part in parts]
    (length, narrow), count = parts[NARROW].shape[1:], len(parts)
    half, seq_rows = length // 2, rows.shape[0] // 2
    block = (seq_rows // columns, rows.shape[1])
    fourth = (columns, half // columns, narrow)
    return pl.pallas_call(
        functools.partial(end_kernel, size, steps, columns, count),
        out_shape=tuple(jax.ShapeDtypeStruct(part.shape[1:], F32) for part in parts)
        + (
            jax.ShapeDtypeStruct(values.shape, F32),
            jax.ShapeDtypeStruct(fourth[1:], F32),
            jax.ShapeDtypeStruct(block, F32),
        ),
        in_specs=[VM] * (count + 2),
        out_specs=(VM,) * (count + 3),
        scratch_shapes=[
            pltpu.VMEM((len(steps),) + values.shape, F32),
            pltpu.VMEM((half, narrow), F32),
            pltpu.VMEM((half, narrow), F32),
            pltpu.VMEM(fourth, F32),
            pltpu.VMEM(fourth, F32),
            pltpu.VMEM((seq_rows, rows.shape[1]), BF16),
            pltpu.VMEM((columns - 1,) + block, BF16),
            pltpu.VMEM((columns - 1,) + block, BF16),
            pltpu.SemaphoreType.DMA((len(steps),)),
            pltpu.SemaphoreType.DMA((len(steps),)),
            pltpu.SemaphoreType.DMA((columns,)),
            pltpu.SemaphoreType.DMA((columns,)),
            pltpu.SemaphoreType.DMA((columns,)),
            pltpu.SemaphoreType.DMA((columns,)),
        ]
        + sum([LineSum.scratch(size, part.shape[1:]) for part in parts], []),
        compiler_params=pltpu.CompilerParams(
            collective_id=3, has_side_effects=True, vmem_limit_bytes=60 * 2**20
        ),
        cost_estimate=lasting(125),
        name="scatter_end",
    )(*parts, values, rows)


def steps_kernel(mixer_ref, out_ref, up_ref, down_ref, small_ref, step_ref, *refs):
    ins, outs = refs[:21], refs[21:]
    rate = MODEL_WIDTH ** (-0.5)
    weights, firsts, seconds = ins[0::3], ins[1::3], ins[2::3]

    def put(number, grad, rate, at=...):
        values = adam_step(weights[number][at], grad, firsts[number][at], seconds[number][at], rate)
        for place, value in enumerate(values):
            outs[3 * number + place][at] = value

    for head in range(weights[0].shape[0]):
        put(0, mixer_ref[:, 128 * head : 128 * (head + 1)], rate, head)
    put(1, step_ref[...].T[0 : weights[1].shape[0]], rate)
    put(2, out_ref[...].T, INNER ** (-0.5))
    put(3, small_ref[:, 0 : 2 * STATE], rate)
    routes = small_ref[:, 2 * STATE :].T
    put(4, routes[ROUTER_AT : ROUTER_AT + weights[4].shape[0]], 0.5 * rate)
    put(5, up_ref[...], rate)
    put(6, down_ref[...], FF_S ** (-0.5))


def last_steps(grads, arrays):
    whole = pl.BlockSpec()
    return pl.pallas_call(
        steps_kernel,
        out_shape=tuple(jax.ShapeDtypeStruct(array.shape, F32) for array in arrays),
        in_specs=[whole] * (6 + len(arrays)),
        out_specs=(whole,) * len(arrays),
        compiler_params=pltpu.CompilerParams(vmem_limit_bytes=56 * 2**20),
        cost_estimate=lasting(10),
        name="last_steps",
    )(*grads, *arrays)


def shared_block(x_ref, g_ref, up_ref, down_ref, hid_ref, dpre_ref, out_ref, dx_ref):
    x, g = x_ref[...], g_ref[:, :MODEL_WIDTH]
    pre = dot_f32(x, up_ref[...])
    asked = dot_t(g, down_ref[...])
    half = down_ref.shape[0]
    for part in range(half // 128):
        lanes = slice(128 * part, 128 * (part + 1))
        upper = slice(half + 128 * part, half + 128 * (part + 1))
        gate, up, want = pre[:, lanes], pre[:, upper], asked[:, lanes]
        sig = jax.nn.sigmoid(gate)
        act = gate * sig
        hid_ref[:, lanes] = (act * up).astype(BF16)
        dpre_ref[:, lanes] = (want * up * (sig * (1.0 + gate * (1.0 - sig)))).astype(BF16)
        dpre_ref[:, upper] = (want * act).astype(BF16)
    out_ref[...] = dot_f32(hid_ref[...], down_ref[...])
    dx_ref[...] = dot_t(dpre_ref[...], up_ref[...])


def shared_expert(tokens, cotangents, up, down):
    rows, width = tokens.shape
    return pl.pallas_call(
        shared_block,
        out_shape=(
            jax.ShapeDtypeStruct((rows, down.shape[0]), BF16),
            jax.ShapeDtypeStruct((rows, up.shape[1]), BF16),
            jax.ShapeDtypeStruct((rows, width), F32),
            jax.ShapeDtypeStruct((rows, width), F32),
        ),
        in_specs=[VM] * 4,
        out_specs=(VM,) * 4,
        compiler_params=pltpu.CompilerParams(vmem_limit_bytes=40 * 2**20),
        cost_estimate=lasting(16),
        name="shared_expert",
    )(tokens, cotangents, up, down)


def expert_block(own, x_ref, g_ref, up, down, router_ref, hid_ref, dpre_ref, mix_ref, dx_ref):
    x, g = x_ref[...], g_ref[:, :MODEL_WIDTH]
    logits = dot_f32(x, router_ref[...])
    named = g_ref[:, MODEL_WIDTH:].astype(F32)
    high = jnp.max(jnp.where(named > 0, logits, -1e30), axis=1, keepdims=True)
    raised = jnp.where(named > 0, jnp.exp(logits - high), 0.0)
    gates = raised / jnp.sum(raised, axis=1, keepdims=True)
    rows = x.shape[0]
    lane = lax.broadcasted_iota(jnp.int32, (rows, 128), 1)
    weights = [
        jnp.sum(jnp.where(lane == own + part, gates, 0.0), axis=1, keepdims=True)
        for part in range(EXP_DEV)
    ]
    half = down.shape[0]
    pre = dot_f32(x, up)
    asked = dot_t(g, down)
    totals = [jnp.zeros((rows, 128), F32) for part in range(EXP_DEV)]
    for part in range(half // 128):
        which = 128 * part // FF_E
        at = 128 * part + FF_E * which
        lanes = slice(128 * part, 128 * (part + 1))
        lower, upper = slice(at, at + 128), slice(at + FF_E, at + FF_E + 128)
        gate, upper_pre, want = pre[:, lower], pre[:, upper], asked[:, lanes]
        sig = jax.nn.sigmoid(gate)
        act = gate * sig
        hidden = act * upper_pre
        totals[which] = totals[which] + hidden * want
        hid_ref[:, lanes] = (weights[which] * hidden).astype(BF16)
        dact = weights[which] * want
        dpre_ref[:, lower] = (dact * upper_pre * (sig * (1.0 + gate * (1.0 - sig)))).astype(BF16)
        dpre_ref[:, upper] = (dact * act).astype(BF16)
    mix_ref[...] = dot_f32(hid_ref[...], down).astype(BF16)
    dx_ref[:, :MODEL_WIDTH] = dot_t(dpre_ref[...], up).astype(BF16)
    sent = jnp.zeros((rows, 128), F32)
    for part in range(EXP_DEV):
        gate_grad = jnp.sum(totals[part], axis=1, keepdims=True)
        coarse = gate_grad.astype(BF16).astype(F32)
        sent = jnp.where(lane == own + part, coarse, sent)
        sent = jnp.where(lane == own + part + REST_AT, gate_grad - coarse, sent)
    dx_ref[:, MODEL_WIDTH:] = sent.astype(BF16)


def expert_kernel(
    size, columns, own_ref, g_ref, router_hbm, *refs
):
    places = 2 * columns
    up_parts, down_parts, full_ref, refs = (
        refs[:places], refs[places : 2 * places], refs[2 * places], refs[2 * places + 1 :]
    )
    outs, (x_now, g_now), stages, (up_ref, down_ref, router_ref) = (
        refs[:4], refs[4:6], refs[6:10], refs[10:13]
    )
    send_sem, recv_sem, local_sem, in_sem, out_sem, weight_sem = refs[13:]
    grid = Grid(size)
    me, z, x = grid.me, grid.z, grid.x
    barrier = pltpu.get_barrier_semaphore()
    grid.greet(barrier)
    pl.semaphore_wait(barrier, grid.count)

    def push(chunk, way, source=None):
        return pltpu.make_async_remote_copy(
            src_ref=full_ref.at[chunk] if source is None else source,
            dst_ref=full_ref.at[chunk],
            send_sem=send_sem.at[way, chunk],
            recv_sem=recv_sem.at[chunk],
            device_id={"dp": me + grid.steps[way]},
            device_id_type=MESH_ID,
        )

    def place(number):
        if grid.across == 2:
            even, first, last = 1 - number % 2, 1 - jnp.minimum(number, 1), number // 7
            step = (1 - even) * ((number + 1) // 2 - last) + even * (number // 2 - 1 + first)
            side = even * (1 - first) + last
        else:
            step, side = number % grid.deep, number // grid.deep
        return block_at(step, side)

    def block_at(step, side):
        zc = near_first(z, step, grid.deep)
        xc = near_first(x, side, grid.across)
        same = xc == x
        ways = (same & (zc >= z), same & (zc <= z), xc >= x, xc <= x)
        return zc * grid.across + xc, [way & there for way, there in zip(ways, grid.exists)]

    for way in range(4):
        @pl.when(grid.exists[way])
        def _():
            push(me, way, own_ref).start()
    row, col = lax.axis_index("row"), lax.axis_index("col")
    weights = [pltpu.make_async_copy(router_hbm, router_ref, weight_sem.at[2 * places])]
    for number in range(places):
        whose = row + (number // columns) * (1 - 2 * row)
        there = whose * columns + (col - number % columns + columns) % columns
        weights.append(
            pltpu.make_async_copy(up_parts[number], up_ref.at[there], weight_sem.at[number])
        )
        weights.append(
            pltpu.make_async_copy(
                down_parts[number], down_ref.at[:, there], weight_sem.at[places + number]
            )
        )
    for copy in weights:
        copy.start()
    keep = pltpu.make_async_copy(own_ref, full_ref.at[me], local_sem)
    keep.start()

    def leave(number, chunk):
        return [
            pltpu.make_async_copy(stage.at[number % 2], out.at[chunk], out_sem.at[place_in, number % 2])
            for place_in, (stage, out) in enumerate(zip(stages, outs))
        ]

    def work(number, _):
        chunk, onward = place(number)
        bring = pltpu.make_async_copy(g_ref.at[chunk], g_now, in_sem.at[0])
        bring.start()

        def pass_on(chunk, onward):
            push(chunk, 0).wait_recv()
            for way in range(4):
                @pl.when(onward[way])
                def _():
                    push(chunk, way).start()

        if grid.across == 2:
            inner = (z * (3 - z)) // 2
            for step, when in ((1, number == 1), (2, number == 3 - 2 * inner), (3, number == 5 - 2 * inner)):
                @pl.when(when)
                def _():
                    pass_on(*block_at(step, 0))

            @pl.when((number > 0) & (chunk % grid.across != x))
            def _():
                push(chunk, 0).wait_recv()
        else:
            @pl.when(number > 0)
            def _():
                pass_on(chunk, onward)

        bring_x = pltpu.make_async_copy(full_ref.at[chunk], x_now, in_sem.at[1])

        @pl.when(number == 0)
        def _():
            pltpu.make_async_copy(own_ref, x_now, in_sem.at[1]).start()
            for copy in weights:
                copy.wait()

        @pl.when(number > 0)
        def _():
            bring_x.start()

        @pl.when(number > 1)
        def _():
            for copy in leave(number, place(number - 2)[0]):
                copy.wait()

        bring.wait()
        bring_x.wait()
        expert_block(
            EXP_DEV * me, x_now, g_now,
            up_ref[...].reshape(-1, up_ref.shape[2]), down_ref[...].reshape(-1, down_ref.shape[3]), router_ref,
            *[stage.at[number % 2] for stage in stages]
        )
        for copy in leave(number, chunk):
            copy.start()
        return 0

    lax.fori_loop(0, size, work, 0)
    for number in (size - 2, size - 1):
        for copy in leave(number, place(number)[0]):
            copy.wait()

    def finish(number, _):
        chunk, onward = place(number)
        for way in range(4):
            @pl.when(onward[way])
            def _():
                push(chunk, way).wait_send()
        return 0

    lax.fori_loop(0, size, finish, 0)
    keep.wait()


def experts(tokens, cotangents, up_parts, down_parts, router, shape):
    size, columns = shape["dp"], shape["col"]
    places = 2 * columns
    rows, width = tokens.shape
    hidden = places * down_parts[0].shape[0]
    down_parts = [part.reshape(EXP_DEV, -1, width) for part in down_parts]
    wide = width + 128
    wides = (hidden, 2 * hidden, width, wide)
    results = pl.pallas_call(
        functools.partial(expert_kernel, size, columns),
        out_shape=tuple(
            jax.ShapeDtypeStruct((size, rows, column), BF16) for column in (width,) + wides
        ),
        in_specs=[ANY] * (3 + 2 * places),
        out_specs=(ANY,) * 5,
        scratch_shapes=[pltpu.VMEM((rows, width), BF16), pltpu.VMEM((rows, wide), BF16)]
        + [pltpu.VMEM((2, rows, column), BF16) for column in wides]
        + [
            pltpu.VMEM((places,) + up_parts[0].shape, BF16),
            pltpu.VMEM((EXP_DEV, places) + down_parts[0].shape[1:], BF16),
            pltpu.VMEM(router.shape, BF16),
            pltpu.SemaphoreType.DMA((4, size)),
            pltpu.SemaphoreType.DMA((size,)),
            pltpu.SemaphoreType.DMA,
            pltpu.SemaphoreType.DMA((2,)),
            pltpu.SemaphoreType.DMA((4, 2)),
            pltpu.SemaphoreType.DMA((2 * places + 1,)),
        ],
        compiler_params=pltpu.CompilerParams(
            collective_id=4, has_side_effects=True, vmem_limit_bytes=56 * 2**20
        ),
        cost_estimate=lasting(85),
        name="experts",
    )(tokens, cotangents.reshape(size, rows, wide), router, *up_parts, *down_parts)
    return [result.reshape(size * rows, -1) for result in results]


def rms_scale(values):
    return lax.rsqrt(jnp.mean(values * values, axis=-1, keepdims=True) + 1e-05)


def rms_back(values, scale, gain, grad_normed):
    weighted = grad_normed * gain[None, :]
    grad_values = scale * weighted - values * scale**3 * jnp.mean(
        weighted * values, axis=-1, keepdims=True
    )
    gain_grad = jnp.sum(grad_normed * values * scale, axis=0)
    return (grad_values, gain_grad)


def silu_gate(pre_values):
    half_size = pre_values.shape[-1] // 2
    return jax.nn.silu(pre_values[..., :half_size]) * pre_values[..., half_size:]


def silu_gate_back(pre_values, grad):
    return jax.vjp(silu_gate, pre_values)[1](grad)[0]


ALL = ("dp", "row", "col")


def gather_dp(values):
    return lax.all_gather(values, "dp", axis=0, tiled=True)


def scatter_dp(values):
    return lax.psum_scatter(values, "dp", scatter_dimension=0, tiled=True)


def body(
    shape,
    hidden_in, segment_ids, routes, out_grad,
    vectors, vectors_first, vectors_second,
    in_weight, in_weight_first, in_weight_second,
    step_weight, step_weight_first, step_weight_second,
    out_weight, out_weight_first, out_weight_second,
    state_weight, state_weight_first, state_weight_second,
    router, router_first, router_second,
    shared_up, shared_up_first, shared_up_second,
    shared_down, shared_down_first, shared_down_second,
    expert_gate_up, expert_gate_up_first, expert_gate_up_second,
    expert_down, expert_down_first, expert_down_second,
):
    dp = lax.axis_index("dp")
    data_count = lax.axis_size("dp")
    seq_devices = lax.axis_size("row") * lax.axis_size("col")
    local_heads = in_weight.shape[1]
    width = 64 * local_heads
    head_start = lax.axis_index(("row", "col")) * local_heads
    own_tokens = hidden_in.shape[1]
    experts_all = router.shape[1]
    rows_dp = in_weight.shape[0]
    seq_columns = shape["col"]
    residual = hidden_in[0].astype(F32)
    count = vectors.shape[0]
    lines = -(-count // 1024) * 8
    vector_rows = jnp.pad(vectors, (0, lines * 128 - count)).reshape(lines, 128)
    gain_one = vectors[0:MODEL_WIDTH]
    gain_two = vectors[MODEL_WIDTH : 2 * MODEL_WIDTH]

    scale_one = rms_scale(residual)
    up_local = jnp.concatenate(
        [expert_gate_up[held].astype(BF16) for held in range(EXP_DEV)], axis=1
    )
    route_ids = routes[0]
    chosen = (
        route_ids[:, :, None] == jnp.arange(experts_all, dtype=jnp.int32)[None, None, :]
    ).any(axis=1)
    grad_low = out_grad[0]
    grad_ext = jnp.concatenate(
        [grad_low, jnp.pad(chosen.astype(BF16), ((0, 0), (0, 128 - experts_all)))], axis=1
    )
    down_local = expert_down.astype(BF16).reshape(-1, MODEL_WIDTH)
    mixer_full, step_full, out_full, shared_up_full, shared_down_full, small_full, normed_all = gather_start(
        hidden_in[0],
        vector_rows,
        in_weight.transpose(1, 0, 2),
        jnp.pad(step_weight.T, ((0, 128 - local_heads), (0, 0))),
        out_weight.reshape(width, -1),
        shared_up,
        shared_down,
        state_weight,
        jnp.pad(router.T, ((0, 128 - experts_all), (0, 0))),
        shape,
    )
    mixer_full, step_full, out_full, small_full, normed_all, segment_ids, grad_ext, up_local, down_local = (
        lax.optimization_barrier(
            (mixer_full, step_full, out_full, small_full, normed_all, segment_ids, grad_ext, up_local, down_local)
        )
    )
    grad_all = gather_dp(grad_ext)
    by_columns = lambda array: [array] + [
        shift(array, "col", by) for by in range(1, lax.axis_size("col"))
    ]
    up_parts, down_parts = by_columns(up_local), by_columns(down_local)
    state_step = jnp.concatenate([small_full[:, : 2 * STATE], step_full], axis=1)

    seg_rows = segment_ids[0].astype(F32).reshape(-1, 1, BLK)
    proj = dot_f32(normed_all, mixer_full).astype(BF16)
    ss = dot_f32(normed_all, state_step)
    valued, squares_part, kept, params = mixer_forward(proj, ss, seg_rows, vector_rows, seq_columns)
    partial_out = dot_t(valued, out_full).astype(BF16)
    partial_out, up_parts, down_parts = lax.optimization_barrier((partial_out, up_parts, down_parts))
    proj_out = scatter_rc(partial_out)
    other_row = lambda parts: parts + [shift(part, "row", 1) for part in parts]
    up_parts, down_parts = other_row(up_parts), other_row(down_parts)
    squares = scatter_squares(squares_part)[:, 0]
    scale_two = lax.rsqrt(squares / INNER + 1e-05)
    residual_two = residual + scale_two[:, None] * proj_out
    scale_three = rms_scale(residual_two)
    normed_two = (residual_two * scale_three * gain_two[None, :]).astype(BF16)

    router_wide = small_full[:, 2 * STATE :]
    router_full = router_wide[:, :experts_all]
    shared_act, shared_pre_grad, shared_out, shared_dx = shared_expert(
        normed_two, grad_low, shared_up_full, shared_down_full
    )
    shared_up_grad = dot_tn(normed_two, shared_pre_grad).astype(BF16)
    shared_down_grad = dot_tn(shared_act, grad_low).astype(BF16)
    shared_up_kept = scatter_row(shared_up_grad, data_count)
    shared_down_kept = scatter_row(shared_down_grad, data_count)
    normed_two, grad_all, shared_up_kept, shared_down_kept, shared_dx, shared_out = (
        lax.optimization_barrier(
            (normed_two, grad_all, shared_up_kept, shared_down_kept, shared_dx, shared_out)
        )
    )
    shared_up_part = scatter_col(shared_up_kept).astype(BF16)
    shared_down_part = scatter_col(shared_down_kept).astype(BF16)
    tokens_all, hidden_low, pre_grad, mixed, rows_grad = experts(
        normed_two, grad_all, up_parts, down_parts, router_wide, shape
    )
    logits = dot_f32(normed_two, router_full)
    gate_all = jax.nn.softmax(jnp.where(chosen, logits, -jnp.inf), axis=-1)
    rows_grad, shared_up_part, shared_down_part = lax.optimization_barrier(
        (rows_grad, shared_up_part, shared_down_part)
    )
    routed_grad, up_grad, down_grad = scatter_blocks(
        rows_grad, tokens_all, pre_grad, hidden_low, grad_all, shape
    )
    routed_grad, mixed = lax.optimization_barrier((routed_grad, mixed))
    mixture = scatter_dp(mixed).astype(F32)
    gate_grad = (
        routed_grad[:, MODEL_WIDTH : MODEL_WIDTH + experts_all]
        + routed_grad[:, MODEL_WIDTH + REST_AT : MODEL_WIDTH + REST_AT + experts_all]
    )
    cotangent = grad_low.astype(F32)
    normed_two_grad = shared_dx + routed_grad[:, :MODEL_WIDTH]
    logits_grad = gate_all * (gate_grad - jnp.sum(gate_all * gate_grad, axis=1, keepdims=True))
    logits_low = jnp.where(chosen, logits_grad, 0.0).astype(BF16)
    normed_two_grad = normed_two_grad + dot_t(logits_low, router_full)
    router_grad = dot_tn(normed_two, logits_low)
    residual_two_grad, gain_two_grad = rms_back(
        residual_two, scale_three, gain_two, normed_two_grad
    )
    residual_two_grad = residual_two_grad + cotangent
    proj_out_grad = (residual_two_grad * scale_two[:, None]).astype(BF16)
    squares_grad = (
        jnp.sum(residual_two_grad * proj_out, axis=1) * -0.5 * scale_two**3 / INNER
    )
    squares_high = squares_grad.astype(BF16)
    squares_rest = (squares_grad - squares_high.astype(F32)).astype(BF16)
    riding = jnp.pad(jnp.stack([squares_high, squares_rest], axis=1), ((0, 0), (0, 126)))
    riders = jnp.concatenate([proj_out_grad, riding], axis=1)
    riders, up_grad, down_grad = lax.optimization_barrier((riders, up_grad, down_grad))
    riders = gather_rc(riders)
    proj_grad_all = riders[:, :MODEL_WIDTH]
    squares_grad_all = jnp.sum(riders[:, MODEL_WIDTH:].astype(F32), axis=1, keepdims=True)
    proj_grad_all, up_grad, down_grad = lax.optimization_barrier((proj_grad_all, up_grad, down_grad))
    up_total = scatter_col(up_grad[None])
    down_total = scatter_col(down_grad.reshape(EXP_DEV, -1, MODEL_WIDTH))
    up_total = jnp.stack(
        [up_total[:, 2 * FF_E * held : 2 * FF_E * (held + 1)] for held in range(EXP_DEV)]
    )
    new_up = adam_step(
        expert_gate_up, up_total, expert_gate_up_first, expert_gate_up_second, MODEL_WIDTH ** (-0.5)
    )
    new_down = adam_step(
        expert_down, down_total.reshape(expert_down.shape), expert_down_first, expert_down_second, FF_E ** (-0.5)
    )

    valued_grad = dot_f32(proj_grad_all, out_full).astype(BF16)
    out_grad_t = dot_tn(proj_grad_all, valued).astype(BF16)
    proj_grad, ss_grad, vector_grad = mixer_backward(
        proj, ss, seg_rows, params, valued_grad, squares_grad_all, kept, lines, seq_columns
    )
    normed_part = dot_t(proj_grad, mixer_full) + dot_t(ss_grad, state_step)
    gain_one_grad = jnp.sum(normed_part * normed_all.astype(F32), axis=0) / gain_one
    router_wide = jnp.pad(
        router_grad, ((0, 0), (2 * STATE + ROUTER_AT, 128 - ROUTER_AT - experts_all))
    )
    mixer_grad = dot_tn(normed_all, proj_grad).astype(BF16)
    small_grad = (dot_tn(normed_all, ss_grad) + router_wide).astype(BF16)
    gains = jnp.concatenate([gain_one_grad, gain_two_grad]).reshape(-1, 128)
    vector_lines = vector_grad + jnp.pad(gains, ((0, lines - gains.shape[0]), (0, 0)))
    mixture, mixer_grad, new_up, new_down = lax.optimization_barrier(
        (mixture, mixer_grad, new_up, new_down)
    )
    hidden_out = (residual_two + mixture + shared_out).astype(BF16)[None]
    (
        mixer_total, small_rows, out_total, shared_up_total, shared_down_total,
        vector_total, small_total, normed_grad,
    ) = scatter_end(
        (mixer_grad, small_grad, out_grad_t, shared_up_part, shared_down_part),
        vector_lines,
        normed_part.astype(BF16),
        shape,
    )
    vector_total = vector_total.reshape(-1)[:count]
    heads_first = lambda array: array.transpose(1, 0, 2)
    flat_out = lambda array: array.reshape(width, -1)
    news = last_steps(
        (
            mixer_total, out_total, shared_up_total, shared_down_total, small_total,
            small_rows[:, 2 * STATE :],
        ),
        (
            *map(heads_first, (in_weight, in_weight_first, in_weight_second)),
            step_weight.T, step_weight_first.T, step_weight_second.T,
            *map(flat_out, (out_weight, out_weight_first, out_weight_second)),
            state_weight, state_weight_first, state_weight_second,
            router.T, router_first.T, router_second.T,
            shared_up, shared_up_first, shared_up_second,
            shared_down, shared_down_first, shared_down_second,
        ),
    )
    residual_grad, _ = rms_back(residual, scale_one, gain_one, normed_grad)
    input_grad = (residual_grad + residual_two_grad)[None]
    return (
        hidden_out,
        input_grad,
        *adam_step(vectors, vector_total, vectors_first, vectors_second, 0.3, 0.0),
        *map(heads_first, news[0:3]),
        *[array.T for array in news[3:6]],
        *[array.reshape(out_weight.shape) for array in news[6:9]],
        *news[9:12],
        *[array.T for array in news[12:15]],
        *news[15:],
        *new_up,
        *new_down,
    )


def solution(mesh):
    tokens = P("dp", ("row", "col"), None)
    by_head = P("dp", ("row", "col"))
    out_spec = P(("row", "col"), None, "dp")
    flat = P(ALL, None)
    weights = (
        (P(),) * 3
        + (tokens,) * 3
        + (by_head,) * 3
        + (out_spec,) * 3
        + (flat,) * 12
        + (tokens,) * 6
    )
    return jax.shard_map(
        functools.partial(body, dict(mesh.shape)),
        mesh=mesh,
        in_specs=(tokens, P("dp", None), tokens, tokens) + weights,
        out_specs=(tokens, tokens) + weights,
        check_vma=False,
    )
```

```python
import functools

import jax
import jax.numpy as jnp
from jax import lax
from jax.experimental import pallas as pl
from jax.experimental.pallas import tpu as pltpu
from jax.sharding import PartitionSpec as P

STATE = 128
KW = 4
BLK = 128
F32 = jnp.float32
BF16 = jnp.bfloat16


def dot_f32(a, b, dims=(((1,), (0,)), ((), ()))):
    return lax.dot_general(a, b, dims, preferred_element_type=F32)


def dot_exact(a, b, dims=(((1,), (0,)), ((), ()))):
    return lax.dot_general(
        a, b, dims, precision=lax.Precision.HIGHEST, preferred_element_type=F32
    )


def spread(values, width):
    rows = values.shape[0]
    low = lax.broadcasted_iota(jnp.int32, (rows, 128), 1) < 64
    parts = []
    for pair in range(width // 128):
        left = jnp.broadcast_to(values[:, 2 * pair : 2 * pair + 1], (rows, 128))
        right = jnp.broadcast_to(values[:, 2 * pair + 1 : 2 * pair + 2], (rows, 128))
        parts.append(jnp.where(low, left, right))
    return jnp.concatenate(parts, axis=1)


def head_sums(values):
    width = values.shape[1]
    ones = (
        lax.broadcasted_iota(jnp.int32, (width, 128), 0) // 64
        == lax.broadcasted_iota(jnp.int32, (width, 128), 1)
    ).astype(BF16)
    high = values.astype(BF16)
    rest = (values - high.astype(F32)).astype(BF16)
    return dot_f32(high, ones) + dot_f32(rest, ones)


def apart(values):
    low = lax.broadcasted_iota(jnp.int32, (values.shape[0], 128), 1) < 64
    gates, inputs = [], []
    for at in range(0, values.shape[1], 256):
        one, two = values[:, at : at + 128], values[:, at + 128 : at + 256]
        gates.append(jnp.where(low, one, pltpu.roll(two, 64, 1)))
        inputs.append(jnp.where(low, pltpu.roll(one, 64, 1), two))
    return jnp.concatenate(gates, axis=1), jnp.concatenate(inputs, axis=1)


def together(gates, inputs):
    low = lax.broadcasted_iota(jnp.int32, (gates.shape[0], 128), 1) < 64
    parts = []
    for at in range(0, gates.shape[1], 128):
        one, two = gates[:, at : at + 128], inputs[:, at : at + 128]
        parts.append(jnp.where(low, one, pltpu.roll(two, 64, 1)))
        parts.append(jnp.where(low, pltpu.roll(one, 64, 1), two))
    return jnp.concatenate(parts, axis=1)


def block_masks(index, seg_ref):
    now = seg_ref[index]
    before = jnp.where(index > 0, seg_ref[jnp.maximum(index - 1, 0)], -1.0)
    lane = lax.broadcasted_iota(jnp.int32, (1, BLK), 1)
    rows = [now]
    for back in range(1, KW):
        earlier = jnp.where(lane < back, pltpu.roll(before, back, 1), pltpu.roll(now, back, 1))
        rows.append((earlier == now).astype(F32))
    last, prior = now[:, BLK - 1 :], before[:, BLK - 1 :]
    rows.append((now == prior).astype(F32))
    rows.append((now == last).astype(F32))
    rows.append(jnp.broadcast_to((prior == last).astype(F32), (1, BLK)))
    rows.append(jnp.zeros((BLK - len(rows), BLK), F32))
    return jnp.concatenate(rows, axis=0).T


def block_common(width, start, index, proj_ref, ss_ref, seg_ref, par_ref):
    rows = pl.ds(start, BLK)
    before = pl.ds(pl.multiple_of(jnp.maximum(start - 8, 0), 8), 8)
    aux = block_masks(index, seg_ref)
    gate, inner = apart(proj_ref[rows, :].astype(F32))
    current = jnp.concatenate([inner, ss_ref[rows, 0 : 2 * STATE]], axis=1)
    earlier = proj_ref[pl.ds(pl.multiple_of(jnp.maximum(start - 16, 0), 16), 16), :]
    previous = jnp.concatenate(
        [apart(earlier.astype(F32)[8:])[1], ss_ref[before, 0 : 2 * STATE]], axis=1
    )
    extended = jnp.concatenate([previous, current], axis=0)
    taps = par_ref[0:KW, :]
    conv = par_ref[KW : KW + 1, :] + taps[KW - 1 : KW, :] * current
    shifted = []
    for back in range(1, KW):
        moved = pltpu.roll(extended, back, 0)[8:] * aux[:, back : back + 1]
        shifted.append(moved)
        conv = conv + taps[KW - 1 - back : KW - back, :] * moved
    sig = jax.nn.sigmoid(conv)
    active = conv * sig
    inputs_x = active[:, :width]
    matrix_b = active[:, width : width + STATE].astype(BF16)
    matrix_c = active[:, width + STATE :].astype(BF16)
    step_in = ss_ref[rows, 2 * STATE :] + par_ref[7:8, 0:128]
    dt = jnp.maximum(step_in, 0.0) + jnp.log1p(jnp.exp(-jnp.abs(step_in)))
    decay = dt * par_ref[6:7, 0:128]
    row_id = lax.broadcasted_iota(jnp.int32, (BLK, BLK), 0)
    col_id = lax.broadcasted_iota(jnp.int32, (BLK, BLK), 1)
    lower = (row_id >= col_id).astype(F32)
    cum = dot_exact(lower, decay)
    cum_t = cum.T
    same = (aux[:, 0:1] == seg_ref[pl.ds(index, 1), 0, :]) & (row_id >= col_id)
    last = cum[BLK - 1 : BLK, :]
    gain_in = jnp.exp(cum) * aux[:, 4:5]
    tail = jnp.exp(last - cum) * aux[:, 5:6]
    carry = jnp.exp(last) * aux[BLK - 1 : BLK, 6:7]
    scores = jnp.where(same, dot_f32(matrix_c, matrix_b, (((1,), (1,)), ((), ()))), 0.0)
    dt_wide = spread(dt, width)
    moved_x = inputs_x * dt_wide
    return dict(
        rows=rows, aux=aux, gate=gate, current=current, shifted=shifted, conv=conv, sig=sig,
        x=inputs_x, b=matrix_b, c=matrix_c, step_in=step_in, dt=dt, cum=cum, cum_t=cum_t,
        same=same, scores=scores, dt_wide=dt_wide, u=moved_x, lower=lower,
        gain_in=spread(gain_in, width), tail=spread(tail, width),
        carry=spread(jnp.broadcast_to(carry, (8, 128)), width)[0:1],
    )


def split_pair(values):
    low = lax.broadcasted_iota(jnp.int32, values.shape, 1) < 64
    zero = jnp.zeros_like(values)
    return jnp.where(low, values, zero), jnp.where(low, zero, values)


GAIN_AT, BIAS_AT, TAPS_AT, HEADS_AT = 24, 48, 74, 178
INNER_LINES, TAP_LINES = 24, 26


def own_place(columns):
    return lax.axis_index("row") * columns + lax.axis_index("col")


def read_params(width, columns, vec_ref, par_ref):
    lines, heads = width // 128, width // 64
    place = own_place(columns)

    def line(at):
        return jnp.concatenate(
            [vec_ref[pl.ds(at + place * lines + one, 1), :] for one in range(lines)], axis=1
        )

    def wide_line(at):
        rest = at + INNER_LINES
        return jnp.concatenate(
            [line(at), vec_ref[rest : rest + 1, :], vec_ref[rest + 1 : rest + 2, :]], axis=1
        )

    par_ref[...] = jnp.zeros_like(par_ref)
    for tap in range(KW):
        par_ref[tap : tap + 1, :] = wide_line(TAPS_AT + TAP_LINES * tap)
    par_ref[KW : KW + 1, :] = wide_line(BIAS_AT)
    par_ref[5:6, 0:width] = line(GAIN_AT)
    flat = jnp.concatenate([vec_ref[HEADS_AT : HEADS_AT + 1, :], vec_ref[HEADS_AT + 1 : HEADS_AT + 2, :]], axis=1)
    flat = jnp.broadcast_to(flat, (8, 256))
    lane = lax.broadcasted_iota(jnp.int32, (8, 128), 1)

    def per_head(which):
        turned = pltpu.roll(flat, 256 - 48 * which - place * heads, 1)[:, 0:128]
        return jnp.where(lane < heads, turned, 0.0)

    par_ref[6:7, 0:128] = jnp.where(lane < heads, -jnp.exp(per_head(0)), 0.0)[0:1]
    par_ref[7:8, 0:128] = per_head(2)[0:1]
    par_ref[8:9, 0:width] = spread(per_head(1), width)[0:1]


def write_params(width, columns, sums, par_ref, vec_ref):
    lines, heads = width // 128, width // 64
    place = own_place(columns)
    vec_ref[...] = jnp.zeros_like(vec_ref)
    total = lambda at: jnp.sum(sums[at : at + 8, :], axis=0, keepdims=True)

    def line(at, row):
        for one in range(lines):
            vec_ref[pl.ds(at + place * lines + one, 1), :] = row[:, 128 * one : 128 * (one + 1)]

    def wide_line(at, row):
        line(at, row)
        rest = at + INNER_LINES
        vec_ref[rest : rest + 1, :] = row[:, width : width + 128]
        vec_ref[rest + 1 : rest + 2, :] = row[:, width + 128 :]

    for tap in range(KW):
        wide_line(TAPS_AT + TAP_LINES * tap, total(8 * tap))
    wide_line(BIAS_AT, total(32))
    line(GAIN_AT, total(48))
    skips = jnp.sum(head_sums(sums[64:72, 0:width]), axis=0, keepdims=True)
    decays = total(56)[:, 0:128] * par_ref[6:7, 0:128]
    flat = jnp.zeros((8, 256), F32)
    lane = lax.broadcasted_iota(jnp.int32, (8, 256), 1)
    for which, row in enumerate((decays, skips, total(72)[:, 0:128])):
        row = jnp.broadcast_to(jnp.concatenate([row, jnp.zeros((1, 128), F32)], axis=1), (8, 256))
        flat = flat + pltpu.roll(jnp.where(lane < heads, row, 0.0), 48 * which + place * heads, 1)
    vec_ref[HEADS_AT : HEADS_AT + 1, :] = flat[0:1, 0:128]
    vec_ref[HEADS_AT + 1 : HEADS_AT + 2, :] = flat[0:1, 128:]


def forward_kernel(
    width, columns, proj_ref, ss_ref, seg_ref, vec_ref, valued_ref, squares_ref, kept_ref, par_ref, state
):
    blocks = proj_ref.shape[0] // BLK
    state[...] = jnp.zeros_like(state)
    read_params(width, columns, vec_ref, par_ref)

    def step(index, _):
        start = pl.multiple_of(index * BLK, BLK)
        got = block_common(width, start, index, proj_ref, ss_ref, seg_ref, par_ref)
        kept_ref[index] = state[...]
        moved = got["u"].astype(BF16)
        parts = []
        for pair in range(width // 128):
            u0, u1 = split_pair(moved[:, 128 * pair : 128 * (pair + 1)])
            mixes = []
            for head in (2 * pair, 2 * pair + 1):
                differ = jnp.minimum(got["cum"][:, head : head + 1] - got["cum_t"][head : head + 1, :], 0.0)
                mixes.append((jnp.exp(differ) * got["scores"]).astype(BF16))
            parts.append(dot_f32(jnp.concatenate(mixes, axis=1), jnp.concatenate([u0, u1], axis=0)))
        within = jnp.concatenate(parts, axis=1)
        from_state = got["gain_in"] * dot_f32(got["c"], state[...].astype(BF16))
        scanned = within + from_state + par_ref[8:9, 0:width] * got["x"]
        state[...] = state[...] * got["carry"] + dot_f32(
            got["b"], (got["tail"] * got["u"]).astype(BF16), (((0,), (0,)), ((), ()))
        )
        gate = got["gate"]
        gated = scanned * (gate * jax.nn.sigmoid(gate))
        squares_ref[got["rows"], :] = jnp.sum(gated * gated, axis=1, keepdims=True)
        valued_ref[got["rows"], :] = (gated * par_ref[5:6, 0:width]).astype(BF16)
        return 0

    lax.fori_loop(0, blocks, step, 0)


def backward_kernel(
    width, columns, proj_ref, ss_ref, seg_ref, par_ref, vgrad_ref, dsq_ref, kept_ref,
    dproj_ref, dss_ref, dvec_ref, dstate, follow, ebuf, sums
):
    blocks = proj_ref.shape[0] // BLK
    dstate[...] = jnp.zeros_like(dstate)
    follow[...] = jnp.zeros_like(follow)
    sums[...] = jnp.zeros_like(sums)

    def fold(values):
        total = values[0:8]
        for part in range(1, BLK // 8):
            total = total + values[8 * part : 8 * part + 8]
        return total

    def step(count, _):
        index = blocks - 1 - count
        start = pl.multiple_of(index * BLK, BLK)
        got = block_common(width, start, index, proj_ref, ss_ref, seg_ref, par_ref)
        rows, aux = got["rows"], got["aux"]
        state_in = kept_ref[index]
        state_low = state_in.astype(BF16)
        moved = got["u"].astype(BF16)
        skip = par_ref[8:9, 0:width]
        gain = par_ref[5:6, 0:width]
        parts = []
        for pair in range(width // 128):
            u0, u1 = split_pair(moved[:, 128 * pair : 128 * (pair + 1)])
            mixes = []
            for head in (2 * pair, 2 * pair + 1):
                differ = jnp.minimum(got["cum"][:, head : head + 1] - got["cum_t"][head : head + 1, :], 0.0)
                level = jnp.exp(differ)
                ebuf[head] = level
                mixes.append((level * got["scores"]).astype(BF16))
            parts.append(dot_f32(jnp.concatenate(mixes, axis=1), jnp.concatenate([u0, u1], axis=0)))
        inner = jnp.concatenate(parts, axis=1) + got["gain_in"] * dot_f32(got["c"], state_low)
        scanned = inner + skip * got["x"]
        gate = got["gate"]
        gate_sig = jax.nn.sigmoid(gate)
        gate_act = gate * gate_sig
        gated = scanned * gate_act
        vgrad = vgrad_ref[rows, :].astype(F32)
        dgated = vgrad * gain + 2.0 * gated * dsq_ref[rows, :]
        sums[48:56, 0:width] += fold(vgrad * gated)
        dy = dgated * gate_act
        dgate = dgated * scanned * (gate_sig * (1.0 + gate * (1.0 - gate_sig)))
        dy_low = dy.astype(BF16)
        dscores = jnp.zeros((BLK, BLK), F32)
        parts = []
        for pair in range(width // 128):
            lanes = slice(128 * pair, 128 * (pair + 1))
            u0, u1 = split_pair(moved[:, lanes])
            d0, d1 = split_pair(dy_low[:, lanes])
            mixes = []
            for head, u_own in ((2 * pair, u0), (2 * pair + 1, u1)):
                level = ebuf[head]
                mixes.append((level * got["scores"]).astype(BF16))
                dscores = dscores + level * dot_f32(
                    dy_low[:, lanes], u_own, (((1,), (1,)), ((), ()))
                )
            parts.append(
                dot_f32(
                    jnp.concatenate(mixes, axis=0),
                    jnp.concatenate([d0, d1], axis=0),
                    (((0,), (0,)), ((), ())),
                )
            )
        du_within = jnp.concatenate(parts, axis=1)
        dscores = jnp.where(got["same"], dscores, 0.0).astype(BF16)
        dstate_now = dstate[...]
        dstate_low = dstate_now.astype(BF16)
        dy_in = (got["gain_in"] * dy).astype(BF16)
        u_tail = got["tail"] * got["u"]
        from_next = dot_f32(got["b"], dstate_low)
        du = du_within + got["tail"] * from_next
        dmat_c = dot_f32(dscores, got["b"]) + dot_f32(dy_in, state_low, (((1,), (1,)), ((), ())))
        dmat_b = dot_f32(dscores, got["c"], (((0,), (0,)), ((), ()))) + dot_f32(
            u_tail.astype(BF16), dstate_low, (((1,), (1,)), ((), ()))
        )
        tail_part = head_sums(u_tail * from_next)
        dcum = (
            head_sums(dy_low.astype(F32) * inner - moved.astype(F32) * du_within) - tail_part
        )
        kept_part = head_sums(fold(got["carry"] * dstate_now * state_in))
        at_last = jnp.sum(tail_part, axis=0, keepdims=True) + jnp.sum(kept_part, axis=0, keepdims=True)
        ddecay = dot_exact(got["lower"], dcum, (((0,), (0,)), ((), ()))) + at_last
        ddt = ddecay * par_ref[6:7, 0:128] + head_sums(du * got["x"])
        sums[56:64, 0:128] += fold(ddecay * got["dt"])
        sums[64:72, 0:width] += fold(dy * got["x"])
        dstep = ddt * jax.nn.sigmoid(got["step_in"])
        sums[72:80, 0:128] += fold(dstep)
        dstate[...] = dstate_now * got["carry"] + dot_f32(got["c"], dy_in, (((0,), (0,)), ((), ())))
        dactive = jnp.concatenate([skip * dy + du * got["dt_wide"], dmat_b, dmat_c], axis=1)
        sig, conv = got["sig"], got["conv"]
        dconv = dactive * (sig * (1.0 + conv * (1.0 - sig)))
        sums[32:40, :] += fold(dconv)
        sums[24:32, :] += fold(dconv * got["current"])
        dinput = par_ref[KW - 1 : KW, :] * dconv
        for back in range(1, KW):
            tap = KW - 1 - back
            sums[8 * tap : 8 * tap + 8, :] += fold(dconv * got["shifted"][back - 1])
            masked = dconv * aux[:, back : back + 1]
            ext = jnp.concatenate([masked, follow[back - 1]], axis=0)
            dinput = dinput + par_ref[tap : tap + 1, :] * pltpu.roll(ext, BLK + 8 - back, 0)[:BLK]
            follow[back - 1] = masked[0:8]
        dproj_ref[rows, :] = together(dgate, dinput[:, :width]).astype(BF16)
        dss_ref[rows, 0 : 2 * STATE] = dinput[:, width:].astype(BF16)
        dss_ref[rows, 2 * STATE :] = dstep.astype(BF16)
        return 0

    lax.fori_loop(0, blocks, step, 0)
    write_params(width, columns, sums, par_ref, dvec_ref)


VM = pl.BlockSpec(memory_space=pltpu.VMEM)


def lasting(micros):
    return pl.CostEstimate(flops=0, bytes_accessed=int(micros * 3.0e6), transcendentals=0)


def mixer_forward(proj, ss, seg, vec, columns):
    length, double = proj.shape
    width = double // 2
    blocks = length // BLK
    return pl.pallas_call(
        functools.partial(forward_kernel, width, columns),
        out_shape=(
            jax.ShapeDtypeStruct((length, width), BF16),
            jax.ShapeDtypeStruct((length, 1), F32),
            jax.ShapeDtypeStruct((blocks, STATE, width), F32),
            jax.ShapeDtypeStruct((16, width + 2 * STATE), F32),
        ),
        in_specs=[VM] * 4,
        out_specs=(VM,) * 4,
        scratch_shapes=[pltpu.VMEM((STATE, width), F32)],
        compiler_params=pltpu.CompilerParams(vmem_limit_bytes=56 * 2**20),
        cost_estimate=lasting(20),
        name="mixer_forward",
    )(proj, ss, seg, vec)


def mixer_backward(proj, ss, seg, par, vgrad, dsq, kept, lines, columns):
    length, double = proj.shape
    width = double // 2
    wide = width + 2 * STATE
    return pl.pallas_call(
        functools.partial(backward_kernel, width, columns),
        out_shape=(
            jax.ShapeDtypeStruct((length, 2 * width), BF16),
            jax.ShapeDtypeStruct((length, 3 * STATE), BF16),
            jax.ShapeDtypeStruct((lines, 128), F32),
        ),
        in_specs=[VM] * 7,
        out_specs=(VM,) * 3,
        scratch_shapes=[
            pltpu.VMEM((STATE, width), F32),
            pltpu.VMEM((KW - 1, 8, wide), F32),
            pltpu.VMEM((width // 64, BLK, BLK), F32),
            pltpu.VMEM((80, wide), F32),
        ],
        compiler_params=pltpu.CompilerParams(vmem_limit_bytes=56 * 2**20),
        cost_estimate=lasting(34),
        name="mixer_backward",
    )(proj, ss, seg, par, vgrad, dsq, kept)


MODEL_WIDTH = 1536
HEADS = 48
FF_E = 512
FF_S = 1024
TOPK = 6
STEP = 10
EXP_DEV = 2
INNER = 3072
ROUTER_AT = 64
REST_AT = 64


def dot_t(a, b):
    return dot_f32(a, b, (((1,), (1,)), ((), ())))


def dot_tn(a, b):
    return dot_f32(a, b, (((0,), (0,)), ((), ())))


def shift(values, axis, by):
    size = lax.axis_size(axis)
    return lax.ppermute(values, axis, [(i, (i + by) % size) for i in range(size)])


def all_places(own):
    rows, columns = lax.axis_index("row"), lax.axis_size("col")
    col = lax.axis_index("col")
    placed = []
    for by, part in enumerate(own):
        there = (col - by) % columns
        placed.append((rows * columns + there, part))
        placed.append(((1 - rows) * columns + there, shift(part, "row", 1)))
    return placed


def assemble(placed, group):
    count = len(placed)
    rows, columns = placed[0][1].shape
    total = jnp.zeros((group, count, rows // group, columns), placed[0][1].dtype)
    for place, part in placed:
        total = lax.dynamic_update_slice(
            total, part.reshape(group, 1, rows // group, columns), (0, place, 0, 0)
        )
    return total.reshape(count * rows, columns)


def gather_rc(values):
    columns = lax.axis_size("col")
    return assemble(
        all_places([values] + [shift(values, "col", by) for by in range(1, columns)]), 1
    )


def block_of(array, at, rows):
    return lax.dynamic_slice_in_dim(array, at * rows, rows)


def scatter_row(values, group=1):
    row = lax.axis_index("row")
    halves = values.reshape(group, 2, -1, values.shape[1])
    pick = lambda which: lax.dynamic_index_in_dim(halves, which, 1, keepdims=False)
    away = shift(pick(1 - row), "row", 1)
    return (pick(row).astype(F32) + away.astype(F32)).astype(values.dtype)


def scatter_col(kept):
    columns, col = lax.axis_size("col"), lax.axis_index("col")
    parts = kept.reshape(kept.shape[0], columns, -1, kept.shape[2])
    pick = lambda which: lax.dynamic_index_in_dim(parts, which, 1, keepdims=False)
    total = pick(col).astype(F32)
    for by in range(1, columns):
        total = total + shift(pick((col + by) % columns), "col", by).astype(F32)
    return total.reshape(-1, kept.shape[2])


def parts_of_columns(kept):
    columns, col = lax.axis_size("col"), lax.axis_index("col")
    parts = kept.reshape(kept.shape[0], columns, -1, kept.shape[2])
    pick = lambda which: lax.dynamic_index_in_dim(parts, which, 1, keepdims=False)
    return [pick((col + by) % columns).reshape(-1, kept.shape[2]) for by in range(columns)]


def scatter_rc(values):
    return scatter_col(scatter_row(values))


def scatter_squares(values):
    columns, col = lax.axis_size("col"), lax.axis_index("col")
    kept = scatter_row(values)[0]
    rows = kept.shape[0] // columns
    total = block_of(kept, col, rows)
    for by in range(1, columns):
        total = total + shift(block_of(kept, (col + by) % columns, rows), "col", by)
    return total


def partners(shape):
    steps = []
    for name in ("dp", "row", "col"):
        bit = 1
        while bit < shape[name]:
            steps.append((name, bit))
            bit *= 2
    return steps


DEEP = 4
MESH_ID = pl.DeviceIdType.MESH
ANY = pl.BlockSpec(memory_space=pl.ANY)


def near_first(place, step, size):
    if size == 1:
        return place
    if size == 2:
        return place + step * (1 - 2 * place)
    side = place // 2
    inner = (place * (3 - place)) // 2
    found = step + inner * (1 - 2 * step) * (1 - step // 2)
    return found + side * (3 - 2 * found)


class Grid:
    def __init__(self, size):
        self.size, self.deep, self.across = size, DEEP, size // DEEP
        self.me = lax.axis_index("dp")
        self.z, self.x = self.me // self.across, self.me % self.across
        self.steps = (-self.across, self.across, -1, 1)
        self.exists = (
            self.z > 0,
            self.z < self.deep - 1,
            self.x > 0,
            self.x < self.across - 1,
        )
        self.count = (
            jnp.minimum(self.z, 1)
            + jnp.minimum(self.deep - 1 - self.z, 1)
            + jnp.minimum(self.x, 1)
            + jnp.minimum(self.across - 1 - self.x, 1)
        )

    def greet(self, barrier):
        for there, step in zip(self.exists, self.steps):
            @pl.when(there)
            def _():
                pl.semaphore_signal(
                    barrier, inc=1, device_id={"dp": self.me + step}, device_id_type=MESH_ID
                )


def gather_kernel(size, columns, *refs):
    count = PLAIN + BOTH
    hidden_ref, vec_ref, in_ref, step_ref, out_ref, up_ref, down_ref, state_ref, router_ref = refs[:9]
    routes_ref, expert_up_ref, expert_down_ref, refs = refs[9], refs[10], refs[11], refs[12:]
    outs, lows, down_came, refs = (
        refs[: count + 1], refs[count + 1 : count + 3], refs[count + 3], refs[count + 4 :]
    )
    ins, refs = refs[: count + 1], refs[count + 1 :]
    dp_send, dp_recv, sh_send, sh_recv, rc_send, rc_recv, keep_sem, side_send, side_recv = refs
    mixer, step, out, mask, up, down, small, tokens = ins
    states = state_ref.shape[1]
    grid = Grid(size)
    me, z, x = grid.me, grid.z, grid.x
    row, col = lax.axis_index("row"), lax.axis_index("col")
    mine, other_row = row * columns + col, {"row": 1 - row}
    to_col = lambda by: {"col": (col + by) % columns}
    from_col = lambda by: row * columns + (col + by) % columns
    barrier = pltpu.get_barrier_semaphore()
    grid.greet(barrier)
    pl.semaphore_signal(barrier, inc=1, device_id=other_row, device_id_type=MESH_ID)
    for by in range(1, columns):
        pl.semaphore_signal(barrier, inc=1, device_id=to_col(by), device_id_type=MESH_ID)
    pl.semaphore_wait(barrier, grid.count + columns)

    def block(which, chunk, place):
        return outs[which].at[chunk] if which < PLAIN else outs[which].at[chunk, place]

    def push(which, chunk, way, source=None):
        ref = block(which, chunk, mine)
        return pltpu.make_async_remote_copy(
            src_ref=ref if source is None else source,
            dst_ref=ref,
            send_sem=dp_send.at[which, way, chunk],
            recv_sem=dp_recv.at[which, chunk],
            device_id={"dp": me + grid.steps[way]},
            device_id_type=MESH_ID,
        )

    def spread(which, chunk, place, index, peer, source=None):
        ref = block(which, chunk, place)
        return pltpu.make_async_remote_copy(
            src_ref=ref if source is None else source,
            dst_ref=ref,
            send_sem=sh_send.at[which - PLAIN, index, chunk],
            recv_sem=sh_recv.at[which - PLAIN, place, chunk],
            device_id=peer,
            device_id_type=MESH_ID,
        )

    def spread_tokens(place, index, peer, source=None):
        ref = outs[count].at[place]
        return pltpu.make_async_remote_copy(
            src_ref=ref if source is None else source,
            dst_ref=ref,
            send_sem=rc_send.at[index],
            recv_sem=rc_recv.at[place],
            device_id=peer,
            device_id_type=MESH_ID,
        )

    def place_of(number):
        if grid.across == 2:
            even, first, last = 1 - number % 2, 1 - jnp.minimum(number, 1), number // 7
            step = (1 - even) * ((number + 1) // 2 - last) + even * (number // 2 - 1 + first)
            side = even * (1 - first) + last
        else:
            step, side = number % grid.deep, number // grid.deep
        zc = near_first(z, step, grid.deep)
        xc = near_first(x, side, grid.across)
        ways = [
            way & there for way, there in zip((zc >= z, zc <= z, xc >= x, xc <= x), grid.exists)
        ]
        same_x, same_z = xc == x, zc == z
        z_first = [same_x & ways[0], same_x & ways[1], ways[2], ways[3]]
        x_first = [ways[0], ways[1], same_z & ways[2], same_z & ways[3]]
        return zc * grid.across + xc, [
            x_first if which in X_FIRST else z_first for which in range(count)
        ]

    def spread_one(which, chunk, source=None):
        spread(which, chunk, mine, 0, other_row, source).start()
        for by in range(1, columns):
            spread(which, chunk, mine, by, to_col(by), source).start()

    def pass_on(number, _):
        chunk, onward = place_of(number)
        for which in SMALL_FIRST:
            push(which, chunk, 0).wait_recv()
            for way in range(4):
                @pl.when(onward[which][way])
                def _():
                    push(which, chunk, way).start()
            if which >= PLAIN:
                spread_one(which, chunk)
        return 0

    def push_own(first, last):
        for way in range(4):
            @pl.when(grid.exists[way])
            def _():
                for which in range(first, last):
                    push(which, me, way, ins[which]).start()

    for head in range(in_ref.shape[0]):
        mixer[:, 128 * head : 128 * (head + 1)] = in_ref[head].astype(BF16)
    push_own(0, 1)
    values = hidden_ref[...].astype(F32)
    gain = jnp.concatenate([vec_ref[line : line + 1, :] for line in range(values.shape[1] // 128)], axis=1)
    mean = jnp.sum(values * values, axis=1, keepdims=True) / values.shape[1]
    tokens[...] = (values * lax.rsqrt(mean + 1e-05) * gain).astype(BF16)
    spread_tokens(mine, 0, other_row, ins[count]).start()
    for by in range(1, columns):
        spread_tokens(mine, by, to_col(by), ins[count]).start()
    step[...] = step_ref[...].T.astype(BF16)
    out[...] = out_ref[...].T.astype(BF16)
    expert = lax.broadcasted_iota(jnp.int32, mask.shape, 0)
    named = expert == routes_ref[0:1, :]
    for route in range(1, TOPK):
        named = named | (expert == routes_ref[route : route + 1, :])
    mask[...] = jnp.where(named, 1.0, 0.0).astype(BF16)
    up[...] = up_ref[...].astype(BF16)
    down[...] = down_ref[...].astype(BF16)
    small[:, 0:states] = state_ref[...].astype(BF16)
    small[:, states:] = router_ref[...].T.astype(BF16)
    push_own(1, count)
    keeps = [
        pltpu.make_async_copy(ins[which], block(which, me, mine), keep_sem.at[which])
        for which in range(count)
    ]
    keeps.append(pltpu.make_async_copy(ins[count], outs[count].at[mine], keep_sem.at[count]))
    for copy in keeps:
        copy.start()
    for held in range(EXP_DEV):
        width = expert_up_ref.shape[2]
        lows[0][:, width * held : width * (held + 1)] = expert_up_ref[held].astype(BF16)
    lows[1][...] = expert_down_ref[...].astype(BF16)
    for by in range(1, columns):
        spread_tokens(from_col(by), columns - 1 + by, other_row).wait_recv()
        spread_tokens(from_col(by), columns - 1 + by, other_row).start()
    sides = [
        pltpu.make_async_remote_copy(
            src_ref=lows[1],
            dst_ref=down_came.at[by - 1],
            send_sem=side_send.at[by - 1],
            recv_sem=side_recv.at[by - 1],
            device_id=to_col(by),
            device_id_type=MESH_ID,
        )
        for by in range(1, columns)
    ]
    for copy in sides:
        copy.start()
    for which in range(PLAIN, count):
        spread_one(which, me, ins[which])
    lax.fori_loop(1, size, pass_on, 0)

    def forward_chunk(number, _):
        chunk = place_of(number)[0]
        for which in range(PLAIN, count):
            for by in range(1, columns):
                place = from_col(by)
                spread(which, chunk, place, columns - 1 + by, other_row).wait_recv()
                spread(which, chunk, place, columns - 1 + by, other_row).start()
        return 0

    lax.fori_loop(0, size, forward_chunk, 0)

    def finish(number, _):
        chunk, onward = place_of(number)
        for which in range(PLAIN, count):
            for by in range(columns):
                spread(which, chunk, (1 - row) * columns + (col + by) % columns, 0, other_row).wait_recv()
            for index in range(2 * columns - 1):
                spread(which, chunk, mine, index, other_row).wait_send()
        for way in range(4):
            for which in range(count):
                @pl.when(onward[which][way])
                def _():
                    push(which, chunk, way).wait_send()
        return 0

    lax.fori_loop(0, size, finish, 0)
    for by in range(columns):
        spread_tokens((1 - row) * columns + (col + by) % columns, 0, other_row).wait_recv()
    for index in range(2 * columns - 1):
        spread_tokens(mine, index, other_row).wait_send()
    for copy in keeps + sides:
        copy.wait()


PLAIN, BOTH = 4, 3
SMALL_FIRST = (3, 6, 1, 5, 4, 2, 0)
X_FIRST = (4,)


def gather_start(
    hidden, vec, in_weight, step, out_weight, shared_up, shared_down, state, router, routes, expert_up, expert_down, shape
):
    size, columns = shape["dp"], shape["col"]
    places, count = 2 * columns, PLAIN + BOTH
    heads, rows = in_weight.shape[:2]
    blocks = [
        (rows, 128 * heads),
        (rows, 128),
        (out_weight.shape[1], out_weight.shape[0]),
        (EXP_DEV * size, hidden.shape[0]),
        shared_up.shape,
        shared_down.shape,
        (state.shape[0], state.shape[1] + 128),
        hidden.shape,
    ]
    lead = [(size,)] * PLAIN + [(size, places)] * BOTH + [(places,)]
    results = pl.pallas_call(
        functools.partial(gather_kernel, size, columns),
        out_shape=tuple(jax.ShapeDtypeStruct(at + block, BF16) for at, block in zip(lead, blocks))
        + (
            jax.ShapeDtypeStruct((expert_up.shape[1], EXP_DEV * expert_up.shape[2]), BF16),
            jax.ShapeDtypeStruct(expert_down.shape, BF16),
            jax.ShapeDtypeStruct((columns - 1,) + expert_down.shape, BF16),
        ),
        in_specs=[VM] * 12,
        out_specs=(ANY,) * (count + 1) + (VM,) * 2 + (ANY,),
        scratch_shapes=[pltpu.VMEM(block, BF16) for block in blocks]
        + [
            pltpu.SemaphoreType.DMA((count, 4, size)),
            pltpu.SemaphoreType.DMA((count, size)),
            pltpu.SemaphoreType.DMA((BOTH, 2 * columns - 1, size)),
            pltpu.SemaphoreType.DMA((BOTH, places, size)),
            pltpu.SemaphoreType.DMA((2 * columns - 1,)),
            pltpu.SemaphoreType.DMA((places,)),
            pltpu.SemaphoreType.DMA((count + 1,)),
            pltpu.SemaphoreType.DMA((columns - 1,)),
            pltpu.SemaphoreType.DMA((columns - 1,)),
        ],
        compiler_params=pltpu.CompilerParams(
            collective_id=2, has_side_effects=True, vmem_limit_bytes=58 * 2**20
        ),
        cost_estimate=lasting(105),
        name="gather_start",
    )(
        hidden, vec, in_weight, step, out_weight, shared_up, shared_down, state, router, routes, expert_up, expert_down
    )
    up, down, down_came = results[count + 1 :]
    return (
        *[result.reshape(-1, result.shape[-1]) for result in results[: count + 1]],
        up,
        [down] + [down_came[by - 1] for by in range(1, columns)],
    )


class LineSum:
    def __init__(self, grid, part_ref, out_ref, sums, from_x, from_z, x_send, x_recv, z_send, z_recv):
        self.grid, self.part_ref, self.out_ref = grid, part_ref, out_ref
        self.sums, self.from_x, self.from_z = sums, from_x, from_z
        self.x_send, self.x_recv, self.z_send, self.z_recv = x_send, x_recv, z_send, z_recv

    @staticmethod
    def scratch(size, chunk):
        pair = size == 2 * DEEP
        return [
            pltpu.VMEM((DEEP if pair else size,) + chunk, BF16),
            pltpu.VMEM((DEEP if pair else 2 * size,) + chunk, BF16),
            pltpu.VMEM((DEEP + 1,) + chunk, BF16),
            pltpu.SemaphoreType.DMA((size,)),
            pltpu.SemaphoreType.DMA((2 * size,)),
            pltpu.SemaphoreType.DMA((DEEP,)),
            pltpu.SemaphoreType.DMA((DEEP + 1,)),
        ]

    def sum_slot(self, line, there):
        return line if self.grid.across == 2 else line * self.grid.across + there

    def x_slot(self, line, there, way):
        return line if self.grid.across == 2 else way * self.grid.size + line * self.grid.across + there

    def along_x(self, line, there, way):
        grid = self.grid
        chunk = line * grid.across + there
        return pltpu.make_async_remote_copy(
            src_ref=self.part_ref.at[chunk] if grid.across == 2 else self.sums.at[self.sum_slot(line, there)],
            dst_ref=self.from_x.at[self.x_slot(line, there, way)],
            send_sem=self.x_send.at[chunk],
            recv_sem=self.x_recv.at[way * grid.size + chunk],
            device_id={"dp": grid.me + 2 * way - 1},
            device_id_type=MESH_ID,
        )

    def along_z(self, line, way, receiving):
        grid = self.grid
        end = grid.z if receiving else grid.z + 2 * way - 1
        slot = line if way else line + (1 - jnp.minimum(jnp.abs(line - end), 1)) * (grid.deep - line)
        return pltpu.make_async_remote_copy(
            src_ref=self.sums.at[self.sum_slot(line, grid.x)],
            dst_ref=self.from_z.at[slot],
            send_sem=self.z_send.at[line],
            recv_sem=self.z_recv.at[slot],
            device_id={"dp": grid.me + (2 * way - 1) * grid.across},
            device_id_type=MESH_ID,
        ), slot

    def collect(self, line):
        grid, out_ref, x = self.grid, self.out_ref, self.grid.x
        out_ref[...] = self.part_ref[line * grid.across + x].astype(F32)
        for way, there in ((1, grid.exists[2]), (0, grid.exists[3])):
            @pl.when(there)
            def _():
                self.along_x(line, x, way).wait_recv()
                out_ref[...] += self.from_x[self.x_slot(line, x, way)].astype(F32)
        for way, comes in (
            (1, grid.exists[0] & (line >= grid.z)), (0, grid.exists[1] & (line <= grid.z))
        ):
            @pl.when(comes)
            def _():
                copy, slot = self.along_z(line, way, True)
                copy.wait_recv()
                out_ref[...] += self.from_z[slot].astype(F32)
        for way, toward in ((1, line > grid.z), (0, line < grid.z)):
            @pl.when(toward)
            def _():
                self.sums[self.sum_slot(line, x)] = out_ref[...].astype(BF16)
                self.along_z(line, way, False)[0].start()

    def wait_sent(self, line, there):
        grid, x = self.grid, self.grid.x
        for way in range(2):
            @pl.when((there > x) if way else (there < x))
            def _():
                self.along_x(line, there, way).wait_send()

            @pl.when((there == x) & ((line > grid.z) if way else (line < grid.z)))
            def _():
                self.along_z(line, way, False)[0].wait_send()

    @staticmethod
    def start(sums):
        grid = sums[0].grid
        x, across = grid.x, grid.across

        def away(number, _):
            line = near_first(grid.z, grid.deep - 1 - number // (across - 1), grid.deep)
            there = near_first(x, across - 1 - number % (across - 1), across)
            for one in sums:
                if across > 2:
                    one.sums[one.sum_slot(line, there)] = one.part_ref[line * across + there]
                for way, beyond in ((1, grid.exists[2]), (0, grid.exists[3])):
                    toward = (there > x) if way else (there < x)
                    if across > 2:
                        @pl.when(toward & beyond)
                        def _():
                            one.along_x(line, there, way).wait_recv()
                            held = one.sums.at[one.sum_slot(line, there)]
                            held[...] = (
                                held[...].astype(F32)
                                + one.from_x[one.x_slot(line, there, way)].astype(F32)
                            ).astype(BF16)
                    @pl.when(toward)
                    def _():
                        one.along_x(line, there, way).start()
            return 0

        lax.fori_loop(0, grid.deep * (across - 1), away, 0)

    @staticmethod
    def finish(sums, between=None, after=None):
        grid = sums[0].grid

        def collect(number, _):
            if between is not None:
                between(number)
            line = near_first(grid.z, grid.deep - 1 - number, grid.deep)
            for place, one in enumerate(sums):
                one.collect(line)
                if after is not None and place == 0:
                    @pl.when(number == grid.deep - 1)
                    def _():
                        after()
            return 0

        lax.fori_loop(0, grid.deep, collect, 0)
        def wait(number, _):
            line = near_first(grid.z, grid.deep - 1 - number // grid.across, grid.deep)
            there = near_first(grid.x, grid.across - 1 - number % grid.across, grid.across)
            for one in sums:
                one.wait_sent(line, there)
            return 0

        lax.fori_loop(0, grid.size, wait, 0)


TILE = 256


def scatter_kernel(size, columns, part_ref, x_ref, dpre_ref, hid_ref, g_ref, out_ref, *refs):
    up_refs, down_refs, refs = refs[:columns], refs[columns : 2 * columns], refs[2 * columns :]
    dpre_now, g_now, left, turned, stage, sent, came = refs[:7]
    whole_sem, left_sem, stage_sem, row_send, row_recv = refs[7:12]
    grid = Grid(size)
    row = lax.axis_index("row")
    barrier = pltpu.get_barrier_semaphore()
    grid.greet(barrier)
    pl.semaphore_signal(barrier, inc=1, device_id={"row": 1 - row}, device_id_type=MESH_ID)
    pl.semaphore_wait(barrier, grid.count + 1)
    sums = [LineSum(grid, part_ref, out_ref, *refs[12:])]
    LineSum.start(sums)

    width = g_now.shape[1]
    part_rows = [columns_of[0].shape[0] for columns_of in (up_refs, down_refs)]
    ups, downs = (columns * rows // TILE for rows in part_rows)
    half = ups + downs
    bring_dpre = pltpu.make_async_copy(dpre_ref, dpre_now, whole_sem.at[0])
    bring_g = pltpu.make_async_copy(g_ref, g_now, whole_sem.at[1])
    begin, end = lambda copy: copy.start(), lambda copy: copy.wait()

    def bring(tile, do):
        whose = row + (1 - tile // half) * (1 - 2 * row)
        within = tile % half

        @pl.when((within < ups) & (tile < 2 * half))
        def _():
            at = pl.ds(pl.multiple_of((whose * ups + within) * TILE, TILE), TILE)
            do(pltpu.make_async_copy(x_ref.at[:, at], left.at[tile % 2], left_sem.at[tile % 2]))

        @pl.when((within >= ups) & (tile < 2 * half))
        def _():
            at = pl.ds(pl.multiple_of(((within - ups) * 2 + whose) * TILE, TILE), TILE)
            do(pltpu.make_async_copy(hid_ref.at[:, at], left.at[tile % 2], left_sem.at[tile % 2]))

    def push(within):
        return pltpu.make_async_remote_copy(
            src_ref=sent.at[within],
            dst_ref=came.at[within],
            send_sem=row_send.at[within],
            recv_sem=row_recv.at[within],
            device_id={"row": 1 - row},
            device_id_type=MESH_ID,
        )

    col = lax.axis_index("col")
    piece = TILE // columns
    up_piece = TILE // 2

    def leave(within, do):
        for at in range(0, TILE, up_piece):
            @pl.when((within >= 0) & (within < ups))
            def _():
                first = within * TILE + at
                whose = (first // part_rows[0] + columns - col) % columns
                rows = pl.ds(pl.multiple_of(first % part_rows[0], up_piece), up_piece)
                for by in range(columns):
                    @pl.when(whose == by)
                    def _():
                        do(
                            pltpu.make_async_copy(
                                stage.at[within % 2, pl.ds(at, up_piece)],
                                up_refs[by].at[rows],
                                stage_sem.at[within % 2, at // up_piece],
                            )
                        )

        for place in range(columns):
            @pl.when(within >= ups)
            def _():
                whose = (place + columns - col) % columns
                rows = pl.ds(pl.multiple_of((within - ups) * piece, piece), piece)
                for by in range(columns):
                    @pl.when(whose == by)
                    def _():
                        do(
                            pltpu.make_async_copy(
                                stage.at[within % 2, pl.ds(place * piece, piece), pl.ds(0, width)],
                                down_refs[by].at[rows],
                                stage_sem.at[within % 2, place],
                            )
                        )

    bring(0, begin)
    bring_dpre.start()
    bring_g.start()
    bring_dpre.wait()
    bring_g.wait()

    def work(tile, _):
        within = tile % half
        bring(tile + 1, begin)
        bring(tile, end)

        @pl.when(tile >= half)
        def _():
            leave(within - 2, end)
            push(within).wait_recv()

        turned[...] = left[tile % 2].T
        for wanted, right in ((within < ups, dpre_now), (within >= ups, g_now)):
            for theirs in (True, False):
                @pl.when(wanted & ((tile < half) if theirs else (tile >= half)))
                def _():
                    for at in range(0, right.shape[1], 512):
                        lanes = slice(at, at + 512)
                        found = dot_f32(turned[...], right[:, lanes])
                        if theirs:
                            sent[within, :, lanes] = found.astype(BF16)
                        else:
                            stage[within % 2, :, lanes] = (
                                found + came[within, :, lanes].astype(F32)
                            ).astype(BF16)

        @pl.when(tile < half)
        def _():
            push(within).start()

        @pl.when(tile >= half)
        def _():
            leave(within, begin)

        return 0

    def between(number):
        done = [0, 2 * half * 2 // 5, 2 * half * 7 // 10, 2 * half * 7 // 10, 2 * half]
        bounds = [jnp.int32(0), jnp.int32(0)]
        for step in range(DEEP):
            now = 1 - jnp.minimum(jnp.abs(number - step), 1)
            bounds = [bounds[0] + now * done[step], bounds[1] + now * done[step + 1]]
        lax.fori_loop(bounds[0], bounds[1], work, 0)

    LineSum.finish(sums, between)
    leave(half - 2, end)
    leave(half - 1, end)

    def sent_all(within, _):
        push(within).wait_send()
        return 0

    lax.fori_loop(0, half, sent_all, 0)


def scatter_blocks(parts, tokens, dpre, hidden, cotangents, shape):
    size, width = shape["dp"], tokens.shape[1]
    if size > 2 * DEEP:
        up = scatter_row(dot_tn(tokens, dpre).astype(BF16))
        down = scatter_row(dot_tn(hidden, cotangents).astype(BF16), EXP_DEV)
        return scatter_dp(parts).astype(F32), parts_of_columns(up), parts_of_columns(down)
    columns = shape["col"]
    parts = parts.reshape((size, -1, parts.shape[1]))
    chunk, count = parts.shape[1:], tokens.shape[0]
    up_half, down_half = width // 2, hidden.shape[1] // 2
    half = (up_half + down_half) // TILE
    results = pl.pallas_call(
        functools.partial(scatter_kernel, size, columns),
        out_shape=(jax.ShapeDtypeStruct(chunk, F32),)
        + (jax.ShapeDtypeStruct((up_half // columns, dpre.shape[1]), BF16),) * columns
        + (jax.ShapeDtypeStruct((down_half // columns, width), BF16),) * columns,
        in_specs=[VM] + [ANY] * 4,
        out_specs=(VM,) + (ANY,) * (2 * columns),
        scratch_shapes=[
            pltpu.VMEM(dpre.shape, BF16),
            pltpu.VMEM((count, width), BF16),
            pltpu.VMEM((2, count, TILE), BF16),
            pltpu.VMEM((TILE, count), BF16),
            pltpu.VMEM((2, TILE, dpre.shape[1]), BF16),
            pltpu.VMEM((half, TILE, dpre.shape[1]), BF16),
            pltpu.VMEM((half, TILE, dpre.shape[1]), BF16),
            pltpu.SemaphoreType.DMA((2,)),
            pltpu.SemaphoreType.DMA((2,)),
            pltpu.SemaphoreType.DMA((2, max(2, columns))),
            pltpu.SemaphoreType.DMA((half,)),
            pltpu.SemaphoreType.DMA((half,)),
        ]
        + LineSum.scratch(size, chunk),
        compiler_params=pltpu.CompilerParams(
            collective_id=5, has_side_effects=True, vmem_limit_bytes=60 * 2**20
        ),
        cost_estimate=lasting(78),
        name="scatter_blocks",
    )(parts, tokens, dpre, hidden, cotangents)
    return results[0], results[1 : 1 + columns], results[1 + columns :]


def adam_step(weight, grad, first, second, rate, decay=0.1):
    first_new = 0.9 * first + 0.1 * grad
    second_new = 0.95 * second + 0.05 * grad * grad
    corrected_one = first_new / (1.0 - 0.9**STEP)
    corrected_two = second_new / (1.0 - 0.95**STEP)
    weight_new = weight - rate * (
        corrected_one / (jnp.sqrt(corrected_two) + 1e-08) + decay * weight
    )
    return (first_new, second_new, weight_new)


SMALL_SUMS = (1, 4, 3, 2, 0)
NARROW = 1


def end_kernel(size, steps, columns, count, *refs):
    take = lambda number: (refs[:number], refs[number:])
    part_refs, refs = take(count)
    (value_ref, seq_ref), refs = take(2)
    out_refs, refs = take(count)
    (total_ref, small_ref, rows_ref), refs = take(3)
    (landed, half_now, half_in, quarter, quarter_in, seq_half, seq_sent, seq_in), refs = take(8)
    (t_send, t_recv, s_send, s_recv, q_send, q_recv), scratch = take(6)
    out_ref = out_refs[NARROW]
    grid = Grid(size)
    row, col = lax.axis_index("row"), lax.axis_index("col")

    def other(name, bit):
        place = lax.axis_index(name)
        return {name: place + bit * (1 - 2 * ((place // bit) % 2))}

    barrier = pltpu.get_barrier_semaphore()
    grid.greet(barrier)
    for name, bit in steps:
        pl.semaphore_signal(barrier, inc=1, device_id=other(name, bit), device_id_type=MESH_ID)
    for by in range(1, columns):
        pl.semaphore_signal(
            barrier, inc=1, device_id={"col": (col + by) % columns}, device_id_type=MESH_ID
        )
    pl.semaphore_wait(barrier, grid.count + len(steps) + columns - 1)

    seq_rows, block = seq_half.shape[0], rows_ref.shape[0]
    swap_rows = pltpu.make_async_remote_copy(
        src_ref=seq_ref.at[pl.ds(pl.multiple_of((1 - row) * seq_rows, 16), seq_rows)],
        dst_ref=seq_half,
        send_sem=q_send.at[0],
        recv_sem=q_recv.at[0],
        device_id={"row": 1 - row},
        device_id_type=MESH_ID,
    )
    swap_rows.start()

    total_ref[...] = value_ref[...]

    def exchange(number):
        name, bit = steps[number]
        copy = pltpu.make_async_remote_copy(
            src_ref=total_ref,
            dst_ref=landed.at[number],
            send_sem=t_send.at[number],
            recv_sem=t_recv.at[number],
            device_id=other(name, bit),
            device_id_type=MESH_ID,
        )
        copy.start()
        copy.wait()
        total_ref[...] += landed[number]

    early = len([1 for name, bit in steps if name == "dp" and bit < grid.across])
    for number in range(early):
        exchange(number)
    sums = [
        LineSum(grid, part_refs[number], out_refs[number], *scratch[7 * number : 7 * number + 7])
        for number in range(count)
    ]
    LineSum.start(sums)

    def both_rows(place):
        mine = seq_ref[pl.ds(pl.multiple_of(row * seq_rows + place * block, 16), block), :]
        theirs = seq_half[pl.ds(pl.multiple_of(place * block, 16), block), :]
        return mine.astype(F32) + theirs.astype(F32)

    swap_rows.wait()
    moves = []
    for by in range(1, columns):
        to = (col + by) % columns
        seq_sent[by - 1] = both_rows(to).astype(BF16)
        moves.append(
            pltpu.make_async_remote_copy(
                src_ref=seq_sent.at[by - 1],
                dst_ref=seq_in.at[by - 1],
                send_sem=q_send.at[by],
                recv_sem=q_recv.at[by],
                device_id={"col": to},
                device_id_type=MESH_ID,
            )
        )
    for number in range(early, len(steps)):
        exchange(number)
    for copy in moves:
        copy.start()
    rows_ref[...] = both_rows(col)
    half, fourth = half_now.shape[0], small_ref.shape[0]
    swap = pltpu.make_async_remote_copy(
        src_ref=half_now,
        dst_ref=half_in,
        send_sem=s_send.at[0],
        recv_sem=s_recv.at[0],
        device_id={"row": 1 - row},
        device_id_type=MESH_ID,
    )

    def swap_narrow():
        half_now[...] = out_ref[pl.ds(pl.multiple_of((1 - row) * half, 8), half), :]
        swap.start()

    LineSum.finish([sums[number] for number in SMALL_SUMS], after=swap_narrow)
    swap.wait()
    both = out_ref[pl.ds(pl.multiple_of(row * half, 8), half), :] + half_in[...]
    for place in range(columns):
        quarter[place] = both[place * fourth : (place + 1) * fourth]
    copies = []
    for by in range(1, columns):
        to = (col + by) % columns
        copies.append(
            pltpu.make_async_remote_copy(
                src_ref=quarter.at[to],
                dst_ref=quarter_in.at[by],
                send_sem=s_send.at[by],
                recv_sem=s_recv.at[by],
                device_id={"col": to},
                device_id_type=MESH_ID,
            )
        )
        copies[-1].start()
    small_ref[...] = quarter[col]
    for by, copy in enumerate(moves):
        copy.wait()
        rows_ref[...] += seq_in[by].astype(F32)
    for by, copy in enumerate(copies):
        copy.wait()
        small_ref[...] += quarter_in[by + 1]


def scatter_end(parts, values, rows, shape):
    size, columns = shape["dp"], shape["col"]
    steps = partners(shape)
    parts = [part.reshape((size, -1, part.shape[1])) for part in parts]
    (length, narrow), count = parts[NARROW].shape[1:], len(parts)
    half, seq_rows = length // 2, rows.shape[0] // 2
    block = (seq_rows // columns, rows.shape[1])
    fourth = (columns, half // columns, narrow)
    return pl.pallas_call(
        functools.partial(end_kernel, size, steps, columns, count),
        out_shape=tuple(jax.ShapeDtypeStruct(part.shape[1:], F32) for part in parts)
        + (
            jax.ShapeDtypeStruct(values.shape, F32),
            jax.ShapeDtypeStruct(fourth[1:], F32),
            jax.ShapeDtypeStruct(block, F32),
        ),
        in_specs=[VM] * (count + 2),
        out_specs=(VM,) * (count + 3),
        scratch_shapes=[
            pltpu.VMEM((len(steps),) + values.shape, F32),
            pltpu.VMEM((half, narrow), F32),
            pltpu.VMEM((half, narrow), F32),
            pltpu.VMEM(fourth, F32),
            pltpu.VMEM(fourth, F32),
            pltpu.VMEM((seq_rows, rows.shape[1]), BF16),
            pltpu.VMEM((columns - 1,) + block, BF16),
            pltpu.VMEM((columns - 1,) + block, BF16),
            pltpu.SemaphoreType.DMA((len(steps),)),
            pltpu.SemaphoreType.DMA((len(steps),)),
            pltpu.SemaphoreType.DMA((columns,)),
            pltpu.SemaphoreType.DMA((columns,)),
            pltpu.SemaphoreType.DMA((columns,)),
            pltpu.SemaphoreType.DMA((columns,)),
        ]
        + sum([LineSum.scratch(size, part.shape[1:]) for part in parts], []),
        compiler_params=pltpu.CompilerParams(
            collective_id=3, has_side_effects=True, vmem_limit_bytes=60 * 2**20
        ),
        cost_estimate=lasting(125),
        name="scatter_end",
    )(*parts, values, rows)


def steps_kernel(mixer_ref, out_ref, up_ref, down_ref, small_ref, step_ref, *refs):
    ins, outs = refs[:21], refs[21:]
    rate = MODEL_WIDTH ** (-0.5)
    weights, firsts, seconds = ins[0::3], ins[1::3], ins[2::3]

    def put(number, grad, rate, at=...):
        values = adam_step(weights[number][at], grad, firsts[number][at], seconds[number][at], rate)
        for place, value in enumerate(values):
            outs[3 * number + place][at] = value

    for head in range(weights[0].shape[0]):
        put(0, mixer_ref[:, 128 * head : 128 * (head + 1)], rate, head)
    put(1, step_ref[...].T[0 : weights[1].shape[0]], rate)
    put(2, out_ref[...].T, INNER ** (-0.5))
    put(3, small_ref[:, 0 : 2 * STATE], rate)
    routes = small_ref[:, 2 * STATE :].T
    put(4, routes[ROUTER_AT : ROUTER_AT + weights[4].shape[0]], 0.5 * rate)
    put(5, up_ref[...], rate)
    put(6, down_ref[...], FF_S ** (-0.5))


def last_steps(grads, arrays):
    whole = pl.BlockSpec()
    return pl.pallas_call(
        steps_kernel,
        out_shape=tuple(jax.ShapeDtypeStruct(array.shape, F32) for array in arrays),
        in_specs=[whole] * (6 + len(arrays)),
        out_specs=(whole,) * len(arrays),
        compiler_params=pltpu.CompilerParams(vmem_limit_bytes=56 * 2**20),
        cost_estimate=lasting(10),
        name="last_steps",
    )(*grads, *arrays)


def shared_kernel(
    x_ref, g_ref, up_ref, down_ref, out_ref, dx_ref, *refs
):
    count = (len(refs) - 9) // 2
    up_outs, down_outs, refs = refs[:count], refs[count : 2 * count], refs[2 * count :]
    hid_ref, dpre_ref, turned, hid_turned, up_grad, down_grad, up_came, down_came, sems = refs
    row, col = lax.axis_index("row"), lax.axis_index("col")
    barrier = pltpu.get_barrier_semaphore()
    pl.semaphore_signal(barrier, inc=1, device_id={"row": 1 - row}, device_id_type=MESH_ID)
    x, g = x_ref[...], g_ref[...]
    pre = dot_f32(x, up_ref[...])
    asked = dot_t(g, down_ref[...])
    half = down_ref.shape[0]
    for part in range(half // 128):
        lanes = slice(128 * part, 128 * (part + 1))
        upper = slice(half + 128 * part, half + 128 * (part + 1))
        gate, up, want = pre[:, lanes], pre[:, upper], asked[:, lanes]
        sig = jax.nn.sigmoid(gate)
        act = gate * sig
        hid_ref[:, lanes] = (act * up).astype(BF16)
        dpre_ref[:, lanes] = (want * up * (sig * (1.0 + gate * (1.0 - sig)))).astype(BF16)
        dpre_ref[:, upper] = (want * act).astype(BF16)
    turned[...] = x.T
    hid_turned[...] = hid_ref[...].T
    pl.semaphore_wait(barrier, 1)
    copies = []
    for number, (left, right, grad, came) in enumerate(
        ((turned, dpre_ref, up_grad, up_came), (hid_turned, g_ref, down_grad, down_came))
    ):
        size, _, rows, _ = grad.shape
        pairs = 2 if size % 2 == 0 else 1
        for chunk in range(0, size, pairs):
            found = dot_f32(left[2 * rows * chunk : 2 * rows * (chunk + pairs), :], right[...]).astype(BF16)
            for at in range(pairs):
                for half_at in range(2):
                    start = (2 * at + half_at) * rows
                    grad[chunk + at, half_at] = found[start : start + rows]
        copies.append(
            pltpu.make_async_remote_copy(
                src_ref=grad.at[:, 1 - row],
                dst_ref=came,
                send_sem=sems.at[number],
                recv_sem=sems.at[2 + number],
                device_id={"row": 1 - row},
                device_id_type=MESH_ID,
            )
        )
        copies[-1].start()
    out_ref[...] = dot_f32(hid_ref[...], down_ref[...])
    dx_ref[...] = dot_t(dpre_ref[...], up_ref[...])
    for copy, grad, came, outs in zip(copies, (up_grad, down_grad), (up_came, down_came), (up_outs, down_outs)):
        copy.wait()
        size, _, rows, _ = grad.shape
        part = rows // count
        for chunk in range(size):
            total = (grad[chunk, row].astype(F32) + came[chunk].astype(F32)).astype(BF16)
            for place in range(count):
                mine = total[place * part : (place + 1) * part]
                for by in range(count):
                    @pl.when(place == (col + by) % count)
                    def _():
                        outs[by][chunk] = mine


def shared_expert(tokens, cotangents, up, down, shape):
    size, columns = shape["dp"], shape["col"]
    rows, width = tokens.shape
    up_rows, down_rows = (array.shape[0] // (2 * columns * size) for array in (up, down))
    results = pl.pallas_call(
        shared_kernel,
        out_shape=(jax.ShapeDtypeStruct((rows, width), F32),) * 2
        + (jax.ShapeDtypeStruct((size, up_rows, up.shape[1]), BF16),) * columns
        + (jax.ShapeDtypeStruct((size, down_rows, width), BF16),) * columns,
        in_specs=[VM] * 4,
        out_specs=(VM,) * (2 + 2 * columns),
        scratch_shapes=[
            pltpu.VMEM((rows, down.shape[0]), BF16),
            pltpu.VMEM((rows, up.shape[1]), BF16),
            pltpu.VMEM((width, rows), BF16),
            pltpu.VMEM((down.shape[0], rows), BF16),
            pltpu.VMEM((size, 2, columns * up_rows, up.shape[1]), BF16),
            pltpu.VMEM((size, 2, columns * down_rows, width), BF16),
            pltpu.VMEM((size, columns * up_rows, up.shape[1]), BF16),
            pltpu.VMEM((size, columns * down_rows, width), BF16),
            pltpu.SemaphoreType.DMA((4,)),
        ],
        compiler_params=pltpu.CompilerParams(
            collective_id=6, has_side_effects=True, vmem_limit_bytes=58 * 2**20
        ),
        cost_estimate=lasting(20),
        name="shared_expert",
    )(tokens, cotangents, up, down)
    return results[0], results[1], results[2 : 2 + columns], results[2 + columns :]


def expert_block(own, x_ref, g_ref, named, up, down, router_ref, hid_ref, dpre_ref, mix_ref, dx_ref):
    x, g = x_ref[...], g_ref[...]
    logits = dot_f32(x, router_ref[...])
    high = jnp.max(jnp.where(named > 0, logits, -1e30), axis=1, keepdims=True)
    raised = jnp.where(named > 0, jnp.exp(logits - high), 0.0)
    gates = raised / jnp.sum(raised, axis=1, keepdims=True)
    rows = x.shape[0]
    lane = lax.broadcasted_iota(jnp.int32, (rows, 128), 1)
    weights = [
        jnp.sum(jnp.where(lane == own + part, gates, 0.0), axis=1, keepdims=True)
        for part in range(EXP_DEV)
    ]
    half = down.shape[0]
    pre = dot_f32(x, up)
    asked = dot_t(g, down)
    totals = [jnp.zeros((rows, 128), F32) for part in range(EXP_DEV)]
    for part in range(half // 128):
        which = 128 * part // FF_E
        at = 128 * part + FF_E * which
        lanes = slice(128 * part, 128 * (part + 1))
        lower, upper = slice(at, at + 128), slice(at + FF_E, at + FF_E + 128)
        gate, upper_pre, want = pre[:, lower], pre[:, upper], asked[:, lanes]
        sig = jax.nn.sigmoid(gate)
        act = gate * sig
        hidden = act * upper_pre
        totals[which] = totals[which] + hidden * want
        hid_ref[:, lanes] = (weights[which] * hidden).astype(BF16)
        dact = weights[which] * want
        dpre_ref[:, lower] = (dact * upper_pre * (sig * (1.0 + gate * (1.0 - sig)))).astype(BF16)
        dpre_ref[:, upper] = (dact * act).astype(BF16)
    mix_ref[...] = dot_f32(hid_ref[...], down).astype(BF16)
    dx_ref[:, :MODEL_WIDTH] = dot_t(dpre_ref[...], up).astype(BF16)
    sent = jnp.zeros((rows, 128), F32)
    for part in range(EXP_DEV):
        gate_grad = jnp.sum(totals[part], axis=1, keepdims=True)
        coarse = gate_grad.astype(BF16).astype(F32)
        sent = jnp.where(lane == own + part, coarse, sent)
        sent = jnp.where(lane == own + part + REST_AT, gate_grad - coarse, sent)
    dx_ref[:, MODEL_WIDTH:] = sent.astype(BF16)


def expert_kernel(
    size, columns, own_ref, g_ref, mask_ref, router_hbm, *refs
):
    places = 2 * columns
    up_parts, down_parts, full_ref, refs = (
        refs[:places], refs[places : 2 * places], refs[2 * places], refs[2 * places + 1 :]
    )
    outs, (x_now, g_now), stages, (up_ref, down_ref, router_ref) = (
        refs[:4], refs[4:6], refs[6:10], refs[10:13]
    )
    send_sem, recv_sem, local_sem, in_sem, out_sem, weight_sem = refs[13:]
    grid = Grid(size)
    me, z, x = grid.me, grid.z, grid.x
    barrier = pltpu.get_barrier_semaphore()
    grid.greet(barrier)
    pl.semaphore_wait(barrier, grid.count)

    def push(chunk, way, source=None):
        return pltpu.make_async_remote_copy(
            src_ref=full_ref.at[chunk] if source is None else source,
            dst_ref=full_ref.at[chunk],
            send_sem=send_sem.at[way, chunk],
            recv_sem=recv_sem.at[chunk],
            device_id={"dp": me + grid.steps[way]},
            device_id_type=MESH_ID,
        )

    def place(number):
        if grid.across == 2:
            even, first, last = 1 - number % 2, 1 - jnp.minimum(number, 1), number // 7
            step = (1 - even) * ((number + 1) // 2 - last) + even * (number // 2 - 1 + first)
            side = even * (1 - first) + last
        else:
            step, side = number % grid.deep, number // grid.deep
        return block_at(step, side)

    def block_at(step, side):
        zc = near_first(z, step, grid.deep)
        xc = near_first(x, side, grid.across)
        same = xc == x
        ways = (same & (zc >= z), same & (zc <= z), xc >= x, xc <= x)
        return zc * grid.across + xc, [way & there for way, there in zip(ways, grid.exists)]

    for way in range(4):
        @pl.when(grid.exists[way])
        def _():
            push(me, way, own_ref).start()
    row, col = lax.axis_index("row"), lax.axis_index("col")
    weights = [pltpu.make_async_copy(router_hbm, router_ref, weight_sem.at[2 * places])]
    for number in range(places):
        whose = row + (number // columns) * (1 - 2 * row)
        there = whose * columns + (col - number % columns + columns) % columns
        weights.append(
            pltpu.make_async_copy(up_parts[number], up_ref.at[there], weight_sem.at[number])
        )
        weights.append(
            pltpu.make_async_copy(
                down_parts[number], down_ref.at[:, there], weight_sem.at[places + number]
            )
        )
    for copy in weights:
        copy.start()
    keep = pltpu.make_async_copy(own_ref, full_ref.at[me], local_sem)
    keep.start()

    def leave(number, chunk):
        return [
            pltpu.make_async_copy(stage.at[number % 2], out.at[chunk], out_sem.at[place_in, number % 2])
            for place_in, (stage, out) in enumerate(zip(stages, outs))
        ]

    def work(number, _):
        chunk, onward = place(number)
        bring = pltpu.make_async_copy(g_ref.at[chunk], g_now, in_sem.at[0])
        bring.start()

        def pass_on(chunk, onward):
            push(chunk, 0).wait_recv()
            for way in range(4):
                @pl.when(onward[way])
                def _():
                    push(chunk, way).start()

        if grid.across == 2:
            inner = (z * (3 - z)) // 2
            for step, when in ((1, number == 1), (2, number == 3 - 2 * inner), (3, number == 5 - 2 * inner)):
                @pl.when(when)
                def _():
                    pass_on(*block_at(step, 0))

            @pl.when((number > 0) & (chunk % grid.across != x))
            def _():
                push(chunk, 0).wait_recv()
        else:
            @pl.when(number > 0)
            def _():
                pass_on(chunk, onward)

        bring_x = pltpu.make_async_copy(full_ref.at[chunk], x_now, in_sem.at[1])

        @pl.when(number == 0)
        def _():
            pltpu.make_async_copy(own_ref, x_now, in_sem.at[1]).start()
            for copy in weights:
                copy.wait()

        @pl.when(number > 0)
        def _():
            bring_x.start()

        @pl.when(number > 1)
        def _():
            for copy in leave(number, place(number - 2)[0]):
                copy.wait()

        bring.wait()
        bring_x.wait()
        experts_named = mask_ref[chunk].astype(F32)
        rest = jnp.zeros((128 - experts_named.shape[0], experts_named.shape[1]), F32)
        named = jnp.concatenate([experts_named, rest], axis=0).T
        expert_block(
            EXP_DEV * me, x_now, g_now, named,
            up_ref[...].reshape(-1, up_ref.shape[2]), down_ref[...].reshape(-1, down_ref.shape[3]), router_ref,
            *[stage.at[number % 2] for stage in stages]
        )
        for copy in leave(number, chunk):
            copy.start()
        return 0

    lax.fori_loop(0, size, work, 0)
    for number in (size - 2, size - 1):
        for copy in leave(number, place(number)[0]):
            copy.wait()

    def finish(number, _):
        chunk, onward = place(number)
        for way in range(4):
            @pl.when(onward[way])
            def _():
                push(chunk, way).wait_send()
        return 0

    lax.fori_loop(0, size, finish, 0)
    keep.wait()


def experts(tokens, cotangents, masks, up_parts, down_parts, router, shape):
    size, columns = shape["dp"], shape["col"]
    places = 2 * columns
    rows, width = tokens.shape
    hidden = places * EXP_DEV * down_parts[0].shape[1]
    wide = width + 128
    wides = (hidden, 2 * hidden, width, wide)
    results = pl.pallas_call(
        functools.partial(expert_kernel, size, columns),
        out_shape=tuple(
            jax.ShapeDtypeStruct((size, rows, column), BF16) for column in (width,) + wides
        ),
        in_specs=[ANY, ANY, VM] + [ANY] * (1 + 2 * places),
        out_specs=(ANY,) * 5,
        scratch_shapes=[pltpu.VMEM((rows, width), BF16)] * 2
        + [pltpu.VMEM((2, rows, column), BF16) for column in wides]
        + [
            pltpu.VMEM((places,) + up_parts[0].shape, BF16),
            pltpu.VMEM((EXP_DEV, places) + down_parts[0].shape[1:], BF16),
            pltpu.VMEM(router.shape, BF16),
            pltpu.SemaphoreType.DMA((4, size)),
            pltpu.SemaphoreType.DMA((size,)),
            pltpu.SemaphoreType.DMA,
            pltpu.SemaphoreType.DMA((2,)),
            pltpu.SemaphoreType.DMA((4, 2)),
            pltpu.SemaphoreType.DMA((2 * places + 1,)),
        ],
        compiler_params=pltpu.CompilerParams(
            collective_id=4, has_side_effects=True, vmem_limit_bytes=56 * 2**20
        ),
        cost_estimate=lasting(85),
        name="experts",
    )(tokens, cotangents.reshape(size, rows, width), masks.reshape(size, -1, rows), router, *up_parts, *down_parts)
    return [result.reshape(size * rows, -1) for result in results]


def rms_scale(values):
    return lax.rsqrt(jnp.mean(values * values, axis=-1, keepdims=True) + 1e-05)


def rms_back(values, scale, gain, grad_normed):
    weighted = grad_normed * gain[None, :]
    grad_values = scale * weighted - values * scale**3 * jnp.mean(
        weighted * values, axis=-1, keepdims=True
    )
    gain_grad = jnp.sum(grad_normed * values * scale, axis=0)
    return (grad_values, gain_grad)


def silu_gate(pre_values):
    half_size = pre_values.shape[-1] // 2
    return jax.nn.silu(pre_values[..., :half_size]) * pre_values[..., half_size:]


def silu_gate_back(pre_values, grad):
    return jax.vjp(silu_gate, pre_values)[1](grad)[0]


ALL = ("dp", "row", "col")


def gather_dp(values):
    return lax.all_gather(values, "dp", axis=0, tiled=True)


def scatter_dp(values):
    return lax.psum_scatter(values, "dp", scatter_dimension=0, tiled=True)


def body(
    shape,
    hidden_in, segment_ids, routes, out_grad,
    vectors, vectors_first, vectors_second,
    in_weight, in_weight_first, in_weight_second,
    step_weight, step_weight_first, step_weight_second,
    out_weight, out_weight_first, out_weight_second,
    state_weight, state_weight_first, state_weight_second,
    router, router_first, router_second,
    shared_up, shared_up_first, shared_up_second,
    shared_down, shared_down_first, shared_down_second,
    expert_gate_up, expert_gate_up_first, expert_gate_up_second,
    expert_down, expert_down_first, expert_down_second,
):
    dp = lax.axis_index("dp")
    data_count = lax.axis_size("dp")
    seq_devices = lax.axis_size("row") * lax.axis_size("col")
    local_heads = in_weight.shape[1]
    width = 64 * local_heads
    head_start = lax.axis_index(("row", "col")) * local_heads
    own_tokens = hidden_in.shape[1]
    experts_all = router.shape[1]
    rows_dp = in_weight.shape[0]
    seq_columns = shape["col"]
    residual = hidden_in[0].astype(F32)
    count = vectors.shape[0]
    lines = -(-count // 1024) * 8
    vector_rows = jnp.pad(vectors, (0, lines * 128 - count)).reshape(lines, 128)
    gain_one = vectors[0:MODEL_WIDTH]
    gain_two = vectors[MODEL_WIDTH : 2 * MODEL_WIDTH]

    scale_one = rms_scale(residual)
    route_ids = routes[0]
    chosen = (
        route_ids[:, :, None] == jnp.arange(experts_all, dtype=jnp.int32)[None, None, :]
    ).any(axis=1)
    grad_low = out_grad[0]
    (
        mixer_full, step_full, out_full, masks, shared_up_full, shared_down_full, small_full, normed_all,
        up_local, down_parts,
    ) = gather_start(
        hidden_in[0],
        vector_rows,
        in_weight.transpose(1, 0, 2),
        jnp.pad(step_weight.T, ((0, 128 - local_heads), (0, 0))),
        out_weight.reshape(width, -1),
        shared_up,
        shared_down,
        state_weight,
        jnp.pad(router.T, ((0, 128 - experts_all), (0, 0))),
        route_ids.T,
        expert_gate_up,
        expert_down,
        shape,
    )
    mixer_full, step_full, out_full, small_full, normed_all, segment_ids, grad_gone, up_local, down_parts = (
        lax.optimization_barrier(
            (mixer_full, step_full, out_full, small_full, normed_all, segment_ids, grad_low, up_local, down_parts)
        )
    )
    grad_all = gather_dp(grad_gone)
    up_parts = [up_local] + [shift(up_local, "col", by) for by in range(1, seq_columns)]
    state_step = jnp.concatenate([small_full[:, : 2 * STATE], step_full], axis=1)

    seg_rows = segment_ids[0].astype(F32).reshape(-1, 1, BLK)
    proj = dot_f32(normed_all, mixer_full).astype(BF16)
    ss = dot_f32(normed_all, state_step)
    valued, squares_part, kept, params = mixer_forward(proj, ss, seg_rows, vector_rows, seq_columns)
    partial_out = dot_t(valued, out_full).astype(BF16)
    partial_out, up_parts = lax.optimization_barrier((partial_out, up_parts))
    proj_out = scatter_rc(partial_out)
    other_row = lambda parts: parts + [shift(part, "row", 1) for part in parts]
    up_parts, down_parts = other_row(up_parts), other_row(down_parts)
    squares = scatter_squares(squares_part)[:, 0]
    scale_two = lax.rsqrt(squares / INNER + 1e-05)
    residual_two = residual + scale_two[:, None] * proj_out
    scale_three = rms_scale(residual_two)
    normed_two = (residual_two * scale_three * gain_two[None, :]).astype(BF16)

    router_wide = small_full[:, 2 * STATE :]
    router_full = router_wide[:, :experts_all]
    shared_out, shared_dx, shared_up_sums, shared_down_sums = shared_expert(
        normed_two, grad_low, shared_up_full, shared_down_full, shape
    )
    normed_two, grad_all, shared_up_sums, shared_down_sums, shared_dx, shared_out = (
        lax.optimization_barrier(
            (normed_two, grad_all, shared_up_sums, shared_down_sums, shared_dx, shared_out)
        )
    )
    from_columns = lambda parts: [
        shift(parts[by], "col", by) for by in range(1, seq_columns)
    ]
    shared_up_came, shared_down_came = from_columns(shared_up_sums), from_columns(shared_down_sums)
    tokens_all, hidden_low, pre_grad, mixed, rows_grad = experts(
        normed_two, grad_all, masks, up_parts, down_parts, router_wide, shape
    )
    logits = dot_f32(normed_two, router_full)
    gate_all = jax.nn.softmax(jnp.where(chosen, logits, -jnp.inf), axis=-1)
    rows_grad, shared_up_came, shared_down_came = lax.optimization_barrier(
        (rows_grad, shared_up_came, shared_down_came)
    )
    add_all = lambda own, came: sum([part.astype(F32) for part in came], own.astype(F32)).astype(BF16)
    shared_up_part = add_all(shared_up_sums[0], shared_up_came).reshape(-1, 2 * FF_S)
    shared_down_part = add_all(shared_down_sums[0], shared_down_came).reshape(-1, MODEL_WIDTH)
    routed_grad, up_grad, down_grad = scatter_blocks(
        rows_grad, tokens_all, pre_grad, hidden_low, grad_all, shape
    )
    routed_grad, mixed = lax.optimization_barrier((routed_grad, mixed))
    mixture = scatter_dp(mixed).astype(F32)
    gate_grad = (
        routed_grad[:, MODEL_WIDTH : MODEL_WIDTH + experts_all]
        + routed_grad[:, MODEL_WIDTH + REST_AT : MODEL_WIDTH + REST_AT + experts_all]
    )
    cotangent = grad_low.astype(F32)
    normed_two_grad = shared_dx + routed_grad[:, :MODEL_WIDTH]
    logits_grad = gate_all * (gate_grad - jnp.sum(gate_all * gate_grad, axis=1, keepdims=True))
    logits_low = jnp.where(chosen, logits_grad, 0.0).astype(BF16)
    normed_two_grad = normed_two_grad + dot_t(logits_low, router_full)
    router_grad = dot_tn(normed_two, logits_low)
    residual_two_grad, gain_two_grad = rms_back(
        residual_two, scale_three, gain_two, normed_two_grad
    )
    residual_two_grad = residual_two_grad + cotangent
    proj_out_grad = (residual_two_grad * scale_two[:, None]).astype(BF16)
    squares_grad = (
        jnp.sum(residual_two_grad * proj_out, axis=1) * -0.5 * scale_two**3 / INNER
    )
    squares_high = squares_grad.astype(BF16)
    squares_rest = (squares_grad - squares_high.astype(F32)).astype(BF16)
    riding = jnp.pad(jnp.stack([squares_high, squares_rest], axis=1), ((0, 0), (0, 126)))
    riders = jnp.concatenate([proj_out_grad, riding], axis=1)
    riders, up_grad, down_grad = lax.optimization_barrier((riders, up_grad, down_grad))
    riders = gather_rc(riders)
    proj_grad_all = riders[:, :MODEL_WIDTH]
    squares_grad_all = jnp.sum(riders[:, MODEL_WIDTH:].astype(F32), axis=1, keepdims=True)
    proj_grad_all, up_grad, down_grad = lax.optimization_barrier((proj_grad_all, up_grad, down_grad))
    sum_all = lambda parts: sum([part.astype(F32) for part in from_columns(parts)], parts[0].astype(F32))
    up_total, down_total = sum_all(up_grad), sum_all(down_grad)
    up_total = jnp.stack(
        [up_total[:, 2 * FF_E * held : 2 * FF_E * (held + 1)] for held in range(EXP_DEV)]
    )
    new_up = adam_step(
        expert_gate_up, up_total, expert_gate_up_first, expert_gate_up_second, MODEL_WIDTH ** (-0.5)
    )
    new_down = adam_step(
        expert_down, down_total.reshape(expert_down.shape), expert_down_first, expert_down_second, FF_E ** (-0.5)
    )

    valued_grad = dot_f32(proj_grad_all, out_full).astype(BF16)
    out_grad_t = dot_tn(proj_grad_all, valued).astype(BF16)
    proj_grad, ss_grad, vector_grad = mixer_backward(
        proj, ss, seg_rows, params, valued_grad, squares_grad_all, kept, lines, seq_columns
    )
    normed_part = dot_t(proj_grad, mixer_full) + dot_t(ss_grad, state_step)
    gain_one_grad = jnp.sum(normed_part * normed_all.astype(F32), axis=0) / gain_one
    router_wide = jnp.pad(
        router_grad, ((0, 0), (2 * STATE + ROUTER_AT, 128 - ROUTER_AT - experts_all))
    )
    mixer_grad = dot_tn(normed_all, proj_grad).astype(BF16)
    small_grad = (dot_tn(normed_all, ss_grad) + router_wide).astype(BF16)
    gains = jnp.concatenate([gain_one_grad, gain_two_grad]).reshape(-1, 128)
    vector_lines = vector_grad + jnp.pad(gains, ((0, lines - gains.shape[0]), (0, 0)))
    mixture, mixer_grad, new_up, new_down = lax.optimization_barrier(
        (mixture, mixer_grad, new_up, new_down)
    )
    hidden_out = (residual_two + mixture + shared_out).astype(BF16)[None]
    (
        mixer_total, small_rows, out_total, shared_up_total, shared_down_total,
        vector_total, small_total, normed_grad,
    ) = scatter_end(
        (mixer_grad, small_grad, out_grad_t, shared_up_part, shared_down_part),
        vector_lines,
        normed_part.astype(BF16),
        shape,
    )
    vector_total = vector_total.reshape(-1)[:count]
    heads_first = lambda array: array.transpose(1, 0, 2)
    flat_out = lambda array: array.reshape(width, -1)
    news = last_steps(
        (
            mixer_total, out_total, shared_up_total, shared_down_total, small_total,
            small_rows[:, 2 * STATE :],
        ),
        (
            *map(heads_first, (in_weight, in_weight_first, in_weight_second)),
            step_weight.T, step_weight_first.T, step_weight_second.T,
            *map(flat_out, (out_weight, out_weight_first, out_weight_second)),
            state_weight, state_weight_first, state_weight_second,
            router.T, router_first.T, router_second.T,
            shared_up, shared_up_first, shared_up_second,
            shared_down, shared_down_first, shared_down_second,
        ),
    )
    residual_grad, _ = rms_back(residual, scale_one, gain_one, normed_grad)
    input_grad = (residual_grad + residual_two_grad)[None]
    return (
        hidden_out,
        input_grad,
        *adam_step(vectors, vector_total, vectors_first, vectors_second, 0.3, 0.0),
        *map(heads_first, news[0:3]),
        *[array.T for array in news[3:6]],
        *[array.reshape(out_weight.shape) for array in news[6:9]],
        *news[9:12],
        *[array.T for array in news[12:15]],
        *news[15:],
        *new_up,
        *new_down,
    )


def solution(mesh):
    tokens = P("dp", ("row", "col"), None)
    by_head = P("dp", ("row", "col"))
    out_spec = P(("row", "col"), None, "dp")
    flat = P(ALL, None)
    weights = (
        (P(),) * 3
        + (tokens,) * 3
        + (by_head,) * 3
        + (out_spec,) * 3
        + (flat,) * 12
        + (tokens,) * 6
    )
    return jax.shard_map(
        functools.partial(body, dict(mesh.shape)),
        mesh=mesh,
        in_specs=(tokens, P("dp", None), tokens, tokens) + weights,
        out_specs=(tokens, tokens) + weights,
        check_vma=False,
    )
```

```python
import functools

import jax
import jax.numpy as jnp
from jax import lax
from jax.experimental import pallas as pl
from jax.experimental.pallas import tpu as pltpu
from jax.sharding import PartitionSpec as P

STATE = 128
KW = 4
BLK = 128
F32 = jnp.float32
BF16 = jnp.bfloat16


def dot_f32(a, b, dims=(((1,), (0,)), ((), ()))):
    return lax.dot_general(a, b, dims, preferred_element_type=F32)


def dot_exact(a, b, dims=(((1,), (0,)), ((), ()))):
    return lax.dot_general(
        a, b, dims, precision=lax.Precision.HIGHEST, preferred_element_type=F32
    )


def spread(values, width):
    rows = values.shape[0]
    low = lax.broadcasted_iota(jnp.int32, (rows, 128), 1) < 64
    parts = []
    for pair in range(width // 128):
        left = jnp.broadcast_to(values[:, 2 * pair : 2 * pair + 1], (rows, 128))
        right = jnp.broadcast_to(values[:, 2 * pair + 1 : 2 * pair + 2], (rows, 128))
        parts.append(jnp.where(low, left, right))
    return jnp.concatenate(parts, axis=1)


def head_sums(values):
    width = values.shape[1]
    ones = (
        lax.broadcasted_iota(jnp.int32, (width, 128), 0) // 64
        == lax.broadcasted_iota(jnp.int32, (width, 128), 1)
    ).astype(BF16)
    high = values.astype(BF16)
    rest = (values - high.astype(F32)).astype(BF16)
    return dot_f32(high, ones) + dot_f32(rest, ones)


def apart(values):
    low = lax.broadcasted_iota(jnp.int32, (values.shape[0], 128), 1) < 64
    gates, inputs = [], []
    for at in range(0, values.shape[1], 256):
        one, two = values[:, at : at + 128], values[:, at + 128 : at + 256]
        gates.append(jnp.where(low, one, pltpu.roll(two, 64, 1)))
        inputs.append(jnp.where(low, pltpu.roll(one, 64, 1), two))
    return jnp.concatenate(gates, axis=1), jnp.concatenate(inputs, axis=1)


def together(gates, inputs):
    low = lax.broadcasted_iota(jnp.int32, (gates.shape[0], 128), 1) < 64
    parts = []
    for at in range(0, gates.shape[1], 128):
        one, two = gates[:, at : at + 128], inputs[:, at : at + 128]
        parts.append(jnp.where(low, one, pltpu.roll(two, 64, 1)))
        parts.append(jnp.where(low, pltpu.roll(one, 64, 1), two))
    return jnp.concatenate(parts, axis=1)


def block_masks(index, seg_ref):
    now = seg_ref[index]
    before = jnp.where(index > 0, seg_ref[jnp.maximum(index - 1, 0)], -1.0)
    lane = lax.broadcasted_iota(jnp.int32, (1, BLK), 1)
    rows = [now]
    for back in range(1, KW):
        earlier = jnp.where(lane < back, pltpu.roll(before, back, 1), pltpu.roll(now, back, 1))
        rows.append((earlier == now).astype(F32))
    last, prior = now[:, BLK - 1 :], before[:, BLK - 1 :]
    rows.append((now == prior).astype(F32))
    rows.append((now == last).astype(F32))
    rows.append(jnp.broadcast_to((prior == last).astype(F32), (1, BLK)))
    rows.append(jnp.zeros((BLK - len(rows), BLK), F32))
    return jnp.concatenate(rows, axis=0).T


def block_common(width, start, index, proj_ref, ss_ref, seg_ref, par_ref):
    rows = pl.ds(start, BLK)
    before = pl.ds(pl.multiple_of(jnp.maximum(start - 8, 0), 8), 8)
    aux = block_masks(index, seg_ref)
    gate, inner = apart(proj_ref[rows, :].astype(F32))
    current = jnp.concatenate([inner, ss_ref[rows, 0 : 2 * STATE]], axis=1)
    earlier = proj_ref[pl.ds(pl.multiple_of(jnp.maximum(start - 16, 0), 16), 16), :]
    previous = jnp.concatenate(
        [apart(earlier.astype(F32)[8:])[1], ss_ref[before, 0 : 2 * STATE]], axis=1
    )
    extended = jnp.concatenate([previous, current], axis=0)
    taps = par_ref[0:KW, :]
    conv = par_ref[KW : KW + 1, :] + taps[KW - 1 : KW, :] * current
    shifted = []
    for back in range(1, KW):
        moved = pltpu.roll(extended, back, 0)[8:] * aux[:, back : back + 1]
        shifted.append(moved)
        conv = conv + taps[KW - 1 - back : KW - back, :] * moved
    sig = jax.nn.sigmoid(conv)
    active = conv * sig
    inputs_x = active[:, :width]
    matrix_b = active[:, width : width + STATE].astype(BF16)
    matrix_c = active[:, width + STATE :].astype(BF16)
    step_in = ss_ref[rows, 2 * STATE :] + par_ref[7:8, 0:128]
    dt = jnp.maximum(step_in, 0.0) + jnp.log1p(jnp.exp(-jnp.abs(step_in)))
    decay = dt * par_ref[6:7, 0:128]
    row_id = lax.broadcasted_iota(jnp.int32, (BLK, BLK), 0)
    col_id = lax.broadcasted_iota(jnp.int32, (BLK, BLK), 1)
    lower = (row_id >= col_id).astype(F32)
    cum = dot_exact(lower, decay)
    cum_t = cum.T
    same = (aux[:, 0:1] == seg_ref[pl.ds(index, 1), 0, :]) & (row_id >= col_id)
    last = cum[BLK - 1 : BLK, :]
    gain_in = jnp.exp(cum) * aux[:, 4:5]
    tail = jnp.exp(last - cum) * aux[:, 5:6]
    carry = jnp.exp(last) * aux[BLK - 1 : BLK, 6:7]
    scores = jnp.where(same, dot_f32(matrix_c, matrix_b, (((1,), (1,)), ((), ()))), 0.0)
    dt_wide = spread(dt, width)
    moved_x = inputs_x * dt_wide
    return dict(
        rows=rows, aux=aux, gate=gate, current=current, shifted=shifted, conv=conv, sig=sig,
        x=inputs_x, b=matrix_b, c=matrix_c, step_in=step_in, dt=dt, cum=cum, cum_t=cum_t,
        same=same, scores=scores, dt_wide=dt_wide, u=moved_x, lower=lower,
        gain_in=spread(gain_in, width), tail=spread(tail, width),
        carry=spread(jnp.broadcast_to(carry, (8, 128)), width)[0:1],
    )


def split_pair(values):
    low = lax.broadcasted_iota(jnp.int32, values.shape, 1) < 64
    zero = jnp.zeros_like(values)
    return jnp.where(low, values, zero), jnp.where(low, zero, values)


GAIN_AT, BIAS_AT, TAPS_AT, HEADS_AT = 24, 48, 74, 178
INNER_LINES, TAP_LINES = 24, 26


def own_place(columns):
    return lax.axis_index("row") * columns + lax.axis_index("col")


def read_params(width, columns, vec_ref, par_ref):
    lines, heads = width // 128, width // 64
    place = own_place(columns)

    def line(at):
        return jnp.concatenate(
            [vec_ref[pl.ds(at + place * lines + one, 1), :] for one in range(lines)], axis=1
        )

    def wide_line(at):
        rest = at + INNER_LINES
        return jnp.concatenate(
            [line(at), vec_ref[rest : rest + 1, :], vec_ref[rest + 1 : rest + 2, :]], axis=1
        )

    par_ref[...] = jnp.zeros_like(par_ref)
    for tap in range(KW):
        par_ref[tap : tap + 1, :] = wide_line(TAPS_AT + TAP_LINES * tap)
    par_ref[KW : KW + 1, :] = wide_line(BIAS_AT)
    par_ref[5:6, 0:width] = line(GAIN_AT)
    flat = jnp.concatenate([vec_ref[HEADS_AT : HEADS_AT + 1, :], vec_ref[HEADS_AT + 1 : HEADS_AT + 2, :]], axis=1)
    flat = jnp.broadcast_to(flat, (8, 256))
    lane = lax.broadcasted_iota(jnp.int32, (8, 128), 1)

    def per_head(which):
        turned = pltpu.roll(flat, 256 - 48 * which - place * heads, 1)[:, 0:128]
        return jnp.where(lane < heads, turned, 0.0)

    par_ref[6:7, 0:128] = jnp.where(lane < heads, -jnp.exp(per_head(0)), 0.0)[0:1]
    par_ref[7:8, 0:128] = per_head(2)[0:1]
    par_ref[8:9, 0:width] = spread(per_head(1), width)[0:1]


def write_params(width, columns, sums, par_ref, vec_ref):
    lines, heads = width // 128, width // 64
    place = own_place(columns)
    vec_ref[...] = jnp.zeros_like(vec_ref)
    total = lambda at: jnp.sum(sums[at : at + 8, :], axis=0, keepdims=True)

    def line(at, row):
        for one in range(lines):
            vec_ref[pl.ds(at + place * lines + one, 1), :] = row[:, 128 * one : 128 * (one + 1)]

    def wide_line(at, row):
        line(at, row)
        rest = at + INNER_LINES
        vec_ref[rest : rest + 1, :] = row[:, width : width + 128]
        vec_ref[rest + 1 : rest + 2, :] = row[:, width + 128 :]

    for tap in range(KW):
        wide_line(TAPS_AT + TAP_LINES * tap, total(8 * tap))
    wide_line(BIAS_AT, total(32))
    line(GAIN_AT, total(48))
    skips = jnp.sum(head_sums(sums[64:72, 0:width]), axis=0, keepdims=True)
    decays = total(56)[:, 0:128] * par_ref[6:7, 0:128]
    flat = jnp.zeros((8, 256), F32)
    lane = lax.broadcasted_iota(jnp.int32, (8, 256), 1)
    for which, row in enumerate((decays, skips, total(72)[:, 0:128])):
        row = jnp.broadcast_to(jnp.concatenate([row, jnp.zeros((1, 128), F32)], axis=1), (8, 256))
        flat = flat + pltpu.roll(jnp.where(lane < heads, row, 0.0), 48 * which + place * heads, 1)
    vec_ref[HEADS_AT : HEADS_AT + 1, :] = flat[0:1, 0:128]
    vec_ref[HEADS_AT + 1 : HEADS_AT + 2, :] = flat[0:1, 128:]


def forward_kernel(
    width, columns, proj_ref, ss_ref, seg_ref, vec_ref, valued_ref, squares_ref, kept_ref, par_ref, state
):
    blocks = proj_ref.shape[0] // BLK
    state[...] = jnp.zeros_like(state)
    read_params(width, columns, vec_ref, par_ref)

    def step(index, _):
        start = pl.multiple_of(index * BLK, BLK)
        got = block_common(width, start, index, proj_ref, ss_ref, seg_ref, par_ref)
        kept_ref[index] = state[...]
        moved = got["u"].astype(BF16)
        parts = []
        for pair in range(width // 128):
            u0, u1 = split_pair(moved[:, 128 * pair : 128 * (pair + 1)])
            mixes = []
            for head in (2 * pair, 2 * pair + 1):
                differ = jnp.minimum(got["cum"][:, head : head + 1] - got["cum_t"][head : head + 1, :], 0.0)
                mixes.append((jnp.exp(differ) * got["scores"]).astype(BF16))
            parts.append(dot_f32(jnp.concatenate(mixes, axis=1), jnp.concatenate([u0, u1], axis=0)))
        within = jnp.concatenate(parts, axis=1)
        from_state = got["gain_in"] * dot_f32(got["c"], state[...].astype(BF16))
        scanned = within + from_state + par_ref[8:9, 0:width] * got["x"]
        state[...] = state[...] * got["carry"] + dot_f32(
            got["b"], (got["tail"] * got["u"]).astype(BF16), (((0,), (0,)), ((), ()))
        )
        gate = got["gate"]
        gated = scanned * (gate * jax.nn.sigmoid(gate))
        squares_ref[got["rows"], :] = jnp.sum(gated * gated, axis=1, keepdims=True)
        valued_ref[got["rows"], :] = (gated * par_ref[5:6, 0:width]).astype(BF16)
        return 0

    lax.fori_loop(0, blocks, step, 0)


def backward_kernel(
    width, columns, proj_ref, ss_ref, seg_ref, par_ref, vgrad_ref, dsq_ref, kept_ref,
    dproj_ref, dss_ref, dvec_ref, dstate, follow, ebuf, sums
):
    blocks = proj_ref.shape[0] // BLK
    dstate[...] = jnp.zeros_like(dstate)
    follow[...] = jnp.zeros_like(follow)
    sums[...] = jnp.zeros_like(sums)

    def fold(values):
        total = values[0:8]
        for part in range(1, BLK // 8):
            total = total + values[8 * part : 8 * part + 8]
        return total

    def step(count, _):
        index = blocks - 1 - count
        start = pl.multiple_of(index * BLK, BLK)
        got = block_common(width, start, index, proj_ref, ss_ref, seg_ref, par_ref)
        rows, aux = got["rows"], got["aux"]
        state_in = kept_ref[index]
        state_low = state_in.astype(BF16)
        moved = got["u"].astype(BF16)
        skip = par_ref[8:9, 0:width]
        gain = par_ref[5:6, 0:width]
        parts = []
        for pair in range(width // 128):
            u0, u1 = split_pair(moved[:, 128 * pair : 128 * (pair + 1)])
            mixes = []
            for head in (2 * pair, 2 * pair + 1):
                differ = jnp.minimum(got["cum"][:, head : head + 1] - got["cum_t"][head : head + 1, :], 0.0)
                level = jnp.exp(differ)
                ebuf[head] = level
                mixes.append((level * got["scores"]).astype(BF16))
            parts.append(dot_f32(jnp.concatenate(mixes, axis=1), jnp.concatenate([u0, u1], axis=0)))
        inner = jnp.concatenate(parts, axis=1) + got["gain_in"] * dot_f32(got["c"], state_low)
        scanned = inner + skip * got["x"]
        gate = got["gate"]
        gate_sig = jax.nn.sigmoid(gate)
        gate_act = gate * gate_sig
        gated = scanned * gate_act
        vgrad = vgrad_ref[rows, :].astype(F32)
        dgated = vgrad * gain + 2.0 * gated * dsq_ref[rows, :]
        sums[48:56, 0:width] += fold(vgrad * gated)
        dy = dgated * gate_act
        dgate = dgated * scanned * (gate_sig * (1.0 + gate * (1.0 - gate_sig)))
        dy_low = dy.astype(BF16)
        dscores = jnp.zeros((BLK, BLK), F32)
        parts = []
        for pair in range(width // 128):
            lanes = slice(128 * pair, 128 * (pair + 1))
            u0, u1 = split_pair(moved[:, lanes])
            d0, d1 = split_pair(dy_low[:, lanes])
            mixes = []
            for head, u_own in ((2 * pair, u0), (2 * pair + 1, u1)):
                level = ebuf[head]
                mixes.append((level * got["scores"]).astype(BF16))
                dscores = dscores + level * dot_f32(
                    dy_low[:, lanes], u_own, (((1,), (1,)), ((), ()))
                )
            parts.append(
                dot_f32(
                    jnp.concatenate(mixes, axis=0),
                    jnp.concatenate([d0, d1], axis=0),
                    (((0,), (0,)), ((), ())),
                )
            )
        du_within = jnp.concatenate(parts, axis=1)
        dscores = jnp.where(got["same"], dscores, 0.0).astype(BF16)
        dstate_now = dstate[...]
        dstate_low = dstate_now.astype(BF16)
        dy_in = (got["gain_in"] * dy).astype(BF16)
        u_tail = got["tail"] * got["u"]
        from_next = dot_f32(got["b"], dstate_low)
        du = du_within + got["tail"] * from_next
        dmat_c = dot_f32(dscores, got["b"]) + dot_f32(dy_in, state_low, (((1,), (1,)), ((), ())))
        dmat_b = dot_f32(dscores, got["c"], (((0,), (0,)), ((), ()))) + dot_f32(
            u_tail.astype(BF16), dstate_low, (((1,), (1,)), ((), ()))
        )
        tail_part = head_sums(u_tail * from_next)
        dcum = (
            head_sums(dy_low.astype(F32) * inner - moved.astype(F32) * du_within) - tail_part
        )
        kept_part = head_sums(fold(got["carry"] * dstate_now * state_in))
        at_last = jnp.sum(tail_part, axis=0, keepdims=True) + jnp.sum(kept_part, axis=0, keepdims=True)
        ddecay = dot_exact(got["lower"], dcum, (((0,), (0,)), ((), ()))) + at_last
        ddt = ddecay * par_ref[6:7, 0:128] + head_sums(du * got["x"])
        sums[56:64, 0:128] += fold(ddecay * got["dt"])
        sums[64:72, 0:width] += fold(dy * got["x"])
        dstep = ddt * jax.nn.sigmoid(got["step_in"])
        sums[72:80, 0:128] += fold(dstep)
        dstate[...] = dstate_now * got["carry"] + dot_f32(got["c"], dy_in, (((0,), (0,)), ((), ())))
        dactive = jnp.concatenate([skip * dy + du * got["dt_wide"], dmat_b, dmat_c], axis=1)
        sig, conv = got["sig"], got["conv"]
        dconv = dactive * (sig * (1.0 + conv * (1.0 - sig)))
        sums[32:40, :] += fold(dconv)
        sums[24:32, :] += fold(dconv * got["current"])
        dinput = par_ref[KW - 1 : KW, :] * dconv
        for back in range(1, KW):
            tap = KW - 1 - back
            sums[8 * tap : 8 * tap + 8, :] += fold(dconv * got["shifted"][back - 1])
            masked = dconv * aux[:, back : back + 1]
            ext = jnp.concatenate([masked, follow[back - 1]], axis=0)
            dinput = dinput + par_ref[tap : tap + 1, :] * pltpu.roll(ext, BLK + 8 - back, 0)[:BLK]
            follow[back - 1] = masked[0:8]
        dproj_ref[rows, :] = together(dgate, dinput[:, :width]).astype(BF16)
        dss_ref[rows, 0 : 2 * STATE] = dinput[:, width:].astype(BF16)
        dss_ref[rows, 2 * STATE :] = dstep.astype(BF16)
        return 0

    lax.fori_loop(0, blocks, step, 0)
    write_params(width, columns, sums, par_ref, dvec_ref)


VM = pl.BlockSpec(memory_space=pltpu.VMEM)


def lasting(micros):
    return pl.CostEstimate(flops=0, bytes_accessed=int(micros * 3.0e6), transcendentals=0)


def mixer_forward(proj, ss, seg, vec, columns):
    length, double = proj.shape
    width = double // 2
    blocks = length // BLK
    return pl.pallas_call(
        functools.partial(forward_kernel, width, columns),
        out_shape=(
            jax.ShapeDtypeStruct((length, width), BF16),
            jax.ShapeDtypeStruct((length, 1), F32),
            jax.ShapeDtypeStruct((blocks, STATE, width), F32),
            jax.ShapeDtypeStruct((16, width + 2 * STATE), F32),
        ),
        in_specs=[VM] * 4,
        out_specs=(VM,) * 4,
        scratch_shapes=[pltpu.VMEM((STATE, width), F32)],
        compiler_params=pltpu.CompilerParams(vmem_limit_bytes=56 * 2**20),
        cost_estimate=lasting(20),
        name="mixer_forward",
    )(proj, ss, seg, vec)


def mixer_backward(proj, ss, seg, par, vgrad, dsq, kept, lines, columns):
    length, double = proj.shape
    width = double // 2
    wide = width + 2 * STATE
    return pl.pallas_call(
        functools.partial(backward_kernel, width, columns),
        out_shape=(
            jax.ShapeDtypeStruct((length, 2 * width), BF16),
            jax.ShapeDtypeStruct((length, 3 * STATE), BF16),
            jax.ShapeDtypeStruct((lines, 128), F32),
        ),
        in_specs=[VM] * 7,
        out_specs=(VM,) * 3,
        scratch_shapes=[
            pltpu.VMEM((STATE, width), F32),
            pltpu.VMEM((KW - 1, 8, wide), F32),
            pltpu.VMEM((width // 64, BLK, BLK), F32),
            pltpu.VMEM((80, wide), F32),
        ],
        compiler_params=pltpu.CompilerParams(vmem_limit_bytes=56 * 2**20),
        cost_estimate=lasting(34),
        name="mixer_backward",
    )(proj, ss, seg, par, vgrad, dsq, kept)


MODEL_WIDTH = 1536
HEADS = 48
FF_E = 512
FF_S = 1024
TOPK = 6
STEP = 10
EXP_DEV = 2
INNER = 3072
ROUTER_AT = 64
REST_AT = 64


def dot_t(a, b):
    return dot_f32(a, b, (((1,), (1,)), ((), ())))


def dot_tn(a, b):
    return dot_f32(a, b, (((0,), (0,)), ((), ())))


def shift(values, axis, by):
    size = lax.axis_size(axis)
    return lax.ppermute(values, axis, [(i, (i + by) % size) for i in range(size)])


def all_places(own):
    rows, columns = lax.axis_index("row"), lax.axis_size("col")
    col = lax.axis_index("col")
    placed = []
    for by, part in enumerate(own):
        there = (col - by) % columns
        placed.append((rows * columns + there, part))
        placed.append(((1 - rows) * columns + there, shift(part, "row", 1)))
    return placed


def assemble(placed, group):
    count = len(placed)
    rows, columns = placed[0][1].shape
    total = jnp.zeros((group, count, rows // group, columns), placed[0][1].dtype)
    for place, part in placed:
        total = lax.dynamic_update_slice(
            total, part.reshape(group, 1, rows // group, columns), (0, place, 0, 0)
        )
    return total.reshape(count * rows, columns)


def gather_rc(values):
    columns = lax.axis_size("col")
    return assemble(
        all_places([values] + [shift(values, "col", by) for by in range(1, columns)]), 1
    )


def block_of(array, at, rows):
    return lax.dynamic_slice_in_dim(array, at * rows, rows)


def scatter_row(values, group=1):
    row = lax.axis_index("row")
    halves = values.reshape(group, 2, -1, values.shape[1])
    pick = lambda which: lax.dynamic_index_in_dim(halves, which, 1, keepdims=False)
    away = shift(pick(1 - row), "row", 1)
    return (pick(row).astype(F32) + away.astype(F32)).astype(values.dtype)


def scatter_col(kept):
    columns, col = lax.axis_size("col"), lax.axis_index("col")
    parts = kept.reshape(kept.shape[0], columns, -1, kept.shape[2])
    pick = lambda which: lax.dynamic_index_in_dim(parts, which, 1, keepdims=False)
    total = pick(col).astype(F32)
    for by in range(1, columns):
        total = total + shift(pick((col + by) % columns), "col", by).astype(F32)
    return total.reshape(-1, kept.shape[2])


def parts_of_columns(kept):
    columns, col = lax.axis_size("col"), lax.axis_index("col")
    parts = kept.reshape(kept.shape[0], columns, -1, kept.shape[2])
    pick = lambda which: lax.dynamic_index_in_dim(parts, which, 1, keepdims=False)
    return [pick((col + by) % columns).reshape(-1, kept.shape[2]) for by in range(columns)]


def scatter_rc(values):
    return scatter_col(scatter_row(values))


def scatter_squares(values):
    columns, col = lax.axis_size("col"), lax.axis_index("col")
    kept = scatter_row(values)[0]
    rows = kept.shape[0] // columns
    total = block_of(kept, col, rows)
    for by in range(1, columns):
        total = total + shift(block_of(kept, (col + by) % columns, rows), "col", by)
    return total


def partners(shape):
    steps = []
    for name in ("dp", "row", "col"):
        bit = 1
        while bit < shape[name]:
            steps.append((name, bit))
            bit *= 2
    return steps


DEEP = 4
MESH_ID = pl.DeviceIdType.MESH
ANY = pl.BlockSpec(memory_space=pl.ANY)


def near_first(place, step, size):
    if size == 1:
        return place
    if size == 2:
        return place + step * (1 - 2 * place)
    side = place // 2
    inner = (place * (3 - place)) // 2
    found = step + inner * (1 - 2 * step) * (1 - step // 2)
    return found + side * (3 - 2 * found)


class Grid:
    def __init__(self, size):
        self.size, self.deep, self.across = size, DEEP, size // DEEP
        self.me = lax.axis_index("dp")
        self.z, self.x = self.me // self.across, self.me % self.across
        self.steps = (-self.across, self.across, -1, 1)
        self.exists = (
            self.z > 0,
            self.z < self.deep - 1,
            self.x > 0,
            self.x < self.across - 1,
        )
        self.count = (
            jnp.minimum(self.z, 1)
            + jnp.minimum(self.deep - 1 - self.z, 1)
            + jnp.minimum(self.x, 1)
            + jnp.minimum(self.across - 1 - self.x, 1)
        )

    def greet(self, barrier):
        for there, step in zip(self.exists, self.steps):
            @pl.when(there)
            def _():
                pl.semaphore_signal(
                    barrier, inc=1, device_id={"dp": self.me + step}, device_id_type=MESH_ID
                )


def gather_kernel(size, columns, *refs):
    count = PLAIN + BOTH
    hidden_ref, vec_ref, in_ref, step_ref, out_ref, up_ref, down_ref, state_ref, router_ref = refs[:9]
    routes_ref, expert_up_ref, expert_down_ref, refs = refs[9], refs[10], refs[11], refs[12:]
    outs, lows, down_came, refs = (
        refs[: count + 1], refs[count + 1 : count + 3], refs[count + 3], refs[count + 4 :]
    )
    ins, refs = refs[: count + 1], refs[count + 1 :]
    step_wide, router_wide, refs = refs[0], refs[1], refs[2:]
    dp_send, dp_recv, sh_send, sh_recv, rc_send, rc_recv, keep_sem, side_send, side_recv = refs
    mixer, step, out, mask, up, down, small, tokens = ins
    states = state_ref.shape[1]
    grid = Grid(size)
    me, z, x = grid.me, grid.z, grid.x
    row, col = lax.axis_index("row"), lax.axis_index("col")
    mine, other_row = row * columns + col, {"row": 1 - row}
    to_col = lambda by: {"col": (col + by) % columns}
    from_col = lambda by: row * columns + (col + by) % columns
    barrier = pltpu.get_barrier_semaphore()
    grid.greet(barrier)
    pl.semaphore_signal(barrier, inc=1, device_id=other_row, device_id_type=MESH_ID)
    for by in range(1, columns):
        pl.semaphore_signal(barrier, inc=1, device_id=to_col(by), device_id_type=MESH_ID)
    pl.semaphore_wait(barrier, grid.count + columns)

    def block(which, chunk, place):
        return outs[which].at[chunk] if which < PLAIN else outs[which].at[chunk, place]

    def push(which, chunk, way, source=None):
        ref = block(which, chunk, mine)
        return pltpu.make_async_remote_copy(
            src_ref=ref if source is None else source,
            dst_ref=ref,
            send_sem=dp_send.at[which, way, chunk],
            recv_sem=dp_recv.at[which, chunk],
            device_id={"dp": me + grid.steps[way]},
            device_id_type=MESH_ID,
        )

    def spread(which, chunk, place, index, peer, source=None):
        ref = block(which, chunk, place)
        return pltpu.make_async_remote_copy(
            src_ref=ref if source is None else source,
            dst_ref=ref,
            send_sem=sh_send.at[which - PLAIN, index, chunk],
            recv_sem=sh_recv.at[which - PLAIN, place, chunk],
            device_id=peer,
            device_id_type=MESH_ID,
        )

    def spread_tokens(place, index, peer, source=None):
        ref = outs[count].at[place]
        return pltpu.make_async_remote_copy(
            src_ref=ref if source is None else source,
            dst_ref=ref,
            send_sem=rc_send.at[index],
            recv_sem=rc_recv.at[place],
            device_id=peer,
            device_id_type=MESH_ID,
        )

    def place_of(number):
        if grid.across == 2:
            even, first, last = 1 - number % 2, 1 - jnp.minimum(number, 1), number // 7
            step = (1 - even) * ((number + 1) // 2 - last) + even * (number // 2 - 1 + first)
            side = even * (1 - first) + last
        else:
            step, side = number % grid.deep, number // grid.deep
        zc = near_first(z, step, grid.deep)
        xc = near_first(x, side, grid.across)
        ways = [
            way & there for way, there in zip((zc >= z, zc <= z, xc >= x, xc <= x), grid.exists)
        ]
        same_x, same_z = xc == x, zc == z
        z_first = [same_x & ways[0], same_x & ways[1], ways[2], ways[3]]
        x_first = [ways[0], ways[1], same_z & ways[2], same_z & ways[3]]
        return zc * grid.across + xc, [
            x_first if which in X_FIRST else z_first for which in range(count)
        ]

    def spread_one(which, chunk, source=None):
        spread(which, chunk, mine, 0, other_row, source).start()
        for by in range(1, columns):
            spread(which, chunk, mine, by, to_col(by), source).start()

    def pass_on(number, _):
        chunk, onward = place_of(number)
        for which in SMALL_FIRST:
            push(which, chunk, 0).wait_recv()
            for way in range(4):
                @pl.when(onward[which][way])
                def _():
                    push(which, chunk, way).start()
            if which >= PLAIN:
                spread_one(which, chunk)
        return 0

    def push_own(first, last):
        for way in range(4):
            @pl.when(grid.exists[way])
            def _():
                for which in range(first, last):
                    push(which, me, way, ins[which]).start()

    for head in range(in_ref.shape[0]):
        mixer[:, 128 * head : 128 * (head + 1)] = in_ref[head].astype(BF16)
    push_own(0, 1)
    values = hidden_ref[...].astype(F32)
    gain = jnp.concatenate([vec_ref[line : line + 1, :] for line in range(values.shape[1] // 128)], axis=1)
    mean = jnp.sum(values * values, axis=1, keepdims=True) / values.shape[1]
    tokens[...] = (values * lax.rsqrt(mean + 1e-05) * gain).astype(BF16)
    spread_tokens(mine, 0, other_row, ins[count]).start()
    for by in range(1, columns):
        spread_tokens(mine, by, to_col(by), ins[count]).start()
    step_wide[...] = jnp.zeros_like(step_wide)
    step_wide[0 : step_ref.shape[0], :] = step_ref[...]
    router_wide[...] = jnp.zeros_like(router_wide)
    router_wide[0 : router_ref.shape[0], :] = router_ref[...]
    step[...] = step_wide[...].T.astype(BF16)
    out[...] = out_ref[...].T.astype(BF16)
    expert = lax.broadcasted_iota(jnp.int32, mask.shape, 0)
    named = expert == routes_ref[0:1, :]
    for route in range(1, TOPK):
        named = named | (expert == routes_ref[route : route + 1, :])
    mask[...] = jnp.where(named, 1.0, 0.0).astype(BF16)
    up[...] = up_ref[...].astype(BF16)
    down[...] = down_ref[...].astype(BF16)
    small[:, 0:states] = state_ref[...].astype(BF16)
    small[:, states:] = router_wide[...].T.astype(BF16)
    push_own(1, count)
    keeps = [
        pltpu.make_async_copy(ins[which], block(which, me, mine), keep_sem.at[which])
        for which in range(count)
    ]
    keeps.append(pltpu.make_async_copy(ins[count], outs[count].at[mine], keep_sem.at[count]))
    for copy in keeps:
        copy.start()
    for held in range(EXP_DEV):
        width = expert_up_ref.shape[2]
        lows[0][:, width * held : width * (held + 1)] = expert_up_ref[held].astype(BF16)
    lows[1][...] = expert_down_ref[...].astype(BF16)
    for by in range(1, columns):
        spread_tokens(from_col(by), columns - 1 + by, other_row).wait_recv()
        spread_tokens(from_col(by), columns - 1 + by, other_row).start()
    sides = [
        pltpu.make_async_remote_copy(
            src_ref=lows[1],
            dst_ref=down_came.at[by - 1],
            send_sem=side_send.at[by - 1],
            recv_sem=side_recv.at[by - 1],
            device_id=to_col(by),
            device_id_type=MESH_ID,
        )
        for by in range(1, columns)
    ]
    for copy in sides:
        copy.start()
    for which in range(PLAIN, count):
        spread_one(which, me, ins[which])
    lax.fori_loop(1, size, pass_on, 0)

    def forward_chunk(number, _):
        chunk = place_of(number)[0]
        for which in range(PLAIN, count):
            for by in range(1, columns):
                place = from_col(by)
                spread(which, chunk, place, columns - 1 + by, other_row).wait_recv()
                spread(which, chunk, place, columns - 1 + by, other_row).start()
        return 0

    lax.fori_loop(0, size, forward_chunk, 0)

    def finish(number, _):
        chunk, onward = place_of(number)
        for which in range(PLAIN, count):
            for by in range(columns):
                spread(which, chunk, (1 - row) * columns + (col + by) % columns, 0, other_row).wait_recv()
            for index in range(2 * columns - 1):
                spread(which, chunk, mine, index, other_row).wait_send()
        for way in range(4):
            for which in range(count):
                @pl.when(onward[which][way])
                def _():
                    push(which, chunk, way).wait_send()
        return 0

    lax.fori_loop(0, size, finish, 0)
    for by in range(columns):
        spread_tokens((1 - row) * columns + (col + by) % columns, 0, other_row).wait_recv()
    for index in range(2 * columns - 1):
        spread_tokens(mine, index, other_row).wait_send()
    for copy in keeps + sides:
        copy.wait()


PLAIN, BOTH = 4, 3
SMALL_FIRST = (3, 6, 1, 5, 4, 2, 0)
X_FIRST = (4,)


def gather_start(
    hidden, vec, in_weight, step, out_weight, shared_up, shared_down, state, router, routes, expert_up, expert_down, shape
):
    size, columns = shape["dp"], shape["col"]
    places, count = 2 * columns, PLAIN + BOTH
    heads, rows = in_weight.shape[:2]
    blocks = [
        (rows, 128 * heads),
        (rows, 128),
        (out_weight.shape[1], out_weight.shape[0]),
        (EXP_DEV * size, hidden.shape[0]),
        shared_up.shape,
        shared_down.shape,
        (state.shape[0], state.shape[1] + 128),
        hidden.shape,
    ]
    lead = [(size,)] * PLAIN + [(size, places)] * BOTH + [(places,)]
    results = pl.pallas_call(
        functools.partial(gather_kernel, size, columns),
        out_shape=tuple(jax.ShapeDtypeStruct(at + block, BF16) for at, block in zip(lead, blocks))
        + (
            jax.ShapeDtypeStruct((expert_up.shape[1], EXP_DEV * expert_up.shape[2]), BF16),
            jax.ShapeDtypeStruct(expert_down.shape, BF16),
            jax.ShapeDtypeStruct((columns - 1,) + expert_down.shape, BF16),
        ),
        in_specs=[VM] * 12,
        out_specs=(ANY,) * (count + 1) + (VM,) * 2 + (ANY,),
        scratch_shapes=[pltpu.VMEM(block, BF16) for block in blocks]
        + [
            pltpu.VMEM((128, rows), F32),
            pltpu.VMEM((128, state.shape[0]), F32),
            pltpu.SemaphoreType.DMA((count, 4, size)),
            pltpu.SemaphoreType.DMA((count, size)),
            pltpu.SemaphoreType.DMA((BOTH, 2 * columns - 1, size)),
            pltpu.SemaphoreType.DMA((BOTH, places, size)),
            pltpu.SemaphoreType.DMA((2 * columns - 1,)),
            pltpu.SemaphoreType.DMA((places,)),
            pltpu.SemaphoreType.DMA((count + 1,)),
            pltpu.SemaphoreType.DMA((columns - 1,)),
            pltpu.SemaphoreType.DMA((columns - 1,)),
        ],
        compiler_params=pltpu.CompilerParams(
            collective_id=2, has_side_effects=True, vmem_limit_bytes=58 * 2**20
        ),
        cost_estimate=lasting(105),
        name="gather_start",
    )(
        hidden, vec, in_weight, step, out_weight, shared_up, shared_down, state, router, routes, expert_up, expert_down
    )
    up, down, down_came = results[count + 1 :]
    return (
        *[result.reshape(-1, result.shape[-1]) for result in results[: count + 1]],
        up,
        [down] + [down_came[by - 1] for by in range(1, columns)],
    )


class LineSum:
    def __init__(
        self, grid, part_ref, out_ref, sums, from_x, from_z, x_send, x_recv, z_send, z_recv, own_ref=None
    ):
        self.grid, self.part_ref, self.out_ref, self.own_ref = grid, part_ref, out_ref, own_ref
        self.sums, self.from_x, self.from_z = sums, from_x, from_z
        self.x_send, self.x_recv, self.z_send, self.z_recv = x_send, x_recv, z_send, z_recv

    @staticmethod
    def scratch(size, chunk):
        pair = size == 2 * DEEP
        return [
            pltpu.VMEM((DEEP if pair else size,) + chunk, BF16),
            pltpu.VMEM((DEEP if pair else 2 * size,) + chunk, BF16),
            pltpu.VMEM((DEEP + 1,) + chunk, BF16),
            pltpu.SemaphoreType.DMA((size,)),
            pltpu.SemaphoreType.DMA((2 * size,)),
            pltpu.SemaphoreType.DMA((DEEP,)),
            pltpu.SemaphoreType.DMA((DEEP + 1,)),
        ]

    def sum_slot(self, line, there):
        return line if self.grid.across == 2 else line * self.grid.across + there

    def x_slot(self, line, there, way):
        return line if self.grid.across == 2 else way * self.grid.size + line * self.grid.across + there

    def along_x(self, line, there, way):
        grid = self.grid
        chunk = line * grid.across + there
        return pltpu.make_async_remote_copy(
            src_ref=self.part_ref.at[chunk] if grid.across == 2 else self.sums.at[self.sum_slot(line, there)],
            dst_ref=self.from_x.at[self.x_slot(line, there, way)],
            send_sem=self.x_send.at[chunk],
            recv_sem=self.x_recv.at[way * grid.size + chunk],
            device_id={"dp": grid.me + 2 * way - 1},
            device_id_type=MESH_ID,
        )

    def along_z(self, line, way, receiving):
        grid = self.grid
        end = grid.z if receiving else grid.z + 2 * way - 1
        slot = line if way else line + (1 - jnp.minimum(jnp.abs(line - end), 1)) * (grid.deep - line)
        return pltpu.make_async_remote_copy(
            src_ref=self.sums.at[self.sum_slot(line, grid.x)],
            dst_ref=self.from_z.at[slot],
            send_sem=self.z_send.at[line],
            recv_sem=self.z_recv.at[slot],
            device_id={"dp": grid.me + (2 * way - 1) * grid.across},
            device_id_type=MESH_ID,
        ), slot

    def collect(self, line):
        grid, out_ref, x = self.grid, self.out_ref, self.grid.x
        mine = self.part_ref[line * grid.across + x] if self.own_ref is None else self.own_ref[line]
        out_ref[...] = mine.astype(F32)
        for way, there in ((1, grid.exists[2]), (0, grid.exists[3])):
            @pl.when(there)
            def _():
                self.along_x(line, x, way).wait_recv()
                out_ref[...] += self.from_x[self.x_slot(line, x, way)].astype(F32)
        for way, comes in (
            (1, grid.exists[0] & (line >= grid.z)), (0, grid.exists[1] & (line <= grid.z))
        ):
            @pl.when(comes)
            def _():
                copy, slot = self.along_z(line, way, True)
                copy.wait_recv()
                out_ref[...] += self.from_z[slot].astype(F32)
        for way, toward in ((1, line > grid.z), (0, line < grid.z)):
            @pl.when(toward)
            def _():
                self.sums[self.sum_slot(line, x)] = out_ref[...].astype(BF16)
                self.along_z(line, way, False)[0].start()

    def wait_sent(self, line, there):
        grid, x = self.grid, self.grid.x
        for way in range(2):
            @pl.when((there > x) if way else (there < x))
            def _():
                self.along_x(line, there, way).wait_send()

            @pl.when((there == x) & ((line > grid.z) if way else (line < grid.z)))
            def _():
                self.along_z(line, way, False)[0].wait_send()

    @staticmethod
    def start(sums):
        grid = sums[0].grid
        x, across = grid.x, grid.across

        def away(number, _):
            line = near_first(grid.z, grid.deep - 1 - number // (across - 1), grid.deep)
            there = near_first(x, across - 1 - number % (across - 1), across)
            for one in sums:
                if across > 2:
                    one.sums[one.sum_slot(line, there)] = one.part_ref[line * across + there]
                for way, beyond in ((1, grid.exists[2]), (0, grid.exists[3])):
                    toward = (there > x) if way else (there < x)
                    if across > 2:
                        @pl.when(toward & beyond)
                        def _():
                            one.along_x(line, there, way).wait_recv()
                            held = one.sums.at[one.sum_slot(line, there)]
                            held[...] = (
                                held[...].astype(F32)
                                + one.from_x[one.x_slot(line, there, way)].astype(F32)
                            ).astype(BF16)
                    @pl.when(toward)
                    def _():
                        one.along_x(line, there, way).start()
            return 0

        lax.fori_loop(0, grid.deep * (across - 1), away, 0)

    @staticmethod
    def finish(sums, between=None, after=None):
        grid = sums[0].grid

        def collect(number, _):
            if between is not None:
                between(number)
            line = near_first(grid.z, grid.deep - 1 - number, grid.deep)
            for place, one in enumerate(sums):
                one.collect(line)
                if after is not None and place == 0:
                    @pl.when(number == grid.deep - 1)
                    def _():
                        after()
            return 0

        lax.fori_loop(0, grid.deep, collect, 0)
        def wait(number, _):
            line = near_first(grid.z, grid.deep - 1 - number // grid.across, grid.deep)
            there = near_first(grid.x, grid.across - 1 - number % grid.across, grid.across)
            for one in sums:
                one.wait_sent(line, there)
            return 0

        lax.fori_loop(0, grid.size, wait, 0)


TILE = 256


def scatter_kernel(size, columns, part_ref, x_ref, dpre_ref, hid_ref, g_ref, out_ref, *refs):
    up_refs, down_refs, refs = refs[:columns], refs[columns : 2 * columns], refs[2 * columns :]
    dpre_now, g_now, left, turned, stage, sent, came = refs[:7]
    whole_sem, left_sem, stage_sem, row_send, row_recv = refs[7:12]
    grid = Grid(size)
    row = lax.axis_index("row")
    barrier = pltpu.get_barrier_semaphore()
    grid.greet(barrier)
    pl.semaphore_signal(barrier, inc=1, device_id={"row": 1 - row}, device_id_type=MESH_ID)
    pl.semaphore_wait(barrier, grid.count + 1)
    own, own_sem = refs[12:14]
    sums = [LineSum(grid, part_ref, out_ref, *refs[14:], own_ref=own)]
    LineSum.start(sums)
    loads = [
        pltpu.make_async_copy(part_ref.at[line * grid.across + grid.x], own.at[line], own_sem.at[line])
        for line in range(DEEP)
    ]
    for copy in loads:
        copy.start()

    width = g_now.shape[1]
    part_rows = [columns_of[0].shape[0] for columns_of in (up_refs, down_refs)]
    ups, downs = (columns * rows // TILE for rows in part_rows)
    half = ups + downs
    bring_dpre = pltpu.make_async_copy(dpre_ref, dpre_now, whole_sem.at[0])
    bring_g = pltpu.make_async_copy(g_ref, g_now, whole_sem.at[1])
    begin, end = lambda copy: copy.start(), lambda copy: copy.wait()

    def bring(tile, do):
        whose = row + (1 - tile // half) * (1 - 2 * row)
        within = tile % half

        @pl.when((within < ups) & (tile < 2 * half))
        def _():
            at = pl.ds(pl.multiple_of((whose * ups + within) * TILE, TILE), TILE)
            do(pltpu.make_async_copy(x_ref.at[:, at], left.at[tile % 2], left_sem.at[tile % 2]))

        @pl.when((within >= ups) & (tile < 2 * half))
        def _():
            at = pl.ds(pl.multiple_of(((within - ups) * 2 + whose) * TILE, TILE), TILE)
            do(pltpu.make_async_copy(hid_ref.at[:, at], left.at[tile % 2], left_sem.at[tile % 2]))

    def push(within):
        return pltpu.make_async_remote_copy(
            src_ref=sent.at[within],
            dst_ref=came.at[within],
            send_sem=row_send.at[within],
            recv_sem=row_recv.at[within],
            device_id={"row": 1 - row},
            device_id_type=MESH_ID,
        )

    col = lax.axis_index("col")
    piece = TILE // columns
    up_piece = TILE // 2

    def leave(within, do):
        for at in range(0, TILE, up_piece):
            @pl.when((within >= 0) & (within < ups))
            def _():
                first = within * TILE + at
                whose = (first // part_rows[0] + columns - col) % columns
                rows = pl.ds(pl.multiple_of(first % part_rows[0], up_piece), up_piece)
                for by in range(columns):
                    @pl.when(whose == by)
                    def _():
                        do(
                            pltpu.make_async_copy(
                                stage.at[within % 2, pl.ds(at, up_piece)],
                                up_refs[by].at[rows],
                                stage_sem.at[within % 2, at // up_piece],
                            )
                        )

        for place in range(columns):
            @pl.when(within >= ups)
            def _():
                whose = (place + columns - col) % columns
                rows = pl.ds(pl.multiple_of((within - ups) * piece, piece), piece)
                for by in range(columns):
                    @pl.when(whose == by)
                    def _():
                        do(
                            pltpu.make_async_copy(
                                stage.at[within % 2, pl.ds(place * piece, piece), pl.ds(0, width)],
                                down_refs[by].at[rows],
                                stage_sem.at[within % 2, place],
                            )
                        )

    bring(0, begin)
    bring_dpre.start()
    bring_g.start()
    bring_dpre.wait()
    bring_g.wait()
    for copy in loads:
        copy.wait()

    def work(tile, _):
        within = tile % half
        bring(tile + 1, begin)
        bring(tile, end)

        @pl.when(tile >= half)
        def _():
            leave(within - 2, end)
            push(within).wait_recv()

        turned[...] = left[tile % 2].T
        for wanted, right in ((within < ups, dpre_now), (within >= ups, g_now)):
            for theirs in (True, False):
                @pl.when(wanted & ((tile < half) if theirs else (tile >= half)))
                def _():
                    for at in range(0, right.shape[1], 512):
                        lanes = slice(at, at + 512)
                        found = dot_f32(turned[...], right[:, lanes])
                        if theirs:
                            sent[within, :, lanes] = found.astype(BF16)
                        else:
                            stage[within % 2, :, lanes] = (
                                found + came[within, :, lanes].astype(F32)
                            ).astype(BF16)

        @pl.when(tile < half)
        def _():
            push(within).start()

        @pl.when(tile >= half)
        def _():
            leave(within, begin)

        return 0

    def between(number):
        done = [0, 2 * half * 2 // 5, 2 * half * 7 // 10, 2 * half * 7 // 10, 2 * half]
        bounds = [jnp.int32(0), jnp.int32(0)]
        for step in range(DEEP):
            now = 1 - jnp.minimum(jnp.abs(number - step), 1)
            bounds = [bounds[0] + now * done[step], bounds[1] + now * done[step + 1]]
        lax.fori_loop(bounds[0], bounds[1], work, 0)

    LineSum.finish(sums, between)
    leave(half - 2, end)
    leave(half - 1, end)

    def sent_all(within, _):
        push(within).wait_send()
        return 0

    lax.fori_loop(0, half, sent_all, 0)


def scatter_blocks(parts, tokens, dpre, hidden, cotangents, shape):
    size, width = shape["dp"], tokens.shape[1]
    if size > 2 * DEEP:
        up = scatter_row(dot_tn(tokens, dpre).astype(BF16))
        down = scatter_row(dot_tn(hidden, cotangents).astype(BF16), EXP_DEV)
        return scatter_dp(parts).astype(F32), parts_of_columns(up), parts_of_columns(down)
    columns = shape["col"]
    parts = parts.reshape((size, -1, parts.shape[1]))
    chunk, count = parts.shape[1:], tokens.shape[0]
    up_half, down_half = width // 2, hidden.shape[1] // 2
    half = (up_half + down_half) // TILE
    results = pl.pallas_call(
        functools.partial(scatter_kernel, size, columns),
        out_shape=(jax.ShapeDtypeStruct(chunk, F32),)
        + (jax.ShapeDtypeStruct((up_half // columns, dpre.shape[1]), BF16),) * columns
        + (jax.ShapeDtypeStruct((down_half // columns, width), BF16),) * columns,
        in_specs=[ANY] * 5,
        out_specs=(VM,) + (ANY,) * (2 * columns),
        scratch_shapes=[
            pltpu.VMEM(dpre.shape, BF16),
            pltpu.VMEM((count, width), BF16),
            pltpu.VMEM((2, count, TILE), BF16),
            pltpu.VMEM((TILE, count), BF16),
            pltpu.VMEM((2, TILE, dpre.shape[1]), BF16),
            pltpu.VMEM((half, TILE, dpre.shape[1]), BF16),
            pltpu.VMEM((half, TILE, dpre.shape[1]), BF16),
            pltpu.SemaphoreType.DMA((2,)),
            pltpu.SemaphoreType.DMA((2,)),
            pltpu.SemaphoreType.DMA((2, max(2, columns))),
            pltpu.SemaphoreType.DMA((half,)),
            pltpu.SemaphoreType.DMA((half,)),
            pltpu.VMEM((DEEP,) + chunk, BF16),
            pltpu.SemaphoreType.DMA((DEEP,)),
        ]
        + LineSum.scratch(size, chunk),
        compiler_params=pltpu.CompilerParams(
            collective_id=5, has_side_effects=True, vmem_limit_bytes=60 * 2**20
        ),
        cost_estimate=lasting(78),
        name="scatter_blocks",
    )(parts, tokens, dpre, hidden, cotangents)
    return results[0], results[1 : 1 + columns], results[1 + columns :]


def adam_step(weight, grad, first, second, rate, decay=0.1):
    first_new = 0.9 * first + 0.1 * grad
    second_new = 0.95 * second + 0.05 * grad * grad
    corrected_one = first_new / (1.0 - 0.9**STEP)
    corrected_two = second_new / (1.0 - 0.95**STEP)
    weight_new = weight - rate * (
        corrected_one / (jnp.sqrt(corrected_two) + 1e-08) + decay * weight
    )
    return (first_new, second_new, weight_new)


SMALL_SUMS = (1, 4, 3, 2, 0)
NARROW = 1


def end_kernel(size, steps, columns, count, *refs):
    take = lambda number: (refs[:number], refs[number:])
    part_refs, refs = take(count)
    (value_ref, seq_ref), refs = take(2)
    out_refs, refs = take(count)
    (total_ref, small_ref, rows_ref), refs = take(3)
    (landed, half_now, half_in, quarter, quarter_in, seq_half, seq_sent, seq_in), refs = take(8)
    (t_send, t_recv, s_send, s_recv, q_send, q_recv), scratch = take(6)
    out_ref = out_refs[NARROW]
    grid = Grid(size)
    row, col = lax.axis_index("row"), lax.axis_index("col")

    def other(name, bit):
        place = lax.axis_index(name)
        return {name: place + bit * (1 - 2 * ((place // bit) % 2))}

    barrier = pltpu.get_barrier_semaphore()
    grid.greet(barrier)
    for name, bit in steps:
        pl.semaphore_signal(barrier, inc=1, device_id=other(name, bit), device_id_type=MESH_ID)
    for by in range(1, columns):
        pl.semaphore_signal(
            barrier, inc=1, device_id={"col": (col + by) % columns}, device_id_type=MESH_ID
        )
    pl.semaphore_wait(barrier, grid.count + len(steps) + columns - 1)

    seq_rows, block = seq_half.shape[0], rows_ref.shape[0]
    swap_rows = pltpu.make_async_remote_copy(
        src_ref=seq_ref.at[pl.ds(pl.multiple_of((1 - row) * seq_rows, 16), seq_rows)],
        dst_ref=seq_half,
        send_sem=q_send.at[0],
        recv_sem=q_recv.at[0],
        device_id={"row": 1 - row},
        device_id_type=MESH_ID,
    )
    swap_rows.start()

    total_ref[...] = value_ref[...]

    def exchange(number):
        name, bit = steps[number]
        copy = pltpu.make_async_remote_copy(
            src_ref=total_ref,
            dst_ref=landed.at[number],
            send_sem=t_send.at[number],
            recv_sem=t_recv.at[number],
            device_id=other(name, bit),
            device_id_type=MESH_ID,
        )
        copy.start()
        copy.wait()
        total_ref[...] += landed[number]

    early = len([1 for name, bit in steps if name == "dp" and bit < grid.across])
    for number in range(early):
        exchange(number)
    sums = [
        LineSum(grid, part_refs[number], out_refs[number], *scratch[7 * number : 7 * number + 7])
        for number in range(count)
    ]
    LineSum.start(sums)

    def both_rows(place):
        mine = seq_ref[pl.ds(pl.multiple_of(row * seq_rows + place * block, 16), block), :]
        theirs = seq_half[pl.ds(pl.multiple_of(place * block, 16), block), :]
        return mine.astype(F32) + theirs.astype(F32)

    swap_rows.wait()
    moves = []
    for by in range(1, columns):
        to = (col + by) % columns
        seq_sent[by - 1] = both_rows(to).astype(BF16)
        moves.append(
            pltpu.make_async_remote_copy(
                src_ref=seq_sent.at[by - 1],
                dst_ref=seq_in.at[by - 1],
                send_sem=q_send.at[by],
                recv_sem=q_recv.at[by],
                device_id={"col": to},
                device_id_type=MESH_ID,
            )
        )
    for number in range(early, len(steps)):
        exchange(number)
    for copy in moves:
        copy.start()
    rows_ref[...] = both_rows(col)
    half, fourth = half_now.shape[0], small_ref.shape[0]
    swap = pltpu.make_async_remote_copy(
        src_ref=half_now,
        dst_ref=half_in,
        send_sem=s_send.at[0],
        recv_sem=s_recv.at[0],
        device_id={"row": 1 - row},
        device_id_type=MESH_ID,
    )

    def swap_narrow():
        half_now[...] = out_ref[pl.ds(pl.multiple_of((1 - row) * half, 8), half), :]
        swap.start()

    LineSum.finish([sums[number] for number in SMALL_SUMS], after=swap_narrow)
    swap.wait()
    both = out_ref[pl.ds(pl.multiple_of(row * half, 8), half), :] + half_in[...]
    for place in range(columns):
        quarter[place] = both[place * fourth : (place + 1) * fourth]
    copies = []
    for by in range(1, columns):
        to = (col + by) % columns
        copies.append(
            pltpu.make_async_remote_copy(
                src_ref=quarter.at[to],
                dst_ref=quarter_in.at[by],
                send_sem=s_send.at[by],
                recv_sem=s_recv.at[by],
                device_id={"col": to},
                device_id_type=MESH_ID,
            )
        )
        copies[-1].start()
    small_ref[...] = quarter[col]
    for by, copy in enumerate(moves):
        copy.wait()
        rows_ref[...] += seq_in[by].astype(F32)
    for by, copy in enumerate(copies):
        copy.wait()
        small_ref[...] += quarter_in[by + 1]


def scatter_end(parts, values, rows, shape):
    size, columns = shape["dp"], shape["col"]
    steps = partners(shape)
    parts = [part.reshape((size, -1, part.shape[1])) for part in parts]
    (length, narrow), count = parts[NARROW].shape[1:], len(parts)
    half, seq_rows = length // 2, rows.shape[0] // 2
    block = (seq_rows // columns, rows.shape[1])
    fourth = (columns, half // columns, narrow)
    return pl.pallas_call(
        functools.partial(end_kernel, size, steps, columns, count),
        out_shape=tuple(jax.ShapeDtypeStruct(part.shape[1:], F32) for part in parts)
        + (
            jax.ShapeDtypeStruct(values.shape, F32),
            jax.ShapeDtypeStruct(fourth[1:], F32),
            jax.ShapeDtypeStruct(block, F32),
        ),
        in_specs=[VM] * (count + 2),
        out_specs=(VM,) * (count + 3),
        scratch_shapes=[
            pltpu.VMEM((len(steps),) + values.shape, F32),
            pltpu.VMEM((half, narrow), F32),
            pltpu.VMEM((half, narrow), F32),
            pltpu.VMEM(fourth, F32),
            pltpu.VMEM(fourth, F32),
            pltpu.VMEM((seq_rows, rows.shape[1]), BF16),
            pltpu.VMEM((columns - 1,) + block, BF16),
            pltpu.VMEM((columns - 1,) + block, BF16),
            pltpu.SemaphoreType.DMA((len(steps),)),
            pltpu.SemaphoreType.DMA((len(steps),)),
            pltpu.SemaphoreType.DMA((columns,)),
            pltpu.SemaphoreType.DMA((columns,)),
            pltpu.SemaphoreType.DMA((columns,)),
            pltpu.SemaphoreType.DMA((columns,)),
        ]
        + sum([LineSum.scratch(size, part.shape[1:]) for part in parts], []),
        compiler_params=pltpu.CompilerParams(
            collective_id=3, has_side_effects=True, vmem_limit_bytes=60 * 2**20
        ),
        cost_estimate=lasting(125),
        name="scatter_end",
    )(*parts, values, rows)


def steps_kernel(mixer_ref, out_ref, up_ref, down_ref, small_ref, step_ref, *refs):
    (two_ref, mixture_ref, shared_ref), (hidden_ref, gain_ref, normed_ref, later_ref), refs = (
        refs[:3], refs[3:7], refs[7:]
    )
    ins, (result_ref, input_ref), outs = refs[:21], refs[21:23], refs[23:]
    result_ref[...] = (two_ref[...] + mixture_ref[...].astype(F32) + shared_ref[...]).astype(BF16)
    values = hidden_ref[...].astype(F32)
    scale = lax.rsqrt(jnp.sum(values * values, axis=1, keepdims=True) / values.shape[1] + 1e-05)
    weighted = normed_ref[...] * gain_ref[...]
    mean = jnp.sum(weighted * values, axis=1, keepdims=True) / values.shape[1]
    input_ref[...] = scale * weighted - values * scale * scale * scale * mean + later_ref[...]
    rate = MODEL_WIDTH ** (-0.5)
    weights, firsts, seconds = ins[0::3], ins[1::3], ins[2::3]

    def put(number, grad, rate, at=...):
        values = adam_step(weights[number][at], grad, firsts[number][at], seconds[number][at], rate)
        for place, value in enumerate(values):
            outs[3 * number + place][at] = value

    for head in range(weights[0].shape[0]):
        put(0, mixer_ref[:, 128 * head : 128 * (head + 1)], rate, head)
    put(1, step_ref[:, 2 * STATE :].T[0 : weights[1].shape[0]], rate)
    put(2, out_ref[...].T, INNER ** (-0.5))
    put(3, small_ref[:, 0 : 2 * STATE], rate)
    routes = small_ref[:, 2 * STATE :].T
    put(4, routes[ROUTER_AT : ROUTER_AT + weights[4].shape[0]], 0.5 * rate)
    put(5, up_ref[...], rate)
    put(6, down_ref[...], FF_S ** (-0.5))


def last_steps(grads, ends, arrays):
    whole = pl.BlockSpec()
    return pl.pallas_call(
        steps_kernel,
        out_shape=(
            jax.ShapeDtypeStruct(ends[0].shape, BF16),
            jax.ShapeDtypeStruct(ends[0].shape, F32),
        )
        + tuple(jax.ShapeDtypeStruct(array.shape, F32) for array in arrays),
        in_specs=[whole] * (13 + len(arrays)),
        out_specs=(whole,) * (2 + len(arrays)),
        compiler_params=pltpu.CompilerParams(vmem_limit_bytes=56 * 2**20),
        cost_estimate=lasting(10),
        name="last_steps",
    )(*grads, *ends, *arrays)


def shared_kernel(
    x_ref, g_ref, up_ref, down_ref, out_ref, dx_ref, *refs
):
    count = (len(refs) - 9) // 2
    up_outs, down_outs, refs = refs[:count], refs[count : 2 * count], refs[2 * count :]
    hid_ref, dpre_ref, turned, hid_turned, up_grad, down_grad, up_came, down_came, sems = refs
    row, col = lax.axis_index("row"), lax.axis_index("col")
    barrier = pltpu.get_barrier_semaphore()
    pl.semaphore_signal(barrier, inc=1, device_id={"row": 1 - row}, device_id_type=MESH_ID)
    x, g = x_ref[...], g_ref[...]
    pre = dot_f32(x, up_ref[...])
    asked = dot_t(g, down_ref[...])
    half = down_ref.shape[0]
    for part in range(half // 128):
        lanes = slice(128 * part, 128 * (part + 1))
        upper = slice(half + 128 * part, half + 128 * (part + 1))
        gate, up, want = pre[:, lanes], pre[:, upper], asked[:, lanes]
        sig = jax.nn.sigmoid(gate)
        act = gate * sig
        hid_ref[:, lanes] = (act * up).astype(BF16)
        dpre_ref[:, lanes] = (want * up * (sig * (1.0 + gate * (1.0 - sig)))).astype(BF16)
        dpre_ref[:, upper] = (want * act).astype(BF16)
    turned[...] = x.T
    hid_turned[...] = hid_ref[...].T
    pl.semaphore_wait(barrier, 1)
    copies = []
    for number, (left, right, grad, came) in enumerate(
        ((turned, dpre_ref, up_grad, up_came), (hid_turned, g_ref, down_grad, down_came))
    ):
        size, _, rows, _ = grad.shape
        pairs = 2 if size % 2 == 0 else 1
        for chunk in range(0, size, pairs):
            found = dot_f32(left[2 * rows * chunk : 2 * rows * (chunk + pairs), :], right[...]).astype(BF16)
            for at in range(pairs):
                for half_at in range(2):
                    start = (2 * at + half_at) * rows
                    grad[chunk + at, half_at] = found[start : start + rows]
        copies.append(
            pltpu.make_async_remote_copy(
                src_ref=grad.at[:, 1 - row],
                dst_ref=came,
                send_sem=sems.at[number],
                recv_sem=sems.at[2 + number],
                device_id={"row": 1 - row},
                device_id_type=MESH_ID,
            )
        )
        copies[-1].start()
    out_ref[...] = dot_f32(hid_ref[...], down_ref[...])
    dx_ref[...] = dot_t(dpre_ref[...], up_ref[...])
    for copy, grad, came, outs in zip(copies, (up_grad, down_grad), (up_came, down_came), (up_outs, down_outs)):
        copy.wait()
        size, _, rows, _ = grad.shape
        part = rows // count
        for chunk in range(size):
            total = (grad[chunk, row].astype(F32) + came[chunk].astype(F32)).astype(BF16)
            for place in range(count):
                mine = total[place * part : (place + 1) * part]
                for by in range(count):
                    @pl.when(place == (col + by) % count)
                    def _():
                        outs[by][chunk] = mine


def shared_expert(tokens, cotangents, up, down, shape):
    size, columns = shape["dp"], shape["col"]
    rows, width = tokens.shape
    up_rows, down_rows = (array.shape[0] // (2 * columns * size) for array in (up, down))
    results = pl.pallas_call(
        shared_kernel,
        out_shape=(jax.ShapeDtypeStruct((rows, width), F32),) * 2
        + (jax.ShapeDtypeStruct((size, up_rows, up.shape[1]), BF16),) * columns
        + (jax.ShapeDtypeStruct((size, down_rows, width), BF16),) * columns,
        in_specs=[VM] * 4,
        out_specs=(VM,) * (2 + 2 * columns),
        scratch_shapes=[
            pltpu.VMEM((rows, down.shape[0]), BF16),
            pltpu.VMEM((rows, up.shape[1]), BF16),
            pltpu.VMEM((width, rows), BF16),
            pltpu.VMEM((down.shape[0], rows), BF16),
            pltpu.VMEM((size, 2, columns * up_rows, up.shape[1]), BF16),
            pltpu.VMEM((size, 2, columns * down_rows, width), BF16),
            pltpu.VMEM((size, columns * up_rows, up.shape[1]), BF16),
            pltpu.VMEM((size, columns * down_rows, width), BF16),
            pltpu.SemaphoreType.DMA((4,)),
        ],
        compiler_params=pltpu.CompilerParams(
            collective_id=6, has_side_effects=True, vmem_limit_bytes=58 * 2**20
        ),
        cost_estimate=lasting(20),
        name="shared_expert",
    )(tokens, cotangents, up, down)
    return results[0], results[1], results[2 : 2 + columns], results[2 + columns :]


def expert_block(own, x_ref, g_ref, named, up, down, router_ref, hid_ref, dpre_ref, mix_ref, dx_ref):
    x, g = x_ref[...], g_ref[...]
    logits = dot_f32(x, router_ref[...])
    high = jnp.max(jnp.where(named > 0, logits, -1e30), axis=1, keepdims=True)
    raised = jnp.where(named > 0, jnp.exp(logits - high), 0.0)
    gates = raised / jnp.sum(raised, axis=1, keepdims=True)
    rows = x.shape[0]
    lane = lax.broadcasted_iota(jnp.int32, (rows, 128), 1)
    weights = [
        jnp.sum(jnp.where(lane == own + part, gates, 0.0), axis=1, keepdims=True)
        for part in range(EXP_DEV)
    ]
    half = down.shape[0]
    pre = dot_f32(x, up)
    asked = dot_t(g, down)
    totals = [jnp.zeros((rows, 128), F32) for part in range(EXP_DEV)]
    for part in range(half // 128):
        which = 128 * part // FF_E
        at = 128 * part + FF_E * which
        lanes = slice(128 * part, 128 * (part + 1))
        lower, upper = slice(at, at + 128), slice(at + FF_E, at + FF_E + 128)
        gate, upper_pre, want = pre[:, lower], pre[:, upper], asked[:, lanes]
        sig = jax.nn.sigmoid(gate)
        act = gate * sig
        hidden = act * upper_pre
        totals[which] = totals[which] + hidden * want
        hid_ref[:, lanes] = (weights[which] * hidden).astype(BF16)
        dact = weights[which] * want
        dpre_ref[:, lower] = (dact * upper_pre * (sig * (1.0 + gate * (1.0 - sig)))).astype(BF16)
        dpre_ref[:, upper] = (dact * act).astype(BF16)
    mix_ref[...] = dot_f32(hid_ref[...], down).astype(BF16)
    dx_ref[:, :MODEL_WIDTH] = dot_t(dpre_ref[...], up).astype(BF16)
    sent = jnp.zeros((rows, 128), F32)
    for part in range(EXP_DEV):
        gate_grad = jnp.sum(totals[part], axis=1, keepdims=True)
        coarse = gate_grad.astype(BF16).astype(F32)
        sent = jnp.where(lane == own + part, coarse, sent)
        sent = jnp.where(lane == own + part + REST_AT, gate_grad - coarse, sent)
    dx_ref[:, MODEL_WIDTH:] = sent.astype(BF16)


def expert_kernel(
    size, columns, own_ref, g_ref, mask_ref, router_hbm, *refs
):
    places = 2 * columns
    up_parts, down_parts, kept_ref, refs = (
        refs[:places], refs[places : 2 * places], refs[2 * places], refs[2 * places + 1 :]
    )
    outs, (full_ref, g_now), stages, (up_ref, down_ref, router_ref) = (
        refs[:4], refs[4:6], refs[6:10], refs[10:13]
    )
    send_sem, recv_sem, local_sem, in_sem, out_sem, weight_sem = refs[13:]
    grid = Grid(size)
    me, z, x = grid.me, grid.z, grid.x
    barrier = pltpu.get_barrier_semaphore()
    grid.greet(barrier)
    pl.semaphore_wait(barrier, grid.count)

    def push(chunk, way, source=None):
        return pltpu.make_async_remote_copy(
            src_ref=full_ref.at[chunk] if source is None else source,
            dst_ref=full_ref.at[chunk],
            send_sem=send_sem.at[way, chunk],
            recv_sem=recv_sem.at[chunk],
            device_id={"dp": me + grid.steps[way]},
            device_id_type=MESH_ID,
        )

    def place(number):
        if grid.across == 2:
            even, first, last = 1 - number % 2, 1 - jnp.minimum(number, 1), number // 7
            step = (1 - even) * ((number + 1) // 2 - last) + even * (number // 2 - 1 + first)
            side = even * (1 - first) + last
        else:
            step, side = number % grid.deep, number // grid.deep
        return block_at(step, side)

    def block_at(step, side):
        zc = near_first(z, step, grid.deep)
        xc = near_first(x, side, grid.across)
        same = xc == x
        ways = (same & (zc >= z), same & (zc <= z), xc >= x, xc <= x)
        return zc * grid.across + xc, [way & there for way, there in zip(ways, grid.exists)]

    for way in range(4):
        @pl.when(grid.exists[way])
        def _():
            push(me, way, own_ref).start()
    row, col = lax.axis_index("row"), lax.axis_index("col")
    weights = [pltpu.make_async_copy(router_hbm, router_ref, weight_sem.at[2 * places])]
    for number in range(places):
        whose = row + (number // columns) * (1 - 2 * row)
        there = whose * columns + (col - number % columns + columns) % columns
        weights.append(
            pltpu.make_async_copy(up_parts[number], up_ref.at[there], weight_sem.at[number])
        )
        weights.append(
            pltpu.make_async_copy(
                down_parts[number], down_ref.at[:, there], weight_sem.at[places + number]
            )
        )
    for copy in weights:
        copy.start()
    keep = pltpu.make_async_copy(own_ref, full_ref.at[me], in_sem.at[1])
    keep.start()

    def leave(number, chunk):
        return [
            pltpu.make_async_copy(stage.at[number % 2], out.at[chunk], out_sem.at[place_in, number % 2])
            for place_in, (stage, out) in enumerate(zip(stages, outs))
        ]

    def work(number, _):
        chunk, onward = place(number)
        bring = pltpu.make_async_copy(g_ref.at[chunk], g_now, in_sem.at[0])
        bring.start()

        def pass_on(chunk, onward):
            push(chunk, 0).wait_recv()
            for way in range(4):
                @pl.when(onward[way])
                def _():
                    push(chunk, way).start()

        if grid.across == 2:
            inner = (z * (3 - z)) // 2
            for step, when in ((1, number == 1), (2, number == 3 - 2 * inner), (3, number == 5 - 2 * inner)):
                @pl.when(when)
                def _():
                    pass_on(*block_at(step, 0))

            @pl.when((number > 0) & (chunk % grid.across != x))
            def _():
                push(chunk, 0).wait_recv()
        else:
            @pl.when(number > 0)
            def _():
                pass_on(chunk, onward)

        @pl.when(number == 0)
        def _():
            keep.wait()
            for copy in weights:
                copy.wait()

        pltpu.make_async_copy(full_ref.at[chunk], kept_ref.at[chunk], local_sem.at[chunk]).start()

        @pl.when(number > 1)
        def _():
            for copy in leave(number, place(number - 2)[0]):
                copy.wait()

        bring.wait()
        experts_named = mask_ref[chunk].astype(F32)
        rest = jnp.zeros((128 - experts_named.shape[0], experts_named.shape[1]), F32)
        named = jnp.concatenate([experts_named, rest], axis=0).T
        expert_block(
            EXP_DEV * me, full_ref.at[chunk], g_now, named,
            up_ref[...].reshape(-1, up_ref.shape[2]), down_ref[...].reshape(-1, down_ref.shape[3]), router_ref,
            *[stage.at[number % 2] for stage in stages]
        )
        for copy in leave(number, chunk):
            copy.start()
        return 0

    lax.fori_loop(0, size, work, 0)
    for number in (size - 2, size - 1):
        for copy in leave(number, place(number)[0]):
            copy.wait()

    def finish(number, _):
        chunk, onward = place(number)
        pltpu.make_async_copy(full_ref.at[chunk], kept_ref.at[chunk], local_sem.at[chunk]).wait()
        for way in range(4):
            @pl.when(onward[way])
            def _():
                push(chunk, way).wait_send()
        return 0

    lax.fori_loop(0, size, finish, 0)


def experts(tokens, cotangents, masks, up_parts, down_parts, router, shape):
    size, columns = shape["dp"], shape["col"]
    places = 2 * columns
    rows, width = tokens.shape
    hidden = places * EXP_DEV * down_parts[0].shape[1]
    wide = width + 128
    wides = (hidden, 2 * hidden, width, wide)
    results = pl.pallas_call(
        functools.partial(expert_kernel, size, columns),
        out_shape=tuple(
            jax.ShapeDtypeStruct((size, rows, column), BF16) for column in (width,) + wides
        ),
        in_specs=[ANY, ANY, VM] + [ANY] * (1 + 2 * places),
        out_specs=(ANY,) * 5,
        scratch_shapes=[pltpu.VMEM((size, rows, width), BF16), pltpu.VMEM((rows, width), BF16)]
        + [pltpu.VMEM((2, rows, column), BF16) for column in wides]
        + [
            pltpu.VMEM((places,) + up_parts[0].shape, BF16),
            pltpu.VMEM((EXP_DEV, places) + down_parts[0].shape[1:], BF16),
            pltpu.VMEM(router.shape, BF16),
            pltpu.SemaphoreType.DMA((4, size)),
            pltpu.SemaphoreType.DMA((size,)),
            pltpu.SemaphoreType.DMA((size,)),
            pltpu.SemaphoreType.DMA((2,)),
            pltpu.SemaphoreType.DMA((4, 2)),
            pltpu.SemaphoreType.DMA((2 * places + 1,)),
        ],
        compiler_params=pltpu.CompilerParams(
            collective_id=4, has_side_effects=True, vmem_limit_bytes=56 * 2**20
        ),
        cost_estimate=lasting(85),
        name="experts",
    )(tokens, cotangents.reshape(size, rows, width), masks.reshape(size, -1, rows), router, *up_parts, *down_parts)
    return [result.reshape(size * rows, -1) for result in results]


def rms_scale(values):
    return lax.rsqrt(jnp.mean(values * values, axis=-1, keepdims=True) + 1e-05)


def rms_back(values, scale, gain, grad_normed):
    weighted = grad_normed * gain[None, :]
    grad_values = scale * weighted - values * scale**3 * jnp.mean(
        weighted * values, axis=-1, keepdims=True
    )
    gain_grad = jnp.sum(grad_normed * values * scale, axis=0)
    return (grad_values, gain_grad)


def silu_gate(pre_values):
    half_size = pre_values.shape[-1] // 2
    return jax.nn.silu(pre_values[..., :half_size]) * pre_values[..., half_size:]


def silu_gate_back(pre_values, grad):
    return jax.vjp(silu_gate, pre_values)[1](grad)[0]


ALL = ("dp", "row", "col")


def gather_dp(values):
    return lax.all_gather(values, "dp", axis=0, tiled=True)


def scatter_dp(values):
    return lax.psum_scatter(values, "dp", scatter_dimension=0, tiled=True)


def body(
    shape,
    hidden_in, segment_ids, routes, out_grad,
    vectors, vectors_first, vectors_second,
    in_weight, in_weight_first, in_weight_second,
    step_weight, step_weight_first, step_weight_second,
    out_weight, out_weight_first, out_weight_second,
    state_weight, state_weight_first, state_weight_second,
    router, router_first, router_second,
    shared_up, shared_up_first, shared_up_second,
    shared_down, shared_down_first, shared_down_second,
    expert_gate_up, expert_gate_up_first, expert_gate_up_second,
    expert_down, expert_down_first, expert_down_second,
):
    dp = lax.axis_index("dp")
    data_count = lax.axis_size("dp")
    seq_devices = lax.axis_size("row") * lax.axis_size("col")
    local_heads = in_weight.shape[1]
    width = 64 * local_heads
    head_start = lax.axis_index(("row", "col")) * local_heads
    own_tokens = hidden_in.shape[1]
    experts_all = router.shape[1]
    rows_dp = in_weight.shape[0]
    seq_columns = shape["col"]
    residual = hidden_in[0].astype(F32)
    count = vectors.shape[0]
    lines = -(-count // 1024) * 8
    vector_rows = jnp.pad(vectors, (0, lines * 128 - count)).reshape(lines, 128)
    gain_one = vectors[0:MODEL_WIDTH]
    gain_two = vectors[MODEL_WIDTH : 2 * MODEL_WIDTH]

    scale_one = rms_scale(residual)
    route_ids = routes[0]
    chosen = (
        route_ids[:, :, None] == jnp.arange(experts_all, dtype=jnp.int32)[None, None, :]
    ).any(axis=1)
    grad_low = out_grad[0]
    (
        mixer_full, step_full, out_full, masks, shared_up_full, shared_down_full, small_full, normed_all,
        up_local, down_parts,
    ) = gather_start(
        hidden_in[0],
        vector_rows,
        in_weight.transpose(1, 0, 2),
        step_weight.T,
        out_weight.reshape(width, -1),
        shared_up,
        shared_down,
        state_weight,
        router.T,
        route_ids.T,
        expert_gate_up,
        expert_down,
        shape,
    )
    mixer_full, step_full, out_full, small_full, normed_all, segment_ids, grad_gone, up_local, down_parts = (
        lax.optimization_barrier(
            (mixer_full, step_full, out_full, small_full, normed_all, segment_ids, grad_low, up_local, down_parts)
        )
    )
    grad_all = gather_dp(grad_gone)
    up_parts = [up_local] + [shift(up_local, "col", by) for by in range(1, seq_columns)]
    state_step = jnp.concatenate([small_full[:, : 2 * STATE], step_full], axis=1)

    seg_rows = segment_ids[0].astype(F32).reshape(-1, 1, BLK)
    proj = dot_f32(normed_all, mixer_full).astype(BF16)
    ss = dot_f32(normed_all, state_step)
    valued, squares_part, kept, params = mixer_forward(proj, ss, seg_rows, vector_rows, seq_columns)
    partial_out = dot_t(valued, out_full).astype(BF16)
    partial_out, up_parts = lax.optimization_barrier((partial_out, up_parts))
    proj_out = scatter_rc(partial_out)
    other_row = lambda parts: parts + [shift(part, "row", 1) for part in parts]
    up_parts, down_parts = other_row(up_parts), other_row(down_parts)
    squares = scatter_squares(squares_part)[:, 0]
    scale_two = lax.rsqrt(squares / INNER + 1e-05)
    residual_two = residual + scale_two[:, None] * proj_out
    scale_three = rms_scale(residual_two)
    normed_two = (residual_two * scale_three * gain_two[None, :]).astype(BF16)

    router_wide = small_full[:, 2 * STATE :]
    router_full = router_wide[:, :experts_all]
    shared_out, shared_dx, shared_up_sums, shared_down_sums = shared_expert(
        normed_two, grad_low, shared_up_full, shared_down_full, shape
    )
    normed_two, grad_all, shared_dx, shared_out = lax.optimization_barrier(
        (normed_two, grad_all, shared_dx, shared_out)
    )
    from_columns = lambda parts: [
        shift(parts[by], "col", by) for by in range(1, seq_columns)
    ]
    shared_up_came, shared_down_came = from_columns(shared_up_sums), from_columns(shared_down_sums)
    tokens_all, hidden_low, pre_grad, mixed, rows_grad = experts(
        normed_two, grad_all, masks, up_parts, down_parts, router_wide, shape
    )
    logits = dot_f32(normed_two, router_full)
    gate_all = jax.nn.softmax(jnp.where(chosen, logits, -jnp.inf), axis=-1)
    rows_grad, shared_up_came, shared_down_came = lax.optimization_barrier(
        (rows_grad, shared_up_came, shared_down_came)
    )
    add_all = lambda own, came: sum([part.astype(F32) for part in came], own.astype(F32)).astype(BF16)
    shared_up_part = add_all(shared_up_sums[0], shared_up_came).reshape(-1, 2 * FF_S)
    shared_down_part = add_all(shared_down_sums[0], shared_down_came).reshape(-1, MODEL_WIDTH)
    routed_grad, up_grad, down_grad = scatter_blocks(
        rows_grad, tokens_all, pre_grad, hidden_low, grad_all, shape
    )
    routed_grad, mixed = lax.optimization_barrier((routed_grad, mixed))
    mixture = scatter_dp(mixed)
    gate_grad = (
        routed_grad[:, MODEL_WIDTH : MODEL_WIDTH + experts_all]
        + routed_grad[:, MODEL_WIDTH + REST_AT : MODEL_WIDTH + REST_AT + experts_all]
    )
    cotangent = grad_low.astype(F32)
    normed_two_grad = shared_dx + routed_grad[:, :MODEL_WIDTH]
    logits_grad = gate_all * (gate_grad - jnp.sum(gate_all * gate_grad, axis=1, keepdims=True))
    logits_low = jnp.where(chosen, logits_grad, 0.0).astype(BF16)
    normed_two_grad = normed_two_grad + dot_t(logits_low, router_full)
    router_grad = dot_tn(normed_two, logits_low)
    residual_two_grad, gain_two_grad = rms_back(
        residual_two, scale_three, gain_two, normed_two_grad
    )
    residual_two_grad = residual_two_grad + cotangent
    proj_out_grad = (residual_two_grad * scale_two[:, None]).astype(BF16)
    squares_grad = (
        jnp.sum(residual_two_grad * proj_out, axis=1) * -0.5 * scale_two**3 / INNER
    )
    squares_high = squares_grad.astype(BF16)
    squares_rest = (squares_grad - squares_high.astype(F32)).astype(BF16)
    riding = jnp.pad(jnp.stack([squares_high, squares_rest], axis=1), ((0, 0), (0, 126)))
    riders = jnp.concatenate([proj_out_grad, riding], axis=1)
    riders, up_grad, down_grad = lax.optimization_barrier((riders, up_grad, down_grad))
    riders = gather_rc(riders)
    proj_grad_all = riders[:, :MODEL_WIDTH]
    squares_grad_all = jnp.sum(riders[:, MODEL_WIDTH:].astype(F32), axis=1, keepdims=True)
    proj_grad_all, up_grad, down_grad = lax.optimization_barrier((proj_grad_all, up_grad, down_grad))
    sum_all = lambda parts: sum([part.astype(F32) for part in from_columns(parts)], parts[0].astype(F32))
    up_total, down_total = sum_all(up_grad), sum_all(down_grad)
    up_total = jnp.stack(
        [up_total[:, 2 * FF_E * held : 2 * FF_E * (held + 1)] for held in range(EXP_DEV)]
    )
    new_up = adam_step(
        expert_gate_up, up_total, expert_gate_up_first, expert_gate_up_second, MODEL_WIDTH ** (-0.5)
    )
    new_down = adam_step(
        expert_down, down_total.reshape(expert_down.shape), expert_down_first, expert_down_second, FF_E ** (-0.5)
    )

    valued_grad = dot_f32(proj_grad_all, out_full).astype(BF16)
    out_grad_t = dot_tn(proj_grad_all, valued).astype(BF16)
    proj_grad, ss_grad, vector_grad = mixer_backward(
        proj, ss, seg_rows, params, valued_grad, squares_grad_all, kept, lines, seq_columns
    )
    normed_part = dot_t(proj_grad, mixer_full) + dot_t(ss_grad, state_step)
    gain_one_grad = jnp.sum(normed_part * normed_all.astype(F32), axis=0) / gain_one
    router_wide = jnp.pad(
        router_grad, ((0, 0), (2 * STATE + ROUTER_AT, 128 - ROUTER_AT - experts_all))
    )
    mixer_grad = dot_tn(normed_all, proj_grad).astype(BF16)
    small_grad = (dot_tn(normed_all, ss_grad) + router_wide).astype(BF16)
    gains = jnp.concatenate([gain_one_grad, gain_two_grad]).reshape(-1, 128)
    vector_lines = vector_grad + jnp.pad(gains, ((0, lines - gains.shape[0]), (0, 0)))
    mixture, mixer_grad, new_up, new_down = lax.optimization_barrier(
        (mixture, mixer_grad, new_up, new_down)
    )
    (
        mixer_total, small_rows, out_total, shared_up_total, shared_down_total,
        vector_total, small_total, normed_grad,
    ) = scatter_end(
        (mixer_grad, small_grad, out_grad_t, shared_up_part, shared_down_part),
        vector_lines,
        normed_part.astype(BF16),
        shape,
    )
    vector_total = vector_total.reshape(-1)[:count]
    heads_first = lambda array: array.transpose(1, 0, 2)
    flat_out = lambda array: array.reshape(width, -1)
    hidden_out, input_grad, *news = last_steps(
        (
            mixer_total, out_total, shared_up_total, shared_down_total, small_total,
            small_rows,
        ),
        (
            residual_two, mixture, shared_out,
            hidden_in[0], gain_one[None, :], normed_grad, residual_two_grad,
        ),
        (
            *map(heads_first, (in_weight, in_weight_first, in_weight_second)),
            step_weight.T, step_weight_first.T, step_weight_second.T,
            *map(flat_out, (out_weight, out_weight_first, out_weight_second)),
            state_weight, state_weight_first, state_weight_second,
            router.T, router_first.T, router_second.T,
            shared_up, shared_up_first, shared_up_second,
            shared_down, shared_down_first, shared_down_second,
        ),
    )
    return (
        hidden_out[None],
        input_grad[None],
        *adam_step(vectors, vector_total, vectors_first, vectors_second, 0.3, 0.0),
        *map(heads_first, news[0:3]),
        *[array.T for array in news[3:6]],
        *[array.reshape(out_weight.shape) for array in news[6:9]],
        *news[9:12],
        *[array.T for array in news[12:15]],
        *news[15:],
        *new_up,
        *new_down,
    )


def solution(mesh):
    tokens = P("dp", ("row", "col"), None)
    by_head = P("dp", ("row", "col"))
    out_spec = P(("row", "col"), None, "dp")
    flat = P(ALL, None)
    weights = (
        (P(),) * 3
        + (tokens,) * 3
        + (by_head,) * 3
        + (out_spec,) * 3
        + (flat,) * 12
        + (tokens,) * 6
    )
    return jax.shard_map(
        functools.partial(body, dict(mesh.shape)),
        mesh=mesh,
        in_specs=(tokens, P("dp", None), tokens, tokens) + weights,
        out_specs=(tokens, tokens) + weights,
        check_vma=False,
    )
```

```python
import functools

import jax
import jax.numpy as jnp
from jax import lax
from jax.experimental import pallas as pl
from jax.experimental.pallas import tpu as pltpu
from jax.sharding import PartitionSpec as P

STATE = 128
KW = 4
BLK = 128
F32 = jnp.float32
BF16 = jnp.bfloat16


def dot_f32(a, b, dims=(((1,), (0,)), ((), ()))):
    return lax.dot_general(a, b, dims, preferred_element_type=F32)


def dot_exact(a, b, dims=(((1,), (0,)), ((), ()))):
    return lax.dot_general(
        a, b, dims, precision=lax.Precision.HIGHEST, preferred_element_type=F32
    )


def spread(values, width):
    rows = values.shape[0]
    low = lax.broadcasted_iota(jnp.int32, (rows, 128), 1) < 64
    parts = []
    for pair in range(width // 128):
        left = jnp.broadcast_to(values[:, 2 * pair : 2 * pair + 1], (rows, 128))
        right = jnp.broadcast_to(values[:, 2 * pair + 1 : 2 * pair + 2], (rows, 128))
        parts.append(jnp.where(low, left, right))
    return jnp.concatenate(parts, axis=1)


def head_sums(values):
    width = values.shape[1]
    ones = (
        lax.broadcasted_iota(jnp.int32, (width, 128), 0) // 64
        == lax.broadcasted_iota(jnp.int32, (width, 128), 1)
    ).astype(BF16)
    high = values.astype(BF16)
    rest = (values - high.astype(F32)).astype(BF16)
    return dot_f32(high, ones) + dot_f32(rest, ones)


def apart(values):
    low = lax.broadcasted_iota(jnp.int32, (values.shape[0], 128), 1) < 64
    gates, inputs = [], []
    for at in range(0, values.shape[1], 256):
        one, two = values[:, at : at + 128], values[:, at + 128 : at + 256]
        gates.append(jnp.where(low, one, pltpu.roll(two, 64, 1)))
        inputs.append(jnp.where(low, pltpu.roll(one, 64, 1), two))
    return jnp.concatenate(gates, axis=1), jnp.concatenate(inputs, axis=1)


def together(gates, inputs):
    low = lax.broadcasted_iota(jnp.int32, (gates.shape[0], 128), 1) < 64
    parts = []
    for at in range(0, gates.shape[1], 128):
        one, two = gates[:, at : at + 128], inputs[:, at : at + 128]
        parts.append(jnp.where(low, one, pltpu.roll(two, 64, 1)))
        parts.append(jnp.where(low, pltpu.roll(one, 64, 1), two))
    return jnp.concatenate(parts, axis=1)


def block_masks(index, seg_ref):
    now = seg_ref[index]
    before = jnp.where(index > 0, seg_ref[jnp.maximum(index - 1, 0)], -1.0)
    lane = lax.broadcasted_iota(jnp.int32, (1, BLK), 1)
    rows = [now]
    for back in range(1, KW):
        earlier = jnp.where(lane < back, pltpu.roll(before, back, 1), pltpu.roll(now, back, 1))
        rows.append((earlier == now).astype(F32))
    last, prior = now[:, BLK - 1 :], before[:, BLK - 1 :]
    rows.append((now == prior).astype(F32))
    rows.append((now == last).astype(F32))
    rows.append(jnp.broadcast_to((prior == last).astype(F32), (1, BLK)))
    rows.append(jnp.zeros((BLK - len(rows), BLK), F32))
    return jnp.concatenate(rows, axis=0).T


def block_common(width, start, index, proj_ref, ss_ref, seg_ref, par_ref):
    rows = pl.ds(start, BLK)
    before = pl.ds(pl.multiple_of(jnp.maximum(start - 8, 0), 8), 8)
    aux = block_masks(index, seg_ref)
    gate, inner = apart(proj_ref[rows, :].astype(F32))
    current = jnp.concatenate([inner, ss_ref[rows, 0 : 2 * STATE]], axis=1)
    earlier = proj_ref[pl.ds(pl.multiple_of(jnp.maximum(start - 16, 0), 16), 16), :]
    previous = jnp.concatenate(
        [apart(earlier.astype(F32)[8:])[1], ss_ref[before, 0 : 2 * STATE]], axis=1
    )
    extended = jnp.concatenate([previous, current], axis=0)
    taps = par_ref[0:KW, :]
    conv = par_ref[KW : KW + 1, :] + taps[KW - 1 : KW, :] * current
    shifted = []
    for back in range(1, KW):
        moved = pltpu.roll(extended, back, 0)[8:] * aux[:, back : back + 1]
        shifted.append(moved)
        conv = conv + taps[KW - 1 - back : KW - back, :] * moved
    sig = jax.nn.sigmoid(conv)
    active = conv * sig
    inputs_x = active[:, :width]
    matrix_b = active[:, width : width + STATE].astype(BF16)
    matrix_c = active[:, width + STATE :].astype(BF16)
    step_in = ss_ref[rows, 2 * STATE :] + par_ref[7:8, 0:128]
    dt = jnp.maximum(step_in, 0.0) + jnp.log1p(jnp.exp(-jnp.abs(step_in)))
    decay = dt * par_ref[6:7, 0:128]
    row_id = lax.broadcasted_iota(jnp.int32, (BLK, BLK), 0)
    col_id = lax.broadcasted_iota(jnp.int32, (BLK, BLK), 1)
    lower = (row_id >= col_id).astype(F32)
    cum = dot_exact(lower, decay)
    cum_t = cum.T
    same = (aux[:, 0:1] == seg_ref[pl.ds(index, 1), 0, :]) & (row_id >= col_id)
    last = cum[BLK - 1 : BLK, :]
    gain_in = jnp.exp(cum) * aux[:, 4:5]
    tail = jnp.exp(last - cum) * aux[:, 5:6]
    carry = jnp.exp(last) * aux[BLK - 1 : BLK, 6:7]
    scores = jnp.where(same, dot_f32(matrix_c, matrix_b, (((1,), (1,)), ((), ()))), 0.0)
    dt_wide = spread(dt, width)
    moved_x = inputs_x * dt_wide
    return dict(
        rows=rows, aux=aux, gate=gate, current=current, shifted=shifted, conv=conv, sig=sig,
        x=inputs_x, b=matrix_b, c=matrix_c, step_in=step_in, dt=dt, cum=cum, cum_t=cum_t,
        same=same, scores=scores, dt_wide=dt_wide, u=moved_x, lower=lower,
        gain_in=spread(gain_in, width), tail=spread(tail, width),
        carry=spread(jnp.broadcast_to(carry, (8, 128)), width)[0:1],
    )


def split_pair(values):
    low = lax.broadcasted_iota(jnp.int32, values.shape, 1) < 64
    zero = jnp.zeros_like(values)
    return jnp.where(low, values, zero), jnp.where(low, zero, values)


GAIN_AT, BIAS_AT, TAPS_AT, HEADS_AT = 24, 48, 74, 178
INNER_LINES, TAP_LINES = 24, 26


def own_place(columns):
    return lax.axis_index("row") * columns + lax.axis_index("col")


def read_params(width, columns, vec_ref, par_ref):
    lines, heads = width // 128, width // 64
    place = own_place(columns)

    def line(at):
        return jnp.concatenate(
            [vec_ref[pl.ds(at + place * lines + one, 1), :] for one in range(lines)], axis=1
        )

    def wide_line(at):
        rest = at + INNER_LINES
        return jnp.concatenate(
            [line(at), vec_ref[rest : rest + 1, :], vec_ref[rest + 1 : rest + 2, :]], axis=1
        )

    par_ref[...] = jnp.zeros_like(par_ref)
    for tap in range(KW):
        par_ref[tap : tap + 1, :] = wide_line(TAPS_AT + TAP_LINES * tap)
    par_ref[KW : KW + 1, :] = wide_line(BIAS_AT)
    par_ref[5:6, 0:width] = line(GAIN_AT)
    flat = jnp.concatenate([vec_ref[HEADS_AT : HEADS_AT + 1, :], vec_ref[HEADS_AT + 1 : HEADS_AT + 2, :]], axis=1)
    flat = jnp.broadcast_to(flat, (8, 256))
    lane = lax.broadcasted_iota(jnp.int32, (8, 128), 1)

    def per_head(which):
        turned = pltpu.roll(flat, 256 - 48 * which - place * heads, 1)[:, 0:128]
        return jnp.where(lane < heads, turned, 0.0)

    par_ref[6:7, 0:128] = jnp.where(lane < heads, -jnp.exp(per_head(0)), 0.0)[0:1]
    par_ref[7:8, 0:128] = per_head(2)[0:1]
    par_ref[8:9, 0:width] = spread(per_head(1), width)[0:1]


def write_params(width, columns, sums, par_ref, vec_ref):
    lines, heads = width // 128, width // 64
    place = own_place(columns)
    vec_ref[...] = jnp.zeros_like(vec_ref)
    total = lambda at: jnp.sum(sums[at : at + 8, :], axis=0, keepdims=True)

    def line(at, row):
        for one in range(lines):
            vec_ref[pl.ds(at + place * lines + one, 1), :] = row[:, 128 * one : 128 * (one + 1)]

    def wide_line(at, row):
        line(at, row)
        rest = at + INNER_LINES
        vec_ref[rest : rest + 1, :] = row[:, width : width + 128]
        vec_ref[rest + 1 : rest + 2, :] = row[:, width + 128 :]

    for tap in range(KW):
        wide_line(TAPS_AT + TAP_LINES * tap, total(8 * tap))
    wide_line(BIAS_AT, total(32))
    line(GAIN_AT, total(48))
    skips = jnp.sum(head_sums(sums[64:72, 0:width]), axis=0, keepdims=True)
    decays = total(56)[:, 0:128] * par_ref[6:7, 0:128]
    flat = jnp.zeros((8, 256), F32)
    lane = lax.broadcasted_iota(jnp.int32, (8, 256), 1)
    for which, row in enumerate((decays, skips, total(72)[:, 0:128])):
        row = jnp.broadcast_to(jnp.concatenate([row, jnp.zeros((1, 128), F32)], axis=1), (8, 256))
        flat = flat + pltpu.roll(jnp.where(lane < heads, row, 0.0), 48 * which + place * heads, 1)
    vec_ref[HEADS_AT : HEADS_AT + 1, :] = flat[0:1, 0:128]
    vec_ref[HEADS_AT + 1 : HEADS_AT + 2, :] = flat[0:1, 128:]


def forward_kernel(
    width, columns, proj_ref, ss_ref, seg_ref, vec_ref, valued_ref, squares_ref, kept_ref, par_ref, state
):
    blocks = proj_ref.shape[0] // BLK
    state[...] = jnp.zeros_like(state)
    read_params(width, columns, vec_ref, par_ref)

    def step(index, _):
        start = pl.multiple_of(index * BLK, BLK)
        got = block_common(width, start, index, proj_ref, ss_ref, seg_ref, par_ref)
        kept_ref[index] = state[...]
        moved = got["u"].astype(BF16)
        parts = []
        for pair in range(width // 128):
            u0, u1 = split_pair(moved[:, 128 * pair : 128 * (pair + 1)])
            mixes = []
            for head in (2 * pair, 2 * pair + 1):
                differ = jnp.minimum(got["cum"][:, head : head + 1] - got["cum_t"][head : head + 1, :], 0.0)
                mixes.append((jnp.exp(differ) * got["scores"]).astype(BF16))
            parts.append(dot_f32(jnp.concatenate(mixes, axis=1), jnp.concatenate([u0, u1], axis=0)))
        within = jnp.concatenate(parts, axis=1)
        from_state = got["gain_in"] * dot_f32(got["c"], state[...].astype(BF16))
        scanned = within + from_state + par_ref[8:9, 0:width] * got["x"]
        state[...] = state[...] * got["carry"] + dot_f32(
            got["b"], (got["tail"] * got["u"]).astype(BF16), (((0,), (0,)), ((), ()))
        )
        gate = got["gate"]
        gated = scanned * (gate * jax.nn.sigmoid(gate))
        squares_ref[got["rows"], :] = jnp.sum(gated * gated, axis=1, keepdims=True)
        valued_ref[got["rows"], :] = (gated * par_ref[5:6, 0:width]).astype(BF16)
        return 0

    lax.fori_loop(0, blocks, step, 0)


def backward_kernel(
    width, columns, proj_ref, ss_ref, seg_ref, par_ref, vgrad_ref, dsq_ref, kept_ref,
    dproj_ref, dss_ref, dvec_ref, dstate, follow, ebuf, sums
):
    blocks = proj_ref.shape[0] // BLK
    dstate[...] = jnp.zeros_like(dstate)
    follow[...] = jnp.zeros_like(follow)
    sums[...] = jnp.zeros_like(sums)

    def fold(values):
        total = values[0:8]
        for part in range(1, BLK // 8):
            total = total + values[8 * part : 8 * part + 8]
        return total

    def step(count, _):
        index = blocks - 1 - count
        start = pl.multiple_of(index * BLK, BLK)
        got = block_common(width, start, index, proj_ref, ss_ref, seg_ref, par_ref)
        rows, aux = got["rows"], got["aux"]
        state_in = kept_ref[index]
        state_low = state_in.astype(BF16)
        moved = got["u"].astype(BF16)
        skip = par_ref[8:9, 0:width]
        gain = par_ref[5:6, 0:width]
        parts = []
        for pair in range(width // 128):
            u0, u1 = split_pair(moved[:, 128 * pair : 128 * (pair + 1)])
            mixes = []
            for head in (2 * pair, 2 * pair + 1):
                differ = jnp.minimum(got["cum"][:, head : head + 1] - got["cum_t"][head : head + 1, :], 0.0)
                level = jnp.exp(differ)
                ebuf[head] = level
                mixes.append((level * got["scores"]).astype(BF16))
            parts.append(dot_f32(jnp.concatenate(mixes, axis=1), jnp.concatenate([u0, u1], axis=0)))
        inner = jnp.concatenate(parts, axis=1) + got["gain_in"] * dot_f32(got["c"], state_low)
        scanned = inner + skip * got["x"]
        gate = got["gate"]
        gate_sig = jax.nn.sigmoid(gate)
        gate_act = gate * gate_sig
        gated = scanned * gate_act
        vgrad = vgrad_ref[rows, :].astype(F32)
        dgated = vgrad * gain + 2.0 * gated * dsq_ref[rows, :]
        sums[48:56, 0:width] += fold(vgrad * gated)
        dy = dgated * gate_act
        dgate = dgated * scanned * (gate_sig * (1.0 + gate * (1.0 - gate_sig)))
        dy_low = dy.astype(BF16)
        dscores = jnp.zeros((BLK, BLK), F32)
        parts = []
        for pair in range(width // 128):
            lanes = slice(128 * pair, 128 * (pair + 1))
            u0, u1 = split_pair(moved[:, lanes])
            d0, d1 = split_pair(dy_low[:, lanes])
            mixes = []
            for head, u_own in ((2 * pair, u0), (2 * pair + 1, u1)):
                level = ebuf[head]
                mixes.append((level * got["scores"]).astype(BF16))
                dscores = dscores + level * dot_f32(
                    dy_low[:, lanes], u_own, (((1,), (1,)), ((), ()))
                )
            parts.append(
                dot_f32(
                    jnp.concatenate(mixes, axis=0),
                    jnp.concatenate([d0, d1], axis=0),
                    (((0,), (0,)), ((), ())),
                )
            )
        du_within = jnp.concatenate(parts, axis=1)
        dscores = jnp.where(got["same"], dscores, 0.0).astype(BF16)
        dstate_now = dstate[...]
        dstate_low = dstate_now.astype(BF16)
        dy_in = (got["gain_in"] * dy).astype(BF16)
        u_tail = got["tail"] * got["u"]
        from_next = dot_f32(got["b"], dstate_low)
        du = du_within + got["tail"] * from_next
        dmat_c = dot_f32(dscores, got["b"]) + dot_f32(dy_in, state_low, (((1,), (1,)), ((), ())))
        dmat_b = dot_f32(dscores, got["c"], (((0,), (0,)), ((), ()))) + dot_f32(
            u_tail.astype(BF16), dstate_low, (((1,), (1,)), ((), ()))
        )
        tail_part = head_sums(u_tail * from_next)
        dcum = (
            head_sums(dy_low.astype(F32) * inner - moved.astype(F32) * du_within) - tail_part
        )
        kept_part = head_sums(fold(got["carry"] * dstate_now * state_in))
        at_last = jnp.sum(tail_part, axis=0, keepdims=True) + jnp.sum(kept_part, axis=0, keepdims=True)
        ddecay = dot_exact(got["lower"], dcum, (((0,), (0,)), ((), ()))) + at_last
        ddt = ddecay * par_ref[6:7, 0:128] + head_sums(du * got["x"])
        sums[56:64, 0:128] += fold(ddecay * got["dt"])
        sums[64:72, 0:width] += fold(dy * got["x"])
        dstep = ddt * jax.nn.sigmoid(got["step_in"])
        sums[72:80, 0:128] += fold(dstep)
        dstate[...] = dstate_now * got["carry"] + dot_f32(got["c"], dy_in, (((0,), (0,)), ((), ())))
        dactive = jnp.concatenate([skip * dy + du * got["dt_wide"], dmat_b, dmat_c], axis=1)
        sig, conv = got["sig"], got["conv"]
        dconv = dactive * (sig * (1.0 + conv * (1.0 - sig)))
        sums[32:40, :] += fold(dconv)
        sums[24:32, :] += fold(dconv * got["current"])
        dinput = par_ref[KW - 1 : KW, :] * dconv
        for back in range(1, KW):
            tap = KW - 1 - back
            sums[8 * tap : 8 * tap + 8, :] += fold(dconv * got["shifted"][back - 1])
            masked = dconv * aux[:, back : back + 1]
            ext = jnp.concatenate([masked, follow[back - 1]], axis=0)
            dinput = dinput + par_ref[tap : tap + 1, :] * pltpu.roll(ext, BLK + 8 - back, 0)[:BLK]
            follow[back - 1] = masked[0:8]
        dproj_ref[rows, :] = together(dgate, dinput[:, :width]).astype(BF16)
        dss_ref[rows, 0 : 2 * STATE] = dinput[:, width:].astype(BF16)
        dss_ref[rows, 2 * STATE :] = dstep.astype(BF16)
        return 0

    lax.fori_loop(0, blocks, step, 0)
    write_params(width, columns, sums, par_ref, dvec_ref)


VM = pl.BlockSpec(memory_space=pltpu.VMEM)


def lasting(micros):
    return pl.CostEstimate(flops=0, bytes_accessed=int(micros * 3.0e6), transcendentals=0)


def mixer_forward(proj, ss, seg, vec, columns):
    length, double = proj.shape
    width = double // 2
    blocks = length // BLK
    return pl.pallas_call(
        functools.partial(forward_kernel, width, columns),
        out_shape=(
            jax.ShapeDtypeStruct((length, width), BF16),
            jax.ShapeDtypeStruct((length, 1), F32),
            jax.ShapeDtypeStruct((blocks, STATE, width), F32),
            jax.ShapeDtypeStruct((16, width + 2 * STATE), F32),
        ),
        in_specs=[VM] * 4,
        out_specs=(VM,) * 4,
        scratch_shapes=[pltpu.VMEM((STATE, width), F32)],
        compiler_params=pltpu.CompilerParams(vmem_limit_bytes=56 * 2**20),
        cost_estimate=lasting(20),
        name="mixer_forward",
    )(proj, ss, seg, vec)


def mixer_backward(proj, ss, seg, par, vgrad, dsq, kept, lines, columns):
    length, double = proj.shape
    width = double // 2
    wide = width + 2 * STATE
    return pl.pallas_call(
        functools.partial(backward_kernel, width, columns),
        out_shape=(
            jax.ShapeDtypeStruct((length, 2 * width), BF16),
            jax.ShapeDtypeStruct((length, 3 * STATE), BF16),
            jax.ShapeDtypeStruct((lines, 128), F32),
        ),
        in_specs=[VM] * 7,
        out_specs=(VM,) * 3,
        scratch_shapes=[
            pltpu.VMEM((STATE, width), F32),
            pltpu.VMEM((KW - 1, 8, wide), F32),
            pltpu.VMEM((width // 64, BLK, BLK), F32),
            pltpu.VMEM((80, wide), F32),
        ],
        compiler_params=pltpu.CompilerParams(vmem_limit_bytes=56 * 2**20),
        cost_estimate=lasting(34),
        name="mixer_backward",
    )(proj, ss, seg, par, vgrad, dsq, kept)


MODEL_WIDTH = 1536
HEADS = 48
FF_E = 512
FF_S = 1024
TOPK = 6
STEP = 10
EXP_DEV = 2
INNER = 3072
ROUTER_AT = 64
REST_AT = 64


def dot_t(a, b):
    return dot_f32(a, b, (((1,), (1,)), ((), ())))


def dot_tn(a, b):
    return dot_f32(a, b, (((0,), (0,)), ((), ())))


def shift(values, axis, by):
    size = lax.axis_size(axis)
    return lax.ppermute(values, axis, [(i, (i + by) % size) for i in range(size)])


def all_places(own):
    rows, columns = lax.axis_index("row"), lax.axis_size("col")
    col = lax.axis_index("col")
    placed = []
    for by, part in enumerate(own):
        there = (col - by) % columns
        placed.append((rows * columns + there, part))
        placed.append(((1 - rows) * columns + there, shift(part, "row", 1)))
    return placed


def assemble(placed, group):
    count = len(placed)
    rows, columns = placed[0][1].shape
    total = jnp.zeros((group, count, rows // group, columns), placed[0][1].dtype)
    for place, part in placed:
        total = lax.dynamic_update_slice(
            total, part.reshape(group, 1, rows // group, columns), (0, place, 0, 0)
        )
    return total.reshape(count * rows, columns)


def gather_rc(values):
    columns = lax.axis_size("col")
    return assemble(
        all_places([values] + [shift(values, "col", by) for by in range(1, columns)]), 1
    )


def block_of(array, at, rows):
    return lax.dynamic_slice_in_dim(array, at * rows, rows)


def scatter_row(values, group=1):
    row = lax.axis_index("row")
    halves = values.reshape(group, 2, -1, values.shape[1])
    pick = lambda which: lax.dynamic_index_in_dim(halves, which, 1, keepdims=False)
    away = shift(pick(1 - row), "row", 1)
    return (pick(row).astype(F32) + away.astype(F32)).astype(values.dtype)


def scatter_col(kept):
    columns, col = lax.axis_size("col"), lax.axis_index("col")
    parts = kept.reshape(kept.shape[0], columns, -1, kept.shape[2])
    pick = lambda which: lax.dynamic_index_in_dim(parts, which, 1, keepdims=False)
    total = pick(col).astype(F32)
    for by in range(1, columns):
        total = total + shift(pick((col + by) % columns), "col", by).astype(F32)
    return total.reshape(-1, kept.shape[2])


def parts_of_columns(kept):
    columns, col = lax.axis_size("col"), lax.axis_index("col")
    parts = kept.reshape(kept.shape[0], columns, -1, kept.shape[2])
    pick = lambda which: lax.dynamic_index_in_dim(parts, which, 1, keepdims=False)
    return [pick((col + by) % columns).reshape(-1, kept.shape[2]) for by in range(columns)]


def scatter_rc(values):
    return scatter_col(scatter_row(values))


def scatter_squares(values):
    columns, col = lax.axis_size("col"), lax.axis_index("col")
    kept = scatter_row(values)[0]
    rows = kept.shape[0] // columns
    total = block_of(kept, col, rows)
    for by in range(1, columns):
        total = total + shift(block_of(kept, (col + by) % columns, rows), "col", by)
    return total


def partners(shape):
    steps = []
    for name in ("dp", "row", "col"):
        bit = 1
        while bit < shape[name]:
            steps.append((name, bit))
            bit *= 2
    return steps


DEEP = 4
MESH_ID = pl.DeviceIdType.MESH
ANY = pl.BlockSpec(memory_space=pl.ANY)


def near_first(place, step, size):
    if size == 1:
        return place
    if size == 2:
        return place + step * (1 - 2 * place)
    side = place // 2
    inner = (place * (3 - place)) // 2
    found = step + inner * (1 - 2 * step) * (1 - step // 2)
    return found + side * (3 - 2 * found)


class Grid:
    def __init__(self, size):
        self.size, self.deep, self.across = size, DEEP, size // DEEP
        self.me = lax.axis_index("dp")
        self.z, self.x = self.me // self.across, self.me % self.across
        self.steps = (-self.across, self.across, -1, 1)
        self.exists = (
            self.z > 0,
            self.z < self.deep - 1,
            self.x > 0,
            self.x < self.across - 1,
        )
        self.count = (
            jnp.minimum(self.z, 1)
            + jnp.minimum(self.deep - 1 - self.z, 1)
            + jnp.minimum(self.x, 1)
            + jnp.minimum(self.across - 1 - self.x, 1)
        )

    def greet(self, barrier):
        for there, step in zip(self.exists, self.steps):
            @pl.when(there)
            def _():
                pl.semaphore_signal(
                    barrier, inc=1, device_id={"dp": self.me + step}, device_id_type=MESH_ID
                )


def gather_kernel(size, columns, *refs):
    count = PLAIN + BOTH
    hidden_ref, vec_ref, in_ref, step_ref, out_ref, up_ref, down_ref, state_ref, router_ref = refs[:9]
    routes_ref, expert_up_ref, expert_down_ref, refs = refs[9], refs[10], refs[11], refs[12:]
    outs, lows, down_came, refs = (
        refs[: count + 1], refs[count + 1 : count + 3], refs[count + 3], refs[count + 4 :]
    )
    ins, refs = refs[: count + 1], refs[count + 1 :]
    step_wide, router_wide, refs = refs[0], refs[1], refs[2:]
    dp_send, dp_recv, sh_send, sh_recv, rc_send, rc_recv, keep_sem, side_send, side_recv = refs
    mixer, step, out, mask, up, down, small, tokens = ins
    states = state_ref.shape[1]
    grid = Grid(size)
    me, z, x = grid.me, grid.z, grid.x
    row, col = lax.axis_index("row"), lax.axis_index("col")
    mine, other_row = row * columns + col, {"row": 1 - row}
    to_col = lambda by: {"col": (col + by) % columns}
    from_col = lambda by: row * columns + (col + by) % columns
    barrier = pltpu.get_barrier_semaphore()
    grid.greet(barrier)
    pl.semaphore_signal(barrier, inc=1, device_id=other_row, device_id_type=MESH_ID)
    for by in range(1, columns):
        pl.semaphore_signal(barrier, inc=1, device_id=to_col(by), device_id_type=MESH_ID)
    pl.semaphore_wait(barrier, grid.count + columns)

    def block(which, chunk, place):
        return outs[which].at[chunk] if which < PLAIN else outs[which].at[chunk, place]

    def push(which, chunk, way, source=None):
        ref = block(which, chunk, mine)
        return pltpu.make_async_remote_copy(
            src_ref=ref if source is None else source,
            dst_ref=ref,
            send_sem=dp_send.at[which, way, chunk],
            recv_sem=dp_recv.at[which, chunk],
            device_id={"dp": me + grid.steps[way]},
            device_id_type=MESH_ID,
        )

    def spread(which, chunk, place, index, peer, source=None):
        ref = block(which, chunk, place)
        return pltpu.make_async_remote_copy(
            src_ref=ref if source is None else source,
            dst_ref=ref,
            send_sem=sh_send.at[which - PLAIN, index, chunk],
            recv_sem=sh_recv.at[which - PLAIN, place, chunk],
            device_id=peer,
            device_id_type=MESH_ID,
        )

    def spread_tokens(place, index, peer, source=None):
        ref = outs[count].at[place]
        return pltpu.make_async_remote_copy(
            src_ref=ref if source is None else source,
            dst_ref=ref,
            send_sem=rc_send.at[index],
            recv_sem=rc_recv.at[place],
            device_id=peer,
            device_id_type=MESH_ID,
        )

    def place_of(number):
        if grid.across == 2:
            even, first, last = 1 - number % 2, 1 - jnp.minimum(number, 1), number // 7
            step = (1 - even) * ((number + 1) // 2 - last) + even * (number // 2 - 1 + first)
            side = even * (1 - first) + last
        else:
            step, side = number % grid.deep, number // grid.deep
        zc = near_first(z, step, grid.deep)
        xc = near_first(x, side, grid.across)
        ways = [
            way & there for way, there in zip((zc >= z, zc <= z, xc >= x, xc <= x), grid.exists)
        ]
        same_x, same_z = xc == x, zc == z
        z_first = [same_x & ways[0], same_x & ways[1], ways[2], ways[3]]
        x_first = [ways[0], ways[1], same_z & ways[2], same_z & ways[3]]
        return zc * grid.across + xc, [
            x_first if which in X_FIRST else z_first for which in range(count)
        ]

    def spread_one(which, chunk, source=None):
        spread(which, chunk, mine, 0, other_row, source).start()
        for by in range(1, columns):
            spread(which, chunk, mine, by, to_col(by), source).start()

    def pass_on(number, _):
        chunk, onward = place_of(number)
        for which in SMALL_FIRST:
            push(which, chunk, 0).wait_recv()
            for way in range(4):
                @pl.when(onward[which][way])
                def _():
                    push(which, chunk, way).start()
            if which >= PLAIN:
                spread_one(which, chunk)
        return 0

    def push_own(first, last):
        for way in range(4):
            @pl.when(grid.exists[way])
            def _():
                for which in range(first, last):
                    push(which, me, way, ins[which]).start()

    for head in range(in_ref.shape[0]):
        mixer[:, 128 * head : 128 * (head + 1)] = in_ref[head].astype(BF16)
    push_own(0, 1)
    values = hidden_ref[...].astype(F32)
    gain = jnp.concatenate([vec_ref[line : line + 1, :] for line in range(values.shape[1] // 128)], axis=1)
    mean = jnp.sum(values * values, axis=1, keepdims=True) / values.shape[1]
    tokens[...] = (values * lax.rsqrt(mean + 1e-05) * gain).astype(BF16)
    spread_tokens(mine, 0, other_row, ins[count]).start()
    for by in range(1, columns):
        spread_tokens(mine, by, to_col(by), ins[count]).start()
    step_wide[...] = jnp.zeros_like(step_wide)
    step_wide[0 : step_ref.shape[0], :] = step_ref[...]
    router_wide[...] = jnp.zeros_like(router_wide)
    router_wide[0 : router_ref.shape[0], :] = router_ref[...]
    step[...] = step_wide[...].T.astype(BF16)
    out[...] = out_ref[...].T.astype(BF16)
    expert = lax.broadcasted_iota(jnp.int32, mask.shape, 0)
    named = expert == routes_ref[0:1, :]
    for route in range(1, TOPK):
        named = named | (expert == routes_ref[route : route + 1, :])
    mask[...] = jnp.where(named, 1.0, 0.0).astype(BF16)
    up[...] = up_ref[...].astype(BF16)
    down[...] = down_ref[...].astype(BF16)
    small[:, 0:states] = state_ref[...].astype(BF16)
    small[:, states:] = router_wide[...].T.astype(BF16)
    push_own(1, count)
    keeps = [
        pltpu.make_async_copy(ins[which], block(which, me, mine), keep_sem.at[which])
        for which in range(count)
    ]
    keeps.append(pltpu.make_async_copy(ins[count], outs[count].at[mine], keep_sem.at[count]))
    for copy in keeps:
        copy.start()
    for held in range(EXP_DEV):
        width = expert_up_ref.shape[2]
        lows[0][:, width * held : width * (held + 1)] = expert_up_ref[held].astype(BF16)
    lows[1][...] = expert_down_ref[...].astype(BF16)
    for by in range(1, columns):
        spread_tokens(from_col(by), columns - 1 + by, other_row).wait_recv()
        spread_tokens(from_col(by), columns - 1 + by, other_row).start()
    sides = [
        pltpu.make_async_remote_copy(
            src_ref=lows[1],
            dst_ref=down_came.at[by - 1],
            send_sem=side_send.at[by - 1],
            recv_sem=side_recv.at[by - 1],
            device_id=to_col(by),
            device_id_type=MESH_ID,
        )
        for by in range(1, columns)
    ]
    for copy in sides:
        copy.start()
    for which in range(PLAIN, count):
        spread_one(which, me, ins[which])
    lax.fori_loop(1, size, pass_on, 0)

    def forward_chunk(number, _):
        chunk = place_of(number)[0]
        for which in range(PLAIN, count):
            for by in range(1, columns):
                place = from_col(by)
                spread(which, chunk, place, columns - 1 + by, other_row).wait_recv()
                spread(which, chunk, place, columns - 1 + by, other_row).start()
        return 0

    lax.fori_loop(0, size, forward_chunk, 0)

    def finish(number, _):
        chunk, onward = place_of(number)
        for which in range(PLAIN, count):
            for by in range(columns):
                spread(which, chunk, (1 - row) * columns + (col + by) % columns, 0, other_row).wait_recv()
            for index in range(2 * columns - 1):
                spread(which, chunk, mine, index, other_row).wait_send()
        for way in range(4):
            for which in range(count):
                @pl.when(onward[which][way])
                def _():
                    push(which, chunk, way).wait_send()
        return 0

    lax.fori_loop(0, size, finish, 0)
    for by in range(columns):
        spread_tokens((1 - row) * columns + (col + by) % columns, 0, other_row).wait_recv()
    for index in range(2 * columns - 1):
        spread_tokens(mine, index, other_row).wait_send()
    for copy in keeps + sides:
        copy.wait()


PLAIN, BOTH = 4, 3
SMALL_FIRST = (3, 6, 1, 5, 4, 2, 0)
X_FIRST = (4,)


def gather_start(
    hidden, vec, in_weight, step, out_weight, shared_up, shared_down, state, router, routes, expert_up, expert_down, shape
):
    size, columns = shape["dp"], shape["col"]
    places, count = 2 * columns, PLAIN + BOTH
    heads, rows = in_weight.shape[:2]
    blocks = [
        (rows, 128 * heads),
        (rows, 128),
        (out_weight.shape[1], out_weight.shape[0]),
        (EXP_DEV * size, hidden.shape[0]),
        shared_up.shape,
        shared_down.shape,
        (state.shape[0], state.shape[1] + 128),
        hidden.shape,
    ]
    lead = [(size,)] * PLAIN + [(size, places)] * BOTH + [(places,)]
    results = pl.pallas_call(
        functools.partial(gather_kernel, size, columns),
        out_shape=tuple(jax.ShapeDtypeStruct(at + block, BF16) for at, block in zip(lead, blocks))
        + (
            jax.ShapeDtypeStruct((expert_up.shape[1], EXP_DEV * expert_up.shape[2]), BF16),
            jax.ShapeDtypeStruct(expert_down.shape, BF16),
            jax.ShapeDtypeStruct((columns - 1,) + expert_down.shape, BF16),
        ),
        in_specs=[VM] * 12,
        out_specs=(ANY,) * (count + 1) + (VM,) * 2 + (ANY,),
        scratch_shapes=[pltpu.VMEM(block, BF16) for block in blocks]
        + [
            pltpu.VMEM((128, rows), F32),
            pltpu.VMEM((128, state.shape[0]), F32),
            pltpu.SemaphoreType.DMA((count, 4, size)),
            pltpu.SemaphoreType.DMA((count, size)),
            pltpu.SemaphoreType.DMA((BOTH, 2 * columns - 1, size)),
            pltpu.SemaphoreType.DMA((BOTH, places, size)),
            pltpu.SemaphoreType.DMA((2 * columns - 1,)),
            pltpu.SemaphoreType.DMA((places,)),
            pltpu.SemaphoreType.DMA((count + 1,)),
            pltpu.SemaphoreType.DMA((columns - 1,)),
            pltpu.SemaphoreType.DMA((columns - 1,)),
        ],
        compiler_params=pltpu.CompilerParams(
            collective_id=2, has_side_effects=True, vmem_limit_bytes=58 * 2**20
        ),
        cost_estimate=lasting(105),
        name="gather_start",
    )(
        hidden, vec, in_weight, step, out_weight, shared_up, shared_down, state, router, routes, expert_up, expert_down
    )
    up, down, down_came = results[count + 1 :]
    return (
        *[result.reshape(-1, result.shape[-1]) for result in results[: count + 1]],
        up,
        [down] + [down_came[by - 1] for by in range(1, columns)],
    )


class LineSum:
    def __init__(
        self, grid, part_ref, out_ref, sums, from_x, from_z, x_send, x_recv, z_send, z_recv, own_ref=None
    ):
        self.grid, self.part_ref, self.out_ref, self.own_ref = grid, part_ref, out_ref, own_ref
        self.sums, self.from_x, self.from_z = sums, from_x, from_z
        self.x_send, self.x_recv, self.z_send, self.z_recv = x_send, x_recv, z_send, z_recv

    @staticmethod
    def scratch(size, chunk):
        pair = size == 2 * DEEP
        return [
            pltpu.VMEM((DEEP if pair else size,) + chunk, BF16),
            pltpu.VMEM((DEEP if pair else 2 * size,) + chunk, BF16),
            pltpu.VMEM((DEEP + 1,) + chunk, BF16),
            pltpu.SemaphoreType.DMA((size,)),
            pltpu.SemaphoreType.DMA((2 * size,)),
            pltpu.SemaphoreType.DMA((DEEP,)),
            pltpu.SemaphoreType.DMA((DEEP + 1,)),
        ]

    def sum_slot(self, line, there):
        return line if self.grid.across == 2 else line * self.grid.across + there

    def x_slot(self, line, there, way):
        return line if self.grid.across == 2 else way * self.grid.size + line * self.grid.across + there

    def along_x(self, line, there, way):
        grid = self.grid
        chunk = line * grid.across + there
        return pltpu.make_async_remote_copy(
            src_ref=self.part_ref.at[chunk] if grid.across == 2 else self.sums.at[self.sum_slot(line, there)],
            dst_ref=self.from_x.at[self.x_slot(line, there, way)],
            send_sem=self.x_send.at[chunk],
            recv_sem=self.x_recv.at[way * grid.size + chunk],
            device_id={"dp": grid.me + 2 * way - 1},
            device_id_type=MESH_ID,
        )

    def along_z(self, line, way, receiving):
        grid = self.grid
        end = grid.z if receiving else grid.z + 2 * way - 1
        slot = line if way else line + (1 - jnp.minimum(jnp.abs(line - end), 1)) * (grid.deep - line)
        return pltpu.make_async_remote_copy(
            src_ref=self.sums.at[self.sum_slot(line, grid.x)],
            dst_ref=self.from_z.at[slot],
            send_sem=self.z_send.at[line],
            recv_sem=self.z_recv.at[slot],
            device_id={"dp": grid.me + (2 * way - 1) * grid.across},
            device_id_type=MESH_ID,
        ), slot

    def collect(self, line):
        grid, out_ref, x = self.grid, self.out_ref, self.grid.x
        mine = self.part_ref[line * grid.across + x] if self.own_ref is None else self.own_ref[line]
        out_ref[...] = mine.astype(F32)
        for way, there in ((1, grid.exists[2]), (0, grid.exists[3])):
            @pl.when(there)
            def _():
                self.along_x(line, x, way).wait_recv()
                out_ref[...] += self.from_x[self.x_slot(line, x, way)].astype(F32)
        for way, comes in (
            (1, grid.exists[0] & (line >= grid.z)), (0, grid.exists[1] & (line <= grid.z))
        ):
            @pl.when(comes)
            def _():
                copy, slot = self.along_z(line, way, True)
                copy.wait_recv()
                out_ref[...] += self.from_z[slot].astype(F32)
        for way, toward in ((1, line > grid.z), (0, line < grid.z)):
            @pl.when(toward)
            def _():
                self.sums[self.sum_slot(line, x)] = out_ref[...].astype(BF16)
                self.along_z(line, way, False)[0].start()

    def wait_sent(self, line, there):
        grid, x = self.grid, self.grid.x
        for way in range(2):
            @pl.when((there > x) if way else (there < x))
            def _():
                self.along_x(line, there, way).wait_send()

            @pl.when((there == x) & ((line > grid.z) if way else (line < grid.z)))
            def _():
                self.along_z(line, way, False)[0].wait_send()

    @staticmethod
    def start(sums):
        grid = sums[0].grid
        x, across = grid.x, grid.across

        def away(number, _):
            line = near_first(grid.z, grid.deep - 1 - number // (across - 1), grid.deep)
            there = near_first(x, across - 1 - number % (across - 1), across)
            for one in sums:
                if across > 2:
                    held = one.sums.at[one.sum_slot(line, there)]
                    if one.own_ref is None:
                        held[...] = one.part_ref[line * across + there]
                    else:
                        pltpu.sync_copy(one.part_ref.at[line * across + there], held)
                for way, beyond in ((1, grid.exists[2]), (0, grid.exists[3])):
                    toward = (there > x) if way else (there < x)
                    if across > 2:
                        @pl.when(toward & beyond)
                        def _():
                            one.along_x(line, there, way).wait_recv()
                            held = one.sums.at[one.sum_slot(line, there)]
                            held[...] = (
                                held[...].astype(F32)
                                + one.from_x[one.x_slot(line, there, way)].astype(F32)
                            ).astype(BF16)
                    @pl.when(toward)
                    def _():
                        one.along_x(line, there, way).start()
            return 0

        lax.fori_loop(0, grid.deep * (across - 1), away, 0)

    @staticmethod
    def finish(sums, between=None, after=None):
        grid = sums[0].grid

        def collect(number, _):
            if between is not None:
                between(number)
            line = near_first(grid.z, grid.deep - 1 - number, grid.deep)
            for place, one in enumerate(sums):
                one.collect(line)
                if after is not None and place == 0:
                    @pl.when(number == grid.deep - 1)
                    def _():
                        after()
            return 0

        lax.fori_loop(0, grid.deep, collect, 0)
        def wait(number, _):
            line = near_first(grid.z, grid.deep - 1 - number // grid.across, grid.deep)
            there = near_first(grid.x, grid.across - 1 - number % grid.across, grid.across)
            for one in sums:
                one.wait_sent(line, there)
            return 0

        lax.fori_loop(0, grid.size, wait, 0)


TILE = 256


def scatter_kernel(size, columns, part_ref, x_ref, dpre_ref, hid_ref, g_ref, out_ref, *refs):
    up_refs, down_refs, refs = refs[:columns], refs[columns : 2 * columns], refs[2 * columns :]
    dpre_now, g_now, left, turned, stage, sent, came = refs[:7]
    whole_sem, left_sem, stage_sem, row_send, row_recv = refs[7:12]
    grid = Grid(size)
    row = lax.axis_index("row")
    barrier = pltpu.get_barrier_semaphore()
    grid.greet(barrier)
    pl.semaphore_signal(barrier, inc=1, device_id={"row": 1 - row}, device_id_type=MESH_ID)
    pl.semaphore_wait(barrier, grid.count + 1)
    own, own_sem = refs[12:14]
    sums = [LineSum(grid, part_ref, out_ref, *refs[14:], own_ref=own)]
    LineSum.start(sums)
    loads = [
        pltpu.make_async_copy(part_ref.at[line * grid.across + grid.x], own.at[line], own_sem.at[line])
        for line in range(DEEP)
    ]
    for copy in loads:
        copy.start()

    width = g_now.shape[1]
    part_rows = [columns_of[0].shape[0] for columns_of in (up_refs, down_refs)]
    ups, downs = (columns * rows // TILE for rows in part_rows)
    half = ups + downs
    bring_dpre = pltpu.make_async_copy(dpre_ref, dpre_now, whole_sem.at[0])
    bring_g = pltpu.make_async_copy(g_ref, g_now, whole_sem.at[1])
    begin, end = lambda copy: copy.start(), lambda copy: copy.wait()

    def bring(tile, do):
        whose = row + (1 - tile // half) * (1 - 2 * row)
        within = tile % half

        @pl.when((within < ups) & (tile < 2 * half))
        def _():
            at = pl.ds(pl.multiple_of((whose * ups + within) * TILE, TILE), TILE)
            do(pltpu.make_async_copy(x_ref.at[:, at], left.at[tile % 2], left_sem.at[tile % 2]))

        @pl.when((within >= ups) & (tile < 2 * half))
        def _():
            at = pl.ds(pl.multiple_of(((within - ups) * 2 + whose) * TILE, TILE), TILE)
            do(pltpu.make_async_copy(hid_ref.at[:, at], left.at[tile % 2], left_sem.at[tile % 2]))

    def push(within):
        return pltpu.make_async_remote_copy(
            src_ref=sent.at[within],
            dst_ref=came.at[within],
            send_sem=row_send.at[within],
            recv_sem=row_recv.at[within],
            device_id={"row": 1 - row},
            device_id_type=MESH_ID,
        )

    col = lax.axis_index("col")
    piece = TILE // columns
    up_piece = TILE // 2

    def leave(within, do):
        for at in range(0, TILE, up_piece):
            @pl.when((within >= 0) & (within < ups))
            def _():
                first = within * TILE + at
                whose = (first // part_rows[0] + columns - col) % columns
                rows = pl.ds(pl.multiple_of(first % part_rows[0], up_piece), up_piece)
                for by in range(columns):
                    @pl.when(whose == by)
                    def _():
                        do(
                            pltpu.make_async_copy(
                                stage.at[within % 2, pl.ds(at, up_piece)],
                                up_refs[by].at[rows],
                                stage_sem.at[within % 2, at // up_piece],
                            )
                        )

        for place in range(columns):
            @pl.when(within >= ups)
            def _():
                whose = (place + columns - col) % columns
                rows = pl.ds(pl.multiple_of((within - ups) * piece, piece), piece)
                for by in range(columns):
                    @pl.when(whose == by)
                    def _():
                        do(
                            pltpu.make_async_copy(
                                stage.at[within % 2, pl.ds(place * piece, piece), pl.ds(0, width)],
                                down_refs[by].at[rows],
                                stage_sem.at[within % 2, place],
                            )
                        )

    bring(0, begin)
    bring_dpre.start()
    bring_g.start()
    bring_dpre.wait()
    bring_g.wait()
    for copy in loads:
        copy.wait()

    def work(tile, _):
        within = tile % half
        bring(tile + 1, begin)
        bring(tile, end)

        @pl.when(tile >= half)
        def _():
            leave(within - 2, end)
            push(within).wait_recv()

        turned[...] = left[tile % 2].T
        for wanted, right in ((within < ups, dpre_now), (within >= ups, g_now)):
            for theirs in (True, False):
                @pl.when(wanted & ((tile < half) if theirs else (tile >= half)))
                def _():
                    for at in range(0, right.shape[1], 512):
                        lanes = slice(at, at + 512)
                        found = dot_f32(turned[...], right[:, lanes])
                        if theirs:
                            sent[within, :, lanes] = found.astype(BF16)
                        else:
                            stage[within % 2, :, lanes] = (
                                found + came[within, :, lanes].astype(F32)
                            ).astype(BF16)

        @pl.when(tile < half)
        def _():
            push(within).start()

        @pl.when(tile >= half)
        def _():
            leave(within, begin)

        return 0

    def between(number):
        done = [0, 2 * half * 2 // 5, 2 * half * 7 // 10, 2 * half * 7 // 10, 2 * half]
        bounds = [jnp.int32(0), jnp.int32(0)]
        for step in range(DEEP):
            now = 1 - jnp.minimum(jnp.abs(number - step), 1)
            bounds = [bounds[0] + now * done[step], bounds[1] + now * done[step + 1]]
        lax.fori_loop(bounds[0], bounds[1], work, 0)

    LineSum.finish(sums, between)
    leave(half - 2, end)
    leave(half - 1, end)

    def sent_all(within, _):
        push(within).wait_send()
        return 0

    lax.fori_loop(0, half, sent_all, 0)


def scatter_blocks(parts, tokens, dpre, hidden, cotangents, shape):
    size, width = shape["dp"], tokens.shape[1]
    if size > 2 * DEEP:
        up = scatter_row(dot_tn(tokens, dpre).astype(BF16))
        down = scatter_row(dot_tn(hidden, cotangents).astype(BF16), EXP_DEV)
        return scatter_dp(parts).astype(F32), parts_of_columns(up), parts_of_columns(down)
    columns = shape["col"]
    parts = parts.reshape((size, -1, parts.shape[1]))
    chunk, count = parts.shape[1:], tokens.shape[0]
    up_half, down_half = width // 2, hidden.shape[1] // 2
    half = (up_half + down_half) // TILE
    results = pl.pallas_call(
        functools.partial(scatter_kernel, size, columns),
        out_shape=(jax.ShapeDtypeStruct(chunk, F32),)
        + (jax.ShapeDtypeStruct((up_half // columns, dpre.shape[1]), BF16),) * columns
        + (jax.ShapeDtypeStruct((down_half // columns, width), BF16),) * columns,
        in_specs=[ANY] * 5,
        out_specs=(VM,) + (ANY,) * (2 * columns),
        scratch_shapes=[
            pltpu.VMEM(dpre.shape, BF16),
            pltpu.VMEM((count, width), BF16),
            pltpu.VMEM((2, count, TILE), BF16),
            pltpu.VMEM((TILE, count), BF16),
            pltpu.VMEM((2, TILE, dpre.shape[1]), BF16),
            pltpu.VMEM((half, TILE, dpre.shape[1]), BF16),
            pltpu.VMEM((half, TILE, dpre.shape[1]), BF16),
            pltpu.SemaphoreType.DMA((2,)),
            pltpu.SemaphoreType.DMA((2,)),
            pltpu.SemaphoreType.DMA((2, max(2, columns))),
            pltpu.SemaphoreType.DMA((half,)),
            pltpu.SemaphoreType.DMA((half,)),
            pltpu.VMEM((DEEP,) + chunk, BF16),
            pltpu.SemaphoreType.DMA((DEEP,)),
        ]
        + LineSum.scratch(size, chunk),
        compiler_params=pltpu.CompilerParams(
            collective_id=5, has_side_effects=True, vmem_limit_bytes=60 * 2**20
        ),
        cost_estimate=lasting(78),
        name="scatter_blocks",
    )(parts, tokens, dpre, hidden, cotangents)
    return results[0], results[1 : 1 + columns], results[1 + columns :]


def adam_step(weight, grad, first, second, rate, decay=0.1):
    first_new = 0.9 * first + 0.1 * grad
    second_new = 0.95 * second + 0.05 * grad * grad
    corrected_one = first_new / (1.0 - 0.9**STEP)
    corrected_two = second_new / (1.0 - 0.95**STEP)
    weight_new = weight - rate * (
        corrected_one / (jnp.sqrt(corrected_two) + 1e-08) + decay * weight
    )
    return (first_new, second_new, weight_new)


SMALL_SUMS = (1, 4, 3, 2, 0)
NARROW = 1


def end_kernel(size, steps, columns, count, *refs):
    take = lambda number: (refs[:number], refs[number:])
    part_refs, refs = take(count)
    (value_ref, seq_ref), refs = take(2)
    out_refs, refs = take(count)
    (total_ref, small_ref, rows_ref), refs = take(3)
    (landed, half_now, half_in, quarter, quarter_in, seq_half, seq_sent, seq_in), refs = take(8)
    (t_send, t_recv, s_send, s_recv, q_send, q_recv), scratch = take(6)
    out_ref = out_refs[NARROW]
    grid = Grid(size)
    row, col = lax.axis_index("row"), lax.axis_index("col")

    def other(name, bit):
        place = lax.axis_index(name)
        return {name: place + bit * (1 - 2 * ((place // bit) % 2))}

    barrier = pltpu.get_barrier_semaphore()
    grid.greet(barrier)
    for name, bit in steps:
        pl.semaphore_signal(barrier, inc=1, device_id=other(name, bit), device_id_type=MESH_ID)
    for by in range(1, columns):
        pl.semaphore_signal(
            barrier, inc=1, device_id={"col": (col + by) % columns}, device_id_type=MESH_ID
        )
    pl.semaphore_wait(barrier, grid.count + len(steps) + columns - 1)

    seq_rows, block = seq_half.shape[0], rows_ref.shape[0]
    swap_rows = pltpu.make_async_remote_copy(
        src_ref=seq_ref.at[pl.ds(pl.multiple_of((1 - row) * seq_rows, 16), seq_rows)],
        dst_ref=seq_half,
        send_sem=q_send.at[0],
        recv_sem=q_recv.at[0],
        device_id={"row": 1 - row},
        device_id_type=MESH_ID,
    )
    swap_rows.start()

    total_ref[...] = value_ref[...]

    def exchange(number, meanwhile=None):
        name, bit = steps[number]
        copy = pltpu.make_async_remote_copy(
            src_ref=total_ref,
            dst_ref=landed.at[number],
            send_sem=t_send.at[number],
            recv_sem=t_recv.at[number],
            device_id=other(name, bit),
            device_id_type=MESH_ID,
        )
        copy.start()
        if meanwhile is not None:
            meanwhile()
        copy.wait()
        total_ref[...] += landed[number]

    early = len([1 for name, bit in steps if name == "dp" and bit < grid.across])
    owns, own_sem, scratch = scratch[:count], scratch[count], scratch[count + 1 :]
    sums = [
        LineSum(
            grid,
            part_refs[number],
            out_refs[number],
            *scratch[7 * number : 7 * number + 7],
            own_ref=owns[number],
        )
        for number in range(count)
    ]
    for number in range(early - 1):
        exchange(number)
    exchange(early - 1, lambda: LineSum.start(sums))
    loads = [
        pltpu.make_async_copy(
            part_refs[number].at[line * grid.across + grid.x], owns[number].at[line], own_sem.at[number, line]
        )
        for line in range(DEEP)
        for number in range(count)
    ]
    for copy in loads:
        copy.start()

    def both_rows(place):
        mine = seq_ref[pl.ds(pl.multiple_of(row * seq_rows + place * block, 16), block), :]
        theirs = seq_half[pl.ds(pl.multiple_of(place * block, 16), block), :]
        return mine.astype(F32) + theirs.astype(F32)

    swap_rows.wait()
    moves = []
    for by in range(1, columns):
        to = (col + by) % columns
        seq_sent[by - 1] = both_rows(to).astype(BF16)
        moves.append(
            pltpu.make_async_remote_copy(
                src_ref=seq_sent.at[by - 1],
                dst_ref=seq_in.at[by - 1],
                send_sem=q_send.at[by],
                recv_sem=q_recv.at[by],
                device_id={"col": to},
                device_id_type=MESH_ID,
            )
        )
    for number in range(early, len(steps)):
        exchange(number)
    for copy in moves:
        copy.start()
    rows_ref[...] = both_rows(col)
    for copy in loads:
        copy.wait()
    half, fourth = half_now.shape[0], small_ref.shape[0]
    swap = pltpu.make_async_remote_copy(
        src_ref=half_now,
        dst_ref=half_in,
        send_sem=s_send.at[0],
        recv_sem=s_recv.at[0],
        device_id={"row": 1 - row},
        device_id_type=MESH_ID,
    )

    def swap_narrow():
        half_now[...] = out_ref[pl.ds(pl.multiple_of((1 - row) * half, 8), half), :]
        swap.start()

    LineSum.finish([sums[number] for number in SMALL_SUMS], after=swap_narrow)
    swap.wait()
    both = out_ref[pl.ds(pl.multiple_of(row * half, 8), half), :] + half_in[...]
    for place in range(columns):
        quarter[place] = both[place * fourth : (place + 1) * fourth]
    copies = []
    for by in range(1, columns):
        to = (col + by) % columns
        copies.append(
            pltpu.make_async_remote_copy(
                src_ref=quarter.at[to],
                dst_ref=quarter_in.at[by],
                send_sem=s_send.at[by],
                recv_sem=s_recv.at[by],
                device_id={"col": to},
                device_id_type=MESH_ID,
            )
        )
        copies[-1].start()
    small_ref[...] = quarter[col]
    for by, copy in enumerate(moves):
        copy.wait()
        rows_ref[...] += seq_in[by].astype(F32)
    for by, copy in enumerate(copies):
        copy.wait()
        small_ref[...] += quarter_in[by + 1]


def scatter_end(parts, values, rows, shape):
    size, columns = shape["dp"], shape["col"]
    steps = partners(shape)
    parts = [part.reshape((size, -1, part.shape[1])) for part in parts]
    (length, narrow), count = parts[NARROW].shape[1:], len(parts)
    half, seq_rows = length // 2, rows.shape[0] // 2
    block = (seq_rows // columns, rows.shape[1])
    fourth = (columns, half // columns, narrow)
    return pl.pallas_call(
        functools.partial(end_kernel, size, steps, columns, count),
        out_shape=tuple(jax.ShapeDtypeStruct(part.shape[1:], F32) for part in parts)
        + (
            jax.ShapeDtypeStruct(values.shape, F32),
            jax.ShapeDtypeStruct(fourth[1:], F32),
            jax.ShapeDtypeStruct(block, F32),
        ),
        in_specs=[ANY] * count + [VM] * 2,
        out_specs=(VM,) * (count + 3),
        scratch_shapes=[
            pltpu.VMEM((len(steps),) + values.shape, F32),
            pltpu.VMEM((half, narrow), F32),
            pltpu.VMEM((half, narrow), F32),
            pltpu.VMEM(fourth, F32),
            pltpu.VMEM(fourth, F32),
            pltpu.VMEM((seq_rows, rows.shape[1]), BF16),
            pltpu.VMEM((columns - 1,) + block, BF16),
            pltpu.VMEM((columns - 1,) + block, BF16),
            pltpu.SemaphoreType.DMA((len(steps),)),
            pltpu.SemaphoreType.DMA((len(steps),)),
            pltpu.SemaphoreType.DMA((columns,)),
            pltpu.SemaphoreType.DMA((columns,)),
            pltpu.SemaphoreType.DMA((columns,)),
            pltpu.SemaphoreType.DMA((columns,)),
        ]
        + [pltpu.VMEM((DEEP,) + part.shape[1:], BF16) for part in parts]
        + [pltpu.SemaphoreType.DMA((count, DEEP))]
        + sum([LineSum.scratch(size, part.shape[1:]) for part in parts], []),
        compiler_params=pltpu.CompilerParams(
            collective_id=3, has_side_effects=True, vmem_limit_bytes=60 * 2**20
        ),
        cost_estimate=lasting(125),
        name="scatter_end",
    )(*parts, values, rows)


def steps_kernel(mixer_ref, out_ref, up_ref, down_ref, small_ref, step_ref, *refs):
    (two_ref, mixture_ref, shared_ref), (hidden_ref, gain_ref, normed_ref, later_ref), refs = (
        refs[:3], refs[3:7], refs[7:]
    )
    ins, (result_ref, input_ref), outs = refs[:21], refs[21:23], refs[23:]
    result_ref[...] = (two_ref[...] + mixture_ref[...].astype(F32) + shared_ref[...]).astype(BF16)
    values = hidden_ref[...].astype(F32)
    scale = lax.rsqrt(jnp.sum(values * values, axis=1, keepdims=True) / values.shape[1] + 1e-05)
    weighted = normed_ref[...] * gain_ref[...]
    mean = jnp.sum(weighted * values, axis=1, keepdims=True) / values.shape[1]
    input_ref[...] = scale * weighted - values * scale * scale * scale * mean + later_ref[...]
    rate = MODEL_WIDTH ** (-0.5)
    weights, firsts, seconds = ins[0::3], ins[1::3], ins[2::3]

    def put(number, grad, rate, at=...):
        values = adam_step(weights[number][at], grad, firsts[number][at], seconds[number][at], rate)
        for place, value in enumerate(values):
            outs[3 * number + place][at] = value

    for head in range(weights[0].shape[0]):
        put(0, mixer_ref[:, 128 * head : 128 * (head + 1)], rate, head)
    put(1, step_ref[:, 2 * STATE :].T[0 : weights[1].shape[0]], rate)
    put(2, out_ref[...].T, INNER ** (-0.5))
    put(3, small_ref[:, 0 : 2 * STATE], rate)
    routes = small_ref[:, 2 * STATE :].T
    put(4, routes[ROUTER_AT : ROUTER_AT + weights[4].shape[0]], 0.5 * rate)
    put(5, up_ref[...], rate)
    put(6, down_ref[...], FF_S ** (-0.5))


def last_steps(grads, ends, arrays):
    whole = pl.BlockSpec()
    return pl.pallas_call(
        steps_kernel,
        out_shape=(
            jax.ShapeDtypeStruct(ends[0].shape, BF16),
            jax.ShapeDtypeStruct(ends[0].shape, F32),
        )
        + tuple(jax.ShapeDtypeStruct(array.shape, F32) for array in arrays),
        in_specs=[whole] * (13 + len(arrays)),
        out_specs=(whole,) * (2 + len(arrays)),
        compiler_params=pltpu.CompilerParams(vmem_limit_bytes=56 * 2**20),
        cost_estimate=lasting(10),
        name="last_steps",
    )(*grads, *ends, *arrays)


def shared_kernel(
    x_ref, g_ref, up_ref, down_ref, out_ref, dx_ref, *refs
):
    count = (len(refs) - 9) // 2
    up_outs, down_outs, refs = refs[:count], refs[count : 2 * count], refs[2 * count :]
    hid_ref, dpre_ref, turned, hid_turned, up_grad, down_grad, up_came, down_came, sems = refs
    row, col = lax.axis_index("row"), lax.axis_index("col")
    barrier = pltpu.get_barrier_semaphore()
    pl.semaphore_signal(barrier, inc=1, device_id={"row": 1 - row}, device_id_type=MESH_ID)
    x, g = x_ref[...], g_ref[...]
    pre = dot_f32(x, up_ref[...])
    asked = dot_t(g, down_ref[...])
    half = down_ref.shape[0]
    for part in range(half // 128):
        lanes = slice(128 * part, 128 * (part + 1))
        upper = slice(half + 128 * part, half + 128 * (part + 1))
        gate, up, want = pre[:, lanes], pre[:, upper], asked[:, lanes]
        sig = jax.nn.sigmoid(gate)
        act = gate * sig
        hid_ref[:, lanes] = (act * up).astype(BF16)
        dpre_ref[:, lanes] = (want * up * (sig * (1.0 + gate * (1.0 - sig)))).astype(BF16)
        dpre_ref[:, upper] = (want * act).astype(BF16)
    turned[...] = x.T
    hid_turned[...] = hid_ref[...].T
    pl.semaphore_wait(barrier, 1)
    copies = []
    for number, (left, right, grad, came) in enumerate(
        ((turned, dpre_ref, up_grad, up_came), (hid_turned, g_ref, down_grad, down_came))
    ):
        size, _, rows, _ = grad.shape
        pairs = 2 if size % 2 == 0 else 1
        for chunk in range(0, size, pairs):
            found = dot_f32(left[2 * rows * chunk : 2 * rows * (chunk + pairs), :], right[...]).astype(BF16)
            for at in range(pairs):
                for half_at in range(2):
                    start = (2 * at + half_at) * rows
                    grad[chunk + at, half_at] = found[start : start + rows]
        copies.append(
            pltpu.make_async_remote_copy(
                src_ref=grad.at[:, 1 - row],
                dst_ref=came,
                send_sem=sems.at[number],
                recv_sem=sems.at[2 + number],
                device_id={"row": 1 - row},
                device_id_type=MESH_ID,
            )
        )
        copies[-1].start()
    out_ref[...] = dot_f32(hid_ref[...], down_ref[...])
    dx_ref[...] = dot_t(dpre_ref[...], up_ref[...])
    for copy, grad, came, outs in zip(copies, (up_grad, down_grad), (up_came, down_came), (up_outs, down_outs)):
        copy.wait()
        size, _, rows, _ = grad.shape
        part = rows // count
        for chunk in range(size):
            total = (grad[chunk, row].astype(F32) + came[chunk].astype(F32)).astype(BF16)
            for place in range(count):
                mine = total[place * part : (place + 1) * part]
                for by in range(count):
                    @pl.when(place == (col + by) % count)
                    def _():
                        outs[by][chunk] = mine


def shared_expert(tokens, cotangents, up, down, shape):
    size, columns = shape["dp"], shape["col"]
    rows, width = tokens.shape
    up_rows, down_rows = (array.shape[0] // (2 * columns * size) for array in (up, down))
    results = pl.pallas_call(
        shared_kernel,
        out_shape=(jax.ShapeDtypeStruct((rows, width), F32),) * 2
        + (jax.ShapeDtypeStruct((size, up_rows, up.shape[1]), BF16),) * columns
        + (jax.ShapeDtypeStruct((size, down_rows, width), BF16),) * columns,
        in_specs=[VM] * 4,
        out_specs=(VM,) * (2 + 2 * columns),
        scratch_shapes=[
            pltpu.VMEM((rows, down.shape[0]), BF16),
            pltpu.VMEM((rows, up.shape[1]), BF16),
            pltpu.VMEM((width, rows), BF16),
            pltpu.VMEM((down.shape[0], rows), BF16),
            pltpu.VMEM((size, 2, columns * up_rows, up.shape[1]), BF16),
            pltpu.VMEM((size, 2, columns * down_rows, width), BF16),
            pltpu.VMEM((size, columns * up_rows, up.shape[1]), BF16),
            pltpu.VMEM((size, columns * down_rows, width), BF16),
            pltpu.SemaphoreType.DMA((4,)),
        ],
        compiler_params=pltpu.CompilerParams(
            collective_id=6, has_side_effects=True, vmem_limit_bytes=58 * 2**20
        ),
        cost_estimate=lasting(20),
        name="shared_expert",
    )(tokens, cotangents, up, down)
    return results[0], results[1], results[2 : 2 + columns], results[2 + columns :]


def expert_block(own, x_ref, g_ref, named, up, down, router_ref, hid_ref, dpre_ref, mix_ref, dx_ref):
    x, g = x_ref[...], g_ref[...]
    logits = dot_f32(x, router_ref[...])
    high = jnp.max(jnp.where(named > 0, logits, -1e30), axis=1, keepdims=True)
    raised = jnp.where(named > 0, jnp.exp(logits - high), 0.0)
    gates = raised / jnp.sum(raised, axis=1, keepdims=True)
    rows = x.shape[0]
    lane = lax.broadcasted_iota(jnp.int32, (rows, 128), 1)
    weights = [
        jnp.sum(jnp.where(lane == own + part, gates, 0.0), axis=1, keepdims=True)
        for part in range(EXP_DEV)
    ]
    half = down.shape[0]
    pre = dot_f32(x, up)
    asked = dot_t(g, down)
    totals = [jnp.zeros((rows, 128), F32) for part in range(EXP_DEV)]
    for part in range(half // 128):
        which = 128 * part // FF_E
        at = 128 * part + FF_E * which
        lanes = slice(128 * part, 128 * (part + 1))
        lower, upper = slice(at, at + 128), slice(at + FF_E, at + FF_E + 128)
        gate, upper_pre, want = pre[:, lower], pre[:, upper], asked[:, lanes]
        sig = jax.nn.sigmoid(gate)
        act = gate * sig
        hidden = act * upper_pre
        totals[which] = totals[which] + hidden * want
        hid_ref[:, lanes] = (weights[which] * hidden).astype(BF16)
        dact = weights[which] * want
        dpre_ref[:, lower] = (dact * upper_pre * (sig * (1.0 + gate * (1.0 - sig)))).astype(BF16)
        dpre_ref[:, upper] = (dact * act).astype(BF16)
    mix_ref[...] = dot_f32(hid_ref[...], down).astype(BF16)
    dx_ref[:, :MODEL_WIDTH] = dot_t(dpre_ref[...], up).astype(BF16)
    sent = jnp.zeros((rows, 128), F32)
    for part in range(EXP_DEV):
        gate_grad = jnp.sum(totals[part], axis=1, keepdims=True)
        coarse = gate_grad.astype(BF16).astype(F32)
        sent = jnp.where(lane == own + part, coarse, sent)
        sent = jnp.where(lane == own + part + REST_AT, gate_grad - coarse, sent)
    dx_ref[:, MODEL_WIDTH:] = sent.astype(BF16)


def expert_kernel(
    size, columns, own_ref, g_ref, mask_ref, router_hbm, *refs
):
    places = 2 * columns
    up_parts, down_parts, kept_ref, refs = (
        refs[:places], refs[places : 2 * places], refs[2 * places], refs[2 * places + 1 :]
    )
    outs, (full_ref, g_now), stages, (up_ref, down_ref, router_ref) = (
        refs[:4], refs[4:6], refs[6:10], refs[10:13]
    )
    send_sem, recv_sem, local_sem, in_sem, out_sem, weight_sem = refs[13:]
    grid = Grid(size)
    me, z, x = grid.me, grid.z, grid.x
    barrier = pltpu.get_barrier_semaphore()
    grid.greet(barrier)
    pl.semaphore_wait(barrier, grid.count)

    def push(chunk, way, source=None):
        return pltpu.make_async_remote_copy(
            src_ref=full_ref.at[chunk] if source is None else source,
            dst_ref=full_ref.at[chunk],
            send_sem=send_sem.at[way, chunk],
            recv_sem=recv_sem.at[chunk],
            device_id={"dp": me + grid.steps[way]},
            device_id_type=MESH_ID,
        )

    def place(number):
        if grid.across == 2:
            even, first, last = 1 - number % 2, 1 - jnp.minimum(number, 1), number // 7
            step = (1 - even) * ((number + 1) // 2 - last) + even * (number // 2 - 1 + first)
            side = even * (1 - first) + last
        else:
            step, side = number % grid.deep, number // grid.deep
        return block_at(step, side)

    def block_at(step, side):
        zc = near_first(z, step, grid.deep)
        xc = near_first(x, side, grid.across)
        same = xc == x
        ways = (same & (zc >= z), same & (zc <= z), xc >= x, xc <= x)
        return zc * grid.across + xc, [way & there for way, there in zip(ways, grid.exists)]

    for way in range(4):
        @pl.when(grid.exists[way])
        def _():
            push(me, way, own_ref).start()
    row, col = lax.axis_index("row"), lax.axis_index("col")
    weights = [pltpu.make_async_copy(router_hbm, router_ref, weight_sem.at[2 * places])]
    for number in range(places):
        whose = row + (number // columns) * (1 - 2 * row)
        there = whose * columns + (col - number % columns + columns) % columns
        weights.append(
            pltpu.make_async_copy(up_parts[number], up_ref.at[there], weight_sem.at[number])
        )
        weights.append(
            pltpu.make_async_copy(
                down_parts[number], down_ref.at[:, there], weight_sem.at[places + number]
            )
        )
    for copy in weights:
        copy.start()
    keep = pltpu.make_async_copy(own_ref, full_ref.at[me], in_sem.at[1])
    keep.start()

    def leave(number, chunk):
        return [
            pltpu.make_async_copy(stage.at[number % 2], out.at[chunk], out_sem.at[place_in, number % 2])
            for place_in, (stage, out) in enumerate(zip(stages, outs))
        ]

    def work(number, _):
        chunk, onward = place(number)
        bring = pltpu.make_async_copy(g_ref.at[chunk], g_now, in_sem.at[0])
        bring.start()

        def pass_on(chunk, onward):
            push(chunk, 0).wait_recv()
            for way in range(4):
                @pl.when(onward[way])
                def _():
                    push(chunk, way).start()

        if grid.across == 2:
            inner = (z * (3 - z)) // 2
            for step, when in ((1, number == 1), (2, number == 3 - 2 * inner), (3, number == 5 - 2 * inner)):
                @pl.when(when)
                def _():
                    pass_on(*block_at(step, 0))

            @pl.when((number > 0) & (chunk % grid.across != x))
            def _():
                push(chunk, 0).wait_recv()
        else:
            @pl.when(number > 0)
            def _():
                pass_on(chunk, onward)

        @pl.when(number == 0)
        def _():
            keep.wait()
            for copy in weights:
                copy.wait()

        pltpu.make_async_copy(full_ref.at[chunk], kept_ref.at[chunk], local_sem.at[chunk]).start()

        @pl.when(number > 1)
        def _():
            for copy in leave(number, place(number - 2)[0]):
                copy.wait()

        bring.wait()
        experts_named = mask_ref[chunk].astype(F32)
        rest = jnp.zeros((128 - experts_named.shape[0], experts_named.shape[1]), F32)
        named = jnp.concatenate([experts_named, rest], axis=0).T
        expert_block(
            EXP_DEV * me, full_ref.at[chunk], g_now, named,
            up_ref[...].reshape(-1, up_ref.shape[2]), down_ref[...].reshape(-1, down_ref.shape[3]), router_ref,
            *[stage.at[number % 2] for stage in stages]
        )
        for copy in leave(number, chunk):
            copy.start()
        return 0

    lax.fori_loop(0, size, work, 0)
    for number in (size - 2, size - 1):
        for copy in leave(number, place(number)[0]):
            copy.wait()

    def finish(number, _):
        chunk, onward = place(number)
        pltpu.make_async_copy(full_ref.at[chunk], kept_ref.at[chunk], local_sem.at[chunk]).wait()
        for way in range(4):
            @pl.when(onward[way])
            def _():
                push(chunk, way).wait_send()
        return 0

    lax.fori_loop(0, size, finish, 0)


def experts(tokens, cotangents, masks, up_parts, down_parts, router, shape):
    size, columns = shape["dp"], shape["col"]
    places = 2 * columns
    rows, width = tokens.shape
    hidden = places * EXP_DEV * down_parts[0].shape[1]
    wide = width + 128
    wides = (hidden, 2 * hidden, width, wide)
    results = pl.pallas_call(
        functools.partial(expert_kernel, size, columns),
        out_shape=tuple(
            jax.ShapeDtypeStruct((size, rows, column), BF16) for column in (width,) + wides
        ),
        in_specs=[ANY, ANY, VM] + [ANY] * (1 + 2 * places),
        out_specs=(ANY,) * 5,
        scratch_shapes=[pltpu.VMEM((size, rows, width), BF16), pltpu.VMEM((rows, width), BF16)]
        + [pltpu.VMEM((2, rows, column), BF16) for column in wides]
        + [
            pltpu.VMEM((places,) + up_parts[0].shape, BF16),
            pltpu.VMEM((EXP_DEV, places) + down_parts[0].shape[1:], BF16),
            pltpu.VMEM(router.shape, BF16),
            pltpu.SemaphoreType.DMA((4, size)),
            pltpu.SemaphoreType.DMA((size,)),
            pltpu.SemaphoreType.DMA((size,)),
            pltpu.SemaphoreType.DMA((2,)),
            pltpu.SemaphoreType.DMA((4, 2)),
            pltpu.SemaphoreType.DMA((2 * places + 1,)),
        ],
        compiler_params=pltpu.CompilerParams(
            collective_id=4, has_side_effects=True, vmem_limit_bytes=56 * 2**20
        ),
        cost_estimate=lasting(85),
        name="experts",
    )(tokens, cotangents.reshape(size, rows, width), masks.reshape(size, -1, rows), router, *up_parts, *down_parts)
    return [result.reshape(size * rows, -1) for result in results]


def rms_scale(values):
    return lax.rsqrt(jnp.mean(values * values, axis=-1, keepdims=True) + 1e-05)


def rms_back(values, scale, gain, grad_normed):
    weighted = grad_normed * gain[None, :]
    grad_values = scale * weighted - values * scale**3 * jnp.mean(
        weighted * values, axis=-1, keepdims=True
    )
    gain_grad = jnp.sum(grad_normed * values * scale, axis=0)
    return (grad_values, gain_grad)


def silu_gate(pre_values):
    half_size = pre_values.shape[-1] // 2
    return jax.nn.silu(pre_values[..., :half_size]) * pre_values[..., half_size:]


def silu_gate_back(pre_values, grad):
    return jax.vjp(silu_gate, pre_values)[1](grad)[0]


ALL = ("dp", "row", "col")


def gather_dp(values):
    return lax.all_gather(values, "dp", axis=0, tiled=True)


def scatter_dp(values):
    return lax.psum_scatter(values, "dp", scatter_dimension=0, tiled=True)


def body(
    shape,
    hidden_in, segment_ids, routes, out_grad,
    vectors, vectors_first, vectors_second,
    in_weight, in_weight_first, in_weight_second,
    step_weight, step_weight_first, step_weight_second,
    out_weight, out_weight_first, out_weight_second,
    state_weight, state_weight_first, state_weight_second,
    router, router_first, router_second,
    shared_up, shared_up_first, shared_up_second,
    shared_down, shared_down_first, shared_down_second,
    expert_gate_up, expert_gate_up_first, expert_gate_up_second,
    expert_down, expert_down_first, expert_down_second,
):
    dp = lax.axis_index("dp")
    data_count = lax.axis_size("dp")
    seq_devices = lax.axis_size("row") * lax.axis_size("col")
    local_heads = in_weight.shape[1]
    width = 64 * local_heads
    head_start = lax.axis_index(("row", "col")) * local_heads
    own_tokens = hidden_in.shape[1]
    experts_all = router.shape[1]
    rows_dp = in_weight.shape[0]
    seq_columns = shape["col"]
    residual = hidden_in[0].astype(F32)
    count = vectors.shape[0]
    lines = -(-count // 1024) * 8
    vector_rows = jnp.pad(vectors, (0, lines * 128 - count)).reshape(lines, 128)
    gain_one = vectors[0:MODEL_WIDTH]
    gain_two = vectors[MODEL_WIDTH : 2 * MODEL_WIDTH]

    scale_one = rms_scale(residual)
    route_ids = routes[0]
    chosen = (
        route_ids[:, :, None] == jnp.arange(experts_all, dtype=jnp.int32)[None, None, :]
    ).any(axis=1)
    grad_low = out_grad[0]
    (
        mixer_full, step_full, out_full, masks, shared_up_full, shared_down_full, small_full, normed_all,
        up_local, down_parts,
    ) = gather_start(
        hidden_in[0],
        vector_rows,
        in_weight.transpose(1, 0, 2),
        step_weight.T,
        out_weight.reshape(width, -1),
        shared_up,
        shared_down,
        state_weight,
        router.T,
        route_ids.T,
        expert_gate_up,
        expert_down,
        shape,
    )
    mixer_full, step_full, out_full, small_full, normed_all, segment_ids, grad_gone, up_local, down_parts = (
        lax.optimization_barrier(
            (mixer_full, step_full, out_full, small_full, normed_all, segment_ids, grad_low, up_local, down_parts)
        )
    )
    grad_all = gather_dp(grad_gone)
    up_parts = [up_local] + [shift(up_local, "col", by) for by in range(1, seq_columns)]
    state_step = jnp.concatenate([small_full[:, : 2 * STATE], step_full], axis=1)

    seg_rows = segment_ids[0].astype(F32).reshape(-1, 1, BLK)
    proj = dot_f32(normed_all, mixer_full).astype(BF16)
    ss = dot_f32(normed_all, state_step)
    valued, squares_part, kept, params = mixer_forward(proj, ss, seg_rows, vector_rows, seq_columns)
    partial_out = dot_t(valued, out_full).astype(BF16)
    partial_out, up_parts = lax.optimization_barrier((partial_out, up_parts))
    proj_out = scatter_rc(partial_out)
    other_row = lambda parts: parts + [shift(part, "row", 1) for part in parts]
    up_parts, down_parts = other_row(up_parts), other_row(down_parts)
    squares = scatter_squares(squares_part)[:, 0]
    scale_two = lax.rsqrt(squares / INNER + 1e-05)
    residual_two = residual + scale_two[:, None] * proj_out
    scale_three = rms_scale(residual_two)
    normed_two = (residual_two * scale_three * gain_two[None, :]).astype(BF16)

    router_wide = small_full[:, 2 * STATE :]
    router_full = router_wide[:, :experts_all]
    shared_out, shared_dx, shared_up_sums, shared_down_sums = shared_expert(
        normed_two, grad_low, shared_up_full, shared_down_full, shape
    )
    normed_two, grad_all, shared_dx, shared_out = lax.optimization_barrier(
        (normed_two, grad_all, shared_dx, shared_out)
    )
    from_columns = lambda parts: [
        shift(parts[by], "col", by) for by in range(1, seq_columns)
    ]
    shared_up_came, shared_down_came = from_columns(shared_up_sums), from_columns(shared_down_sums)
    tokens_all, hidden_low, pre_grad, mixed, rows_grad = experts(
        normed_two, grad_all, masks, up_parts, down_parts, router_wide, shape
    )
    logits = dot_f32(normed_two, router_full)
    gate_all = jax.nn.softmax(jnp.where(chosen, logits, -jnp.inf), axis=-1)
    rows_grad, shared_up_came, shared_down_came = lax.optimization_barrier(
        (rows_grad, shared_up_came, shared_down_came)
    )
    add_all = lambda own, came: sum([part.astype(F32) for part in came], own.astype(F32)).astype(BF16)
    shared_up_part = add_all(shared_up_sums[0], shared_up_came).reshape(-1, 2 * FF_S)
    shared_down_part = add_all(shared_down_sums[0], shared_down_came).reshape(-1, MODEL_WIDTH)
    routed_grad, up_grad, down_grad = scatter_blocks(
        rows_grad, tokens_all, pre_grad, hidden_low, grad_all, shape
    )
    routed_grad, mixed = lax.optimization_barrier((routed_grad, mixed))
    mixture = scatter_dp(mixed)
    gate_grad = (
        routed_grad[:, MODEL_WIDTH : MODEL_WIDTH + experts_all]
        + routed_grad[:, MODEL_WIDTH + REST_AT : MODEL_WIDTH + REST_AT + experts_all]
    )
    cotangent = grad_low.astype(F32)
    normed_two_grad = shared_dx + routed_grad[:, :MODEL_WIDTH]
    logits_grad = gate_all * (gate_grad - jnp.sum(gate_all * gate_grad, axis=1, keepdims=True))
    logits_low = jnp.where(chosen, logits_grad, 0.0).astype(BF16)
    normed_two_grad = normed_two_grad + dot_t(logits_low, router_full)
    router_grad = dot_tn(normed_two, logits_low)
    residual_two_grad, gain_two_grad = rms_back(
        residual_two, scale_three, gain_two, normed_two_grad
    )
    residual_two_grad = residual_two_grad + cotangent
    proj_out_grad = (residual_two_grad * scale_two[:, None]).astype(BF16)
    squares_grad = (
        jnp.sum(residual_two_grad * proj_out, axis=1) * -0.5 * scale_two**3 / INNER
    )
    squares_high = squares_grad.astype(BF16)
    squares_rest = (squares_grad - squares_high.astype(F32)).astype(BF16)
    riding = jnp.pad(jnp.stack([squares_high, squares_rest], axis=1), ((0, 0), (0, 126)))
    riders = jnp.concatenate([proj_out_grad, riding], axis=1)
    riders, up_grad, down_grad = lax.optimization_barrier((riders, up_grad, down_grad))
    riders = gather_rc(riders)
    proj_grad_all = riders[:, :MODEL_WIDTH]
    squares_grad_all = jnp.sum(riders[:, MODEL_WIDTH:].astype(F32), axis=1, keepdims=True)
    proj_grad_all, up_grad, down_grad = lax.optimization_barrier((proj_grad_all, up_grad, down_grad))
    sum_all = lambda parts: sum([part.astype(F32) for part in from_columns(parts)], parts[0].astype(F32))
    up_total, down_total = sum_all(up_grad), sum_all(down_grad)
    up_total = jnp.stack(
        [up_total[:, 2 * FF_E * held : 2 * FF_E * (held + 1)] for held in range(EXP_DEV)]
    )
    new_up = adam_step(
        expert_gate_up, up_total, expert_gate_up_first, expert_gate_up_second, MODEL_WIDTH ** (-0.5)
    )
    new_down = adam_step(
        expert_down, down_total.reshape(expert_down.shape), expert_down_first, expert_down_second, FF_E ** (-0.5)
    )

    valued_grad = dot_f32(proj_grad_all, out_full).astype(BF16)
    out_grad_t = dot_tn(proj_grad_all, valued).astype(BF16)
    proj_grad, ss_grad, vector_grad = mixer_backward(
        proj, ss, seg_rows, params, valued_grad, squares_grad_all, kept, lines, seq_columns
    )
    normed_part = dot_t(proj_grad, mixer_full) + dot_t(ss_grad, state_step)
    gain_one_grad = jnp.sum(normed_part * normed_all.astype(F32), axis=0) / gain_one
    router_wide = jnp.pad(
        router_grad, ((0, 0), (2 * STATE + ROUTER_AT, 128 - ROUTER_AT - experts_all))
    )
    mixer_grad = dot_tn(normed_all, proj_grad).astype(BF16)
    small_grad = (dot_tn(normed_all, ss_grad) + router_wide).astype(BF16)
    gains = jnp.concatenate([gain_one_grad, gain_two_grad]).reshape(-1, 128)
    vector_lines = vector_grad + jnp.pad(gains, ((0, lines - gains.shape[0]), (0, 0)))
    mixture, mixer_grad, new_up, new_down = lax.optimization_barrier(
        (mixture, mixer_grad, new_up, new_down)
    )
    (
        mixer_total, small_rows, out_total, shared_up_total, shared_down_total,
        vector_total, small_total, normed_grad,
    ) = scatter_end(
        (mixer_grad, small_grad, out_grad_t, shared_up_part, shared_down_part),
        vector_lines,
        normed_part.astype(BF16),
        shape,
    )
    vector_total = vector_total.reshape(-1)[:count]
    heads_first = lambda array: array.transpose(1, 0, 2)
    flat_out = lambda array: array.reshape(width, -1)
    hidden_out, input_grad, *news = last_steps(
        (
            mixer_total, out_total, shared_up_total, shared_down_total, small_total,
            small_rows,
        ),
        (
            residual_two, mixture, shared_out,
            hidden_in[0], gain_one[None, :], normed_grad, residual_two_grad,
        ),
        (
            *map(heads_first, (in_weight, in_weight_first, in_weight_second)),
            step_weight.T, step_weight_first.T, step_weight_second.T,
            *map(flat_out, (out_weight, out_weight_first, out_weight_second)),
            state_weight, state_weight_first, state_weight_second,
            router.T, router_first.T, router_second.T,
            shared_up, shared_up_first, shared_up_second,
            shared_down, shared_down_first, shared_down_second,
        ),
    )
    return (
        hidden_out[None],
        input_grad[None],
        *adam_step(vectors, vector_total, vectors_first, vectors_second, 0.3, 0.0),
        *map(heads_first, news[0:3]),
        *[array.T for array in news[3:6]],
        *[array.reshape(out_weight.shape) for array in news[6:9]],
        *news[9:12],
        *[array.T for array in news[12:15]],
        *news[15:],
        *new_up,
        *new_down,
    )


def solution(mesh):
    tokens = P("dp", ("row", "col"), None)
    by_head = P("dp", ("row", "col"))
    out_spec = P(("row", "col"), None, "dp")
    flat = P(ALL, None)
    weights = (
        (P(),) * 3
        + (tokens,) * 3
        + (by_head,) * 3
        + (out_spec,) * 3
        + (flat,) * 12
        + (tokens,) * 6
    )
    return jax.shard_map(
        functools.partial(body, dict(mesh.shape)),
        mesh=mesh,
        in_specs=(tokens, P("dp", None), tokens, tokens) + weights,
        out_specs=(tokens, tokens) + weights,
        check_vma=False,
    )
```

```python
import functools

import jax
import jax.numpy as jnp
from jax import lax
from jax.experimental import pallas as pl
from jax.experimental.pallas import tpu as pltpu
from jax.sharding import PartitionSpec as P

STATE = 128
KW = 4
BLK = 128
F32 = jnp.float32
BF16 = jnp.bfloat16


def dot_f32(a, b, dims=(((1,), (0,)), ((), ()))):
    return lax.dot_general(a, b, dims, preferred_element_type=F32)


def dot_exact(a, b, dims=(((1,), (0,)), ((), ()))):
    return lax.dot_general(
        a, b, dims, precision=lax.Precision.HIGHEST, preferred_element_type=F32
    )


def spread(values, width):
    rows = values.shape[0]
    low = lax.broadcasted_iota(jnp.int32, (rows, 128), 1) < 64
    parts = []
    for pair in range(width // 128):
        left = jnp.broadcast_to(values[:, 2 * pair : 2 * pair + 1], (rows, 128))
        right = jnp.broadcast_to(values[:, 2 * pair + 1 : 2 * pair + 2], (rows, 128))
        parts.append(jnp.where(low, left, right))
    return jnp.concatenate(parts, axis=1)


def head_sums(values):
    width = values.shape[1]
    ones = (
        lax.broadcasted_iota(jnp.int32, (width, 128), 0) // 64
        == lax.broadcasted_iota(jnp.int32, (width, 128), 1)
    ).astype(BF16)
    high = values.astype(BF16)
    rest = (values - high.astype(F32)).astype(BF16)
    return dot_f32(high, ones) + dot_f32(rest, ones)


def apart(values):
    low = lax.broadcasted_iota(jnp.int32, (values.shape[0], 128), 1) < 64
    gates, inputs = [], []
    for at in range(0, values.shape[1], 256):
        one, two = values[:, at : at + 128], values[:, at + 128 : at + 256]
        gates.append(jnp.where(low, one, pltpu.roll(two, 64, 1)))
        inputs.append(jnp.where(low, pltpu.roll(one, 64, 1), two))
    return jnp.concatenate(gates, axis=1), jnp.concatenate(inputs, axis=1)


def together(gates, inputs):
    low = lax.broadcasted_iota(jnp.int32, (gates.shape[0], 128), 1) < 64
    parts = []
    for at in range(0, gates.shape[1], 128):
        one, two = gates[:, at : at + 128], inputs[:, at : at + 128]
        parts.append(jnp.where(low, one, pltpu.roll(two, 64, 1)))
        parts.append(jnp.where(low, pltpu.roll(one, 64, 1), two))
    return jnp.concatenate(parts, axis=1)


def block_masks(index, seg_ref):
    now = seg_ref[index]
    before = jnp.where(index > 0, seg_ref[jnp.maximum(index - 1, 0)], -1.0)
    lane = lax.broadcasted_iota(jnp.int32, (1, BLK), 1)
    rows = [now]
    for back in range(1, KW):
        earlier = jnp.where(lane < back, pltpu.roll(before, back, 1), pltpu.roll(now, back, 1))
        rows.append((earlier == now).astype(F32))
    last, prior = now[:, BLK - 1 :], before[:, BLK - 1 :]
    rows.append((now == prior).astype(F32))
    rows.append((now == last).astype(F32))
    rows.append(jnp.broadcast_to((prior == last).astype(F32), (1, BLK)))
    rows.append(jnp.zeros((BLK - len(rows), BLK), F32))
    return jnp.concatenate(rows, axis=0).T


def block_common(width, start, index, proj_ref, ss_ref, seg_ref, par_ref):
    rows = pl.ds(start, BLK)
    before = pl.ds(pl.multiple_of(jnp.maximum(start - 8, 0), 8), 8)
    aux = block_masks(index, seg_ref)
    gate, inner = apart(proj_ref[rows, :].astype(F32))
    current = jnp.concatenate([inner, ss_ref[rows, 0 : 2 * STATE]], axis=1)
    earlier = proj_ref[pl.ds(pl.multiple_of(jnp.maximum(start - 16, 0), 16), 16), :]
    previous = jnp.concatenate(
        [apart(earlier.astype(F32)[8:])[1], ss_ref[before, 0 : 2 * STATE]], axis=1
    )
    extended = jnp.concatenate([previous, current], axis=0)
    taps = par_ref[0:KW, :]
    conv = par_ref[KW : KW + 1, :] + taps[KW - 1 : KW, :] * current
    shifted = []
    for back in range(1, KW):
        moved = pltpu.roll(extended, back, 0)[8:] * aux[:, back : back + 1]
        shifted.append(moved)
        conv = conv + taps[KW - 1 - back : KW - back, :] * moved
    sig = jax.nn.sigmoid(conv)
    active = conv * sig
    inputs_x = active[:, :width]
    matrix_b = active[:, width : width + STATE].astype(BF16)
    matrix_c = active[:, width + STATE :].astype(BF16)
    step_in = ss_ref[rows, 2 * STATE :] + par_ref[7:8, 0:128]
    dt = jnp.maximum(step_in, 0.0) + jnp.log1p(jnp.exp(-jnp.abs(step_in)))
    decay = dt * par_ref[6:7, 0:128]
    row_id = lax.broadcasted_iota(jnp.int32, (BLK, BLK), 0)
    col_id = lax.broadcasted_iota(jnp.int32, (BLK, BLK), 1)
    lower = (row_id >= col_id).astype(F32)
    cum = dot_exact(lower, decay)
    cum_t = cum.T
    same = (aux[:, 0:1] == seg_ref[pl.ds(index, 1), 0, :]) & (row_id >= col_id)
    last = cum[BLK - 1 : BLK, :]
    gain_in = jnp.exp(cum) * aux[:, 4:5]
    tail = jnp.exp(last - cum) * aux[:, 5:6]
    carry = jnp.exp(last) * aux[BLK - 1 : BLK, 6:7]
    scores = jnp.where(same, dot_f32(matrix_c, matrix_b, (((1,), (1,)), ((), ()))), 0.0)
    dt_wide = spread(dt, width)
    moved_x = inputs_x * dt_wide
    return dict(
        rows=rows, aux=aux, gate=gate, current=current, shifted=shifted, conv=conv, sig=sig,
        x=inputs_x, b=matrix_b, c=matrix_c, step_in=step_in, dt=dt, cum=cum, cum_t=cum_t,
        same=same, scores=scores, dt_wide=dt_wide, u=moved_x, lower=lower,
        gain_in=spread(gain_in, width), tail=spread(tail, width),
        carry=spread(jnp.broadcast_to(carry, (8, 128)), width)[0:1],
    )


def split_pair(values):
    low = lax.broadcasted_iota(jnp.int32, values.shape, 1) < 64
    zero = jnp.zeros_like(values)
    return jnp.where(low, values, zero), jnp.where(low, zero, values)


GAIN_AT, BIAS_AT, TAPS_AT, HEADS_AT = 24, 48, 74, 178
INNER_LINES, TAP_LINES = 24, 26


def own_place(columns):
    return lax.axis_index("row") * columns + lax.axis_index("col")


def read_params(width, columns, vec_ref, par_ref):
    lines, heads = width // 128, width // 64
    place = own_place(columns)

    def line(at):
        return jnp.concatenate(
            [vec_ref[pl.ds(at + place * lines + one, 1), :] for one in range(lines)], axis=1
        )

    def wide_line(at):
        rest = at + INNER_LINES
        return jnp.concatenate(
            [line(at), vec_ref[rest : rest + 1, :], vec_ref[rest + 1 : rest + 2, :]], axis=1
        )

    par_ref[...] = jnp.zeros_like(par_ref)
    for tap in range(KW):
        par_ref[tap : tap + 1, :] = wide_line(TAPS_AT + TAP_LINES * tap)
    par_ref[KW : KW + 1, :] = wide_line(BIAS_AT)
    par_ref[5:6, 0:width] = line(GAIN_AT)
    flat = jnp.concatenate([vec_ref[HEADS_AT : HEADS_AT + 1, :], vec_ref[HEADS_AT + 1 : HEADS_AT + 2, :]], axis=1)
    flat = jnp.broadcast_to(flat, (8, 256))
    lane = lax.broadcasted_iota(jnp.int32, (8, 128), 1)

    def per_head(which):
        turned = pltpu.roll(flat, 256 - 48 * which - place * heads, 1)[:, 0:128]
        return jnp.where(lane < heads, turned, 0.0)

    par_ref[6:7, 0:128] = jnp.where(lane < heads, -jnp.exp(per_head(0)), 0.0)[0:1]
    par_ref[7:8, 0:128] = per_head(2)[0:1]
    par_ref[8:9, 0:width] = spread(per_head(1), width)[0:1]


def write_params(width, columns, sums, par_ref, vec_ref):
    lines, heads = width // 128, width // 64
    place = own_place(columns)
    vec_ref[...] = jnp.zeros_like(vec_ref)
    total = lambda at: jnp.sum(sums[at : at + 8, :], axis=0, keepdims=True)

    def line(at, row):
        for one in range(lines):
            vec_ref[pl.ds(at + place * lines + one, 1), :] = row[:, 128 * one : 128 * (one + 1)]

    def wide_line(at, row):
        line(at, row)
        rest = at + INNER_LINES
        vec_ref[rest : rest + 1, :] = row[:, width : width + 128]
        vec_ref[rest + 1 : rest + 2, :] = row[:, width + 128 :]

    for tap in range(KW):
        wide_line(TAPS_AT + TAP_LINES * tap, total(8 * tap))
    wide_line(BIAS_AT, total(32))
    line(GAIN_AT, total(48))
    skips = jnp.sum(head_sums(sums[64:72, 0:width]), axis=0, keepdims=True)
    decays = total(56)[:, 0:128] * par_ref[6:7, 0:128]
    flat = jnp.zeros((8, 256), F32)
    lane = lax.broadcasted_iota(jnp.int32, (8, 256), 1)
    for which, row in enumerate((decays, skips, total(72)[:, 0:128])):
        row = jnp.broadcast_to(jnp.concatenate([row, jnp.zeros((1, 128), F32)], axis=1), (8, 256))
        flat = flat + pltpu.roll(jnp.where(lane < heads, row, 0.0), 48 * which + place * heads, 1)
    vec_ref[HEADS_AT : HEADS_AT + 1, :] = flat[0:1, 0:128]
    vec_ref[HEADS_AT + 1 : HEADS_AT + 2, :] = flat[0:1, 128:]


def forward_kernel(
    width, columns, proj_ref, ss_ref, seg_ref, vec_ref, valued_ref, squares_ref, kept_ref, par_ref, state
):
    blocks = proj_ref.shape[0] // BLK
    state[...] = jnp.zeros_like(state)
    read_params(width, columns, vec_ref, par_ref)

    def step(index, _):
        start = pl.multiple_of(index * BLK, BLK)
        got = block_common(width, start, index, proj_ref, ss_ref, seg_ref, par_ref)
        kept_ref[index] = state[...]
        moved = got["u"].astype(BF16)
        parts = []
        for pair in range(width // 128):
            u0, u1 = split_pair(moved[:, 128 * pair : 128 * (pair + 1)])
            mixes = []
            for head in (2 * pair, 2 * pair + 1):
                differ = jnp.minimum(got["cum"][:, head : head + 1] - got["cum_t"][head : head + 1, :], 0.0)
                mixes.append((jnp.exp(differ) * got["scores"]).astype(BF16))
            parts.append(dot_f32(jnp.concatenate(mixes, axis=1), jnp.concatenate([u0, u1], axis=0)))
        within = jnp.concatenate(parts, axis=1)
        from_state = got["gain_in"] * dot_f32(got["c"], state[...].astype(BF16))
        scanned = within + from_state + par_ref[8:9, 0:width] * got["x"]
        state[...] = state[...] * got["carry"] + dot_f32(
            got["b"], (got["tail"] * got["u"]).astype(BF16), (((0,), (0,)), ((), ()))
        )
        gate = got["gate"]
        gated = scanned * (gate * jax.nn.sigmoid(gate))
        squares_ref[got["rows"], :] = jnp.sum(gated * gated, axis=1, keepdims=True)
        valued_ref[got["rows"], :] = (gated * par_ref[5:6, 0:width]).astype(BF16)
        return 0

    lax.fori_loop(0, blocks, step, 0)


def backward_kernel(
    width, columns, proj_ref, ss_ref, seg_ref, par_ref, vgrad_ref, dsq_ref, kept_ref,
    dproj_ref, dss_ref, dvec_ref, dstate, follow, ebuf, sums
):
    blocks = proj_ref.shape[0] // BLK
    dstate[...] = jnp.zeros_like(dstate)
    follow[...] = jnp.zeros_like(follow)
    sums[...] = jnp.zeros_like(sums)

    def fold(values):
        total = values[0:8]
        for part in range(1, BLK // 8):
            total = total + values[8 * part : 8 * part + 8]
        return total

    def step(count, _):
        index = blocks - 1 - count
        start = pl.multiple_of(index * BLK, BLK)
        got = block_common(width, start, index, proj_ref, ss_ref, seg_ref, par_ref)
        rows, aux = got["rows"], got["aux"]
        state_in = kept_ref[index]
        state_low = state_in.astype(BF16)
        moved = got["u"].astype(BF16)
        skip = par_ref[8:9, 0:width]
        gain = par_ref[5:6, 0:width]
        parts = []
        for pair in range(width // 128):
            u0, u1 = split_pair(moved[:, 128 * pair : 128 * (pair + 1)])
            mixes = []
            for head in (2 * pair, 2 * pair + 1):
                differ = jnp.minimum(got["cum"][:, head : head + 1] - got["cum_t"][head : head + 1, :], 0.0)
                level = jnp.exp(differ)
                ebuf[head] = level
                mixes.append((level * got["scores"]).astype(BF16))
            parts.append(dot_f32(jnp.concatenate(mixes, axis=1), jnp.concatenate([u0, u1], axis=0)))
        inner = jnp.concatenate(parts, axis=1) + got["gain_in"] * dot_f32(got["c"], state_low)
        scanned = inner + skip * got["x"]
        gate = got["gate"]
        gate_sig = jax.nn.sigmoid(gate)
        gate_act = gate * gate_sig
        gated = scanned * gate_act
        vgrad = vgrad_ref[rows, :].astype(F32)
        dgated = vgrad * gain + 2.0 * gated * dsq_ref[rows, :]
        sums[48:56, 0:width] += fold(vgrad * gated)
        dy = dgated * gate_act
        dgate = dgated * scanned * (gate_sig * (1.0 + gate * (1.0 - gate_sig)))
        dy_low = dy.astype(BF16)
        dscores = jnp.zeros((BLK, BLK), F32)
        parts = []
        for pair in range(width // 128):
            lanes = slice(128 * pair, 128 * (pair + 1))
            u0, u1 = split_pair(moved[:, lanes])
            d0, d1 = split_pair(dy_low[:, lanes])
            mixes = []
            for head, u_own in ((2 * pair, u0), (2 * pair + 1, u1)):
                level = ebuf[head]
                mixes.append((level * got["scores"]).astype(BF16))
                dscores = dscores + level * dot_f32(
                    dy_low[:, lanes], u_own, (((1,), (1,)), ((), ()))
                )
            parts.append(
                dot_f32(
                    jnp.concatenate(mixes, axis=0),
                    jnp.concatenate([d0, d1], axis=0),
                    (((0,), (0,)), ((), ())),
                )
            )
        du_within = jnp.concatenate(parts, axis=1)
        dscores = jnp.where(got["same"], dscores, 0.0).astype(BF16)
        dstate_now = dstate[...]
        dstate_low = dstate_now.astype(BF16)
        dy_in = (got["gain_in"] * dy).astype(BF16)
        u_tail = got["tail"] * got["u"]
        from_next = dot_f32(got["b"], dstate_low)
        du = du_within + got["tail"] * from_next
        dmat_c = dot_f32(dscores, got["b"]) + dot_f32(dy_in, state_low, (((1,), (1,)), ((), ())))
        dmat_b = dot_f32(dscores, got["c"], (((0,), (0,)), ((), ()))) + dot_f32(
            u_tail.astype(BF16), dstate_low, (((1,), (1,)), ((), ()))
        )
        tail_part = head_sums(u_tail * from_next)
        dcum = (
            head_sums(dy_low.astype(F32) * inner - moved.astype(F32) * du_within) - tail_part
        )
        kept_part = head_sums(fold(got["carry"] * dstate_now * state_in))
        at_last = jnp.sum(tail_part, axis=0, keepdims=True) + jnp.sum(kept_part, axis=0, keepdims=True)
        ddecay = dot_exact(got["lower"], dcum, (((0,), (0,)), ((), ()))) + at_last
        ddt = ddecay * par_ref[6:7, 0:128] + head_sums(du * got["x"])
        sums[56:64, 0:128] += fold(ddecay * got["dt"])
        sums[64:72, 0:width] += fold(dy * got["x"])
        dstep = ddt * jax.nn.sigmoid(got["step_in"])
        sums[72:80, 0:128] += fold(dstep)
        dstate[...] = dstate_now * got["carry"] + dot_f32(got["c"], dy_in, (((0,), (0,)), ((), ())))
        dactive = jnp.concatenate([skip * dy + du * got["dt_wide"], dmat_b, dmat_c], axis=1)
        sig, conv = got["sig"], got["conv"]
        dconv = dactive * (sig * (1.0 + conv * (1.0 - sig)))
        sums[32:40, :] += fold(dconv)
        sums[24:32, :] += fold(dconv * got["current"])
        dinput = par_ref[KW - 1 : KW, :] * dconv
        for back in range(1, KW):
            tap = KW - 1 - back
            sums[8 * tap : 8 * tap + 8, :] += fold(dconv * got["shifted"][back - 1])
            masked = dconv * aux[:, back : back + 1]
            ext = jnp.concatenate([masked, follow[back - 1]], axis=0)
            dinput = dinput + par_ref[tap : tap + 1, :] * pltpu.roll(ext, BLK + 8 - back, 0)[:BLK]
            follow[back - 1] = masked[0:8]
        dproj_ref[rows, :] = together(dgate, dinput[:, :width]).astype(BF16)
        dss_ref[rows, 0 : 2 * STATE] = dinput[:, width:].astype(BF16)
        dss_ref[rows, 2 * STATE :] = dstep.astype(BF16)
        return 0

    lax.fori_loop(0, blocks, step, 0)
    write_params(width, columns, sums, par_ref, dvec_ref)


VM = pl.BlockSpec(memory_space=pltpu.VMEM)


def lasting(micros):
    return pl.CostEstimate(flops=0, bytes_accessed=int(micros * 3.0e6), transcendentals=0)


def mixer_forward(proj, ss, seg, vec, columns):
    length, double = proj.shape
    width = double // 2
    blocks = length // BLK
    return pl.pallas_call(
        functools.partial(forward_kernel, width, columns),
        out_shape=(
            jax.ShapeDtypeStruct((length, width), BF16),
            jax.ShapeDtypeStruct((length, 1), F32),
            jax.ShapeDtypeStruct((blocks, STATE, width), F32),
            jax.ShapeDtypeStruct((16, width + 2 * STATE), F32),
        ),
        in_specs=[VM] * 4,
        out_specs=(VM,) * 4,
        scratch_shapes=[pltpu.VMEM((STATE, width), F32)],
        compiler_params=pltpu.CompilerParams(vmem_limit_bytes=56 * 2**20),
        cost_estimate=lasting(20),
        name="mixer_forward",
    )(proj, ss, seg, vec)


def mixer_backward(proj, ss, seg, par, vgrad, dsq, kept, lines, columns):
    length, double = proj.shape
    width = double // 2
    wide = width + 2 * STATE
    return pl.pallas_call(
        functools.partial(backward_kernel, width, columns),
        out_shape=(
            jax.ShapeDtypeStruct((length, 2 * width), BF16),
            jax.ShapeDtypeStruct((length, 3 * STATE), BF16),
            jax.ShapeDtypeStruct((lines, 128), F32),
        ),
        in_specs=[VM] * 7,
        out_specs=(VM,) * 3,
        scratch_shapes=[
            pltpu.VMEM((STATE, width), F32),
            pltpu.VMEM((KW - 1, 8, wide), F32),
            pltpu.VMEM((width // 64, BLK, BLK), F32),
            pltpu.VMEM((80, wide), F32),
        ],
        compiler_params=pltpu.CompilerParams(vmem_limit_bytes=56 * 2**20),
        cost_estimate=lasting(34),
        name="mixer_backward",
    )(proj, ss, seg, par, vgrad, dsq, kept)


MODEL_WIDTH = 1536
HEADS = 48
FF_E = 512
FF_S = 1024
TOPK = 6
STEP = 10
EXP_DEV = 2
INNER = 3072
ROUTER_AT = 64
REST_AT = 64


def dot_t(a, b):
    return dot_f32(a, b, (((1,), (1,)), ((), ())))


def dot_tn(a, b):
    return dot_f32(a, b, (((0,), (0,)), ((), ())))


def shift(values, axis, by):
    size = lax.axis_size(axis)
    return lax.ppermute(values, axis, [(i, (i + by) % size) for i in range(size)])


def all_places(own):
    rows, columns = lax.axis_index("row"), lax.axis_size("col")
    col = lax.axis_index("col")
    placed = []
    for by, part in enumerate(own):
        there = (col - by) % columns
        placed.append((rows * columns + there, part))
        placed.append(((1 - rows) * columns + there, shift(part, "row", 1)))
    return placed


def assemble(placed, group):
    count = len(placed)
    rows, columns = placed[0][1].shape
    total = jnp.zeros((group, count, rows // group, columns), placed[0][1].dtype)
    for place, part in placed:
        total = lax.dynamic_update_slice(
            total, part.reshape(group, 1, rows // group, columns), (0, place, 0, 0)
        )
    return total.reshape(count * rows, columns)


def gather_rc(values):
    columns = lax.axis_size("col")
    return assemble(
        all_places([values] + [shift(values, "col", by) for by in range(1, columns)]), 1
    )


def block_of(array, at, rows):
    return lax.dynamic_slice_in_dim(array, at * rows, rows)


def scatter_row(values, group=1):
    row = lax.axis_index("row")
    halves = values.reshape(group, 2, -1, values.shape[1])
    pick = lambda which: lax.dynamic_index_in_dim(halves, which, 1, keepdims=False)
    away = shift(pick(1 - row), "row", 1)
    return (pick(row).astype(F32) + away.astype(F32)).astype(values.dtype)


def scatter_col(kept):
    columns, col = lax.axis_size("col"), lax.axis_index("col")
    parts = kept.reshape(kept.shape[0], columns, -1, kept.shape[2])
    pick = lambda which: lax.dynamic_index_in_dim(parts, which, 1, keepdims=False)
    total = pick(col).astype(F32)
    for by in range(1, columns):
        total = total + shift(pick((col + by) % columns), "col", by).astype(F32)
    return total.reshape(-1, kept.shape[2])


def parts_of_columns(kept):
    columns, col = lax.axis_size("col"), lax.axis_index("col")
    parts = kept.reshape(kept.shape[0], columns, -1, kept.shape[2])
    pick = lambda which: lax.dynamic_index_in_dim(parts, which, 1, keepdims=False)
    return [pick((col + by) % columns).reshape(-1, kept.shape[2]) for by in range(columns)]


def scatter_rc(values):
    return scatter_col(scatter_row(values))


def scatter_squares(values):
    columns, col = lax.axis_size("col"), lax.axis_index("col")
    kept = scatter_row(values)[0]
    rows = kept.shape[0] // columns
    total = block_of(kept, col, rows)
    for by in range(1, columns):
        total = total + shift(block_of(kept, (col + by) % columns, rows), "col", by)
    return total


def partners(shape):
    steps = []
    for name in ("dp", "row", "col"):
        bit = 1
        while bit < shape[name]:
            steps.append((name, bit))
            bit *= 2
    return steps


DEEP = 4
MESH_ID = pl.DeviceIdType.MESH
ANY = pl.BlockSpec(memory_space=pl.ANY)


def near_first(place, step, size):
    if size == 1:
        return place
    if size == 2:
        return place + step * (1 - 2 * place)
    side = place // 2
    inner = (place * (3 - place)) // 2
    found = step + inner * (1 - 2 * step) * (1 - step // 2)
    return found + side * (3 - 2 * found)


class Grid:
    def __init__(self, size):
        self.size, self.deep, self.across = size, DEEP, size // DEEP
        self.me = lax.axis_index("dp")
        self.z, self.x = self.me // self.across, self.me % self.across
        self.steps = (-self.across, self.across, -1, 1)
        self.exists = (
            self.z > 0,
            self.z < self.deep - 1,
            self.x > 0,
            self.x < self.across - 1,
        )
        self.count = (
            jnp.minimum(self.z, 1)
            + jnp.minimum(self.deep - 1 - self.z, 1)
            + jnp.minimum(self.x, 1)
            + jnp.minimum(self.across - 1 - self.x, 1)
        )

    def greet(self, barrier):
        for there, step in zip(self.exists, self.steps):
            @pl.when(there)
            def _():
                pl.semaphore_signal(
                    barrier, inc=1, device_id={"dp": self.me + step}, device_id_type=MESH_ID
                )


def gather_kernel(size, columns, *refs):
    count = PLAIN + BOTH
    hidden_ref, vec_ref, in_ref, step_ref, out_ref, up_ref, down_ref, state_ref, router_ref = refs[:9]
    routes_ref, expert_up_ref, expert_down_ref, refs = refs[9], refs[10], refs[11], refs[12:]
    outs, lows, down_came, refs = (
        refs[: count + 1], refs[count + 1 : count + 3], refs[count + 3], refs[count + 4 :]
    )
    ins, refs = refs[: count + 1], refs[count + 1 :]
    step_wide, router_wide, refs = refs[0], refs[1], refs[2:]
    dp_send, dp_recv, sh_send, sh_recv, rc_send, rc_recv, keep_sem, side_send, side_recv = refs
    mixer, step, out, mask, up, down, small, tokens = ins
    states = state_ref.shape[1]
    grid = Grid(size)
    me, z, x = grid.me, grid.z, grid.x
    row, col = lax.axis_index("row"), lax.axis_index("col")
    mine, other_row = row * columns + col, {"row": 1 - row}
    to_col = lambda by: {"col": (col + by) % columns}
    from_col = lambda by: row * columns + (col + by) % columns
    barrier = pltpu.get_barrier_semaphore()
    grid.greet(barrier)
    pl.semaphore_signal(barrier, inc=1, device_id=other_row, device_id_type=MESH_ID)
    for by in range(1, columns):
        pl.semaphore_signal(barrier, inc=1, device_id=to_col(by), device_id_type=MESH_ID)
    pl.semaphore_wait(barrier, grid.count + columns)

    def block(which, chunk, place):
        return outs[which].at[chunk] if which < PLAIN else outs[which].at[chunk, place]

    def push(which, chunk, way, source=None):
        ref = block(which, chunk, mine)
        return pltpu.make_async_remote_copy(
            src_ref=ref if source is None else source,
            dst_ref=ref,
            send_sem=dp_send.at[which, way, chunk],
            recv_sem=dp_recv.at[which, chunk],
            device_id={"dp": me + grid.steps[way]},
            device_id_type=MESH_ID,
        )

    def spread(which, chunk, place, index, peer, source=None):
        ref = block(which, chunk, place)
        return pltpu.make_async_remote_copy(
            src_ref=ref if source is None else source,
            dst_ref=ref,
            send_sem=sh_send.at[which - PLAIN, index, chunk],
            recv_sem=sh_recv.at[which - PLAIN, place, chunk],
            device_id=peer,
            device_id_type=MESH_ID,
        )

    def spread_tokens(place, index, peer, source=None):
        ref = outs[count].at[place]
        return pltpu.make_async_remote_copy(
            src_ref=ref if source is None else source,
            dst_ref=ref,
            send_sem=rc_send.at[index],
            recv_sem=rc_recv.at[place],
            device_id=peer,
            device_id_type=MESH_ID,
        )

    def place_of(number):
        if grid.across == 2:
            even, first, last = 1 - number % 2, 1 - jnp.minimum(number, 1), number // 7
            step = (1 - even) * ((number + 1) // 2 - last) + even * (number // 2 - 1 + first)
            side = even * (1 - first) + last
        else:
            step, side = number % grid.deep, number // grid.deep
        zc = near_first(z, step, grid.deep)
        xc = near_first(x, side, grid.across)
        ways = [
            way & there for way, there in zip((zc >= z, zc <= z, xc >= x, xc <= x), grid.exists)
        ]
        same_x, same_z = xc == x, zc == z
        z_first = [same_x & ways[0], same_x & ways[1], ways[2], ways[3]]
        x_first = [ways[0], ways[1], same_z & ways[2], same_z & ways[3]]
        return zc * grid.across + xc, [
            x_first if which in X_FIRST else z_first for which in range(count)
        ]

    def spread_one(which, chunk, source=None):
        spread(which, chunk, mine, 0, other_row, source).start()
        for by in range(1, columns):
            spread(which, chunk, mine, by, to_col(by), source).start()

    def pass_on(number, _):
        chunk, onward = place_of(number)
        for which in SMALL_FIRST:
            push(which, chunk, 0).wait_recv()
            for way in range(4):
                @pl.when(onward[which][way])
                def _():
                    push(which, chunk, way).start()
            if which >= PLAIN:
                spread_one(which, chunk)
        return 0

    def push_own(first, last):
        for way in range(4):
            @pl.when(grid.exists[way])
            def _():
                for which in range(first, last):
                    push(which, me, way, ins[which]).start()

    for head in range(in_ref.shape[0]):
        mixer[:, 128 * head : 128 * (head + 1)] = in_ref[head].astype(BF16)
    push_own(0, 1)
    values = hidden_ref[...].astype(F32)
    gain = jnp.concatenate([vec_ref[line : line + 1, :] for line in range(values.shape[1] // 128)], axis=1)
    mean = jnp.sum(values * values, axis=1, keepdims=True) / values.shape[1]
    tokens[...] = (values * lax.rsqrt(mean + 1e-05) * gain).astype(BF16)
    spread_tokens(mine, 0, other_row, ins[count]).start()
    for by in range(1, columns):
        spread_tokens(mine, by, to_col(by), ins[count]).start()
    step_wide[...] = jnp.zeros_like(step_wide)
    step_wide[0 : step_ref.shape[0], :] = step_ref[...]
    router_wide[...] = jnp.zeros_like(router_wide)
    router_wide[0 : router_ref.shape[0], :] = router_ref[...]
    step[...] = step_wide[...].T.astype(BF16)
    out[...] = out_ref[...].T.astype(BF16)
    expert = lax.broadcasted_iota(jnp.int32, mask.shape, 0)
    named = expert == routes_ref[0:1, :]
    for route in range(1, TOPK):
        named = named | (expert == routes_ref[route : route + 1, :])
    mask[...] = jnp.where(named, 1.0, 0.0).astype(BF16)
    up[...] = up_ref[...].astype(BF16)
    down[...] = down_ref[...].astype(BF16)
    small[:, 0:states] = state_ref[...].astype(BF16)
    small[:, states:] = router_wide[...].T.astype(BF16)
    push_own(1, count)
    keeps = [
        pltpu.make_async_copy(ins[which], block(which, me, mine), keep_sem.at[which])
        for which in range(count)
    ]
    keeps.append(pltpu.make_async_copy(ins[count], outs[count].at[mine], keep_sem.at[count]))
    for copy in keeps:
        copy.start()
    for held in range(EXP_DEV):
        width = expert_up_ref.shape[2]
        lows[0][:, width * held : width * (held + 1)] = expert_up_ref[held].astype(BF16)
    lows[1][...] = expert_down_ref[...].astype(BF16)
    for by in range(1, columns):
        spread_tokens(from_col(by), columns - 1 + by, other_row).wait_recv()
        spread_tokens(from_col(by), columns - 1 + by, other_row).start()
    sides = [
        pltpu.make_async_remote_copy(
            src_ref=lows[1],
            dst_ref=down_came.at[by - 1],
            send_sem=side_send.at[by - 1],
            recv_sem=side_recv.at[by - 1],
            device_id=to_col(by),
            device_id_type=MESH_ID,
        )
        for by in range(1, columns)
    ]
    for copy in sides:
        copy.start()
    for which in range(PLAIN, count):
        spread_one(which, me, ins[which])
    lax.fori_loop(1, size, pass_on, 0)

    def forward_chunk(number, _):
        chunk = place_of(number)[0]
        for which in range(PLAIN, count):
            for by in range(1, columns):
                place = from_col(by)
                spread(which, chunk, place, columns - 1 + by, other_row).wait_recv()
                spread(which, chunk, place, columns - 1 + by, other_row).start()
        return 0

    lax.fori_loop(0, size, forward_chunk, 0)

    def finish(number, _):
        chunk, onward = place_of(number)
        for which in range(PLAIN, count):
            for by in range(columns):
                spread(which, chunk, (1 - row) * columns + (col + by) % columns, 0, other_row).wait_recv()
            for index in range(2 * columns - 1):
                spread(which, chunk, mine, index, other_row).wait_send()
        for way in range(4):
            for which in range(count):
                @pl.when(onward[which][way])
                def _():
                    push(which, chunk, way).wait_send()
        return 0

    lax.fori_loop(0, size, finish, 0)
    for by in range(columns):
        spread_tokens((1 - row) * columns + (col + by) % columns, 0, other_row).wait_recv()
    for index in range(2 * columns - 1):
        spread_tokens(mine, index, other_row).wait_send()
    for copy in keeps + sides:
        copy.wait()


PLAIN, BOTH = 4, 3
SMALL_FIRST = (3, 6, 1, 5, 4, 2, 0)
X_FIRST = (4,)


def gather_start(
    hidden, vec, in_weight, step, out_weight, shared_up, shared_down, state, router, routes, expert_up, expert_down, shape
):
    size, columns = shape["dp"], shape["col"]
    places, count = 2 * columns, PLAIN + BOTH
    heads, rows = in_weight.shape[:2]
    blocks = [
        (rows, 128 * heads),
        (rows, 128),
        (out_weight.shape[1], out_weight.shape[0]),
        (EXP_DEV * size, hidden.shape[0]),
        shared_up.shape,
        shared_down.shape,
        (state.shape[0], state.shape[1] + 128),
        hidden.shape,
    ]
    lead = [(size,)] * PLAIN + [(size, places)] * BOTH + [(places,)]
    results = pl.pallas_call(
        functools.partial(gather_kernel, size, columns),
        out_shape=tuple(jax.ShapeDtypeStruct(at + block, BF16) for at, block in zip(lead, blocks))
        + (
            jax.ShapeDtypeStruct((expert_up.shape[1], EXP_DEV * expert_up.shape[2]), BF16),
            jax.ShapeDtypeStruct(expert_down.shape, BF16),
            jax.ShapeDtypeStruct((columns - 1,) + expert_down.shape, BF16),
        ),
        in_specs=[VM] * 12,
        out_specs=(ANY,) * (count + 1) + (VM,) * 2 + (ANY,),
        scratch_shapes=[pltpu.VMEM(block, BF16) for block in blocks]
        + [
            pltpu.VMEM((128, rows), F32),
            pltpu.VMEM((128, state.shape[0]), F32),
            pltpu.SemaphoreType.DMA((count, 4, size)),
            pltpu.SemaphoreType.DMA((count, size)),
            pltpu.SemaphoreType.DMA((BOTH, 2 * columns - 1, size)),
            pltpu.SemaphoreType.DMA((BOTH, places, size)),
            pltpu.SemaphoreType.DMA((2 * columns - 1,)),
            pltpu.SemaphoreType.DMA((places,)),
            pltpu.SemaphoreType.DMA((count + 1,)),
            pltpu.SemaphoreType.DMA((columns - 1,)),
            pltpu.SemaphoreType.DMA((columns - 1,)),
        ],
        compiler_params=pltpu.CompilerParams(
            collective_id=2, has_side_effects=True, vmem_limit_bytes=58 * 2**20
        ),
        cost_estimate=lasting(105),
        name="gather_start",
    )(
        hidden, vec, in_weight, step, out_weight, shared_up, shared_down, state, router, routes, expert_up, expert_down
    )
    up, down, down_came = results[count + 1 :]
    return (
        *[result.reshape(-1, result.shape[-1]) for result in results[: count + 1]],
        up,
        [down] + [down_came[by - 1] for by in range(1, columns)],
    )


class LineSum:
    def __init__(
        self, grid, part_ref, out_ref, sums, from_x, from_z, x_send, x_recv, z_send, z_recv, own_ref=None
    ):
        self.grid, self.part_ref, self.out_ref, self.own_ref = grid, part_ref, out_ref, own_ref
        self.sums, self.from_x, self.from_z = sums, from_x, from_z
        self.x_send, self.x_recv, self.z_send, self.z_recv = x_send, x_recv, z_send, z_recv

    @staticmethod
    def scratch(size, chunk):
        pair = size == 2 * DEEP
        return [
            pltpu.VMEM((DEEP if pair else size,) + chunk, BF16),
            pltpu.VMEM((DEEP if pair else 2 * size,) + chunk, BF16),
            pltpu.VMEM((DEEP + 1,) + chunk, BF16),
            pltpu.SemaphoreType.DMA((size,)),
            pltpu.SemaphoreType.DMA((2 * size,)),
            pltpu.SemaphoreType.DMA((DEEP,)),
            pltpu.SemaphoreType.DMA((DEEP + 1,)),
        ]

    def sum_slot(self, line, there):
        return line if self.grid.across == 2 else line * self.grid.across + there

    def x_slot(self, line, there, way):
        return line if self.grid.across == 2 else way * self.grid.size + line * self.grid.across + there

    def along_x(self, line, there, way):
        grid = self.grid
        chunk = line * grid.across + there
        return pltpu.make_async_remote_copy(
            src_ref=self.part_ref.at[chunk] if grid.across == 2 else self.sums.at[self.sum_slot(line, there)],
            dst_ref=self.from_x.at[self.x_slot(line, there, way)],
            send_sem=self.x_send.at[chunk],
            recv_sem=self.x_recv.at[way * grid.size + chunk],
            device_id={"dp": grid.me + 2 * way - 1},
            device_id_type=MESH_ID,
        )

    def along_z(self, line, way, receiving):
        grid = self.grid
        end = grid.z if receiving else grid.z + 2 * way - 1
        slot = line if way else line + (1 - jnp.minimum(jnp.abs(line - end), 1)) * (grid.deep - line)
        return pltpu.make_async_remote_copy(
            src_ref=self.sums.at[self.sum_slot(line, grid.x)],
            dst_ref=self.from_z.at[slot],
            send_sem=self.z_send.at[line],
            recv_sem=self.z_recv.at[slot],
            device_id={"dp": grid.me + (2 * way - 1) * grid.across},
            device_id_type=MESH_ID,
        ), slot

    def collect(self, line):
        grid, out_ref, x = self.grid, self.out_ref, self.grid.x
        mine = self.part_ref[line * grid.across + x] if self.own_ref is None else self.own_ref[line]
        out_ref[...] = mine.astype(F32)
        for way, there in ((1, grid.exists[2]), (0, grid.exists[3])):
            @pl.when(there)
            def _():
                self.along_x(line, x, way).wait_recv()
                out_ref[...] += self.from_x[self.x_slot(line, x, way)].astype(F32)
        for way, comes in (
            (1, grid.exists[0] & (line >= grid.z)), (0, grid.exists[1] & (line <= grid.z))
        ):
            @pl.when(comes)
            def _():
                copy, slot = self.along_z(line, way, True)
                copy.wait_recv()
                out_ref[...] += self.from_z[slot].astype(F32)
        for way, toward in ((1, line > grid.z), (0, line < grid.z)):
            @pl.when(toward)
            def _():
                self.sums[self.sum_slot(line, x)] = out_ref[...].astype(BF16)
                self.along_z(line, way, False)[0].start()

    def wait_sent(self, line, there):
        grid, x = self.grid, self.grid.x
        for way in range(2):
            @pl.when((there > x) if way else (there < x))
            def _():
                self.along_x(line, there, way).wait_send()

            @pl.when((there == x) & ((line > grid.z) if way else (line < grid.z)))
            def _():
                self.along_z(line, way, False)[0].wait_send()

    @staticmethod
    def start(sums):
        grid = sums[0].grid
        x, across = grid.x, grid.across

        def away(number, _):
            line = near_first(grid.z, grid.deep - 1 - number // (across - 1), grid.deep)
            there = near_first(x, across - 1 - number % (across - 1), across)
            for one in sums:
                if across > 2:
                    held = one.sums.at[one.sum_slot(line, there)]
                    if one.own_ref is None:
                        held[...] = one.part_ref[line * across + there]
                    else:
                        pltpu.sync_copy(one.part_ref.at[line * across + there], held)
                for way, beyond in ((1, grid.exists[2]), (0, grid.exists[3])):
                    toward = (there > x) if way else (there < x)
                    if across > 2:
                        @pl.when(toward & beyond)
                        def _():
                            one.along_x(line, there, way).wait_recv()
                            held = one.sums.at[one.sum_slot(line, there)]
                            held[...] = (
                                held[...].astype(F32)
                                + one.from_x[one.x_slot(line, there, way)].astype(F32)
                            ).astype(BF16)
                    @pl.when(toward)
                    def _():
                        one.along_x(line, there, way).start()
            return 0

        lax.fori_loop(0, grid.deep * (across - 1), away, 0)

    @staticmethod
    def finish(sums, between=None, after=None):
        grid = sums[0].grid

        def collect(number, _):
            if between is not None:
                between(number)
            line = near_first(grid.z, grid.deep - 1 - number, grid.deep)
            for place, one in enumerate(sums):
                one.collect(line)
                if after is not None and place == 0:
                    @pl.when(number == grid.deep - 1)
                    def _():
                        after()
            return 0

        lax.fori_loop(0, grid.deep, collect, 0)
        def wait(number, _):
            line = near_first(grid.z, grid.deep - 1 - number // grid.across, grid.deep)
            there = near_first(grid.x, grid.across - 1 - number % grid.across, grid.across)
            for one in sums:
                one.wait_sent(line, there)
            return 0

        lax.fori_loop(0, grid.size, wait, 0)


TILE = 256


def scatter_kernel(size, columns, part_ref, x_ref, dpre_ref, hid_ref, g_ref, out_ref, *refs):
    up_refs, down_refs, refs = refs[:columns], refs[columns : 2 * columns], refs[2 * columns :]
    dpre_now, g_now, left, turned, stage, sent, came = refs[:7]
    whole_sem, left_sem, stage_sem, row_send, row_recv = refs[7:12]
    grid = Grid(size)
    row = lax.axis_index("row")
    barrier = pltpu.get_barrier_semaphore()
    grid.greet(barrier)
    pl.semaphore_signal(barrier, inc=1, device_id={"row": 1 - row}, device_id_type=MESH_ID)
    pl.semaphore_wait(barrier, grid.count + 1)
    own, own_sem = refs[12:14]
    sums = [LineSum(grid, part_ref, out_ref, *refs[14:], own_ref=own)]
    LineSum.start(sums)
    loads = [
        pltpu.make_async_copy(part_ref.at[line * grid.across + grid.x], own.at[line], own_sem.at[line])
        for line in range(DEEP)
    ]
    for copy in loads:
        copy.start()

    width = g_now.shape[1]
    part_rows = [columns_of[0].shape[0] for columns_of in (up_refs, down_refs)]
    ups, downs = (columns * rows // TILE for rows in part_rows)
    half = ups + downs
    bring_dpre = pltpu.make_async_copy(dpre_ref, dpre_now, whole_sem.at[0])
    bring_g = pltpu.make_async_copy(g_ref, g_now, whole_sem.at[1])
    begin, end = lambda copy: copy.start(), lambda copy: copy.wait()

    def bring(tile, do):
        whose = row + (1 - tile // half) * (1 - 2 * row)
        within = tile % half

        @pl.when((within < ups) & (tile < 2 * half))
        def _():
            at = pl.ds(pl.multiple_of((whose * ups + within) * TILE, TILE), TILE)
            do(pltpu.make_async_copy(x_ref.at[:, at], left.at[tile % 2], left_sem.at[tile % 2]))

        @pl.when((within >= ups) & (tile < 2 * half))
        def _():
            at = pl.ds(pl.multiple_of(((within - ups) * 2 + whose) * TILE, TILE), TILE)
            do(pltpu.make_async_copy(hid_ref.at[:, at], left.at[tile % 2], left_sem.at[tile % 2]))

    def push(within):
        return pltpu.make_async_remote_copy(
            src_ref=sent.at[within],
            dst_ref=came.at[within],
            send_sem=row_send.at[within],
            recv_sem=row_recv.at[within],
            device_id={"row": 1 - row},
            device_id_type=MESH_ID,
        )

    col = lax.axis_index("col")
    piece = TILE // columns
    up_piece = TILE // 2

    def leave(within, do):
        for at in range(0, TILE, up_piece):
            @pl.when((within >= 0) & (within < ups))
            def _():
                first = within * TILE + at
                whose = (first // part_rows[0] + columns - col) % columns
                rows = pl.ds(pl.multiple_of(first % part_rows[0], up_piece), up_piece)
                for by in range(columns):
                    @pl.when(whose == by)
                    def _():
                        do(
                            pltpu.make_async_copy(
                                stage.at[within % 2, pl.ds(at, up_piece)],
                                up_refs[by].at[rows],
                                stage_sem.at[within % 2, at // up_piece],
                            )
                        )

        for place in range(columns):
            @pl.when(within >= ups)
            def _():
                whose = (place + columns - col) % columns
                rows = pl.ds(pl.multiple_of((within - ups) * piece, piece), piece)
                for by in range(columns):
                    @pl.when(whose == by)
                    def _():
                        do(
                            pltpu.make_async_copy(
                                stage.at[within % 2, pl.ds(place * piece, piece), pl.ds(0, width)],
                                down_refs[by].at[rows],
                                stage_sem.at[within % 2, place],
                            )
                        )

    bring(0, begin)
    bring_dpre.start()
    bring_g.start()
    bring_dpre.wait()
    bring_g.wait()
    for copy in loads:
        copy.wait()

    def work(tile, _):
        within = tile % half
        bring(tile + 1, begin)
        bring(tile, end)

        @pl.when(tile >= half)
        def _():
            leave(within - 2, end)
            push(within).wait_recv()

        turned[...] = left[tile % 2].T
        for wanted, right in ((within < ups, dpre_now), (within >= ups, g_now)):
            for theirs in (True, False):
                @pl.when(wanted & ((tile < half) if theirs else (tile >= half)))
                def _():
                    for at in range(0, right.shape[1], 512):
                        lanes = slice(at, at + 512)
                        found = dot_f32(turned[...], right[:, lanes])
                        if theirs:
                            sent[within, :, lanes] = found.astype(BF16)
                        else:
                            stage[within % 2, :, lanes] = (
                                found + came[within, :, lanes].astype(F32)
                            ).astype(BF16)

        @pl.when(tile < half)
        def _():
            push(within).start()

        @pl.when(tile >= half)
        def _():
            leave(within, begin)

        return 0

    def between(number):
        done = [0, 2 * half * 2 // 5, 2 * half * 7 // 10, 2 * half * 7 // 10, 2 * half]
        bounds = [jnp.int32(0), jnp.int32(0)]
        for step in range(DEEP):
            now = 1 - jnp.minimum(jnp.abs(number - step), 1)
            bounds = [bounds[0] + now * done[step], bounds[1] + now * done[step + 1]]
        lax.fori_loop(bounds[0], bounds[1], work, 0)

    LineSum.finish(sums, between)
    leave(half - 2, end)
    leave(half - 1, end)

    def sent_all(within, _):
        push(within).wait_send()
        return 0

    lax.fori_loop(0, half, sent_all, 0)


def scatter_blocks(parts, tokens, dpre, hidden, cotangents, shape):
    size, width = shape["dp"], tokens.shape[1]
    if size > 2 * DEEP:
        up = scatter_row(dot_tn(tokens, dpre).astype(BF16))
        down = scatter_row(dot_tn(hidden, cotangents).astype(BF16), EXP_DEV)
        return scatter_dp(parts).astype(F32), parts_of_columns(up), parts_of_columns(down)
    columns = shape["col"]
    parts = parts.reshape((size, -1, parts.shape[1]))
    chunk, count = parts.shape[1:], tokens.shape[0]
    up_half, down_half = width // 2, hidden.shape[1] // 2
    half = (up_half + down_half) // TILE
    results = pl.pallas_call(
        functools.partial(scatter_kernel, size, columns),
        out_shape=(jax.ShapeDtypeStruct(chunk, F32),)
        + (jax.ShapeDtypeStruct((up_half // columns, dpre.shape[1]), BF16),) * columns
        + (jax.ShapeDtypeStruct((down_half // columns, width), BF16),) * columns,
        in_specs=[ANY] * 5,
        out_specs=(VM,) + (ANY,) * (2 * columns),
        scratch_shapes=[
            pltpu.VMEM(dpre.shape, BF16),
            pltpu.VMEM((count, width), BF16),
            pltpu.VMEM((2, count, TILE), BF16),
            pltpu.VMEM((TILE, count), BF16),
            pltpu.VMEM((2, TILE, dpre.shape[1]), BF16),
            pltpu.VMEM((half, TILE, dpre.shape[1]), BF16),
            pltpu.VMEM((half, TILE, dpre.shape[1]), BF16),
            pltpu.SemaphoreType.DMA((2,)),
            pltpu.SemaphoreType.DMA((2,)),
            pltpu.SemaphoreType.DMA((2, max(2, columns))),
            pltpu.SemaphoreType.DMA((half,)),
            pltpu.SemaphoreType.DMA((half,)),
            pltpu.VMEM((DEEP,) + chunk, BF16),
            pltpu.SemaphoreType.DMA((DEEP,)),
        ]
        + LineSum.scratch(size, chunk),
        compiler_params=pltpu.CompilerParams(
            collective_id=5, has_side_effects=True, vmem_limit_bytes=60 * 2**20
        ),
        cost_estimate=lasting(78),
        name="scatter_blocks",
    )(parts, tokens, dpre, hidden, cotangents)
    return results[0], results[1 : 1 + columns], results[1 + columns :]


def adam_step(weight, grad, first, second, rate, decay=0.1):
    first_new = 0.9 * first + 0.1 * grad
    second_new = 0.95 * second + 0.05 * grad * grad
    corrected_one = first_new / (1.0 - 0.9**STEP)
    corrected_two = second_new / (1.0 - 0.95**STEP)
    weight_new = weight - rate * (
        corrected_one / (jnp.sqrt(corrected_two) + 1e-08) + decay * weight
    )
    return (first_new, second_new, weight_new)


SMALL_SUMS = (1, 4, 3, 2, 0)
NARROW = 1


def end_kernel(size, steps, columns, count, *refs):
    take = lambda number: (refs[:number], refs[number:])
    part_refs, refs = take(count)
    (value_ref, seq_ref), refs = take(2)
    out_refs, refs = take(count)
    (total_ref, small_ref, rows_ref), refs = take(3)
    (landed, half_now, half_in, quarter, quarter_in, seq_half, seq_sent, seq_in), refs = take(8)
    (t_send, t_recv, s_send, s_recv, q_send, q_recv), scratch = take(6)
    out_ref = out_refs[NARROW]
    grid = Grid(size)
    row, col = lax.axis_index("row"), lax.axis_index("col")

    def other(name, bit):
        place = lax.axis_index(name)
        return {name: place + bit * (1 - 2 * ((place // bit) % 2))}

    barrier = pltpu.get_barrier_semaphore()
    grid.greet(barrier)
    for name, bit in steps:
        pl.semaphore_signal(barrier, inc=1, device_id=other(name, bit), device_id_type=MESH_ID)
    for by in range(1, columns):
        pl.semaphore_signal(
            barrier, inc=1, device_id={"col": (col + by) % columns}, device_id_type=MESH_ID
        )
    pl.semaphore_wait(barrier, grid.count + len(steps) + columns - 1)

    seq_rows, block = seq_half.shape[0], rows_ref.shape[0]
    swap_rows = pltpu.make_async_remote_copy(
        src_ref=seq_ref.at[pl.ds(pl.multiple_of((1 - row) * seq_rows, 16), seq_rows)],
        dst_ref=seq_half,
        send_sem=q_send.at[0],
        recv_sem=q_recv.at[0],
        device_id={"row": 1 - row},
        device_id_type=MESH_ID,
    )
    swap_rows.start()

    total_ref[...] = value_ref[...]

    def exchange(number, meanwhile=None):
        name, bit = steps[number]
        copy = pltpu.make_async_remote_copy(
            src_ref=total_ref,
            dst_ref=landed.at[number],
            send_sem=t_send.at[number],
            recv_sem=t_recv.at[number],
            device_id=other(name, bit),
            device_id_type=MESH_ID,
        )
        copy.start()
        if meanwhile is not None:
            meanwhile()
        copy.wait()
        total_ref[...] += landed[number]

    early = len([1 for name, bit in steps if name == "dp" and bit < grid.across])
    owns, own_sem, scratch = scratch[:count], scratch[count], scratch[count + 1 :]
    sums = [
        LineSum(
            grid,
            part_refs[number],
            out_refs[number],
            *scratch[7 * number : 7 * number + 7],
            own_ref=owns[number],
        )
        for number in range(count)
    ]
    for number in range(early - 1):
        exchange(number)
    exchange(early - 1, lambda: LineSum.start(sums))
    loads = [
        pltpu.make_async_copy(
            part_refs[number].at[line * grid.across + grid.x], owns[number].at[line], own_sem.at[number, line]
        )
        for line in range(DEEP)
        for number in range(count)
    ]
    for copy in loads:
        copy.start()

    def both_rows(place):
        mine = seq_ref[pl.ds(pl.multiple_of(row * seq_rows + place * block, 16), block), :]
        theirs = seq_half[pl.ds(pl.multiple_of(place * block, 16), block), :]
        return mine.astype(F32) + theirs.astype(F32)

    swap_rows.wait()
    moves = []
    for by in range(1, columns):
        to = (col + by) % columns
        seq_sent[by - 1] = both_rows(to).astype(BF16)
        moves.append(
            pltpu.make_async_remote_copy(
                src_ref=seq_sent.at[by - 1],
                dst_ref=seq_in.at[by - 1],
                send_sem=q_send.at[by],
                recv_sem=q_recv.at[by],
                device_id={"col": to},
                device_id_type=MESH_ID,
            )
        )
    for number in range(early, len(steps)):
        exchange(number)
    for copy in moves:
        copy.start()
    rows_ref[...] = both_rows(col)
    for copy in loads:
        copy.wait()
    half, fourth = half_now.shape[0], small_ref.shape[0]
    swap = pltpu.make_async_remote_copy(
        src_ref=half_now,
        dst_ref=half_in,
        send_sem=s_send.at[0],
        recv_sem=s_recv.at[0],
        device_id={"row": 1 - row},
        device_id_type=MESH_ID,
    )

    def swap_narrow():
        half_now[...] = out_ref[pl.ds(pl.multiple_of((1 - row) * half, 8), half), :]
        swap.start()

    LineSum.finish([sums[number] for number in SMALL_SUMS], after=swap_narrow)
    swap.wait()
    both = out_ref[pl.ds(pl.multiple_of(row * half, 8), half), :] + half_in[...]
    for place in range(columns):
        quarter[place] = both[place * fourth : (place + 1) * fourth]
    copies = []
    for by in range(1, columns):
        to = (col + by) % columns
        copies.append(
            pltpu.make_async_remote_copy(
                src_ref=quarter.at[to],
                dst_ref=quarter_in.at[by],
                send_sem=s_send.at[by],
                recv_sem=s_recv.at[by],
                device_id={"col": to},
                device_id_type=MESH_ID,
            )
        )
        copies[-1].start()
    small_ref[...] = quarter[col]
    for by, copy in enumerate(moves):
        copy.wait()
        rows_ref[...] += seq_in[by].astype(F32)
    for by, copy in enumerate(copies):
        copy.wait()
        small_ref[...] += quarter_in[by + 1]


def scatter_end(parts, values, rows, shape):
    size, columns = shape["dp"], shape["col"]
    steps = partners(shape)
    parts = [part.reshape((size, -1, part.shape[1])) for part in parts]
    (length, narrow), count = parts[NARROW].shape[1:], len(parts)
    half, seq_rows = length // 2, rows.shape[0] // 2
    block = (seq_rows // columns, rows.shape[1])
    fourth = (columns, half // columns, narrow)
    return pl.pallas_call(
        functools.partial(end_kernel, size, steps, columns, count),
        out_shape=tuple(jax.ShapeDtypeStruct(part.shape[1:], F32) for part in parts)
        + (
            jax.ShapeDtypeStruct(values.shape, F32),
            jax.ShapeDtypeStruct(fourth[1:], F32),
            jax.ShapeDtypeStruct(block, F32),
        ),
        in_specs=[ANY] * count + [VM] * 2,
        out_specs=(VM,) * (count + 3),
        scratch_shapes=[
            pltpu.VMEM((len(steps),) + values.shape, F32),
            pltpu.VMEM((half, narrow), F32),
            pltpu.VMEM((half, narrow), F32),
            pltpu.VMEM(fourth, F32),
            pltpu.VMEM(fourth, F32),
            pltpu.VMEM((seq_rows, rows.shape[1]), BF16),
            pltpu.VMEM((columns - 1,) + block, BF16),
            pltpu.VMEM((columns - 1,) + block, BF16),
            pltpu.SemaphoreType.DMA((len(steps),)),
            pltpu.SemaphoreType.DMA((len(steps),)),
            pltpu.SemaphoreType.DMA((columns,)),
            pltpu.SemaphoreType.DMA((columns,)),
            pltpu.SemaphoreType.DMA((columns,)),
            pltpu.SemaphoreType.DMA((columns,)),
        ]
        + [pltpu.VMEM((DEEP,) + part.shape[1:], BF16) for part in parts]
        + [pltpu.SemaphoreType.DMA((count, DEEP))]
        + sum([LineSum.scratch(size, part.shape[1:]) for part in parts], []),
        compiler_params=pltpu.CompilerParams(
            collective_id=3, has_side_effects=True, vmem_limit_bytes=60 * 2**20
        ),
        cost_estimate=lasting(1),
        name="scatter_end",
    )(*parts, values, rows)


def steps_kernel(mixer_ref, out_ref, up_ref, down_ref, small_ref, step_ref, *refs):
    (two_ref, mixture_ref, shared_ref), (hidden_ref, gain_ref, normed_ref, later_ref), refs = (
        refs[:3], refs[3:7], refs[7:]
    )
    ins, (result_ref, input_ref), outs = refs[:21], refs[21:23], refs[23:]
    result_ref[...] = (two_ref[...] + mixture_ref[...].astype(F32) + shared_ref[...]).astype(BF16)
    values = hidden_ref[...].astype(F32)
    scale = lax.rsqrt(jnp.sum(values * values, axis=1, keepdims=True) / values.shape[1] + 1e-05)
    weighted = normed_ref[...] * gain_ref[...]
    mean = jnp.sum(weighted * values, axis=1, keepdims=True) / values.shape[1]
    input_ref[...] = scale * weighted - values * scale * scale * scale * mean + later_ref[...]
    rate = MODEL_WIDTH ** (-0.5)
    weights, firsts, seconds = ins[0::3], ins[1::3], ins[2::3]

    def put(number, grad, rate, at=...):
        values = adam_step(weights[number][at], grad, firsts[number][at], seconds[number][at], rate)
        for place, value in enumerate(values):
            outs[3 * number + place][at] = value

    for head in range(weights[0].shape[0]):
        put(0, mixer_ref[:, 128 * head : 128 * (head + 1)], rate, head)
    put(1, step_ref[:, 2 * STATE :].T[0 : weights[1].shape[0]], rate)
    put(2, out_ref[...].T, INNER ** (-0.5))
    put(3, small_ref[:, 0 : 2 * STATE], rate)
    routes = small_ref[:, 2 * STATE :].T
    put(4, routes[ROUTER_AT : ROUTER_AT + weights[4].shape[0]], 0.5 * rate)
    put(5, up_ref[...], rate)
    put(6, down_ref[...], FF_S ** (-0.5))


def held_kernel(rate, count, *refs):
    grads, (weight, first, second), outs = refs[:count], refs[count : count + 3], refs[count + 3 :]
    grad = grads[0][...].astype(F32)
    for more in grads[1:]:
        grad = grad + more[...].astype(F32)
    for out, value in zip(outs, adam_step(weight[0], grad, first[0], second[0], rate)):
        out[0] = value


def expert_steps(grads, arrays, rate, by_rows):
    held, rows, width = arrays[0].shape
    tile = rows // 2
    grad_at = (lambda h, i: (2 * h + i, 0)) if by_rows else (lambda h, i: (i, h))
    block = pl.BlockSpec((1, tile, width), lambda h, i: (h, i, 0))
    return pl.pallas_call(
        functools.partial(held_kernel, rate, len(grads)),
        grid=(held, 2),
        out_shape=(jax.ShapeDtypeStruct(arrays[0].shape, F32),) * 3,
        in_specs=[pl.BlockSpec((tile, width), grad_at)] * len(grads) + [block] * 3,
        out_specs=(block,) * 3,
        compiler_params=pltpu.CompilerParams(vmem_limit_bytes=32 * 2**20),
        cost_estimate=lasting(6),
        name="expert_steps",
    )(*grads, *arrays)


def last_steps(grads, ends, arrays):
    whole = pl.BlockSpec()
    return pl.pallas_call(
        steps_kernel,
        out_shape=(
            jax.ShapeDtypeStruct(ends[0].shape, BF16),
            jax.ShapeDtypeStruct(ends[0].shape, F32),
        )
        + tuple(jax.ShapeDtypeStruct(array.shape, F32) for array in arrays),
        in_specs=[whole] * (13 + len(arrays)),
        out_specs=(whole,) * (2 + len(arrays)),
        compiler_params=pltpu.CompilerParams(vmem_limit_bytes=56 * 2**20),
        cost_estimate=lasting(10),
        name="last_steps",
    )(*grads, *ends, *arrays)


def shared_kernel(
    x_ref, g_ref, up_ref, down_ref, out_ref, dx_ref, *refs
):
    count = (len(refs) - 9) // 2
    up_outs, down_outs, refs = refs[:count], refs[count : 2 * count], refs[2 * count :]
    hid_ref, dpre_ref, turned, hid_turned, up_grad, down_grad, up_came, down_came, sems = refs
    row, col = lax.axis_index("row"), lax.axis_index("col")
    barrier = pltpu.get_barrier_semaphore()
    pl.semaphore_signal(barrier, inc=1, device_id={"row": 1 - row}, device_id_type=MESH_ID)
    x, g = x_ref[...], g_ref[...]
    pre = dot_f32(x, up_ref[...])
    asked = dot_t(g, down_ref[...])
    half = down_ref.shape[0]
    for part in range(half // 128):
        lanes = slice(128 * part, 128 * (part + 1))
        upper = slice(half + 128 * part, half + 128 * (part + 1))
        gate, up, want = pre[:, lanes], pre[:, upper], asked[:, lanes]
        sig = jax.nn.sigmoid(gate)
        act = gate * sig
        hid_ref[:, lanes] = (act * up).astype(BF16)
        dpre_ref[:, lanes] = (want * up * (sig * (1.0 + gate * (1.0 - sig)))).astype(BF16)
        dpre_ref[:, upper] = (want * act).astype(BF16)
    turned[...] = x.T
    hid_turned[...] = hid_ref[...].T
    pl.semaphore_wait(barrier, 1)
    copies = []
    for number, (left, right, grad, came) in enumerate(
        ((turned, dpre_ref, up_grad, up_came), (hid_turned, g_ref, down_grad, down_came))
    ):
        size, _, rows, _ = grad.shape
        pairs = 2 if size % 2 == 0 else 1
        for chunk in range(0, size, pairs):
            found = dot_f32(left[2 * rows * chunk : 2 * rows * (chunk + pairs), :], right[...]).astype(BF16)
            for at in range(pairs):
                for half_at in range(2):
                    start = (2 * at + half_at) * rows
                    grad[chunk + at, half_at] = found[start : start + rows]
        copies.append(
            pltpu.make_async_remote_copy(
                src_ref=grad.at[:, 1 - row],
                dst_ref=came,
                send_sem=sems.at[number],
                recv_sem=sems.at[2 + number],
                device_id={"row": 1 - row},
                device_id_type=MESH_ID,
            )
        )
        copies[-1].start()
    out_ref[...] = dot_f32(hid_ref[...], down_ref[...])
    dx_ref[...] = dot_t(dpre_ref[...], up_ref[...])
    for copy, grad, came, outs in zip(copies, (up_grad, down_grad), (up_came, down_came), (up_outs, down_outs)):
        copy.wait()
        size, _, rows, _ = grad.shape
        part = rows // count
        for chunk in range(size):
            total = (grad[chunk, row].astype(F32) + came[chunk].astype(F32)).astype(BF16)
            for place in range(count):
                mine = total[place * part : (place + 1) * part]
                for by in range(count):
                    @pl.when(place == (col + by) % count)
                    def _():
                        outs[by][chunk] = mine


def shared_expert(tokens, cotangents, up, down, shape):
    size, columns = shape["dp"], shape["col"]
    rows, width = tokens.shape
    up_rows, down_rows = (array.shape[0] // (2 * columns * size) for array in (up, down))
    results = pl.pallas_call(
        shared_kernel,
        out_shape=(jax.ShapeDtypeStruct((rows, width), F32),) * 2
        + (jax.ShapeDtypeStruct((size, up_rows, up.shape[1]), BF16),) * columns
        + (jax.ShapeDtypeStruct((size, down_rows, width), BF16),) * columns,
        in_specs=[VM] * 4,
        out_specs=(VM,) * (2 + 2 * columns),
        scratch_shapes=[
            pltpu.VMEM((rows, down.shape[0]), BF16),
            pltpu.VMEM((rows, up.shape[1]), BF16),
            pltpu.VMEM((width, rows), BF16),
            pltpu.VMEM((down.shape[0], rows), BF16),
            pltpu.VMEM((size, 2, columns * up_rows, up.shape[1]), BF16),
            pltpu.VMEM((size, 2, columns * down_rows, width), BF16),
            pltpu.VMEM((size, columns * up_rows, up.shape[1]), BF16),
            pltpu.VMEM((size, columns * down_rows, width), BF16),
            pltpu.SemaphoreType.DMA((4,)),
        ],
        compiler_params=pltpu.CompilerParams(
            collective_id=6, has_side_effects=True, vmem_limit_bytes=58 * 2**20
        ),
        cost_estimate=lasting(20),
        name="shared_expert",
    )(tokens, cotangents, up, down)
    return results[0], results[1], results[2 : 2 + columns], results[2 + columns :]


def expert_block(own, x_ref, g_ref, named, up, down, router_ref, hid_ref, dpre_ref, mix_ref, dx_ref):
    x, g = x_ref[...], g_ref[...]
    logits = dot_f32(x, router_ref[...])
    high = jnp.max(jnp.where(named > 0, logits, -1e30), axis=1, keepdims=True)
    raised = jnp.where(named > 0, jnp.exp(logits - high), 0.0)
    gates = raised / jnp.sum(raised, axis=1, keepdims=True)
    rows = x.shape[0]
    lane = lax.broadcasted_iota(jnp.int32, (rows, 128), 1)
    weights = [
        jnp.sum(jnp.where(lane == own + part, gates, 0.0), axis=1, keepdims=True)
        for part in range(EXP_DEV)
    ]
    half = down.shape[0]
    pre = dot_f32(x, up)
    asked = dot_t(g, down)
    totals = [jnp.zeros((rows, 128), F32) for part in range(EXP_DEV)]
    for part in range(half // 128):
        which = 128 * part // FF_E
        at = 128 * part + FF_E * which
        lanes = slice(128 * part, 128 * (part + 1))
        lower, upper = slice(at, at + 128), slice(at + FF_E, at + FF_E + 128)
        gate, upper_pre, want = pre[:, lower], pre[:, upper], asked[:, lanes]
        sig = jax.nn.sigmoid(gate)
        act = gate * sig
        hidden = act * upper_pre
        totals[which] = totals[which] + hidden * want
        hid_ref[:, lanes] = (weights[which] * hidden).astype(BF16)
        dact = weights[which] * want
        dpre_ref[:, lower] = (dact * upper_pre * (sig * (1.0 + gate * (1.0 - sig)))).astype(BF16)
        dpre_ref[:, upper] = (dact * act).astype(BF16)
    mix_ref[...] = dot_f32(hid_ref[...], down).astype(BF16)
    dx_ref[:, :MODEL_WIDTH] = dot_t(dpre_ref[...], up).astype(BF16)
    sent = jnp.zeros((rows, 128), F32)
    for part in range(EXP_DEV):
        gate_grad = jnp.sum(totals[part], axis=1, keepdims=True)
        coarse = gate_grad.astype(BF16).astype(F32)
        sent = jnp.where(lane == own + part, coarse, sent)
        sent = jnp.where(lane == own + part + REST_AT, gate_grad - coarse, sent)
    dx_ref[:, MODEL_WIDTH:] = sent.astype(BF16)


def expert_kernel(
    size, columns, own_ref, g_ref, mask_ref, router_hbm, *refs
):
    places = 2 * columns
    up_parts, down_parts, kept_ref, refs = (
        refs[:places], refs[places : 2 * places], refs[2 * places], refs[2 * places + 1 :]
    )
    outs, (full_ref, g_now), stages, (up_ref, down_ref, router_ref) = (
        refs[:4], refs[4:6], refs[6:10], refs[10:13]
    )
    send_sem, recv_sem, local_sem, in_sem, out_sem, weight_sem = refs[13:]
    grid = Grid(size)
    me, z, x = grid.me, grid.z, grid.x
    barrier = pltpu.get_barrier_semaphore()
    grid.greet(barrier)
    pl.semaphore_wait(barrier, grid.count)

    def push(chunk, way, source=None):
        return pltpu.make_async_remote_copy(
            src_ref=full_ref.at[chunk] if source is None else source,
            dst_ref=full_ref.at[chunk],
            send_sem=send_sem.at[way, chunk],
            recv_sem=recv_sem.at[chunk],
            device_id={"dp": me + grid.steps[way]},
            device_id_type=MESH_ID,
        )

    def place(number):
        if grid.across == 2:
            even, first, last = 1 - number % 2, 1 - jnp.minimum(number, 1), number // 7
            step = (1 - even) * ((number + 1) // 2 - last) + even * (number // 2 - 1 + first)
            side = even * (1 - first) + last
        else:
            step, side = number % grid.deep, number // grid.deep
        return block_at(step, side)

    def block_at(step, side):
        zc = near_first(z, step, grid.deep)
        xc = near_first(x, side, grid.across)
        same = xc == x
        ways = (same & (zc >= z), same & (zc <= z), xc >= x, xc <= x)
        return zc * grid.across + xc, [way & there for way, there in zip(ways, grid.exists)]

    for way in range(4):
        @pl.when(grid.exists[way])
        def _():
            push(me, way, own_ref).start()
    row, col = lax.axis_index("row"), lax.axis_index("col")
    weights = [pltpu.make_async_copy(router_hbm, router_ref, weight_sem.at[2 * places])]
    for number in range(places):
        whose = row + (number // columns) * (1 - 2 * row)
        there = whose * columns + (col - number % columns + columns) % columns
        weights.append(
            pltpu.make_async_copy(up_parts[number], up_ref.at[there], weight_sem.at[number])
        )
        weights.append(
            pltpu.make_async_copy(
                down_parts[number], down_ref.at[:, there], weight_sem.at[places + number]
            )
        )
    for copy in weights:
        copy.start()
    keep = pltpu.make_async_copy(own_ref, full_ref.at[me], in_sem.at[1])
    keep.start()

    def leave(number, chunk):
        return [
            pltpu.make_async_copy(stage.at[number % 2], out.at[chunk], out_sem.at[place_in, number % 2])
            for place_in, (stage, out) in enumerate(zip(stages, outs))
        ]

    def work(number, _):
        chunk, onward = place(number)
        bring = pltpu.make_async_copy(g_ref.at[chunk], g_now, in_sem.at[0])
        bring.start()

        def pass_on(chunk, onward):
            push(chunk, 0).wait_recv()
            for way in range(4):
                @pl.when(onward[way])
                def _():
                    push(chunk, way).start()

        if grid.across == 2:
            inner = (z * (3 - z)) // 2
            for step, when in ((1, number == 1), (2, number == 3 - 2 * inner), (3, number == 5 - 2 * inner)):
                @pl.when(when)
                def _():
                    pass_on(*block_at(step, 0))

            @pl.when((number > 0) & (chunk % grid.across != x))
            def _():
                push(chunk, 0).wait_recv()
        else:
            @pl.when(number > 0)
            def _():
                pass_on(chunk, onward)

        @pl.when(number == 0)
        def _():
            keep.wait()
            for copy in weights:
                copy.wait()

        pltpu.make_async_copy(full_ref.at[chunk], kept_ref.at[chunk], local_sem.at[chunk]).start()

        @pl.when(number > 1)
        def _():
            for copy in leave(number, place(number - 2)[0]):
                copy.wait()

        bring.wait()
        experts_named = mask_ref[chunk].astype(F32)
        rest = jnp.zeros((128 - experts_named.shape[0], experts_named.shape[1]), F32)
        named = jnp.concatenate([experts_named, rest], axis=0).T
        expert_block(
            EXP_DEV * me, full_ref.at[chunk], g_now, named,
            up_ref[...].reshape(-1, up_ref.shape[2]), down_ref[...].reshape(-1, down_ref.shape[3]), router_ref,
            *[stage.at[number % 2] for stage in stages]
        )
        for copy in leave(number, chunk):
            copy.start()
        return 0

    lax.fori_loop(0, size, work, 0)
    for number in (size - 2, size - 1):
        for copy in leave(number, place(number)[0]):
            copy.wait()

    def finish(number, _):
        chunk, onward = place(number)
        pltpu.make_async_copy(full_ref.at[chunk], kept_ref.at[chunk], local_sem.at[chunk]).wait()
        for way in range(4):
            @pl.when(onward[way])
            def _():
                push(chunk, way).wait_send()
        return 0

    lax.fori_loop(0, size, finish, 0)


def experts(tokens, cotangents, masks, up_parts, down_parts, router, shape):
    size, columns = shape["dp"], shape["col"]
    places = 2 * columns
    rows, width = tokens.shape
    hidden = places * EXP_DEV * down_parts[0].shape[1]
    wide = width + 128
    wides = (hidden, 2 * hidden, width, wide)
    results = pl.pallas_call(
        functools.partial(expert_kernel, size, columns),
        out_shape=tuple(
            jax.ShapeDtypeStruct((size, rows, column), BF16) for column in (width,) + wides
        ),
        in_specs=[ANY, ANY, VM] + [ANY] * (1 + 2 * places),
        out_specs=(ANY,) * 5,
        scratch_shapes=[pltpu.VMEM((size, rows, width), BF16), pltpu.VMEM((rows, width), BF16)]
        + [pltpu.VMEM((2, rows, column), BF16) for column in wides]
        + [
            pltpu.VMEM((places,) + up_parts[0].shape, BF16),
            pltpu.VMEM((EXP_DEV, places) + down_parts[0].shape[1:], BF16),
            pltpu.VMEM(router.shape, BF16),
            pltpu.SemaphoreType.DMA((4, size)),
            pltpu.SemaphoreType.DMA((size,)),
            pltpu.SemaphoreType.DMA((size,)),
            pltpu.SemaphoreType.DMA((2,)),
            pltpu.SemaphoreType.DMA((4, 2)),
            pltpu.SemaphoreType.DMA((2 * places + 1,)),
        ],
        compiler_params=pltpu.CompilerParams(
            collective_id=4, has_side_effects=True, vmem_limit_bytes=56 * 2**20
        ),
        cost_estimate=lasting(85),
        name="experts",
    )(tokens, cotangents.reshape(size, rows, width), masks.reshape(size, -1, rows), router, *up_parts, *down_parts)
    return [result.reshape(size * rows, -1) for result in results]


def rms_scale(values):
    return lax.rsqrt(jnp.mean(values * values, axis=-1, keepdims=True) + 1e-05)


def rms_back(values, scale, gain, grad_normed):
    weighted = grad_normed * gain[None, :]
    grad_values = scale * weighted - values * scale**3 * jnp.mean(
        weighted * values, axis=-1, keepdims=True
    )
    gain_grad = jnp.sum(grad_normed * values * scale, axis=0)
    return (grad_values, gain_grad)


def silu_gate(pre_values):
    half_size = pre_values.shape[-1] // 2
    return jax.nn.silu(pre_values[..., :half_size]) * pre_values[..., half_size:]


def silu_gate_back(pre_values, grad):
    return jax.vjp(silu_gate, pre_values)[1](grad)[0]


ALL = ("dp", "row", "col")


def gather_dp(values):
    return lax.all_gather(values, "dp", axis=0, tiled=True)


def scatter_dp(values):
    return lax.psum_scatter(values, "dp", scatter_dimension=0, tiled=True)


def body(
    shape,
    hidden_in, segment_ids, routes, out_grad,
    vectors, vectors_first, vectors_second,
    in_weight, in_weight_first, in_weight_second,
    step_weight, step_weight_first, step_weight_second,
    out_weight, out_weight_first, out_weight_second,
    state_weight, state_weight_first, state_weight_second,
    router, router_first, router_second,
    shared_up, shared_up_first, shared_up_second,
    shared_down, shared_down_first, shared_down_second,
    expert_gate_up, expert_gate_up_first, expert_gate_up_second,
    expert_down, expert_down_first, expert_down_second,
):
    dp = lax.axis_index("dp")
    data_count = lax.axis_size("dp")
    seq_devices = lax.axis_size("row") * lax.axis_size("col")
    local_heads = in_weight.shape[1]
    width = 64 * local_heads
    head_start = lax.axis_index(("row", "col")) * local_heads
    own_tokens = hidden_in.shape[1]
    experts_all = router.shape[1]
    rows_dp = in_weight.shape[0]
    seq_columns = shape["col"]
    residual = hidden_in[0].astype(F32)
    count = vectors.shape[0]
    lines = -(-count // 1024) * 8
    vector_rows = jnp.pad(vectors, (0, lines * 128 - count)).reshape(lines, 128)
    gain_one = vectors[0:MODEL_WIDTH]
    gain_two = vectors[MODEL_WIDTH : 2 * MODEL_WIDTH]

    scale_one = rms_scale(residual)
    route_ids = routes[0]
    chosen = (
        route_ids[:, :, None] == jnp.arange(experts_all, dtype=jnp.int32)[None, None, :]
    ).any(axis=1)
    grad_low = out_grad[0]
    (
        mixer_full, step_full, out_full, masks, shared_up_full, shared_down_full, small_full, normed_all,
        up_local, down_parts,
    ) = gather_start(
        hidden_in[0],
        vector_rows,
        in_weight.transpose(1, 0, 2),
        step_weight.T,
        out_weight.reshape(width, -1),
        shared_up,
        shared_down,
        state_weight,
        router.T,
        route_ids.T,
        expert_gate_up,
        expert_down,
        shape,
    )
    mixer_full, step_full, out_full, small_full, normed_all, segment_ids, grad_gone, up_local, down_parts = (
        lax.optimization_barrier(
            (mixer_full, step_full, out_full, small_full, normed_all, segment_ids, grad_low, up_local, down_parts)
        )
    )
    grad_all = gather_dp(grad_gone)
    up_parts = [up_local] + [shift(up_local, "col", by) for by in range(1, seq_columns)]
    state_step = jnp.concatenate([small_full[:, : 2 * STATE], step_full], axis=1)

    seg_rows = segment_ids[0].astype(F32).reshape(-1, 1, BLK)
    proj = dot_f32(normed_all, mixer_full).astype(BF16)
    ss = dot_f32(normed_all, state_step)
    valued, squares_part, kept, params = mixer_forward(proj, ss, seg_rows, vector_rows, seq_columns)
    partial_out = dot_t(valued, out_full).astype(BF16)
    partial_out, up_parts = lax.optimization_barrier((partial_out, up_parts))
    proj_out = scatter_rc(partial_out)
    other_row = lambda parts: parts + [shift(part, "row", 1) for part in parts]
    up_parts, down_parts = other_row(up_parts), other_row(down_parts)
    squares = scatter_squares(squares_part)[:, 0]
    scale_two = lax.rsqrt(squares / INNER + 1e-05)
    residual_two = residual + scale_two[:, None] * proj_out
    scale_three = rms_scale(residual_two)
    normed_two = (residual_two * scale_three * gain_two[None, :]).astype(BF16)

    router_wide = small_full[:, 2 * STATE :]
    router_full = router_wide[:, :experts_all]
    shared_out, shared_dx, shared_up_sums, shared_down_sums = shared_expert(
        normed_two, grad_low, shared_up_full, shared_down_full, shape
    )
    normed_two, grad_all, shared_dx, shared_out = lax.optimization_barrier(
        (normed_two, grad_all, shared_dx, shared_out)
    )
    from_columns = lambda parts: [
        shift(parts[by], "col", by) for by in range(1, seq_columns)
    ]
    shared_up_came, shared_down_came = from_columns(shared_up_sums), from_columns(shared_down_sums)
    tokens_all, hidden_low, pre_grad, mixed, rows_grad = experts(
        normed_two, grad_all, masks, up_parts, down_parts, router_wide, shape
    )
    logits = dot_f32(normed_two, router_full)
    gate_all = jax.nn.softmax(jnp.where(chosen, logits, -jnp.inf), axis=-1)
    rows_grad, shared_up_came, shared_down_came = lax.optimization_barrier(
        (rows_grad, shared_up_came, shared_down_came)
    )
    add_all = lambda own, came: sum([part.astype(F32) for part in came], own.astype(F32)).astype(BF16)
    shared_up_part = add_all(shared_up_sums[0], shared_up_came).reshape(-1, 2 * FF_S)
    shared_down_part = add_all(shared_down_sums[0], shared_down_came).reshape(-1, MODEL_WIDTH)
    routed_grad, up_grad, down_grad = scatter_blocks(
        rows_grad, tokens_all, pre_grad, hidden_low, grad_all, shape
    )
    routed_grad, mixed = lax.optimization_barrier((routed_grad, mixed))
    mixture = scatter_dp(mixed)
    gate_grad = (
        routed_grad[:, MODEL_WIDTH : MODEL_WIDTH + experts_all]
        + routed_grad[:, MODEL_WIDTH + REST_AT : MODEL_WIDTH + REST_AT + experts_all]
    )
    cotangent = grad_low.astype(F32)
    normed_two_grad = shared_dx + routed_grad[:, :MODEL_WIDTH]
    logits_grad = gate_all * (gate_grad - jnp.sum(gate_all * gate_grad, axis=1, keepdims=True))
    logits_low = jnp.where(chosen, logits_grad, 0.0).astype(BF16)
    normed_two_grad = normed_two_grad + dot_t(logits_low, router_full)
    router_grad = dot_tn(normed_two, logits_low)
    residual_two_grad, gain_two_grad = rms_back(
        residual_two, scale_three, gain_two, normed_two_grad
    )
    residual_two_grad = residual_two_grad + cotangent
    proj_out_grad = (residual_two_grad * scale_two[:, None]).astype(BF16)
    squares_grad = (
        jnp.sum(residual_two_grad * proj_out, axis=1) * -0.5 * scale_two**3 / INNER
    )
    squares_high = squares_grad.astype(BF16)
    squares_rest = (squares_grad - squares_high.astype(F32)).astype(BF16)
    riding = jnp.pad(jnp.stack([squares_high, squares_rest], axis=1), ((0, 0), (0, 126)))
    riders = jnp.concatenate([proj_out_grad, riding], axis=1)
    riders, up_grad, down_grad = lax.optimization_barrier((riders, up_grad, down_grad))
    riders = gather_rc(riders)
    proj_grad_all = riders[:, :MODEL_WIDTH]
    squares_grad_all = jnp.sum(riders[:, MODEL_WIDTH:].astype(F32), axis=1, keepdims=True)
    proj_grad_all, up_grad, down_grad = lax.optimization_barrier((proj_grad_all, up_grad, down_grad))
    up_came, down_came = from_columns(up_grad), from_columns(down_grad)

    valued_grad = dot_f32(proj_grad_all, out_full).astype(BF16)
    out_grad_t = dot_tn(proj_grad_all, valued).astype(BF16)
    proj_grad, ss_grad, vector_grad = mixer_backward(
        proj, ss, seg_rows, params, valued_grad, squares_grad_all, kept, lines, seq_columns
    )
    normed_part = dot_t(proj_grad, mixer_full) + dot_t(ss_grad, state_step)
    gain_one_grad = jnp.sum(normed_part * normed_all.astype(F32), axis=0) / gain_one
    router_wide = jnp.pad(
        router_grad, ((0, 0), (2 * STATE + ROUTER_AT, 128 - ROUTER_AT - experts_all))
    )
    mixer_grad = dot_tn(normed_all, proj_grad).astype(BF16)
    small_grad = (dot_tn(normed_all, ss_grad) + router_wide).astype(BF16)
    gains = jnp.concatenate([gain_one_grad, gain_two_grad]).reshape(-1, 128)
    vector_lines = vector_grad + jnp.pad(gains, ((0, lines - gains.shape[0]), (0, 0)))
    (
        mixer_total, small_rows, out_total, shared_up_total, shared_down_total,
        vector_total, small_total, normed_grad,
    ) = scatter_end(
        (mixer_grad, small_grad, out_grad_t, shared_up_part, shared_down_part),
        vector_lines,
        normed_part.astype(BF16),
        shape,
    )
    vector_total = vector_total.reshape(-1)[:count]
    heads_first = lambda array: array.transpose(1, 0, 2)
    flat_out = lambda array: array.reshape(width, -1)
    mixer_total, up_own, down_own = lax.optimization_barrier((mixer_total, up_grad[0], down_grad[0]))
    new_up = expert_steps(
        [up_own, *up_came],
        (expert_gate_up, expert_gate_up_first, expert_gate_up_second),
        MODEL_WIDTH ** (-0.5),
        False,
    )
    new_down = expert_steps(
        [down_own, *down_came], (expert_down, expert_down_first, expert_down_second), FF_E ** (-0.5), True
    )
    hidden_out, input_grad, *news = last_steps(
        (
            mixer_total, out_total, shared_up_total, shared_down_total, small_total,
            small_rows,
        ),
        (
            residual_two, mixture, shared_out,
            hidden_in[0], gain_one[None, :], normed_grad, residual_two_grad,
        ),
        (
            *map(heads_first, (in_weight, in_weight_first, in_weight_second)),
            step_weight.T, step_weight_first.T, step_weight_second.T,
            *map(flat_out, (out_weight, out_weight_first, out_weight_second)),
            state_weight, state_weight_first, state_weight_second,
            router.T, router_first.T, router_second.T,
            shared_up, shared_up_first, shared_up_second,
            shared_down, shared_down_first, shared_down_second,
        ),
    )
    return (
        hidden_out[None],
        input_grad[None],
        *adam_step(vectors, vector_total, vectors_first, vectors_second, 0.3, 0.0),
        *map(heads_first, news[0:3]),
        *[array.T for array in news[3:6]],
        *[array.reshape(out_weight.shape) for array in news[6:9]],
        *news[9:12],
        *[array.T for array in news[12:15]],
        *news[15:],
        *new_up,
        *new_down,
    )


def solution(mesh):
    tokens = P("dp", ("row", "col"), None)
    by_head = P("dp", ("row", "col"))
    out_spec = P(("row", "col"), None, "dp")
    flat = P(ALL, None)
    weights = (
        (P(),) * 3
        + (tokens,) * 3
        + (by_head,) * 3
        + (out_spec,) * 3
        + (flat,) * 12
        + (tokens,) * 6
    )
    return jax.shard_map(
        functools.partial(body, dict(mesh.shape)),
        mesh=mesh,
        in_specs=(tokens, P("dp", None), tokens, tokens) + weights,
        out_specs=(tokens, tokens) + weights,
        check_vma=False,
    )
```
